32 devices in a mesh: replica: 2 (over y), shard: 8 (over z, x), ctx: 2 (over core).
Axes of the slice: x: 2, y: 2, z: 4, core: 2. Of those that a mesh axis runs over, the one named last changes fastest.
Arguments:
- layer_input: bfloat16 [64, 512, 1024], P(('replica', 'shard'), 'ctx'), may hold values from -6 to 6
- segment_ids: int32 [64, 512], P(('replica', 'shard')), may hold values from 0 to 4, as said below
- out_cotangent: bfloat16 [64, 512, 1024], P(('replica', 'shard'), 'ctx'), may hold values from -6 to 6
- attn_master: float32 [4, 1024, 1024], P(None, 'shard')
- inner_master: float32 [1024, 4096], P('shard'), may hold values from -0.1875 to 0.1875
- outer_master: float32 [4096, 1024], P('shard'), may hold values from -0.09375 to 0.09375
- vector_master: float32 [12, 1024], P(None, 'shard')
- attn_moment: float32 [4, 1024, 1024], P(None, 'shard')
- inner_moment: float32 [1024, 4096], P('shard')
- outer_moment: float32 [4096, 1024], P('shard')
- vector_moment: float32 [12, 1024], P(None, 'shard')
- attn_square: float32 [4, 1024, 1024], P(None, 'shard'), as said below
- inner_square: float32 [1024, 4096], P('shard'), as said below
- outer_square: float32 [4096, 1024], P('shard'), as said below
- vector_square: float32 [12, 1024], P(None, 'shard'), as said below
Outputs:
- layer_output: bfloat16 [64, 512, 1024], P(('replica', 'shard'), 'ctx')
- input_grad: float32 [64, 512, 1024], P(('replica', 'shard'), 'ctx')
- attn_moment_new: float32 [4, 1024, 1024], P(None, 'shard')
- inner_moment_new: float32 [1024, 4096], P('shard')
- outer_moment_new: float32 [4096, 1024], P('shard')
- vector_moment_new: float32 [12, 1024], P(None, 'shard')
- attn_square_new: float32 [4, 1024, 1024], P(None, 'shard')
- inner_square_new: float32 [1024, 4096], P('shard')
- outer_square_new: float32 [4096, 1024], P('shard')
- vector_square_new: float32 [12, 1024], P(None, 'shard')
- attn_new: float32 [4, 1024, 1024], P(None, 'shard')
- inner_new: float32 [1024, 4096], P('shard')
- outer_new: float32 [4096, 1024], P('shard')
- vector_new: float32 [12, 1024], P(None, 'shard')
- attn_low: bfloat16 [4, 1024, 1024], P(None, 'shard')
- inner_low: bfloat16 [1024, 4096], P('shard')
- outer_low: bfloat16 [4096, 1024], P('shard')
- vector_low: bfloat16 [12, 1024], P(None, 'shard')
The draws below stay inside these ranges and needn't reach their ends.
Inputs may be any that keep to these rules, and one draw needn't show every extreme that they name: `segment_ids`: along each sequence the ids never fall, start at 0 and end at 4; positions 192 to 320 carry one id. `attn_square`: every entry is positive. `inner_square`: every entry is positive. `outer_square`: every entry is positive. `vector_square`: every entry is positive.
All inputs are finite; a program needn't handle non-finite values.
Results may differ from the reference program's by a relative error of at most 0.024.
Values may be sent and summed in bfloat16 or wider, within the bound.
No kernel may reach another device: no remote copies, remote signals or barrier semaphores. Data moves between devices by JAX's collectives and lax.ppermute only.
A program may use at most 320 MiB of HBM per device.

```python
import jax
import jax.numpy as jnp
from jax import lax

D = 1024
FF = 4096
H = 16
HD = 64
LEN = 512
STEP = 5
NSEQ = 64
TOKENS = 32768


def spread_draw(key, shape, scale):
    base = jax.random.normal(key, shape, jnp.float32)
    return base * scale


def square_draw(key, shape, scale):
    factor = jnp.exp(jax.random.uniform(key, shape, jnp.float32, -0.356675, 0.993252))
    return factor * scale * scale


def attn_scale():
    return jnp.array([0.5, 0.5, 0.45, 0.125], jnp.float32).reshape(4, 1, 1) * jnp.sqrt(jnp.float32(TOKENS))


def draw_segment_ids(key, part):
    key = jax.random.fold_in(key, 1)
    window = 2 * (LEN // 8)
    lower = LEN // 2 - LEN // 8
    cuts = jax.random.randint(key, (NSEQ, 4), 1, LEN - window)
    placed = jnp.where(cuts <= lower, cuts, cuts + window)
    position = jnp.arange(LEN, dtype=jnp.int32)
    return jnp.sum((position[None, None, :] >= placed[:, :, None]).astype(jnp.int32), axis=1).astype(jnp.int32)


def draw_attn_master(key, part):
    key = jax.random.fold_in(key, 2)
    scale = jnp.array([1.0, 1.0, 1.0, 5.0], jnp.float32).reshape(4, 1, 1) / jnp.sqrt(jnp.float32(D))
    return spread_draw(key, (4, D, D), scale)


def draw_vector_master(key, part):
    key = jax.random.fold_in(key, 3)
    base = spread_draw(key, (12, D), 1.0)
    gains = jnp.zeros((12, 1), jnp.float32).at[3, 0].set(1.0).at[6, 0].set(1.0)
    return gains + base * jnp.where(gains > 0.5, 0.1, 0.2)


def draw_attn_moment(key, part):
    key = jax.random.fold_in(key, 4)
    return spread_draw(key, (4, D, D), attn_scale())


def draw_inner_moment(key, part):
    key = jax.random.fold_in(key, 5)
    return spread_draw(key, (D, FF), 0.2 * jnp.sqrt(jnp.float32(TOKENS)))


def draw_outer_moment(key, part):
    key = jax.random.fold_in(key, 6)
    return spread_draw(key, (FF, D), 0.3 * jnp.sqrt(jnp.float32(TOKENS)))


def draw_vector_moment(key, part):
    key = jax.random.fold_in(key, 7)
    return spread_draw(key, (12, D), 0.5 * jnp.sqrt(jnp.float32(TOKENS)))


def draw_attn_square(key, part):
    key = jax.random.fold_in(key, 8)
    return square_draw(key, (4, D, D), 0.8165 * attn_scale())


def draw_inner_square(key, part):
    key = jax.random.fold_in(key, 9)
    return square_draw(key, (D, FF), 0.8165 * 0.2 * jnp.sqrt(jnp.float32(TOKENS)))


def draw_outer_square(key, part):
    key = jax.random.fold_in(key, 10)
    return square_draw(key, (FF, D), 0.8165 * 0.3 * jnp.sqrt(jnp.float32(TOKENS)))


def draw_vector_square(key, part):
    key = jax.random.fold_in(key, 11)
    return square_draw(key, (12, D), 0.8165 * 0.5 * jnp.sqrt(jnp.float32(TOKENS)))


def block_levels(own_key, shape, shards, low, largest):
    level = 1.0
    for axis_at, shards_of in shards:
        steps = jax.random.uniform(jax.random.fold_in(jax.random.fold_in(own_key, 6), axis_at), (shards_of,), jnp.float32, low / len(shards), largest / len(shards))
        level = level * jnp.repeat(jnp.exp(steps), shape[axis_at] // shards_of).reshape((-1,) + (1,) * (len(shape) - 1 - axis_at))
    return level


def scatter_about(key, extent, spread, most, shards=(), held_as=jnp.bfloat16):
    factor_of = block_levels(key, extent, shards, -0.22, 0.18) if shards else 1.0
    values = jax.random.normal(key, extent, jnp.float32) * spread * factor_of
    return jnp.minimum(jnp.maximum(values, -most), most).astype(held_as)


def setup_inputs(seed: int = 0) -> dict:
    seeds = jax.random.split(jax.random.key(seed), 16)
    layer_input = scatter_about(seeds[0], (NSEQ, LEN, D), 1.0, 6.0, ((0, 16), (1, 2)))
    segment_ids = draw_segment_ids(jax.random.fold_in(seeds[15], 71), 0)
    out_cotangent = scatter_about(seeds[2], (NSEQ, LEN, D), 1.0, 6.0, ((0, 16), (1, 2)))
    attn_master = draw_attn_master(jax.random.fold_in(seeds[15], 71), 0)
    inner_master = scatter_about(seeds[4], (D, FF), D ** -0.5, 0.1875, ((0, 8),), jnp.float32)
    outer_master = scatter_about(seeds[5], (FF, D), FF ** -0.5, 0.09375, ((0, 8),), jnp.float32)
    vector_master = draw_vector_master(jax.random.fold_in(seeds[15], 71), 0)
    attn_moment = draw_attn_moment(jax.random.fold_in(seeds[15], 71), 0)
    inner_moment = draw_inner_moment(jax.random.fold_in(seeds[15], 71), 0)
    outer_moment = draw_outer_moment(jax.random.fold_in(seeds[15], 71), 0)
    vector_moment = draw_vector_moment(jax.random.fold_in(seeds[15], 71), 0)
    attn_square = draw_attn_square(jax.random.fold_in(seeds[15], 71), 0)
    inner_square = draw_inner_square(jax.random.fold_in(seeds[15], 71), 0)
    outer_square = draw_outer_square(jax.random.fold_in(seeds[15], 71), 0)
    vector_square = draw_vector_square(jax.random.fold_in(seeds[15], 71), 0)
    return dict(layer_input=layer_input, segment_ids=segment_ids, out_cotangent=out_cotangent, attn_master=attn_master, inner_master=inner_master, outer_master=outer_master, vector_master=vector_master, attn_moment=attn_moment, inner_moment=inner_moment, outer_moment=outer_moment, vector_moment=vector_moment, attn_square=attn_square, inner_square=inner_square, outer_square=outer_square, vector_square=vector_square)


EPS_NORM = 1e-05
BETA_ONE = 0.5
BETA_TWO = 0.6
RATE_MATRIX = 0.02
RATE_VECTOR = 0.1
DECAY = 0.01
EPS_ADAM = 1e-06

@jax.custom_vjp
def low(v):
    return lax.optimization_barrier(v.astype(jnp.bfloat16)).astype(jnp.float32)

@jax.custom_vjp
def low_back(v):
    return v

def low_keep(v):
    return (low(v), None)

def low_pass(kept, grad):
    return (grad,)

def back_keep(v):
    return (v, None)

def back_low(kept, grad):
    return (low(grad),)
low.defvjp(low_keep, low_pass)
low_back.defvjp(back_keep, back_low)

def rounded(value):
    return low(low_back(value))

def matmul(left, right):
    return jnp.dot(left, right, precision=lax.Precision.HIGHEST, preferred_element_type=jnp.float32)

def normalize(resid, gain, shift):
    centre = resid - lax.optimization_barrier(jnp.mean(resid, -1, keepdims=True))
    return centre * lax.rsqrt(lax.optimization_barrier(jnp.mean(centre * centre, -1, keepdims=True)) + EPS_NORM) * gain + shift

def attend(block):
    query, keys, values, seg = block
    raw = jnp.einsum('bqhd,bkhd->bhqk', query, keys, precision=lax.Precision.HIGHEST)
    scaled = low_back(raw * HD ** (-0.5))
    same = seg[:, None, :, None] == seg[:, None, None, :]
    scores = jnp.where(same, scaled, -1e+30)
    top = lax.optimization_barrier(jnp.max(scores, -1, keepdims=True))
    expo = jnp.exp(scores - top)
    probs = rounded(expo / lax.optimization_barrier(jnp.sum(expo, -1, keepdims=True)))
    return jnp.einsum('bhqk,bkhd->bqhd', probs, values, precision=lax.Precision.HIGHEST)

def forward(inputs, attn, inner, outer, vector, segment_ids):
    attn_w = low(attn)
    inner_w = low(inner)
    outer_w = low(outer)
    vec = low(vector)
    rows = inputs.reshape(NSEQ * LEN, D)
    query = rounded(matmul(rows, attn_w[0]) + vec[0])
    keys = rounded(matmul(rows, attn_w[1]))
    values = rounded(matmul(rows, attn_w[2]) + vec[1])
    shape = (NSEQ // 8, 8, LEN, H, HD)
    mixed = lax.map(jax.checkpoint(attend), (query.reshape(shape), keys.reshape(shape), values.reshape(shape), segment_ids.reshape(NSEQ // 8, 8, LEN)))
    heads_out = rounded(mixed.reshape(NSEQ * LEN, D))
    branch = low_back(matmul(heads_out, attn_w[3]) + vec[2])
    hidden = normalize(rows + branch, vec[3], vec[4])
    hidden_low = rounded(hidden)
    pre_act = low_back(matmul(hidden_low, inner_w) + vec[8:].reshape(FF))
    active = rounded(jax.nn.gelu(pre_act, approximate=False))
    ffn_out = low_back(matmul(active, outer_w) + vec[5])
    result = normalize(hidden + ffn_out, vec[6], vec[7])
    return result.reshape(NSEQ, LEN, D)

def adamw(grad, moment, square, weight, rate):
    moment_new = BETA_ONE * moment + (1.0 - BETA_ONE) * grad
    square_new = BETA_TWO * square + (1.0 - BETA_TWO) * grad * grad
    stepped = moment_new / (1.0 - BETA_ONE ** STEP) / (jnp.sqrt(square_new / (1.0 - BETA_TWO ** STEP)) + EPS_ADAM)
    weight_new = weight - rate * (stepped + DECAY * weight)
    return (moment_new, square_new, weight_new)

def reference(layer_input, segment_ids, out_cotangent, attn_master, inner_master, outer_master, vector_master, attn_moment, inner_moment, outer_moment, vector_moment, attn_square, inner_square, outer_square, vector_square):
    inputs = layer_input.astype(jnp.float32)

    def run(x_in, attn, inner, outer, vector):
        return forward(x_in, attn, inner, outer, vector, segment_ids)
    result, pull = jax.vjp(run, inputs, attn_master, inner_master, outer_master, vector_master)
    grads = pull(out_cotangent.astype(jnp.float32))
    input_grad = grads[0]
    masters = (attn_master, inner_master, outer_master, vector_master)
    moments = (attn_moment, inner_moment, outer_moment, vector_moment)
    squares = (attn_square, inner_square, outer_square, vector_square)
    rates = (RATE_MATRIX, RATE_MATRIX, RATE_MATRIX, RATE_VECTOR)
    news = [adamw(grads[i + 1], moments[i], squares[i], masters[i], rates[i]) for i in range(4)]
    return (result.astype(jnp.bfloat16), input_grad, news[0][0], news[1][0], news[2][0], news[3][0], news[0][1], news[1][1], news[2][1], news[3][1], news[0][2], news[1][2], news[2][2], news[3][2], news[0][2].astype(jnp.bfloat16), news[1][2].astype(jnp.bfloat16), news[2][2].astype(jnp.bfloat16), news[3][2].astype(jnp.bfloat16))
```

```python
import jax
import jax.numpy as jnp
from jax import lax
from jax.sharding import PartitionSpec as P

HD = 64
STEP = 5
EVERY = ("shard", "replica", "ctx")


EPS_NORM = 1e-05
BETA_ONE = 0.5
BETA_TWO = 0.6
RATE_MATRIX = 0.02
RATE_VECTOR = 0.1
DECAY = 0.01
EPS_ADAM = 1e-06


def matmul(left, right):
    return jnp.dot(left, right, preferred_element_type=jnp.float32)


def contract_rows(left, right):
    return jnp.einsum("rd,re->de", left, right, preferred_element_type=jnp.float32)


def times_trans(left, right):
    return jnp.einsum("re,de->rd", left, right, preferred_element_type=jnp.float32)


def normalize(resid):
    centre = resid - jnp.mean(resid, -1, keepdims=True)
    scale = lax.rsqrt(jnp.mean(centre * centre, -1, keepdims=True) + EPS_NORM)
    return (centre * scale, scale)


def norm_back(grad, normed, scale):
    return scale * (
        grad
        - jnp.mean(grad, -1, keepdims=True)
        - normed * jnp.mean(grad * normed, -1, keepdims=True)
    )


def exact_gelu(value):
    return jax.nn.gelu(value, approximate=False)


def round_trip(value):
    return value.astype(jnp.bfloat16).astype(jnp.float32)


def adamw(grad, moment, square, weight, rate):
    moment_new = BETA_ONE * moment + (1.0 - BETA_ONE) * grad
    square_new = BETA_TWO * square + (1.0 - BETA_TWO) * grad * grad
    stepped = (
        moment_new
        / (1.0 - BETA_ONE**STEP)
        / (jnp.sqrt(square_new / (1.0 - BETA_TWO**STEP)) + EPS_ADAM)
    )
    weight_new = weight - rate * (stepped + DECAY * weight)
    return (moment_new, square_new, weight_new)


def body(
    layer_input,
    segment_ids,
    out_cotangent,
    attn_master,
    inner_master,
    outer_master,
    vector_master,
    attn_moment,
    inner_moment,
    outer_moment,
    vector_moment,
    attn_square,
    inner_square,
    outer_square,
    vector_square,
):
    seqs, half, width = layer_input.shape
    count = seqs * half
    heads = width // HD
    scale = HD ** (-0.5)
    copies = lax.axis_size("replica") * lax.axis_size("ctx")
    copy_at = lax.axis_index("replica") * lax.axis_size("ctx") + lax.axis_index("ctx")

    def gather_rows(block):
        part = block.shape[0] // copies
        mine = lax.dynamic_slice_in_dim(block, copy_at * part, part, 0)
        return lax.all_gather(mine.astype(jnp.bfloat16), EVERY, axis=0, tiled=True)

    def reduce_rows(grad):
        mine = lax.psum_scatter(
            grad.astype(jnp.bfloat16), EVERY, scatter_dimension=0, tiled=True
        )
        return lax.all_gather(mine, ("replica", "ctx"), axis=0, tiled=True).astype(jnp.float32)

    vec_low = lax.all_gather(vector_master.astype(jnp.bfloat16), "shard", axis=1, tiled=True)
    owned_rows = attn_master.shape[1]
    qkv_w = gather_rows(attn_master[:3].transpose(1, 0, 2).reshape(owned_rows, 3 * width))
    out_w = gather_rows(attn_master[3])
    inner_w = gather_rows(inner_master)
    outer_w = gather_rows(outer_master)
    attn_w = [qkv_w[:, i * width : (i + 1) * width] for i in range(3)] + [out_w]
    vec = vec_low.astype(jnp.float32)
    rows = layer_input.reshape(count, width)
    query = (matmul(rows, attn_w[0]) + vec[0]).astype(jnp.bfloat16)
    keys = matmul(rows, attn_w[1]).astype(jnp.bfloat16)
    values = (matmul(rows, attn_w[2]) + vec[1]).astype(jnp.bfloat16)
    keys_all, values_all = (
        lax.all_gather(keys.reshape(seqs, half, width), "ctx", axis=1, tiled=True),
        lax.all_gather(values.reshape(seqs, half, width), "ctx", axis=1, tiled=True),
    )
    length = keys_all.shape[1]
    start = lax.axis_index("ctx") * half
    query_seg = lax.dynamic_slice_in_dim(segment_ids, start, half, 1)
    same = query_seg[:, None, :, None] == segment_ids[:, None, None, :]
    query4 = query.reshape(seqs, half, heads, HD)
    keys4 = keys_all.reshape(seqs, length, heads, HD)
    values4 = values_all.reshape(seqs, length, heads, HD)

    def scores():
        raw = jnp.einsum("sqhd,skhd->shqk", query4, keys4, preferred_element_type=jnp.float32)
        return jnp.where(same, raw * scale, -1e30)

    masked = scores()
    top = jnp.max(masked, -1, keepdims=True)
    expo = jnp.exp(masked - top)
    total = jnp.sum(expo, -1, keepdims=True)
    probs_low = (expo / total).astype(jnp.bfloat16)
    log_total = top + jnp.log(total)
    mixed = jnp.einsum("shqk,skhd->sqhd", probs_low, values4, preferred_element_type=jnp.float32)
    heads_out = mixed.reshape(count, width).astype(jnp.bfloat16)
    branch = matmul(heads_out, attn_w[3]) + vec[2]
    normed_one, scale_one = normalize(rows.astype(jnp.float32) + branch)
    hidden = normed_one * vec[3] + vec[4]
    hidden_low = hidden.astype(jnp.bfloat16)
    pre_act = matmul(hidden_low, inner_w) + vec[8:].reshape(-1)
    active = exact_gelu(pre_act).astype(jnp.bfloat16)
    ffn_out = matmul(active, outer_w) + vec[5]
    normed_two, scale_two = normalize(hidden + ffn_out)
    result = normed_two * vec[6] + vec[7]
    cotan = out_cotangent.reshape(count, width).astype(jnp.float32)
    gain_two_grad = jnp.sum(cotan * normed_two, 0)
    shift_two_grad = jnp.sum(cotan, 0)
    resid_two_grad = norm_back(cotan * vec[6], normed_two, scale_two)
    ffn_grad = resid_two_grad.astype(jnp.bfloat16)
    bias_two_grad = jnp.sum(ffn_grad.astype(jnp.float32), 0)
    outer_grad = contract_rows(active, ffn_grad)
    active_grad = round_trip(times_trans(ffn_grad, outer_w))
    unused, gelu_pull = jax.vjp(exact_gelu, pre_act)
    pre_grad = gelu_pull(active_grad)[0].astype(jnp.bfloat16)
    bias_one_grad = jnp.sum(pre_grad.astype(jnp.float32), 0)
    inner_grad = contract_rows(hidden_low, pre_grad)
    hidden_grad = resid_two_grad + round_trip(times_trans(pre_grad, inner_w))
    gain_one_grad = jnp.sum(hidden_grad * normed_one, 0)
    shift_one_grad = jnp.sum(hidden_grad, 0)
    resid_one_grad = norm_back(hidden_grad * vec[3], normed_one, scale_one)
    branch_grad = resid_one_grad.astype(jnp.bfloat16)
    bias_out_grad = jnp.sum(branch_grad.astype(jnp.float32), 0)
    proj_out_grad = contract_rows(heads_out, branch_grad)
    heads_grad_low = times_trans(branch_grad, attn_w[3]).astype(jnp.bfloat16)
    heads_grad = heads_grad_low.reshape(seqs, half, heads, HD)
    probs = jnp.exp(scores() - log_total)
    prob_grad = round_trip(
        jnp.einsum("sqhd,skhd->shqk", heads_grad, values4, preferred_element_type=jnp.float32)
    )
    delta = jnp.sum(prob_grad * probs, -1, keepdims=True)
    score_grad = (probs * (prob_grad - delta)).astype(jnp.bfloat16)
    query_grad = (
        jnp.einsum("shqk,skhd->sqhd", score_grad, keys4, preferred_element_type=jnp.float32) * scale
    )
    probs_again = probs.astype(jnp.bfloat16)
    keys_part = (
        jnp.einsum("shqk,sqhd->skhd", score_grad, query4, preferred_element_type=jnp.float32)
        * scale
    )
    values_part = jnp.einsum(
        "shqk,sqhd->skhd", probs_again, heads_grad, preferred_element_type=jnp.float32
    )
    keys_grad, values_grad = (
        lax.psum_scatter(
            keys_part.reshape(seqs, length, width).astype(jnp.bfloat16),
            "ctx",
            scatter_dimension=1,
            tiled=True,
        ).astype(jnp.float32),
        lax.psum_scatter(
            values_part.reshape(seqs, length, width).astype(jnp.bfloat16),
            "ctx",
            scatter_dimension=1,
            tiled=True,
        ).astype(jnp.float32),
    )
    query_low = query_grad.reshape(count, width).astype(jnp.bfloat16)
    keys_low = keys_grad.reshape(count, width).astype(jnp.bfloat16)
    values_low = values_grad.reshape(count, width).astype(jnp.bfloat16)
    bias_query_grad = jnp.sum(query_low.astype(jnp.float32), 0)
    bias_value_grad = jnp.sum(values_low.astype(jnp.float32), 0)
    qkv_low = jnp.concatenate([query_low, keys_low, values_low], 1)
    qkv_grad = contract_rows(rows, qkv_low)
    input_grad = (
        resid_one_grad
        + times_trans(query_low, attn_w[0])
        + times_trans(keys_low, attn_w[1])
        + times_trans(values_low, attn_w[2])
    )
    vector_grad = jnp.concatenate(
        [
            jnp.stack(
                [
                    bias_query_grad,
                    bias_value_grad,
                    bias_out_grad,
                    gain_one_grad,
                    shift_one_grad,
                    bias_two_grad,
                    gain_two_grad,
                    shift_two_grad,
                ]
            ),
            bias_one_grad.reshape(-1, width),
        ],
        0,
    )
    masters = (attn_master, inner_master, outer_master, vector_master)
    moments = (attn_moment, inner_moment, outer_moment, vector_moment)
    squares = (attn_square, inner_square, outer_square, vector_square)
    rates = (RATE_MATRIX, RATE_MATRIX, RATE_MATRIX, RATE_VECTOR)
    qkv_sum = reduce_rows(qkv_grad)
    attn_sum = jnp.stack(
        [qkv_sum[:, i * width : (i + 1) * width] for i in range(3)] + [reduce_rows(proj_out_grad)]
    )
    summed = (
        attn_sum,
        reduce_rows(inner_grad),
        reduce_rows(outer_grad),
        lax.psum(
            lax.psum_scatter(
                vector_grad.astype(jnp.bfloat16), "shard", scatter_dimension=1, tiled=True
            ),
            ("replica", "ctx"),
        ).astype(jnp.float32),
    )
    updates = [adamw(summed[i], moments[i], squares[i], masters[i], rates[i]) for i in range(4)]
    moment_out = [item[0] for item in updates]
    square_out = [item[1] for item in updates]
    weight_out = [item[2] for item in updates]
    return (
        result.reshape(seqs, half, width).astype(jnp.bfloat16),
        input_grad.reshape(seqs, half, width),
        moment_out[0],
        moment_out[1],
        moment_out[2],
        moment_out[3],
        square_out[0],
        square_out[1],
        square_out[2],
        square_out[3],
        weight_out[0],
        weight_out[1],
        weight_out[2],
        weight_out[3],
        weight_out[0].astype(jnp.bfloat16),
        weight_out[1].astype(jnp.bfloat16),
        weight_out[2].astype(jnp.bfloat16),
        weight_out[3].astype(jnp.bfloat16),
    )


def solution(mesh):
    in_specs = (
        P(("replica", "shard"), "ctx", None),
        P(("replica", "shard"), None),
        P(("replica", "shard"), "ctx", None),
        P(None, "shard", None),
        P("shard", None),
        P("shard", None),
        P(None, "shard"),
        P(None, "shard", None),
        P("shard", None),
        P("shard", None),
        P(None, "shard"),
        P(None, "shard", None),
        P("shard", None),
        P("shard", None),
        P(None, "shard"),
    )
    out_specs = (
        P(("replica", "shard"), "ctx", None),
        P(("replica", "shard"), "ctx", None),
        P(None, "shard", None),
        P("shard", None),
        P("shard", None),
        P(None, "shard"),
        P(None, "shard", None),
        P("shard", None),
        P("shard", None),
        P(None, "shard"),
        P(None, "shard", None),
        P("shard", None),
        P("shard", None),
        P(None, "shard"),
        P(None, "shard", None),
        P("shard", None),
        P("shard", None),
        P(None, "shard"),
    )
    return jax.shard_map(body, mesh=mesh, in_specs=in_specs, out_specs=out_specs, check_vma=False)
```

```python
import functools

import jax
import jax.numpy as jnp
from jax import lax
from jax.experimental import pallas as pl
from jax.experimental.pallas import tpu as pltpu
from jax.sharding import PartitionSpec as P

HD = 64
PAIR = 2 * HD
STEP = 5
OUTER = 4
EVERY = ("shard", "replica", "ctx")

EPS_NORM = 1e-05
BETA_ONE = 0.5
BETA_TWO = 0.6
RATE_MATRIX = 0.02
RATE_VECTOR = 0.1
DECAY = 0.01
EPS_ADAM = 1e-06
MASKED = -1e30
F32 = jnp.float32
BF16 = jnp.bfloat16
NT = (((1,), (1,)), ((), ()))
TN = (((0,), (0,)), ((), ()))


def matmul(left, right):
    return jnp.dot(left, right, preferred_element_type=F32)


def contract_rows(left, right):
    return jnp.einsum("rd,re->de", left, right, preferred_element_type=F32)


def times_trans(left, right):
    return jnp.einsum("re,de->rd", left, right, preferred_element_type=F32)


def normalize(resid):
    centre = resid - jnp.mean(resid, -1, keepdims=True)
    scale = lax.rsqrt(jnp.mean(centre * centre, -1, keepdims=True) + EPS_NORM)
    return (centre * scale, scale)


def norm_back(grad, normed, scale):
    return scale * (
        grad
        - jnp.mean(grad, -1, keepdims=True)
        - normed * jnp.mean(grad * normed, -1, keepdims=True)
    )


def exact_gelu(value):
    return jax.nn.gelu(value, approximate=False)


def round_trip(value):
    return value.astype(BF16).astype(F32)


def adamw(grad, moment, square, weight, rate):
    moment_new = BETA_ONE * moment + (1.0 - BETA_ONE) * grad
    square_new = BETA_TWO * square + (1.0 - BETA_TWO) * grad * grad
    stepped = (
        moment_new
        / (1.0 - BETA_ONE**STEP)
        / (jnp.sqrt(square_new / (1.0 - BETA_TWO**STEP)) + EPS_ADAM)
    )
    weight_new = weight - rate * (stepped + DECAY * weight)
    return (moment_new, square_new, weight_new)


def swap_cores(value):
    return lax.ppermute(value, "ctx", [(0, 1), (1, 0)])


def shift_outer(value, step):
    inner = lax.axis_size("shard") // OUTER
    pairs = [
        (o * inner + i, ((o + step) % OUTER) * inner + i) for o in range(OUTER) for i in range(inner)
    ]
    return lax.ppermute(value, "shard", pairs)


def shift_inner(value, step):
    inner = lax.axis_size("shard") // OUTER
    pairs = [
        (o * inner + i, o * inner + (i + step) % inner) for o in range(OUTER) for i in range(inner)
    ]
    return lax.ppermute(value, "shard", pairs)


def shift_replica(value, step):
    size = lax.axis_size("replica")
    return lax.ppermute(value, "replica", [(r, (r + step) % size) for r in range(size)])


def ring_gather(piece):
    inner = lax.axis_size("shard") // OUTER
    found = []
    held = piece
    for k in range(OUTER):
        if k:
            held = shift_outer(held, -1)
        found.append([held] + [shift_inner(held, -e) for e in range(1, inner)])
    return [item for group in found for item in group]


def slot_owners():
    inner = lax.axis_size("shard") // OUTER
    at = lax.axis_index("shard")
    o, i = at // inner, at % inner
    return [
        lax.rem(o + k, OUTER) * inner + lax.rem(i + e, inner)
        for k in range(OUTER)
        for e in range(inner)
    ]


def pick(array, index, axis):
    return lax.dynamic_index_in_dim(array, index, axis, keepdims=False)


def sum_to_owner(chip_sum):
    shards = lax.axis_size("shard")
    inner = shards // OUTER
    at = lax.axis_index("shard")
    o, i = at // inner, at % inner
    grid = chip_sum.reshape(OUTER, inner, *chip_sum.shape[1:])
    got = [shift_inner(pick(grid, lax.rem(i + e, inner), 1), e) for e in range(1, inner)]
    line = pick(grid, i, 1).astype(F32)
    for item in got:
        line = line + item.astype(F32)
    line = line.astype(BF16)
    got = [shift_outer(pick(line, lax.rem(o + d, OUTER), 0), d) for d in range(1, OUTER)]
    total = pick(line, o, 0).astype(F32)
    for item in got:
        total = total + item.astype(F32)
    total = total.astype(BF16)
    got = [shift_replica(total, r) for r in range(1, lax.axis_size("replica"))]
    whole = total.astype(F32)
    for item in got:
        whole = whole + item.astype(F32)
    return whole.astype(BF16)


def sum_everywhere(value):
    value = value + swap_cores(value)
    got = [shift_replica(value, r) for r in range(1, lax.axis_size("replica"))]
    value = functools.reduce(jnp.add, got, value)
    inner = lax.axis_size("shard") // OUTER
    got = [shift_inner(value, e) for e in range(1, inner)]
    value = functools.reduce(jnp.add, got, value)
    got = [shift_outer(value, d) for d in range(1, OUTER)]
    return functools.reduce(jnp.add, got, value)


def project_kernel(owners_ref, rows_ref, bias_ref, factor_ref, *rest):
    pieces, (out_ref, weight_ref) = rest[:-2], rest[-2:]
    part = pieces[0].shape[0]

    @pl.when(pl.program_id(0) == 0)
    def _():
        for slot, piece in enumerate(pieces):
            start = pl.multiple_of(owners_ref[slot] * part, part)
            weight_ref[pl.ds(start, part), :] = piece[...]

    acc = jnp.dot(rows_ref[...], weight_ref[...], preferred_element_type=F32)
    out_ref[...] = ((acc + bias_ref[...]) * factor_ref[...]).astype(BF16)


def project(rows, pieces, owners, bias, factor):
    count, width = rows.shape
    columns = pieces[0].shape[1]
    tile = 256
    whole = lambda shape: pl.BlockSpec(shape, lambda m, owners: (0, 0))
    return pl.pallas_call(
        project_kernel,
        grid_spec=pltpu.PrefetchScalarGridSpec(
            num_scalar_prefetch=1,
            grid=(count // tile,),
            in_specs=[
                pl.BlockSpec((tile, width), lambda m, owners: (m, 0)),
                whole((1, columns)),
                whole((1, columns)),
            ]
            + [whole(pieces[0].shape)] * len(pieces),
            out_specs=[
                pl.BlockSpec((tile, columns), lambda m, owners: (m, 0)),
                whole((width, columns)),
            ],
        ),
        out_shape=[
            jax.ShapeDtypeStruct((count, columns), BF16),
            jax.ShapeDtypeStruct((width, columns), BF16),
        ],
        compiler_params=pltpu.CompilerParams(vmem_limit_bytes=40 * 1024 * 1024),
        cost_estimate=pl.CostEstimate(
            flops=2 * count * width * columns,
            bytes_accessed=2 * (count * width + count * columns + 2 * width * columns),
            transcendentals=0,
        ),
        name="project",
    )(jnp.stack(owners).astype(jnp.int32), rows, bias, factor, *pieces)


def attend_kernel(seg_row_ref, seg_col_ref, qkv_ref, out_ref, lse_ref, bias_ref, stat_ref):
    pair = pl.program_id(1)
    length = bias_ref.shape[0]
    chunk = 128

    @pl.when(pair == 0)
    def _():
        bias_ref[...] = jnp.where(seg_col_ref[0] == seg_row_ref[0], 0.0, MASKED)
        stat_ref[...] = jnp.zeros_like(stat_ref)

    block = qkv_ref[:, 0].reshape(length, 3 * PAIR)
    q, k, v = (block[:, i * PAIR : (i + 1) * PAIR] for i in range(3))
    lane = lax.broadcasted_iota(jnp.int32, (chunk, PAIR), 1)
    for c in range(length // chunk):
        rows = slice(c * chunk, (c + 1) * chunk)
        qc = q[rows]
        mixed = jnp.zeros((chunk, PAIR), F32)
        stat = stat_ref[rows, :]
        for h in range(2):
            mine = (lane // HD) == h
            qh = jnp.where(mine, qc, jnp.zeros_like(qc))
            s = lax.dot_general(qh, k, NT, preferred_element_type=F32) + bias_ref[rows, :]
            top = jnp.max(s, axis=1, keepdims=True)
            e = jnp.exp(s - top)
            total = jnp.sum(e, axis=1, keepdims=True)
            got = jnp.dot(e.astype(BF16), v, preferred_element_type=F32) / total
            mixed = jnp.where(mine, got, mixed)
            stat = jnp.where(lane == 2 * pair + h, top + jnp.log(total), stat)
        stat_ref[rows, :] = stat
        part = c * chunk // out_ref.shape[2]
        at = c * chunk % out_ref.shape[2]
        out_ref[part, 0, at : at + chunk, :] = mixed.astype(BF16)

    @pl.when(pair == pl.num_programs(1) - 1)
    def _():
        lse_ref[0] = jnp.transpose(stat_ref[...])[: lse_ref.shape[1]]


def attend_back_kernel(
    seg_row_ref, seg_col_ref, qkv_ref, out_ref, grad_ref, lse_ref, dqkv_ref, bias_ref, ds_ref
):
    pair = pl.program_id(1)
    length = bias_ref.shape[0]
    half = qkv_ref.shape[2]
    chunk = 128

    @pl.when(pair == 0)
    def _():
        bias_ref[...] = jnp.where(seg_col_ref[0] == seg_row_ref[0], 0.0, MASKED)

    block = qkv_ref[:, 0].reshape(length, 3 * PAIR)
    q, k, v = (block[:, i * PAIR : (i + 1) * PAIR] for i in range(3))
    out = out_ref[:, 0].reshape(length, PAIR)
    grad = grad_ref[:, 0].reshape(length, PAIR)
    lane = lax.broadcasted_iota(jnp.int32, (length, PAIR), 1)
    zero = jnp.zeros_like(q)
    product = jnp.transpose(out.astype(F32) * grad.astype(F32))
    dq = jnp.zeros((length, PAIR), F32)
    chunks = length // chunk
    dk = [jnp.zeros((chunk, PAIR), F32) for _ in range(chunks)]
    dv = [jnp.zeros((chunk, PAIR), F32) for _ in range(chunks)]
    for h in range(2):
        mine = (lane // HD) == h
        qh = jnp.where(mine, q, zero)
        kh = jnp.where(mine, k, zero)
        gh = jnp.where(mine, grad, zero)
        delta = jnp.sum(product[h * HD : (h + 1) * HD], axis=0, keepdims=True)
        lse = lse_ref[0, pl.ds(2 * pair + h, 1), :]
        for c in range(chunks):
            rows = slice(c * chunk, (c + 1) * chunk)
            s = lax.dot_general(k[rows], qh, NT, preferred_element_type=F32) + bias_ref[rows, :]
            p = jnp.exp(s - lse)
            dp = lax.dot_general(v[rows], gh, NT, preferred_element_type=F32)
            ds = (p * (dp - delta)).astype(BF16)
            ds_ref[rows, :] = ds
            dv[c] = dv[c] + jnp.dot(p.astype(BF16), gh, preferred_element_type=F32)
            dk[c] = dk[c] + jnp.dot(ds, qh, preferred_element_type=F32)
        dq = dq + lax.dot_general(ds_ref[...], kh, TN, preferred_element_type=F32)
    dqkv_ref[:, 0, :, :PAIR] = (dq * HD**-0.5).astype(BF16).reshape(-1, half, PAIR)
    for c in range(chunks):
        part, at = c * chunk // half, c * chunk % half
        dqkv_ref[part, 0, at : at + chunk, PAIR : 2 * PAIR] = dk[c].astype(BF16)
        dqkv_ref[part, 0, at : at + chunk, 2 * PAIR :] = dv[c].astype(BF16)


def attention_call(kernel, seg, arrays, outs, scratch, flops, exps, name):
    parts, seqs, half, columns = arrays[0].shape
    pairs = columns // (3 * PAIR)
    length = parts * half

    def spec(shape):
        if len(shape) == 3:
            return pl.BlockSpec((1,) + shape[1:], lambda s, p: (s, 0, 0))
        return pl.BlockSpec((parts, 1, half, shape[3] // pairs), lambda s, p: (0, s, 0, p))

    operands = [seg[:, None, :], seg[:, :, None]] + arrays
    moved = sum(a.size * a.dtype.itemsize for a in arrays + outs)
    return pl.pallas_call(
        kernel,
        grid=(seqs, pairs),
        in_specs=[spec(a.shape) for a in operands],
        out_specs=[spec(a.shape) for a in outs],
        out_shape=outs,
        scratch_shapes=scratch(length),
        compiler_params=pltpu.CompilerParams(vmem_limit_bytes=40 * 1024 * 1024),
        cost_estimate=pl.CostEstimate(
            flops=flops * 2 * seqs * pairs * length * length * PAIR * 4,
            bytes_accessed=moved,
            transcendentals=exps * seqs * pairs * 2 * length * length,
        ),
        name=name,
    )(*operands)


def attend(qkv, seg):
    parts, seqs, half, columns = qkv.shape
    heads = columns // (3 * HD)
    outs = [
        jax.ShapeDtypeStruct((parts, seqs, half, columns // 3), BF16),
        jax.ShapeDtypeStruct((seqs, heads, parts * half), F32),
    ]
    scratch = lambda length: [pltpu.VMEM((length, length), F32), pltpu.VMEM((length, PAIR), F32)]
    return attention_call(attend_kernel, seg, [qkv], outs, scratch, 2, 1, "attend")


def attend_back(qkv, seg, out, grad, lse):
    outs = [jax.ShapeDtypeStruct(qkv.shape, BF16)]
    scratch = lambda length: [pltpu.VMEM((length, length), F32), pltpu.VMEM((length, length), BF16)]
    arrays = [qkv, out, grad, lse]
    return attention_call(attend_back_kernel, seg, arrays, outs, scratch, 5, 1, "attend_back")[0]


def body(
    layer_input,
    segment_ids,
    out_cotangent,
    attn_master,
    inner_master,
    outer_master,
    vector_master,
    attn_moment,
    inner_moment,
    outer_moment,
    vector_moment,
    attn_square,
    inner_square,
    outer_square,
    vector_square,
):
    seqs, half, width = layer_input.shape
    count = seqs * half
    hidden_units = inner_master.shape[1]
    pairs = width // (2 * PAIR)
    part_cols = width // 2
    shards = lax.axis_size("shard")
    owned_rows = attn_master.shape[1]
    core = lax.axis_index("ctx")
    first = core == 0

    def own_half(array, axis):
        size = array.shape[axis] // 2
        return lax.dynamic_slice_in_dim(array, core * size, size, axis)

    def other_half(array, axis):
        size = array.shape[axis] // 2
        return lax.dynamic_slice_in_dim(array, (1 - core) * size, size, axis)

    def in_order(mine, theirs, axis):
        return jnp.concatenate(
            [jnp.where(first, mine, theirs), jnp.where(first, theirs, mine)], axis
        )

    owners = slot_owners()
    rows = layer_input.reshape(count, width)
    rows_chip = jnp.concatenate([rows, swap_cores(rows)], 0)

    vec_low = vector_master.astype(BF16)
    vec_slots = jnp.stack(ring_gather(vec_low))
    slot_of = jnp.stack(owners)
    place = (jnp.arange(shards)[:, None] == slot_of[None, :]).astype(F32)
    vec = jnp.einsum("ps,srw->rpw", place, vec_slots.astype(F32)).reshape(-1, width)

    qkv_piece = own_half(attn_master[:3], 2).astype(BF16)
    qkv_piece = (
        qkv_piece.reshape(3, owned_rows, pairs, PAIR)
        .transpose(1, 2, 0, 3)
        .reshape(owned_rows, 3 * part_cols)
    )
    pieces = ring_gather(qkv_piece)

    copies = lax.axis_size("replica") * 2
    copy_at = lax.axis_index("replica") * 2 + core
    quarter = lambda block: lax.dynamic_slice_in_dim(
        block, copy_at * (block.shape[0] // copies), block.shape[0] // copies, 0
    ).astype(BF16)
    out_q, inner_q, outer_q = quarter(attn_master[3]), quarter(inner_master), quarter(outer_master)
    wide = hidden_units // width
    small = out_q.shape[0]
    inner_q = inner_q.reshape(small, wide, width).transpose(1, 0, 2).reshape(-1, width)
    big = outer_q.shape[0]
    packed = lax.all_gather(jnp.concatenate([outer_q, inner_q, out_q], 0), EVERY, axis=0)
    outer_w = packed[:, :big].reshape(-1, width)
    inner_w = (
        packed[:, big : 2 * big]
        .reshape(-1, wide, small, width)
        .transpose(0, 2, 1, 3)
        .reshape(width, hidden_units)
    )
    out_w = packed[:, 2 * big :].reshape(width, width)

    halves = own_half(vec[:2], 1).reshape(2, pairs, PAIR)
    bias = jnp.stack([halves[0], jnp.zeros_like(halves[0]), halves[1]], 1).reshape(1, -1)
    ones = jnp.ones((pairs, PAIR), F32)
    factor = jnp.stack([ones * HD**-0.5, ones, ones], 1).reshape(1, -1)
    qkv, qkv_w = project(rows_chip, pieces, owners, bias, factor)
    qkv = qkv.reshape(2, seqs, half, 3 * part_cols)
    seg = jnp.concatenate([own_half(segment_ids, 1), other_half(segment_ids, 1)], 1)
    mixed, lse = attend(qkv, seg)
    mixed_back = swap_cores(mixed[1].reshape(count, part_cols))
    heads_out = in_order(mixed[0].reshape(count, part_cols), mixed_back, 1)

    branch = matmul(heads_out, out_w) + vec[2]
    normed_one, scale_one = normalize(rows.astype(F32) + branch)
    hidden = normed_one * vec[3] + vec[4]
    hidden_low = hidden.astype(BF16)
    pre_act = matmul(hidden_low, inner_w) + vec[8:].reshape(-1)
    active = exact_gelu(pre_act).astype(BF16)
    ffn_out = matmul(active, outer_w) + vec[5]
    normed_two, scale_two = normalize(hidden + ffn_out)
    result = normed_two * vec[6] + vec[7]
    cotan = out_cotangent.reshape(count, width).astype(F32)
    gain_two_grad = jnp.sum(cotan * normed_two, 0)
    shift_two_grad = jnp.sum(cotan, 0)
    resid_two_grad = norm_back(cotan * vec[6], normed_two, scale_two)
    ffn_grad = resid_two_grad.astype(BF16)
    bias_two_grad = jnp.sum(ffn_grad.astype(F32), 0)

    def core_sum(left, right):
        theirs = swap_cores(contract_rows(left, other_half(right, 1)).astype(BF16))
        mine = contract_rows(left, own_half(right, 1)) + theirs.astype(F32)
        return mine.astype(BF16).reshape(shards, -1, mine.shape[1])

    outer_sum = sum_to_owner(core_sum(active, ffn_grad))
    active_grad = round_trip(times_trans(ffn_grad, outer_w))
    unused, gelu_pull = jax.vjp(exact_gelu, pre_act)
    pre_grad = gelu_pull(active_grad)[0].astype(BF16)
    bias_one_grad = jnp.sum(pre_grad.astype(F32), 0)
    inner_sum = sum_to_owner(core_sum(hidden_low, pre_grad))
    hidden_grad = resid_two_grad + round_trip(times_trans(pre_grad, inner_w))
    gain_one_grad = jnp.sum(hidden_grad * normed_one, 0)
    shift_one_grad = jnp.sum(hidden_grad, 0)
    resid_one_grad = norm_back(hidden_grad * vec[3], normed_one, scale_one)
    branch_grad = resid_one_grad.astype(BF16)
    bias_out_grad = jnp.sum(branch_grad.astype(F32), 0)
    out_sum = sum_to_owner(core_sum(heads_out, branch_grad))
    mixed_grad = times_trans(branch_grad, out_w).astype(BF16)
    mixed_grad = jnp.stack(
        [own_half(mixed_grad, 1), swap_cores(other_half(mixed_grad, 1))], 0
    ).reshape(mixed.shape)
    qkv_grad = attend_back(qkv, seg, mixed, mixed_grad, lse).reshape(2 * count, 3 * part_cols)
    qkv_sum = sum_to_owner(
        contract_rows(rows_chip, qkv_grad).astype(BF16).reshape(shards, -1, 3 * part_cols)
    )
    bias_qkv = jnp.sum(qkv_grad.astype(F32), 0).reshape(pairs, 3, PAIR)
    blank = jnp.zeros((part_cols,), F32)
    bias_query_grad = in_order(bias_qkv[:, 0].reshape(-1), blank, 0)
    bias_value_grad = in_order(bias_qkv[:, 2].reshape(-1), blank, 0)
    theirs_part = times_trans(qkv_grad[count:], qkv_w).astype(BF16)
    input_grad = (
        resid_one_grad + times_trans(qkv_grad[:count], qkv_w) + swap_cores(theirs_part).astype(F32)
    )
    vector_grad = jnp.concatenate(
        [
            jnp.stack(
                [
                    bias_query_grad,
                    bias_value_grad,
                    bias_out_grad,
                    gain_one_grad,
                    shift_one_grad,
                    bias_two_grad,
                    gain_two_grad,
                    shift_two_grad,
                ]
            ),
            bias_one_grad.reshape(-1, width),
        ],
        0,
    )
    vector_sum = sum_everywhere(vector_grad)
    vector_sum = lax.dynamic_slice_in_dim(
        vector_sum, lax.axis_index("shard") * (width // shards), width // shards, 1
    )

    def both_halves(mine, axis):
        return in_order(mine, swap_cores(mine), axis).astype(F32)

    qkv_whole = both_halves(qkv_sum[None], 0).reshape(2, owned_rows, pairs, 3, PAIR)
    qkv_whole = qkv_whole.transpose(3, 1, 0, 2, 4).reshape(3, owned_rows, width)
    summed = (
        jnp.concatenate([qkv_whole, both_halves(out_sum, 1)[None]], 0),
        both_halves(inner_sum, 1),
        both_halves(outer_sum, 1),
        vector_sum,
    )
    masters = (attn_master, inner_master, outer_master, vector_master)
    moments = (attn_moment, inner_moment, outer_moment, vector_moment)
    squares = (attn_square, inner_square, outer_square, vector_square)
    rates = (RATE_MATRIX, RATE_MATRIX, RATE_MATRIX, RATE_VECTOR)
    updates = [adamw(summed[i], moments[i], squares[i], masters[i], rates[i]) for i in range(4)]
    return (
        result.reshape(seqs, half, width).astype(BF16),
        input_grad.reshape(seqs, half, width),
        *[item[0] for item in updates],
        *[item[1] for item in updates],
        *[item[2] for item in updates],
        *[item[2].astype(BF16) for item in updates],
    )


def solution(mesh):
    tokens = P(("replica", "shard"), "ctx", None)
    states = (P(None, "shard", None), P("shard", None), P("shard", None), P(None, "shard"))
    in_specs = (tokens, P(("replica", "shard"), None), tokens) + states * 3
    out_specs = (tokens, tokens) + states * 4
    return jax.shard_map(body, mesh=mesh, in_specs=in_specs, out_specs=out_specs, check_vma=False)
```

```python
import functools

import jax
import jax.numpy as jnp
from jax import lax
from jax.experimental import pallas as pl
from jax.experimental.pallas import tpu as pltpu
from jax.sharding import PartitionSpec as P

HD = 64
PAIR = 2 * HD
STEP = 5
OUTER = 4
EVERY = ("shard", "replica", "ctx")

EPS_NORM = 1e-05
BETA_ONE = 0.5
BETA_TWO = 0.6
RATE_MATRIX = 0.02
RATE_VECTOR = 0.1
DECAY = 0.01
EPS_ADAM = 1e-06
MASKED = -1e30
F32 = jnp.float32
BF16 = jnp.bfloat16
PARTS = 32
VMEM = 56 * 1024 * 1024
NT = (((1,), (1,)), ((), ()))
TN = (((0,), (0,)), ((), ()))


def matmul(left, right):
    return jnp.dot(left, right, preferred_element_type=F32)


def contract_rows(left, right):
    return jnp.einsum("rd,re->de", left, right, preferred_element_type=F32)


def times_trans(left, right):
    return jnp.einsum("re,de->rd", left, right, preferred_element_type=F32)


def normalize(resid):
    centre = resid - jnp.mean(resid, -1, keepdims=True)
    scale = lax.rsqrt(jnp.mean(centre * centre, -1, keepdims=True) + EPS_NORM)
    return (centre * scale, scale)


def norm_back(grad, normed, scale):
    return scale * (
        grad
        - jnp.mean(grad, -1, keepdims=True)
        - normed * jnp.mean(grad * normed, -1, keepdims=True)
    )


def exact_gelu(value):
    return jax.nn.gelu(value, approximate=False)


def round_trip(value):
    return value.astype(BF16).astype(F32)


def adamw(grad, moment, square, weight, rate):
    moment_new = BETA_ONE * moment + (1.0 - BETA_ONE) * grad
    square_new = BETA_TWO * square + (1.0 - BETA_TWO) * grad * grad
    stepped = (
        moment_new
        / (1.0 - BETA_ONE**STEP)
        / (jnp.sqrt(square_new / (1.0 - BETA_TWO**STEP)) + EPS_ADAM)
    )
    weight_new = weight - rate * (stepped + DECAY * weight)
    return (moment_new, square_new, weight_new)


def swap_cores(value):
    return lax.ppermute(value, "ctx", [(0, 1), (1, 0)])


def shift_outer(value, step):
    inner = lax.axis_size("shard") // OUTER
    pairs = [
        (o * inner + i, ((o + step) % OUTER) * inner + i) for o in range(OUTER) for i in range(inner)
    ]
    return lax.ppermute(value, "shard", pairs)


def shift_inner(value, step):
    inner = lax.axis_size("shard") // OUTER
    pairs = [
        (o * inner + i, o * inner + (i + step) % inner) for o in range(OUTER) for i in range(inner)
    ]
    return lax.ppermute(value, "shard", pairs)


def shift_replica(value, step):
    size = lax.axis_size("replica")
    return lax.ppermute(value, "replica", [(r, (r + step) % size) for r in range(size)])


def ring_gather(piece):
    inner = lax.axis_size("shard") // OUTER
    found = []
    held = piece
    for k in range(OUTER):
        if k:
            held = shift_outer(held, -1)
        found.append([held] + [shift_inner(held, -e) for e in range(1, inner)])
    return [item for group in found for item in group]


def slot_owners():
    inner = lax.axis_size("shard") // OUTER
    at = lax.axis_index("shard")
    o, i = at // inner, at % inner
    return [
        lax.rem(o + k, OUTER) * inner + lax.rem(i + e, inner)
        for k in range(OUTER)
        for e in range(inner)
    ]


def pick(array, index, axis):
    return lax.dynamic_index_in_dim(array, index, axis, keepdims=False)


def add_low(value, *others):
    total = value.astype(F32)
    for item in others:
        total = total + item.astype(F32)
    return total.astype(BF16)


def position():
    inner = lax.axis_size("shard") // OUTER
    at = lax.axis_index("shard")
    return at // inner, at % inner, lax.axis_index("replica"), inner


def is_square():
    return lax.axis_size("replica") == 2 and lax.axis_size("shard") == 2 * OUTER


def sum_plane_one(chip_sum):
    o, i, y, inner = position()
    if not is_square():
        grid = chip_sum.reshape(OUTER, inner, *chip_sum.shape[1:])
        got = [shift_inner(pick(grid, lax.rem(i + e, inner), 1), e) for e in range(1, inner)]
        return (add_low(pick(grid, i, 1), *got),)
    shape = chip_sum.shape
    grid = chip_sum.reshape(OUTER, 2, 2, 2, shape[1] // 4, shape[2])
    got_x = shift_inner(pick(grid[:, :, 0], 1 - i, 1), 1)
    got_y = shift_replica(pick(grid[:, :, 1], 1 - y, 2), 1)
    return add_low(pick(grid[:, :, 0], i, 1), got_x), add_low(pick(grid[:, :, 1], y, 2), got_y)


def sum_plane_two(parts):
    if not is_square():
        return parts[0]
    o, i, y, inner = position()
    got_y = shift_replica(pick(parts[0], 1 - y, 1), 1)
    got_x = shift_inner(pick(parts[1], 1 - i, 1), 1)
    return jnp.stack(
        [add_low(pick(parts[0], y, 1), got_y), add_low(pick(parts[1], i, 1), got_x)], 1
    )


def sum_line(line):
    o = position()[0]
    got = [shift_outer(pick(line, lax.rem(o + d, OUTER), 0), d) for d in range(1, OUTER)]
    return add_low(pick(line, o, 0), *got)


def sum_share(total):
    if not is_square():
        got = [shift_replica(total, r) for r in range(1, lax.axis_size("replica"))]
        mine = add_low(total, *got)
        return mine, swap_cores(mine)
    y = lax.axis_index("replica")
    columns = total.shape[-1]

    def join(own, other):
        low, high = jnp.where(y == 0, own, other), jnp.where(y == 0, other, own)
        return jnp.stack([low, high], 1).reshape(-1, columns)

    pairs = [(a, 3 - a) for a in range(4)]
    crossed = lax.ppermute(total, ("replica", "ctx"), pairs)
    return join(total, shift_replica(total, 1)), join(swap_cores(total), crossed)


def gather_quarters(quarter):
    line = jnp.stack([quarter] + [shift_outer(quarter, -k) for k in range(1, OUTER)])
    near_x = shift_inner(line, 1)
    near_y = shift_replica(line, 1)
    far_x = shift_inner(near_y[: OUTER // 2], 1)
    far_y = shift_replica(near_x[OUTER // 2 :], 1)
    o, i, y, inner = position()
    row = lambda k, across: lax.rem(o + k, OUTER) * 2 + (1 - i if across else i)
    places = [(row(k, False), y) for k in range(OUTER)] + [(row(k, True), y) for k in range(OUTER)]
    places += [(row(k, False), 1 - y) for k in range(OUTER)]
    places += [(row(k, True), 1 - y) for k in range(OUTER)]
    return [line, near_x, near_y, far_x, far_y], places


def project_kernel(row_ref, column_ref, rows_ref, bias_ref, factor_ref, *rest):
    stacks, (out_ref, weight_ref) = rest[:-2], rest[-2:]
    columns = stacks[0].shape[2]
    part = weight_ref.shape[0] * weight_ref.shape[1] // columns
    part = part // sum(stack.shape[0] for stack in stacks)

    @pl.when(pl.program_id(0) == 0)
    def _():
        slot = 0
        for stack in stacks:
            for k in range(stack.shape[0]):
                start = pl.multiple_of(row_ref[slot] * part, part)
                left = pl.multiple_of(column_ref[slot] * columns, PAIR)
                weight_ref[pl.ds(start, part), pl.ds(left, columns)] = stack[k, :part, :]
                slot += 1

    acc = jnp.dot(rows_ref[...], weight_ref[...], preferred_element_type=F32)
    out_ref[...] = ((acc + bias_ref[...]) * factor_ref[...]).astype(BF16)


def project(rows, stacks, places, bias, factor):
    count, width = rows.shape
    columns = bias.shape[1]
    tile = 512
    whole = lambda shape: pl.BlockSpec(shape, lambda m, *_: (0,) * len(shape))
    tables = [jnp.stack([p[axis] for p in places]).astype(jnp.int32) for axis in range(2)]
    return pl.pallas_call(
        project_kernel,
        grid_spec=pltpu.PrefetchScalarGridSpec(
            num_scalar_prefetch=2,
            grid=(count // tile,),
            in_specs=[
                pl.BlockSpec((tile, width), lambda m, *_: (m, 0)),
                whole((1, columns)),
                whole((1, columns)),
            ]
            + [whole(stack.shape) for stack in stacks],
            out_specs=[
                pl.BlockSpec((tile, columns), lambda m, *_: (m, 0)),
                whole((width, columns)),
            ],
        ),
        out_shape=[
            jax.ShapeDtypeStruct((count, columns), BF16),
            jax.ShapeDtypeStruct((width, columns), BF16),
        ],
        compiler_params=pltpu.CompilerParams(vmem_limit_bytes=VMEM),
        cost_estimate=pl.CostEstimate(
            flops=2 * count * width * columns,
            bytes_accessed=2 * (count * width + count * columns + 2 * width * columns),
            transcendentals=0,
        ),
        name="project",
    )(*tables, rows, bias, factor, *stacks)


def gelu_and_slope(u):
    a = jnp.abs(u) * (0.5**0.5)
    t = 1.0 / (1.0 + 0.3275911 * a)
    e = jnp.exp(-a * a)
    series = 1.061405429 * t - 1.453152027
    series = series * t + 1.421413741
    series = series * t - 0.284496736
    series = series * t + 0.254829592
    tail = 0.5 * series * t * e
    normal = jnp.where(u >= 0.0, 1.0 - tail, tail)
    return u * normal, normal + u * (0.3989422804014327 * e)


def total_rows(value):
    return jnp.sum(value, axis=0, keepdims=True)


def ffn_kernel(
    mixed_ref,
    rows_ref,
    cotan_ref,
    vec_ref,
    out_w_ref,
    inner_w_ref,
    outer_w_ref,
    active_ref,
    slope_ref,
    hidden_ref,
    normed_ref,
    scale_ref,
    result_ref,
    grad_ref,
    sums_ref,
    resid,
    acc,
):
    m, w = pl.program_id(0), pl.program_id(1)
    tile, width = acc.shape
    vec = lambda at: vec_ref[at : at + 1, :]
    parts = [slice(a, a + 128) for a in range(0, tile, 128)]

    @pl.when(w == 0)
    def _():
        acc[...] = jnp.dot(
            mixed_ref[...], out_w_ref[...].reshape(width, width), preferred_element_type=F32
        )
        for part in parts:
            normed, scale = normalize(acc[part, :] + vec(2) + rows_ref[part, :].astype(F32))
            normed_ref[part, :] = normed.astype(BF16)
            scale_ref[part, :] = scale
            hidden = normed * vec(3) + vec(4)
            resid[part, :] = hidden + vec(5)
            hidden_ref[part, :] = hidden.astype(BF16)
            acc[part, :] = jnp.zeros((128, width), F32)

    bias = vec_ref[pl.ds(8 + w, 1), :]
    inner_w = inner_w_ref[...].reshape(width, width)
    for left in range(0, width, 256):
        cut = slice(left, left + 256)
        pre = jnp.dot(hidden_ref[...], inner_w[:, cut], preferred_element_type=F32) + bias[:, cut]
        active, slope = gelu_and_slope(pre)
        active_ref[:, cut] = active.astype(BF16)
        slope_ref[:, cut] = slope.astype(BF16)
    acc[...] += jnp.dot(
        active_ref[...], outer_w_ref[...].reshape(width, width), preferred_element_type=F32
    )

    @pl.when((m == 0) & (w == 0))
    def _():
        sums_ref[...] = jnp.zeros_like(sums_ref)

    @pl.when(w == pl.num_programs(1) - 1)
    def _():
        for part in parts:
            normed, scale = normalize(resid[part, :] + acc[part, :])
            result_ref[part, :] = (normed * vec(6) + vec(7)).astype(BF16)
            cotan = cotan_ref[part, :].astype(F32)
            grad = norm_back(cotan * vec(6), normed, scale).astype(BF16)
            grad_ref[part, :] = grad
            sums_ref[0:1, :] += total_rows(cotan * normed)
            sums_ref[1:2, :] += total_rows(cotan)
            sums_ref[2:3, :] += total_rows(grad.astype(F32))


def ffn_back_kernel(
    grad_ref,
    slope_ref,
    normed_ref,
    scale_ref,
    vec_ref,
    out_w_ref,
    inner_w_ref,
    outer_w_ref,
    after_ref,
    pre_grad_ref,
    branch_ref,
    mixed_ref,
    sums_ref,
    acc,
):
    m, w = pl.program_id(0), pl.program_id(1)
    tile, width = acc.shape
    vec = lambda at: vec_ref[at : at + 1, :]
    parts = [slice(a, a + 128) for a in range(0, tile, 128)]

    @pl.when((m == 0) & (w == 0))
    def _():
        sums_ref[...] = jnp.zeros_like(sums_ref)

    outer_w = outer_w_ref[...].reshape(width, width)
    sums = []
    for left in range(0, width, 256):
        cut = slice(left, left + 256)
        back = lax.dot_general(grad_ref[...], outer_w[cut, :], NT, preferred_element_type=F32)
        back = (back.astype(BF16).astype(F32) * slope_ref[:, cut].astype(F32)).astype(BF16)
        pre_grad_ref[:, cut] = back
        sums.append(total_rows(back.astype(F32)))
    sums_ref[pl.ds(4 + w, 1), :] += jnp.concatenate(sums, 1)
    more = lax.dot_general(
        pre_grad_ref[...],
        inner_w_ref[...].reshape(width, width),
        NT,
        preferred_element_type=F32,
    )

    @pl.when(w == 0)
    def _():
        acc[...] = more

    @pl.when(w > 0)
    def _():
        acc[...] += more

    @pl.when(w == pl.num_programs(1) - 1)
    def _():
        for part in parts:
            through = acc[part, :].astype(BF16).astype(F32) + grad_ref[part, :].astype(F32)
            normed = normed_ref[part, :].astype(F32)
            branch = norm_back(through * vec(3), normed, scale_ref[part, :]).astype(BF16)
            branch_ref[part, :] = branch
            sums_ref[0:1, :] += total_rows(through * normed)
            sums_ref[1:2, :] += total_rows(through)
            sums_ref[2:3, :] += total_rows(branch.astype(F32))
        mixed_ref[...] = lax.dot_general(
            branch_ref[...], out_w_ref[...].reshape(width, width), NT, preferred_element_type=F32
        ).astype(BF16)


def packed_specs(width):
    small = width // PARTS
    return [
        pl.BlockSpec((PARTS, small, width), lambda m, w: (0, 8, 0)),
        pl.BlockSpec((PARTS, small, width), lambda m, w: (0, 4 + w, 0)),
        pl.BlockSpec((PARTS // 4, 4 * small, width), lambda m, w: (w, 0, 0)),
    ]


def ffn(mixed, rows, cotan, vec, packed, hidden_units):
    count, width = rows.shape
    tile = count // 2
    steps = hidden_units // width
    line = pl.BlockSpec((tile, width), lambda m, w: (m, 0))
    block = pl.BlockSpec((tile, width), lambda m, w: (m, w))
    column = pl.BlockSpec((tile, 1), lambda m, w: (m, 0))
    whole = lambda shape: pl.BlockSpec(shape, lambda m, w: (0, 0))
    low = jax.ShapeDtypeStruct((count, width), BF16)
    wide = jax.ShapeDtypeStruct((count, hidden_units), BF16)
    return pl.pallas_call(
        ffn_kernel,
        grid=(2, steps),
        in_specs=[line, line, line, whole(vec.shape)] + packed_specs(width),
        out_specs=[block, block, line, line, column, line, line, whole((8, width))],
        out_shape=[
            wide,
            wide,
            low,
            low,
            jax.ShapeDtypeStruct((count, 1), F32),
            low,
            low,
            jax.ShapeDtypeStruct((8, width), F32),
        ],
        scratch_shapes=[pltpu.VMEM((tile, width), F32)] * 2,
        compiler_params=pltpu.CompilerParams(vmem_limit_bytes=VMEM),
        cost_estimate=pl.CostEstimate(
            flops=2 * count * width * (2 * hidden_units + width),
            bytes_accessed=4 * count * (hidden_units + 4 * width) + 8 * width * hidden_units,
            transcendentals=2 * count * hidden_units,
        ),
        name="ffn",
    )(mixed, rows, cotan, vec, packed, packed, packed)


def ffn_back(grad, slope, normed, scale, vec, packed, after):
    count, width = grad.shape
    hidden_units = slope.shape[1]
    tile = count // 2
    steps = hidden_units // width
    line = pl.BlockSpec((tile, width), lambda m, w: (m, 0))
    block = pl.BlockSpec((tile, width), lambda m, w: (m, w))
    column = pl.BlockSpec((tile, 1), lambda m, w: (m, 0))
    whole = lambda shape: pl.BlockSpec(shape, lambda m, w: (0, 0))
    low = jax.ShapeDtypeStruct((count, width), BF16)
    return pl.pallas_call(
        ffn_back_kernel,
        grid=(2, steps),
        in_specs=[line, block, line, column, whole(vec.shape)]
        + packed_specs(width)
        + [pl.BlockSpec(memory_space=pl.ANY)],
        out_specs=[block, line, line, whole((8, width))],
        out_shape=[
            jax.ShapeDtypeStruct((count, hidden_units), BF16),
            low,
            low,
            jax.ShapeDtypeStruct((8, width), F32),
        ],
        scratch_shapes=[pltpu.VMEM((tile, width), F32)],
        compiler_params=pltpu.CompilerParams(vmem_limit_bytes=VMEM),
        cost_estimate=pl.CostEstimate(
            flops=2 * count * width * (2 * hidden_units + width),
            bytes_accessed=4 * count * (hidden_units + 2 * width) + 8 * width * hidden_units,
            transcendentals=0,
        ),
        name="ffn_back",
    )(grad, slope, normed, scale, vec, packed, packed, packed, after)


def attend_kernel(seg_row_ref, seg_col_ref, qkv_ref, out_ref, lse_ref, bias_ref, stat_ref):
    pair = pl.program_id(1)
    length = bias_ref.shape[0]
    chunk = 128

    @pl.when(pair == 0)
    def _():
        bias_ref[...] = jnp.where(seg_col_ref[0] == seg_row_ref[0], 0.0, MASKED)
        stat_ref[...] = jnp.zeros_like(stat_ref)

    block = qkv_ref[:, 0].reshape(length, 3 * PAIR)
    q, k, v = (block[:, i * PAIR : (i + 1) * PAIR] for i in range(3))
    lane = lax.broadcasted_iota(jnp.int32, (length, PAIR), 1)
    low = lane < HD
    zero, one = jnp.zeros_like(q), jnp.ones_like(v)
    q_heads = [jnp.where(low, q, zero), jnp.where(low, zero, q)]
    v_heads = [jnp.where(low, v, one), jnp.where(low, one, v)]
    lane, low = lane[:chunk], low[:chunk]
    for c in range(length // chunk):
        rows = slice(c * chunk, (c + 1) * chunk)
        got, tops = [], []
        for h in range(2):
            s = lax.dot_general(q_heads[h][rows], k, NT, preferred_element_type=F32)
            s = s + bias_ref[rows, :]
            top = jnp.max(s, axis=1, keepdims=True)
            e = jnp.exp(s - top).astype(BF16)
            got.append(jnp.dot(e, v_heads[h], preferred_element_type=F32))
            tops.append(top)
        total = jnp.where(low, got[1], got[0])
        mixed = jnp.where(low, got[0], got[1]) / pltpu.roll(total, HD, 1)
        log = jnp.log(total)
        stat = stat_ref[rows, :]
        stat = jnp.where(lane == 2 * pair, tops[0] + log[:, HD : HD + 1], stat)
        stat_ref[rows, :] = jnp.where(lane == 2 * pair + 1, tops[1] + log[:, :1], stat)
        part = c * chunk // out_ref.shape[2]
        at = c * chunk % out_ref.shape[2]
        out_ref[part, 0, at : at + chunk, :] = mixed.astype(BF16)

    @pl.when(pair == pl.num_programs(1) - 1)
    def _():
        lse_ref[0] = jnp.transpose(stat_ref[...])[: lse_ref.shape[1]]


def attend_back_kernel(first_pair, after, *refs):
    seg_row_ref, seg_col_ref, qkv_ref, out_ref, grad_ref, lse_ref = refs[:6]
    dqkv_ref, bias_ref, ds_ref = refs[6 + after :]
    pair = pl.program_id(1)
    length = bias_ref.shape[0]
    half = qkv_ref.shape[2]
    chunk = 128

    @pl.when(pair == 0)
    def _():
        bias_ref[...] = jnp.where(seg_col_ref[0] == seg_row_ref[0], 0.0, MASKED)

    block = qkv_ref[:, 0].reshape(length, 3 * PAIR)
    q, k, v = (block[:, i * PAIR : (i + 1) * PAIR] for i in range(3))
    out = out_ref[:, 0].reshape(length, PAIR)
    grad = grad_ref[:, 0].reshape(length, PAIR)
    lane = lax.broadcasted_iota(jnp.int32, (length, PAIR), 1)
    zero = jnp.zeros_like(q)
    product = jnp.transpose(out.astype(F32) * grad.astype(F32))
    dq = jnp.zeros((length, PAIR), F32)
    chunks = length // chunk
    dk = [jnp.zeros((chunk, PAIR), F32) for _ in range(chunks)]
    dv = [jnp.zeros((chunk, PAIR), F32) for _ in range(chunks)]
    for h in range(2):
        mine = (lane // HD) == h
        qh = jnp.where(mine, q, zero)
        kh = jnp.where(mine, k, zero)
        gh = jnp.where(mine, grad, zero)
        delta = jnp.sum(product[h * HD : (h + 1) * HD], axis=0, keepdims=True)
        lse = lse_ref[0, pl.ds(2 * (first_pair + pair) + h, 1), :]
        for c in range(chunks):
            rows = slice(c * chunk, (c + 1) * chunk)
            s = lax.dot_general(k[rows], qh, NT, preferred_element_type=F32) + bias_ref[rows, :]
            p = jnp.exp(s - lse)
            dp = lax.dot_general(v[rows], gh, NT, preferred_element_type=F32)
            ds = (p * (dp - delta)).astype(BF16)
            ds_ref[rows, :] = ds
            dv[c] = dv[c] + jnp.dot(p.astype(BF16), gh, preferred_element_type=F32)
            dk[c] = dk[c] + jnp.dot(ds, qh, preferred_element_type=F32)
        dq = dq + lax.dot_general(ds_ref[...], kh, TN, preferred_element_type=F32)
    dqkv_ref[:, 0, :, :PAIR] = (dq * HD**-0.5).astype(BF16).reshape(-1, half, PAIR)
    for c in range(chunks):
        part, at = c * chunk // half, c * chunk % half
        dqkv_ref[part, 0, at : at + chunk, PAIR : 2 * PAIR] = dk[c].astype(BF16)
        dqkv_ref[part, 0, at : at + chunk, 2 * PAIR :] = dv[c].astype(BF16)


def attention_call(kernel, seg, arrays, outs, scratch, flops, name, first=0, after=()):
    parts, seqs, half, columns = arrays[0].shape
    length = parts * half

    def spec(array, first):
        shape = array.shape
        if len(shape) == 3:
            return pl.BlockSpec((1,) + shape[1:], lambda s, p: (s, 0, 0))
        size = 3 * PAIR if shape[3] % (3 * PAIR) == 0 else PAIR
        return pl.BlockSpec((parts, 1, half, size), lambda s, p: (0, s, 0, first + p))

    size = 3 * PAIR if outs[0].shape[3] % (3 * PAIR) == 0 else PAIR
    pairs = outs[0].shape[3] // size
    operands = [seg[:, None, :], seg[:, :, None]] + arrays
    moved = sum(a.size * a.dtype.itemsize for a in arrays + outs)
    return pl.pallas_call(
        kernel,
        grid=(seqs, pairs),
        in_specs=[spec(a, first) for a in operands]
        + [pl.BlockSpec(memory_space=pl.ANY)] * len(after),
        out_specs=[spec(a, 0) for a in outs],
        out_shape=outs,
        scratch_shapes=scratch(length),
        compiler_params=pltpu.CompilerParams(vmem_limit_bytes=VMEM),
        cost_estimate=pl.CostEstimate(
            flops=flops * 2 * seqs * pairs * length * length * PAIR * 4,
            bytes_accessed=moved,
            transcendentals=seqs * pairs * 2 * length * length,
        ),
        name=name,
    )(*operands, *after)


def attend(qkv, seg):
    parts, seqs, half, columns = qkv.shape
    heads = columns // (3 * HD)
    outs = [
        jax.ShapeDtypeStruct((parts, seqs, half, columns // 3), BF16),
        jax.ShapeDtypeStruct((seqs, heads, parts * half), F32),
    ]
    scratch = lambda length: [pltpu.VMEM((length, length), F32), pltpu.VMEM((length, PAIR), F32)]
    return attention_call(attend_kernel, seg, [qkv], outs, scratch, 2, "attend")


def attend_back(qkv, seg, out, grad, lse, first, pairs, after):
    outs = [jax.ShapeDtypeStruct(qkv.shape[:3] + (3 * PAIR * pairs,), BF16)]
    scratch = lambda length: [pltpu.VMEM((length, length), F32), pltpu.VMEM((length, length), BF16)]
    kernel = functools.partial(attend_back_kernel, first, len(after))
    arrays = [qkv, out, grad, lse]
    name = "attend_back"
    return attention_call(kernel, seg, arrays, outs, scratch, 5, name, first, after)[0]


def body(
    layer_input,
    segment_ids,
    out_cotangent,
    attn_master,
    inner_master,
    outer_master,
    vector_master,
    attn_moment,
    inner_moment,
    outer_moment,
    vector_moment,
    attn_square,
    inner_square,
    outer_square,
    vector_square,
):
    seqs, half, width = layer_input.shape
    count = seqs * half
    hidden_units = inner_master.shape[1]
    pairs = width // (2 * PAIR)
    part_cols = width // 2
    shards = lax.axis_size("shard")
    owned_rows = attn_master.shape[1]
    core = lax.axis_index("ctx")
    first = core == 0

    def own_half(array, axis):
        size = array.shape[axis] // 2
        return lax.dynamic_slice_in_dim(array, core * size, size, axis)

    def other_half(array, axis):
        size = array.shape[axis] // 2
        return lax.dynamic_slice_in_dim(array, (1 - core) * size, size, axis)

    def in_order(mine, theirs, axis):
        return jnp.concatenate(
            [jnp.where(first, mine, theirs), jnp.where(first, theirs, mine)], axis
        )

    rows = layer_input.reshape(count, width)
    rows_chip = jnp.concatenate([rows, swap_cores(rows)], 0)
    square = is_square()

    piece = own_half(attn_master[:3], 2).astype(BF16).reshape(3, owned_rows, pairs, PAIR)
    piece = piece.transpose(1, 2, 0, 3).reshape(owned_rows, 3 * part_cols)
    vec_low = vector_master.astype(BF16)
    rider = vec_low[:2].reshape(1, -1)
    if square:
        piece = lax.dynamic_slice_in_dim(
            piece, lax.axis_index("replica") * (piece.shape[1] // 2), piece.shape[1] // 2, 1
        )
    rider = jnp.pad(rider, ((0, 15), (0, piece.shape[1] - rider.shape[1])))
    piece = jnp.concatenate([piece, rider], 0)
    if square:
        stacks, places = gather_quarters(piece)
    else:
        stacks = [item[None] for item in ring_gather(piece)]
        places = [(owner, 0) for owner in slot_owners()]
    riders = jnp.concatenate([stack[:, owned_rows] for stack in stacks], 0)[:shards]
    riders = riders[:, : 2 * width // shards].reshape(shards, 2, -1).astype(F32)
    slot_of = jnp.stack([place[0] for place in places[:shards]])
    chosen = (jnp.arange(shards)[:, None] == slot_of[None, :]).astype(F32)
    biases = jnp.einsum("ps,srw->rpw", chosen, riders).reshape(2, width)

    copies = lax.axis_size("replica") * 2
    copy_at = lax.axis_index("replica") * 2 + core
    quarter = lambda block: lax.dynamic_slice_in_dim(
        block, copy_at * (block.shape[0] // copies), block.shape[0] // copies, 0
    ).astype(BF16)
    out_q, inner_q, outer_q = quarter(attn_master[3]), quarter(inner_master), quarter(outer_master)
    wide = hidden_units // width
    small = out_q.shape[0]
    inner_q = inner_q.reshape(small, wide, width).transpose(1, 0, 2).reshape(-1, width)
    big = outer_q.shape[0]
    vec_q = vec_low.reshape(-1)
    vec_q = jnp.pad(vec_q, (0, 16 * width - vec_q.shape[0])).reshape(16, width)
    packed = lax.all_gather(jnp.concatenate([outer_q, inner_q, out_q, vec_q], 0), EVERY, axis=0)
    vec = packed[::copies, 2 * big + small :].reshape(shards, -1)[:, : vec_low.size]
    vec = vec.reshape((shards,) + vec_low.shape).transpose(1, 0, 2).reshape(-1, width).astype(F32)
    if packed.shape[0] != PARTS:
        outer_w = packed[:, :big].reshape(PARTS, -1, width)
        inner_w = packed[:, big : 2 * big].reshape(-1, wide, small, width).transpose(0, 2, 1, 3)
        inner_w = inner_w.reshape(PARTS, -1, wide, width).transpose(0, 2, 1, 3)
        out_w = packed[:, 2 * big : 2 * big + small].reshape(PARTS, -1, width)
        packed = jnp.concatenate([outer_w, inner_w.reshape(PARTS, -1, width), out_w], 1)

    halves = own_half(biases, 1).reshape(2, pairs, PAIR)
    bias = jnp.stack([halves[0], jnp.zeros_like(halves[0]), halves[1]], 1).reshape(1, -1)
    ones = jnp.ones((pairs, PAIR), F32)
    factor = jnp.stack([ones * HD**-0.5, ones, ones], 1).reshape(1, -1)
    qkv, qkv_w = project(rows_chip, stacks, places, bias, factor)
    qkv = qkv.reshape(2, seqs, half, 3 * part_cols)
    seg = jnp.concatenate([own_half(segment_ids, 1), other_half(segment_ids, 1)], 1)
    mixed, lse = attend(qkv, seg)
    mixed_back = swap_cores(mixed[1].reshape(count, part_cols))
    heads_out = in_order(mixed[0].reshape(count, part_cols), mixed_back, 1)

    cotan = out_cotangent.reshape(count, width)
    active, slope, hidden_low, normed, scale, result, ffn_grad, sums_two = ffn(
        heads_out, rows, cotan, vec, packed, hidden_units
    )

    def send_half(left, right):
        return contract_rows(left, other_half(right, 1)).astype(BF16)

    def keep_half(left, right, sent):
        mine = contract_rows(left, own_half(right, 1)) + swap_cores(sent).astype(F32)
        return mine.astype(BF16).reshape(shards, -1, mine.shape[1])

    outer_sent = send_half(active, ffn_grad)
    pre_grad, branch_grad, mixed_grad, sums_one = ffn_back(
        ffn_grad, slope, normed, scale, vec, packed, outer_sent
    )
    mixed_grad = jnp.stack(
        [own_half(mixed_grad, 1), swap_cores(other_half(mixed_grad, 1))], 0
    ).reshape(mixed.shape)
    outer_chip = keep_half(active, ffn_grad, outer_sent)
    inner_sent = send_half(hidden_low, pre_grad)
    out_sent = send_half(heads_out, branch_grad)
    outer_one = sum_plane_one(outer_chip)
    grad_a = attend_back(
        qkv, seg, mixed, mixed_grad, lse, 0, pairs // 2, (outer_chip, inner_sent, out_sent)
    ).reshape(2 * count, -1)
    inner_chip = keep_half(hidden_low, pre_grad, inner_sent)
    out_chip = keep_half(heads_out, branch_grad, out_sent)
    inner_one = sum_plane_one(inner_chip)
    by_shard = lambda array: array.astype(BF16).reshape(shards, owned_rows, -1)
    chip_a = jnp.concatenate([by_shard(contract_rows(rows_chip, grad_a)), out_chip], 2)
    one_a = sum_plane_one(chip_a)
    grad_b = attend_back(
        qkv, seg, mixed, mixed_grad, lse, pairs // 2, pairs - pairs // 2,
        (inner_chip, chip_a) + outer_one,
    ).reshape(2 * count, -1)
    outer_line = sum_plane_two(outer_one)
    inner_line = sum_plane_two(inner_one)

    def bias_sums(grad):
        sums = jnp.sum(grad.astype(F32), 0).reshape(-1, 3, PAIR)
        return sums[:, 0].reshape(-1), sums[:, 2].reshape(-1)

    bias_a, bias_b = bias_sums(grad_a), bias_sums(grad_b)
    blank = jnp.zeros((part_cols,), F32)
    attn_biases = [
        in_order(jnp.concatenate([bias_a[at], bias_b[at]]), blank, 0) for at in range(2)
    ]
    vector_grad = jnp.concatenate(
        [jnp.stack(attn_biases), sums_one[2:3], sums_one[:2], sums_two[2:3], sums_two[:2]]
        + [sums_one[4:8]],
        0,
    )
    vector_grad = vector_grad.reshape(-1, shards, width // shards).transpose(1, 0, 2)
    vector_grad = jnp.pad(vector_grad, ((0, 0), (0, owned_rows - vector_grad.shape[1]), (0, 0)))
    chip_b = jnp.concatenate(
        [by_shard(contract_rows(rows_chip, grad_b)), vector_grad.astype(BF16)], 2
    )
    one_b = sum_plane_one(chip_b)
    outer_total = sum_line(outer_line)
    grad_a, grad_b, *_ = lax.optimization_barrier((grad_a, grad_b, chip_b) + one_a)
    cut = grad_a.shape[1]

    def rows_back(part):
        return times_trans(grad_a[part], qkv_w[:, :cut]) + times_trans(grad_b[part], qkv_w[:, cut:])

    theirs_part = rows_back(slice(count, None)).astype(BF16)
    input_grad = (
        branch_grad.astype(F32) + rows_back(slice(0, count)) + swap_cores(theirs_part).astype(F32)
    )
    line_a, line_b = sum_plane_two(one_a), sum_plane_two(one_b)
    outer_sum = sum_share(outer_total)
    inner_sum = sum_share(sum_line(inner_line))
    sum_a = sum_share(sum_line(line_a))
    sum_b = sum_share(sum_line(line_b))

    def both_halves(pair, axis):
        return in_order(pair[0], pair[1], axis).astype(F32)

    def attn_columns(at):
        part = jnp.concatenate([sum_a[at][:, :cut], sum_b[at][:, : 3 * part_cols - cut]], 1)
        return part.reshape(1, owned_rows, pairs, 3, PAIR)

    qkv_whole = both_halves((attn_columns(0), attn_columns(1)), 0)
    qkv_whole = qkv_whole.transpose(3, 1, 0, 2, 4).reshape(3, owned_rows, width)
    out_sum = both_halves((sum_a[0][:, cut:], sum_a[1][:, cut:]), 1)
    rest = slice(3 * part_cols - cut, None)
    vector_sum = sum_b[0][: vec_low.shape[0], rest].astype(F32)
    vector_sum = vector_sum + sum_b[1][: vec_low.shape[0], rest].astype(F32)
    summed = (
        jnp.concatenate([qkv_whole, out_sum[None]], 0),
        both_halves(inner_sum, 1),
        both_halves(outer_sum, 1),
        vector_sum,
    )
    masters = (attn_master, inner_master, outer_master, vector_master)
    moments = (attn_moment, inner_moment, outer_moment, vector_moment)
    squares = (attn_square, inner_square, outer_square, vector_square)
    rates = (RATE_MATRIX, RATE_MATRIX, RATE_MATRIX, RATE_VECTOR)
    updates = [adamw(summed[i], moments[i], squares[i], masters[i], rates[i]) for i in range(4)]
    return (
        result.reshape(seqs, half, width).astype(BF16),
        input_grad.reshape(seqs, half, width),
        *[item[0] for item in updates],
        *[item[1] for item in updates],
        *[item[2] for item in updates],
        *[item[2].astype(BF16) for item in updates],
    )


def solution(mesh):
    tokens = P(("replica", "shard"), "ctx", None)
    states = (P(None, "shard", None), P("shard", None), P("shard", None), P(None, "shard"))
    in_specs = (tokens, P(("replica", "shard"), None), tokens) + states * 3
    out_specs = (tokens, tokens) + states * 4
    return jax.shard_map(body, mesh=mesh, in_specs=in_specs, out_specs=out_specs, check_vma=False)
```

```python
import functools

import jax
import jax.numpy as jnp
from jax import lax
from jax.experimental import pallas as pl
from jax.experimental.pallas import tpu as pltpu
from jax.sharding import PartitionSpec as P

HD = 64
PAIR = 2 * HD
STEP = 5
OUTER = 4
EVERY = ("shard", "replica", "ctx")

EPS_NORM = 1e-05
BETA_ONE = 0.5
BETA_TWO = 0.6
RATE_MATRIX = 0.02
RATE_VECTOR = 0.1
DECAY = 0.01
EPS_ADAM = 1e-06
MASKED = -1e30
F32 = jnp.float32
BF16 = jnp.bfloat16
PARTS = 32
VMEM = 56 * 1024 * 1024
NT = (((1,), (1,)), ((), ()))
TN = (((0,), (0,)), ((), ()))


def contract_rows(left, right):
    return jnp.einsum("rd,re->de", left, right, preferred_element_type=F32)


def normalize(resid):
    centre = resid - jnp.mean(resid, -1, keepdims=True)
    scale = lax.rsqrt(jnp.mean(centre * centre, -1, keepdims=True) + EPS_NORM)
    return (centre * scale, scale)


def norm_back(grad, normed, scale):
    return scale * (
        grad
        - jnp.mean(grad, -1, keepdims=True)
        - normed * jnp.mean(grad * normed, -1, keepdims=True)
    )


def adamw(grad, moment, square, weight, rate):
    moment_new = BETA_ONE * moment + (1.0 - BETA_ONE) * grad
    square_new = BETA_TWO * square + (1.0 - BETA_TWO) * grad * grad
    stepped = (
        moment_new
        / (1.0 - BETA_ONE**STEP)
        / (jnp.sqrt(square_new / (1.0 - BETA_TWO**STEP)) + EPS_ADAM)
    )
    weight_new = weight - rate * (stepped + DECAY * weight)
    return (moment_new, square_new, weight_new)


def swap_cores(value):
    return lax.ppermute(value, "ctx", [(0, 1), (1, 0)])


def shift_outer(value, step):
    inner = lax.axis_size("shard") // OUTER
    pairs = [
        (o * inner + i, ((o + step) % OUTER) * inner + i) for o in range(OUTER) for i in range(inner)
    ]
    return lax.ppermute(value, "shard", pairs)


def shift_inner(value, step):
    inner = lax.axis_size("shard") // OUTER
    pairs = [
        (o * inner + i, o * inner + (i + step) % inner) for o in range(OUTER) for i in range(inner)
    ]
    return lax.ppermute(value, "shard", pairs)


def shift_replica(value, step):
    size = lax.axis_size("replica")
    return lax.ppermute(value, "replica", [(r, (r + step) % size) for r in range(size)])


def ring_gather(piece):
    inner = lax.axis_size("shard") // OUTER
    found = []
    held = piece
    for k in range(OUTER):
        if k:
            held = shift_outer(held, -1)
        found.append([held] + [shift_inner(held, -e) for e in range(1, inner)])
    return [item for group in found for item in group]


def slot_owners():
    inner = lax.axis_size("shard") // OUTER
    at = lax.axis_index("shard")
    o, i = at // inner, at % inner
    return [
        lax.rem(o + k, OUTER) * inner + lax.rem(i + e, inner)
        for k in range(OUTER)
        for e in range(inner)
    ]


def pick(array, index, axis):
    return lax.dynamic_index_in_dim(array, index, axis, keepdims=False)


def add_low(value, *others):
    total = value.astype(F32)
    for item in others:
        total = total + item.astype(F32)
    return total.astype(BF16)


def position():
    inner = lax.axis_size("shard") // OUTER
    at = lax.axis_index("shard")
    return at // inner, at % inner, lax.axis_index("replica"), inner


def is_square():
    return lax.axis_size("replica") == 2 and lax.axis_size("shard") == 2 * OUTER


def swap_cross(value):
    return lax.ppermute(value, ("replica", "ctx"), [(a, 3 - a) for a in range(4)])


def sum_apart(chip_sum):
    o, i, y, inner = position()
    grid = chip_sum.reshape(OUTER, inner, *chip_sum.shape[1:])
    got = [shift_inner(pick(grid, lax.rem(i + e, inner), 1), e) for e in range(1, inner)]
    line = add_low(pick(grid, i, 1), *got)
    got = [shift_outer(pick(line, lax.rem(o + d, OUTER), 0), d) for d in range(1, OUTER)]
    total = add_low(pick(line, o, 0), *got)
    got = [shift_replica(total, r) for r in range(1, lax.axis_size("replica"))]
    mine = add_low(total, *got)[None]
    return [mine, swap_cores(mine)]


def small_call(kernel, where, grid, ins, outs, after, name):
    operands, in_specs = zip(*ins)
    shapes, out_specs = zip(*outs)
    moved = sum(a.size * a.dtype.itemsize for a in operands)
    return pl.pallas_call(
        functools.partial(kernel, len(ins), len(after)),
        grid_spec=pltpu.PrefetchScalarGridSpec(
            num_scalar_prefetch=1,
            grid=grid,
            in_specs=list(in_specs) + [pl.BlockSpec(memory_space=pl.ANY)] * len(after),
            out_specs=list(out_specs),
        ),
        out_shape=list(shapes),
        compiler_params=pltpu.CompilerParams(vmem_limit_bytes=VMEM),
        cost_estimate=pl.CostEstimate(flops=moved, bytes_accessed=2 * moved, transcendentals=0),
        name=name,
    )(where, *operands, *after)


def split_kernel(count, after, where_ref, p_ref, q_ref, *rest):
    send_p, send_q = rest[after:]
    send_p[0] = p_ref[0, 0, 0]
    for at in range(2):
        send_q[0, at] = q_ref[0, at, 0, 0]


def fold_plane_kernel(count, after, where_ref, p_ref, q_ref, got_p, got_q, *rest):
    keep_p, send_p, keep_q, send_q = rest[after:]
    i, y = where_ref[1], where_ref[2]
    for out, at in ((keep_p, y), (send_p, 1 - y)):
        out[0] = add_low(p_ref[0, 0, 0, at], got_p[0, at])
    for out, at in ((keep_q, i), (send_q, 1 - i)):
        out[0] = add_low(q_ref[0, at, 0, 0], got_q[0, at])


def fold_cross_kernel(count, after, where_ref, keep_p, got_p, keep_q, got_q, *rest):
    for d, out in enumerate(rest[after:]):
        at = lax.rem(where_ref[0] + d, OUTER)
        out[0] = add_low(keep_p[at], got_p[at])
        out[1] = add_low(keep_q[at], got_q[at])


def fold_line_kernel(count, after, where_ref, *rest):
    rest[count + after][...] = add_low(*(ref[...] for ref in rest[:count]))


class Sum:
    def __init__(self, where, chip_sum):
        rows, self.columns = chip_sum.shape[1:]
        self.where, self.rows = where, rows // 4
        self.chip = chip_sum.reshape(OUTER, 2, 2, 2, self.rows, self.columns)

    def picked(self, flip):
        block = (self.rows, self.columns)
        across = lambda at: 1 - at if flip else at
        return [
            (self.chip, pl.BlockSpec((1, 1, 1, 2) + block, lambda o, w: (o, across(w[1]), 0, 0, 0, 0))),
            (self.chip, pl.BlockSpec((1, 2, 1, 1) + block, lambda o, w: (o, 0, 1, across(w[2]), 0, 0))),
        ]

    def shape(self, *lead):
        return jax.ShapeDtypeStruct(lead + (self.rows, self.columns), BF16)

    def split(self, after=()):
        spec = pl.BlockSpec((1, 2, self.rows, self.columns), lambda o, w: (o, 0, 0, 0))
        outs = [(self.shape(OUTER, 2), spec)] * 2
        self.sent = small_call(
            split_kernel, self.where, (OUTER,), self.picked(True), outs, after, "split"
        )
        self.got = [shift_inner(self.sent[0], 1), shift_replica(self.sent[1], 1)]
        return tuple(self.sent)

    def plane(self, after=()):
        pair = pl.BlockSpec((1, 2, self.rows, self.columns), lambda o, w: (o, 0, 0, 0))
        one = pl.BlockSpec((1, self.rows, self.columns), lambda o, w: (o, 0, 0))
        ins = self.picked(False) + [(got, pair) for got in self.got]
        outs = [(self.shape(OUTER), one)] * 4
        keep_p, send_p, keep_q, send_q = small_call(
            fold_plane_kernel, self.where, (OUTER,), ins, outs, after, "fold_plane"
        )
        self.kept = [keep_p, shift_replica(send_p, 1), keep_q, shift_inner(send_q, 1)]
        return (send_p, send_q)

    def cross(self, after=()):
        whole = pl.BlockSpec((OUTER, self.rows, self.columns), lambda o, w: (0, 0, 0))
        part = pl.BlockSpec((2, self.rows, self.columns), lambda o, w: (0, 0, 0))
        ins = [(item, whole) for item in self.kept]
        outs = [(self.shape(2), part)] * OUTER
        kept, *sent = small_call(
            fold_cross_kernel, self.where, (1,), ins, outs, after, "fold_cross"
        )
        self.line_parts = [kept] + [shift_outer(item, d + 1) for d, item in enumerate(sent)]
        return tuple(sent)

    def line(self, after=()):
        part = pl.BlockSpec((2, self.rows, self.columns), lambda o, w: (0, 0, 0))
        ins = [(item, part) for item in self.line_parts]
        (total,) = small_call(
            fold_line_kernel, self.where, (1,), ins, [(self.shape(2), part)], after, "fold_line"
        )
        self.shares = [total, shift_replica(total, 1), swap_cores(total), swap_cross(total)]
        return (total,)


def update_kernel(groups, after, where_ref, *refs):
    states, shares = refs[:3], refs[3 : 3 + sum(groups)]
    outs, grad_ref = refs[3 + sum(groups) + after : -1], refs[-1]
    for n in range(groups[0]):

        @pl.when(pl.program_id(1) == n)
        def _():
            if len(groups) == 1:
                grad_ref[...] = shares[n][0].astype(F32)
            else:
                left, right = shares[n], shares[groups[0] + n]
                width = grad_ref.shape[2]
                pairs = width // PAIR
                for t in range(3):
                    for p in range(pairs):
                        side, at = (left, p) if 2 * p < pairs else (right, p - pairs // 2)
                        part = side[0, :, (3 * at + t) * PAIR : (3 * at + t + 1) * PAIR]
                        grad_ref[t, :, p * PAIR : (p + 1) * PAIR] = part.astype(F32)
                cut = 3 * PAIR * (pairs // 2)
                grad_ref[3] = left[0, :, cut : cut + width].astype(F32)

    new = adamw(grad_ref[...], states[1][...], states[2][...], states[0][...], RATE_MATRIX)
    for out, value in zip(outs, new + (new[2],)):
        out[...] = value.astype(out.dtype)


def update(where, states, groups, after=()):
    parts, rows = groups[0][0].shape[:2]
    ways = len(groups[0])
    lead = states[0].shape[:-2]
    columns = states[0].shape[-1] // 2

    def place(p, v, w):
        if ways == 2:
            return (0,) * len(lead) + (p, w[3] + v - 2 * w[3] * v)
        across, core = lax.rem(v, 2), v // 2
        row = 2 * p + w[2] + across - 2 * w[2] * across
        return (0,) * len(lead) + (row, w[3] + core - 2 * w[3] * core)

    block = pl.BlockSpec(lead + (rows, columns), place)
    shares = [share for group in groups for share in group]
    share_specs = [pl.BlockSpec((1,) + a.shape[1:], lambda p, v, w: (p, 0, 0)) for a in shares]
    kinds = (F32, F32, F32, BF16)
    return pl.pallas_call(
        functools.partial(update_kernel, [len(group) for group in groups], len(after)),
        grid_spec=pltpu.PrefetchScalarGridSpec(
            num_scalar_prefetch=1,
            grid=(parts, ways),
            in_specs=[block] * 3 + share_specs + [pl.BlockSpec(memory_space=pl.ANY)] * len(after),
            out_specs=[block] * 4,
            scratch_shapes=[pltpu.VMEM(lead + (rows, columns), F32)],
        ),
        out_shape=[jax.ShapeDtypeStruct(states[0].shape, kind) for kind in kinds],
        compiler_params=pltpu.CompilerParams(vmem_limit_bytes=VMEM),
        cost_estimate=pl.CostEstimate(
            flops=20 * states[0].size, bytes_accessed=28 * states[0].size, transcendentals=0
        ),
        name="update",
    )(where, *states, *shares, *after)


def input_back_kernel(a_ref, b_ref, left_ref, right_ref, *rest):
    out_ref = rest[-1]
    total = lax.dot_general(a_ref[...], left_ref[...], NT, preferred_element_type=F32)
    total += lax.dot_general(b_ref[...], right_ref[...], NT, preferred_element_type=F32)
    if out_ref.dtype == F32:
        total += rest[0][...].astype(F32) + rest[1][...].astype(F32)
    out_ref[...] = total.astype(out_ref.dtype)


def input_back(grad_a, grad_b, weight, added, after):
    count, cut = grad_a.shape[0] // 2, grad_a.shape[1]
    width = weight.shape[0]
    tile = count // 2
    first = 0 if added else 2
    side = pl.BlockSpec((tile, cut), lambda m: (first + m, 0))
    line = pl.BlockSpec((tile, width), lambda m: (m, 0))
    return pl.pallas_call(
        input_back_kernel,
        grid=(2,),
        in_specs=[side, side]
        + [pl.BlockSpec((width, cut), lambda m, at=at: (0, at)) for at in range(2)]
        + [line] * len(added)
        + [pl.BlockSpec(memory_space=pl.ANY)] * len(after),
        out_specs=line,
        out_shape=jax.ShapeDtypeStruct((count, width), F32 if added else BF16),
        compiler_params=pltpu.CompilerParams(vmem_limit_bytes=VMEM),
        cost_estimate=pl.CostEstimate(
            flops=4 * count * width * cut, bytes_accessed=8 * count * width, transcendentals=0
        ),
        name="input_back",
    )(grad_a, grad_b, weight, weight, *added, *after)


def gather_quarters(quarter):
    line = jnp.stack([quarter] + [shift_outer(quarter, -k) for k in range(1, OUTER)])
    near_x = shift_inner(line, 1)
    near_y = shift_replica(line, 1)
    far_x = shift_inner(near_y[: OUTER // 2], 1)
    far_y = shift_replica(near_x[OUTER // 2 :], 1)
    o, i, y, inner = position()
    row = lambda k, across: lax.rem(o + k, OUTER) * 2 + (1 - i if across else i)
    places = [(row(k, False), y) for k in range(OUTER)] + [(row(k, True), y) for k in range(OUTER)]
    places += [(row(k, False), 1 - y) for k in range(OUTER)]
    places += [(row(k, True), 1 - y) for k in range(OUTER)]
    return [line, near_x, near_y, far_x, far_y], places


def project_kernel(row_ref, column_ref, rows_ref, bias_ref, factor_ref, *rest):
    stacks, (out_ref, weight_ref) = rest[:-2], rest[-2:]
    columns = stacks[0].shape[2]
    part = weight_ref.shape[0] * weight_ref.shape[1] // columns
    part = part // sum(stack.shape[0] for stack in stacks)

    @pl.when(pl.program_id(0) == 0)
    def _():
        slot = 0
        for stack in stacks:
            for k in range(stack.shape[0]):
                start = pl.multiple_of(row_ref[slot] * part, part)
                left = pl.multiple_of(column_ref[slot] * columns, PAIR)
                weight_ref[pl.ds(start, part), pl.ds(left, columns)] = stack[k, :part, :]
                slot += 1

    acc = jnp.dot(rows_ref[...], weight_ref[...], preferred_element_type=F32)
    out_ref[...] = ((acc + bias_ref[...]) * factor_ref[...]).astype(BF16)


def project(rows, stacks, places, bias, factor):
    count, width = rows.shape
    columns = bias.shape[1]
    tile = 512
    whole = lambda shape: pl.BlockSpec(shape, lambda m, *_: (0,) * len(shape))
    tables = [jnp.stack([p[axis] for p in places]).astype(jnp.int32) for axis in range(2)]
    return pl.pallas_call(
        project_kernel,
        grid_spec=pltpu.PrefetchScalarGridSpec(
            num_scalar_prefetch=2,
            grid=(count // tile,),
            in_specs=[
                pl.BlockSpec((tile, width), lambda m, *_: (m, 0)),
                whole((1, columns)),
                whole((1, columns)),
            ]
            + [whole(stack.shape) for stack in stacks],
            out_specs=[
                pl.BlockSpec((tile, columns), lambda m, *_: (m, 0)),
                whole((width, columns)),
            ],
        ),
        out_shape=[
            jax.ShapeDtypeStruct((count, columns), BF16),
            jax.ShapeDtypeStruct((width, columns), BF16),
        ],
        compiler_params=pltpu.CompilerParams(vmem_limit_bytes=VMEM),
        cost_estimate=pl.CostEstimate(
            flops=2 * count * width * columns,
            bytes_accessed=2 * (count * width + count * columns + 2 * width * columns),
            transcendentals=0,
        ),
        name="project",
    )(*tables, rows, bias, factor, *stacks)


def gelu_and_slope(u):
    a = jnp.abs(u) * (0.5**0.5)
    t = 1.0 / (1.0 + 0.3275911 * a)
    e = jnp.exp(-a * a)
    series = 1.061405429 * t - 1.453152027
    series = series * t + 1.421413741
    series = series * t - 0.284496736
    series = series * t + 0.254829592
    tail = 0.5 * series * t * e
    normal = jnp.where(u >= 0.0, 1.0 - tail, tail)
    return u * normal, normal + u * (0.3989422804014327 * e)


def total_rows(value):
    return jnp.sum(value, axis=0, keepdims=True)


def ffn_kernel(
    mixed_ref,
    rows_ref,
    cotan_ref,
    vec_ref,
    out_w_ref,
    inner_w_ref,
    outer_w_ref,
    active_ref,
    slope_ref,
    hidden_ref,
    normed_ref,
    scale_ref,
    result_ref,
    grad_ref,
    sums_ref,
    resid,
    acc,
):
    m, w = pl.program_id(0), pl.program_id(1)
    tile, width = acc.shape
    vec = lambda at: vec_ref[at : at + 1, :]
    parts = [slice(a, a + 128) for a in range(0, tile, 128)]

    @pl.when(w == 0)
    def _():
        acc[...] = jnp.dot(
            mixed_ref[...], out_w_ref[...].reshape(width, width), preferred_element_type=F32
        )
        for part in parts:
            normed, scale = normalize(acc[part, :] + vec(2) + rows_ref[part, :].astype(F32))
            normed_ref[part, :] = normed.astype(BF16)
            scale_ref[part, :] = scale
            hidden = normed * vec(3) + vec(4)
            resid[part, :] = hidden + vec(5)
            hidden_ref[part, :] = hidden.astype(BF16)
            acc[part, :] = jnp.zeros((128, width), F32)

    bias = vec_ref[pl.ds(8 + w, 1), :]
    inner_w = inner_w_ref[...].reshape(width, width)
    for left in range(0, width, 256):
        cut = slice(left, left + 256)
        pre = jnp.dot(hidden_ref[...], inner_w[:, cut], preferred_element_type=F32) + bias[:, cut]
        active, slope = gelu_and_slope(pre)
        active_ref[:, cut] = active.astype(BF16)
        slope_ref[:, cut] = slope.astype(BF16)
    acc[...] += jnp.dot(
        active_ref[...], outer_w_ref[...].reshape(width, width), preferred_element_type=F32
    )

    @pl.when((m == 0) & (w == 0))
    def _():
        sums_ref[...] = jnp.zeros_like(sums_ref)

    @pl.when(w == pl.num_programs(1) - 1)
    def _():
        for part in parts:
            normed, scale = normalize(resid[part, :] + acc[part, :])
            result_ref[part, :] = (normed * vec(6) + vec(7)).astype(BF16)
            cotan = cotan_ref[part, :].astype(F32)
            grad = norm_back(cotan * vec(6), normed, scale).astype(BF16)
            grad_ref[part, :] = grad
            sums_ref[0:1, :] += total_rows(cotan * normed)
            sums_ref[1:2, :] += total_rows(cotan)
            sums_ref[2:3, :] += total_rows(grad.astype(F32))


def ffn_back_kernel(
    grad_ref,
    slope_ref,
    normed_ref,
    scale_ref,
    vec_ref,
    out_w_ref,
    inner_w_ref,
    outer_w_ref,
    after_ref,
    pre_grad_ref,
    branch_ref,
    mixed_ref,
    again_ref,
    sums_ref,
    acc,
):
    m, w = pl.program_id(0), pl.program_id(1)
    tile, width = acc.shape
    vec = lambda at: vec_ref[at : at + 1, :]
    parts = [slice(a, a + 128) for a in range(0, tile, 128)]

    @pl.when((m == 0) & (w == 0))
    def _():
        sums_ref[...] = jnp.zeros_like(sums_ref)

    outer_w = outer_w_ref[...].reshape(width, width)
    sums = []
    for left in range(0, width, 256):
        cut = slice(left, left + 256)
        back = lax.dot_general(grad_ref[...], outer_w[cut, :], NT, preferred_element_type=F32)
        back = (back.astype(BF16).astype(F32) * slope_ref[:, cut].astype(F32)).astype(BF16)
        pre_grad_ref[:, cut] = back
        sums.append(total_rows(back.astype(F32)))
    sums_ref[pl.ds(4 + w, 1), :] += jnp.concatenate(sums, 1)
    more = lax.dot_general(
        pre_grad_ref[...],
        inner_w_ref[...].reshape(width, width),
        NT,
        preferred_element_type=F32,
    )

    @pl.when(w == 0)
    def _():
        acc[...] = more

    @pl.when(w > 0)
    def _():
        acc[...] += more

    @pl.when(w == pl.num_programs(1) - 1)
    def _():
        for part in parts:
            through = acc[part, :].astype(BF16).astype(F32) + grad_ref[part, :].astype(F32)
            normed = normed_ref[part, :].astype(F32)
            branch = norm_back(through * vec(3), normed, scale_ref[part, :]).astype(BF16)
            branch_ref[part, :] = branch
            again_ref[part, :] = grad_ref[part, :]
            sums_ref[0:1, :] += total_rows(through * normed)
            sums_ref[1:2, :] += total_rows(through)
            sums_ref[2:3, :] += total_rows(branch.astype(F32))
        mixed_ref[...] = lax.dot_general(
            branch_ref[...], out_w_ref[...].reshape(width, width), NT, preferred_element_type=F32
        ).astype(BF16)


def packed_specs(width):
    small = width // PARTS
    return [
        pl.BlockSpec((PARTS, small, width), lambda m, w: (0, 8, 0)),
        pl.BlockSpec((PARTS, small, width), lambda m, w: (0, 4 + w, 0)),
        pl.BlockSpec((PARTS // 4, 4 * small, width), lambda m, w: (w, 0, 0)),
    ]


def ffn(mixed, rows, cotan, vec, packed, hidden_units):
    count, width = rows.shape
    tile = count // 2
    steps = hidden_units // width
    line = pl.BlockSpec((tile, width), lambda m, w: (m, 0))
    block = pl.BlockSpec((tile, width), lambda m, w: (m, w))
    column = pl.BlockSpec((tile, 1), lambda m, w: (m, 0))
    whole = lambda shape: pl.BlockSpec(shape, lambda m, w: (0, 0))
    low = jax.ShapeDtypeStruct((count, width), BF16)
    wide = jax.ShapeDtypeStruct((count, hidden_units), BF16)
    return pl.pallas_call(
        ffn_kernel,
        grid=(2, steps),
        in_specs=[line, line, line, whole(vec.shape)] + packed_specs(width),
        out_specs=[block, block, line, line, column, line, line, whole((8, width))],
        out_shape=[
            wide,
            wide,
            low,
            low,
            jax.ShapeDtypeStruct((count, 1), F32),
            low,
            low,
            jax.ShapeDtypeStruct((8, width), F32),
        ],
        scratch_shapes=[pltpu.VMEM((tile, width), F32)] * 2,
        compiler_params=pltpu.CompilerParams(vmem_limit_bytes=VMEM),
        cost_estimate=pl.CostEstimate(
            flops=2 * count * width * (2 * hidden_units + width),
            bytes_accessed=4 * count * (hidden_units + 4 * width) + 8 * width * hidden_units,
            transcendentals=2 * count * hidden_units,
        ),
        name="ffn",
    )(mixed, rows, cotan, vec, packed, packed, packed)


def ffn_back(grad, slope, normed, scale, vec, packed, after):
    count, width = grad.shape
    hidden_units = slope.shape[1]
    tile = count // 2
    steps = hidden_units // width
    line = pl.BlockSpec((tile, width), lambda m, w: (m, 0))
    block = pl.BlockSpec((tile, width), lambda m, w: (m, w))
    column = pl.BlockSpec((tile, 1), lambda m, w: (m, 0))
    whole = lambda shape: pl.BlockSpec(shape, lambda m, w: (0, 0))
    low = jax.ShapeDtypeStruct((count, width), BF16)
    return pl.pallas_call(
        ffn_back_kernel,
        grid=(2, steps),
        in_specs=[line, block, line, column, whole(vec.shape)]
        + packed_specs(width)
        + [pl.BlockSpec(memory_space=pl.ANY)],
        out_specs=[block, line, line, line, whole((8, width))],
        out_shape=[
            jax.ShapeDtypeStruct((count, hidden_units), BF16),
            low,
            low,
            low,
            jax.ShapeDtypeStruct((8, width), F32),
        ],
        scratch_shapes=[pltpu.VMEM((tile, width), F32)],
        compiler_params=pltpu.CompilerParams(vmem_limit_bytes=VMEM),
        cost_estimate=pl.CostEstimate(
            flops=2 * count * width * (2 * hidden_units + width),
            bytes_accessed=4 * count * (hidden_units + 2 * width) + 8 * width * hidden_units,
            transcendentals=0,
        ),
        name="ffn_back",
    )(grad, slope, normed, scale, vec, packed, packed, packed, after)


def attend_kernel(seg_row_ref, seg_col_ref, qkv_ref, out_ref, lse_ref, bias_ref, stat_ref):
    pair = pl.program_id(1)
    length = bias_ref.shape[0]
    chunk = 128

    @pl.when(pair == 0)
    def _():
        bias_ref[...] = jnp.where(seg_col_ref[0] == seg_row_ref[0], 0.0, MASKED)
        stat_ref[...] = jnp.zeros_like(stat_ref)

    block = qkv_ref[:, 0].reshape(length, 3 * PAIR)
    q, k, v = (block[:, i * PAIR : (i + 1) * PAIR] for i in range(3))
    lane = lax.broadcasted_iota(jnp.int32, (length, PAIR), 1)
    low = lane < HD
    zero, one = jnp.zeros_like(q), jnp.ones_like(v)
    q_heads = [jnp.where(low, q, zero), jnp.where(low, zero, q)]
    v_heads = [jnp.where(low, v, one), jnp.where(low, one, v)]
    lane, low = lane[:chunk], low[:chunk]
    for c in range(length // chunk):
        rows = slice(c * chunk, (c + 1) * chunk)
        got, tops = [], []
        for h in range(2):
            s = lax.dot_general(q_heads[h][rows], k, NT, preferred_element_type=F32)
            s = s + bias_ref[rows, :]
            top = jnp.max(s, axis=1, keepdims=True)
            e = jnp.exp(s - top).astype(BF16)
            got.append(jnp.dot(e, v_heads[h], preferred_element_type=F32))
            tops.append(top)
        total = jnp.where(low, got[1], got[0])
        mixed = jnp.where(low, got[0], got[1]) / pltpu.roll(total, HD, 1)
        log = jnp.log(total)
        stat = stat_ref[rows, :]
        stat = jnp.where(lane == 2 * pair, tops[0] + log[:, HD : HD + 1], stat)
        stat_ref[rows, :] = jnp.where(lane == 2 * pair + 1, tops[1] + log[:, :1], stat)
        part = c * chunk // out_ref.shape[2]
        at = c * chunk % out_ref.shape[2]
        out_ref[part, 0, at : at + chunk, :] = mixed.astype(BF16)

    @pl.when(pair == pl.num_programs(1) - 1)
    def _():
        lse_ref[0] = jnp.transpose(stat_ref[...])[: lse_ref.shape[1]]


def attend_back_kernel(first_pair, after, *refs):
    seg_row_ref, seg_col_ref, qkv_ref, out_ref, grad_ref, lse_ref = refs[:6]
    dqkv_ref, bias_ref, ds_ref = refs[6 + after :]
    pair = pl.program_id(1)
    length = bias_ref.shape[0]
    half = qkv_ref.shape[2]
    chunk = 128

    @pl.when(pair == 0)
    def _():
        bias_ref[...] = jnp.where(seg_col_ref[0] == seg_row_ref[0], 0.0, MASKED)

    block = qkv_ref[:, 0].reshape(length, 3 * PAIR)
    q, k, v = (block[:, i * PAIR : (i + 1) * PAIR] for i in range(3))
    out = out_ref[:, 0].reshape(length, PAIR)
    grad = grad_ref[:, 0].reshape(length, PAIR)
    lane = lax.broadcasted_iota(jnp.int32, (length, PAIR), 1)
    zero = jnp.zeros_like(q)
    product = jnp.transpose(out.astype(F32) * grad.astype(F32))
    dq = jnp.zeros((length, PAIR), F32)
    chunks = length // chunk
    dk = [jnp.zeros((chunk, PAIR), F32) for _ in range(chunks)]
    dv = [jnp.zeros((chunk, PAIR), F32) for _ in range(chunks)]
    for h in range(2):
        mine = (lane // HD) == h
        qh = jnp.where(mine, q, zero)
        kh = jnp.where(mine, k, zero)
        gh = jnp.where(mine, grad, zero)
        delta = jnp.sum(product[h * HD : (h + 1) * HD], axis=0, keepdims=True)
        lse = lse_ref[0, pl.ds(2 * (first_pair + pair) + h, 1), :]
        for c in range(chunks):
            rows = slice(c * chunk, (c + 1) * chunk)
            s = lax.dot_general(k[rows], qh, NT, preferred_element_type=F32) + bias_ref[rows, :]
            p = jnp.exp(s - lse)
            dp = lax.dot_general(v[rows], gh, NT, preferred_element_type=F32)
            ds = (p * (dp - delta)).astype(BF16)
            ds_ref[rows, :] = ds
            dv[c] = dv[c] + jnp.dot(p.astype(BF16), gh, preferred_element_type=F32)
            dk[c] = dk[c] + jnp.dot(ds, qh, preferred_element_type=F32)
        dq = dq + lax.dot_general(ds_ref[...], kh, TN, preferred_element_type=F32)
    dqkv_ref[:, 0, :, :PAIR] = (dq * HD**-0.5).astype(BF16).reshape(-1, half, PAIR)
    for c in range(chunks):
        part, at = c * chunk // half, c * chunk % half
        dqkv_ref[part, 0, at : at + chunk, PAIR : 2 * PAIR] = dk[c].astype(BF16)
        dqkv_ref[part, 0, at : at + chunk, 2 * PAIR :] = dv[c].astype(BF16)


def attention_call(kernel, seg, arrays, outs, scratch, flops, name, first=0, after=()):
    parts, seqs, half, columns = arrays[0].shape
    length = parts * half

    def spec(array, first):
        shape = array.shape
        if len(shape) == 3:
            return pl.BlockSpec((1,) + shape[1:], lambda s, p: (s, 0, 0))
        size = 3 * PAIR if shape[3] % (3 * PAIR) == 0 else PAIR
        return pl.BlockSpec((parts, 1, half, size), lambda s, p: (0, s, 0, first + p))

    size = 3 * PAIR if outs[0].shape[3] % (3 * PAIR) == 0 else PAIR
    pairs = outs[0].shape[3] // size
    operands = [seg[:, None, :], seg[:, :, None]] + arrays
    moved = sum(a.size * a.dtype.itemsize for a in arrays + outs)
    return pl.pallas_call(
        kernel,
        grid=(seqs, pairs),
        in_specs=[spec(a, first) for a in operands]
        + [pl.BlockSpec(memory_space=pl.ANY)] * len(after),
        out_specs=[spec(a, 0) for a in outs],
        out_shape=outs,
        scratch_shapes=scratch(length),
        compiler_params=pltpu.CompilerParams(vmem_limit_bytes=VMEM),
        cost_estimate=pl.CostEstimate(
            flops=flops * 2 * seqs * pairs * length * length * PAIR * 4,
            bytes_accessed=moved,
            transcendentals=seqs * pairs * 2 * length * length,
        ),
        name=name,
    )(*operands, *after)


def attend(qkv, seg):
    parts, seqs, half, columns = qkv.shape
    heads = columns // (3 * HD)
    outs = [
        jax.ShapeDtypeStruct((parts, seqs, half, columns // 3), BF16),
        jax.ShapeDtypeStruct((seqs, heads, parts * half), F32),
    ]
    scratch = lambda length: [pltpu.VMEM((length, length), F32), pltpu.VMEM((length, PAIR), F32)]
    return attention_call(attend_kernel, seg, [qkv], outs, scratch, 2, "attend")


def attend_back(qkv, seg, out, grad, lse, first, pairs, after):
    outs = [jax.ShapeDtypeStruct(qkv.shape[:3] + (3 * PAIR * pairs,), BF16)]
    scratch = lambda length: [pltpu.VMEM((length, length), F32), pltpu.VMEM((length, length), BF16)]
    kernel = functools.partial(attend_back_kernel, first, len(after))
    arrays = [qkv, out, grad, lse]
    name = "attend_back"
    return attention_call(kernel, seg, arrays, outs, scratch, 5, name, first, after)[0]


def body(
    layer_input,
    segment_ids,
    out_cotangent,
    attn_master,
    inner_master,
    outer_master,
    vector_master,
    attn_moment,
    inner_moment,
    outer_moment,
    vector_moment,
    attn_square,
    inner_square,
    outer_square,
    vector_square,
):
    seqs, half, width = layer_input.shape
    count = seqs * half
    hidden_units = inner_master.shape[1]
    pairs = width // (2 * PAIR)
    part_cols = width // 2
    shards = lax.axis_size("shard")
    owned_rows = attn_master.shape[1]
    core = lax.axis_index("ctx")
    first = core == 0

    def own_half(array, axis):
        size = array.shape[axis] // 2
        return lax.dynamic_slice_in_dim(array, core * size, size, axis)

    def other_half(array, axis):
        size = array.shape[axis] // 2
        return lax.dynamic_slice_in_dim(array, (1 - core) * size, size, axis)

    def in_order(mine, theirs, axis):
        return jnp.concatenate(
            [jnp.where(first, mine, theirs), jnp.where(first, theirs, mine)], axis
        )

    rows = layer_input.reshape(count, width)
    rows_chip = jnp.concatenate([rows, swap_cores(rows)], 0)
    square = is_square()

    piece = own_half(attn_master[:3], 2).astype(BF16).reshape(3, owned_rows, pairs, PAIR)
    piece = piece.transpose(1, 2, 0, 3).reshape(owned_rows, 3 * part_cols)
    vec_low = vector_master.astype(BF16)
    rider = vec_low[:2].reshape(1, -1)
    if square:
        piece = lax.dynamic_slice_in_dim(
            piece, lax.axis_index("replica") * (piece.shape[1] // 2), piece.shape[1] // 2, 1
        )
    rider = jnp.pad(rider, ((0, 15), (0, piece.shape[1] - rider.shape[1])))
    piece = jnp.concatenate([piece, rider], 0)
    if square:
        stacks, places = gather_quarters(piece)
    else:
        stacks = [item[None] for item in ring_gather(piece)]
        places = [(owner, 0) for owner in slot_owners()]
    riders = jnp.concatenate([stack[:, owned_rows] for stack in stacks], 0)[:shards]
    riders = riders[:, : 2 * width // shards].reshape(shards, 2, -1).astype(F32)
    slot_of = jnp.stack([place[0] for place in places[:shards]])
    chosen = (jnp.arange(shards)[:, None] == slot_of[None, :]).astype(F32)
    biases = jnp.einsum("ps,srw->rpw", chosen, riders).reshape(2, width)

    copies = lax.axis_size("replica") * 2
    copy_at = lax.axis_index("replica") * 2 + core
    quarter = lambda block: lax.dynamic_slice_in_dim(
        block, copy_at * (block.shape[0] // copies), block.shape[0] // copies, 0
    ).astype(BF16)
    out_q, inner_q, outer_q = quarter(attn_master[3]), quarter(inner_master), quarter(outer_master)
    wide = hidden_units // width
    small = out_q.shape[0]
    inner_q = inner_q.reshape(small, wide, width).transpose(1, 0, 2).reshape(-1, width)
    big = outer_q.shape[0]
    vec_q = vec_low.reshape(-1)
    vec_q = jnp.pad(vec_q, (0, 16 * width - vec_q.shape[0])).reshape(16, width)
    packed = lax.all_gather(jnp.concatenate([outer_q, inner_q, out_q, vec_q], 0), EVERY, axis=0)
    vec = packed[::copies, 2 * big + small :].reshape(shards, -1)[:, : vec_low.size]
    vec = vec.reshape((shards,) + vec_low.shape).transpose(1, 0, 2).reshape(-1, width).astype(F32)
    if packed.shape[0] != PARTS:
        outer_w = packed[:, :big].reshape(PARTS, -1, width)
        inner_w = packed[:, big : 2 * big].reshape(-1, wide, small, width).transpose(0, 2, 1, 3)
        inner_w = inner_w.reshape(PARTS, -1, wide, width).transpose(0, 2, 1, 3)
        out_w = packed[:, 2 * big : 2 * big + small].reshape(PARTS, -1, width)
        packed = jnp.concatenate([outer_w, inner_w.reshape(PARTS, -1, width), out_w], 1)

    halves = own_half(biases, 1).reshape(2, pairs, PAIR)
    bias = jnp.stack([halves[0], jnp.zeros_like(halves[0]), halves[1]], 1).reshape(1, -1)
    ones = jnp.ones((pairs, PAIR), F32)
    factor = jnp.stack([ones * HD**-0.5, ones, ones], 1).reshape(1, -1)
    qkv, qkv_w = project(rows_chip, stacks, places, bias, factor)
    qkv = qkv.reshape(2, seqs, half, 3 * part_cols)
    seg = jnp.concatenate([own_half(segment_ids, 1), other_half(segment_ids, 1)], 1)
    mixed, lse = attend(qkv, seg)
    mixed_back = swap_cores(mixed[1].reshape(count, part_cols))
    heads_out = in_order(mixed[0].reshape(count, part_cols), mixed_back, 1)

    cotan = out_cotangent.reshape(count, width)
    active, slope, hidden_low, normed, scale, result, ffn_grad, sums_two = ffn(
        heads_out, rows, cotan, vec, packed, hidden_units
    )

    def send_half(left, right):
        return contract_rows(left, other_half(right, 1)).astype(BF16)

    def keep_half(left, right, sent):
        mine = contract_rows(left, own_half(right, 1)) + swap_cores(sent).astype(F32)
        return mine.astype(BF16).reshape(shards, -1, mine.shape[1])

    o, i, y, inner = position()
    where = jnp.stack([o, i, y, core]).astype(jnp.int32)
    outer_sent = send_half(active, ffn_grad)
    pre_grad, branch_grad, mixed_grad, grad_again, sums_one = ffn_back(
        ffn_grad, slope, normed, scale, vec, packed, outer_sent
    )
    mixed_grad = jnp.stack(
        [own_half(mixed_grad, 1), swap_cores(other_half(mixed_grad, 1))], 0
    ).reshape(mixed.shape)
    inner_sent = send_half(hidden_low, pre_grad)
    out_sent = send_half(heads_out, branch_grad)
    outer_chip = keep_half(active, grad_again, outer_sent)
    inner_chip = keep_half(hidden_low, pre_grad, inner_sent)
    out_chip = keep_half(heads_out, branch_grad, out_sent)
    by_shard = lambda array: array.astype(BF16).reshape(shards, owned_rows, -1)

    def back(first, after):
        return attend_back(
            qkv, seg, mixed, mixed_grad, lse, first, pairs // 2, after
        ).reshape(2 * count, -1)

    def bias_sums(grad):
        sums = jnp.sum(grad.astype(F32), 0).reshape(-1, 3, PAIR)
        return sums[:, 0].reshape(-1), sums[:, 2].reshape(-1)

    def make_chip_a(grad):
        return jnp.concatenate([by_shard(contract_rows(rows_chip, grad)), out_chip], 2)

    def make_chip_b(grad_a, grad_b):
        bias_a, bias_b = bias_sums(grad_a), bias_sums(grad_b)
        blank = jnp.zeros((part_cols,), F32)
        attn_biases = [
            in_order(jnp.concatenate([bias_a[at], bias_b[at]]), blank, 0) for at in range(2)
        ]
        sums = [jnp.stack(attn_biases), sums_one[2:3], sums_one[:2], sums_two[2:3], sums_two[:2]]
        sums = jnp.concatenate(sums + [sums_one[4:8]], 0)
        sums = sums.reshape(-1, shards, width // shards).transpose(1, 0, 2)
        sums = jnp.pad(sums, ((0, 0), (0, owned_rows - sums.shape[1]), (0, 0)))
        return jnp.concatenate([by_shard(contract_rows(rows_chip, grad_b)), sums.astype(BF16)], 2)

    outer_states = (outer_master, outer_moment, outer_square)
    inner_states = (inner_master, inner_moment, inner_square)
    attn_states = (attn_master, attn_moment, attn_square)
    if square:
        outer, inner = Sum(where, outer_chip), Sum(where, inner_chip)
        done = outer.split()
        done = inner.split(done)
        grad_a = back(0, done + (out_sent,))
        done = outer.plane((grad_a,))
        sum_a = Sum(where, make_chip_a(grad_a))
        done = sum_a.split(done)
        grad_b = back(pairs // 2, done)
        done = inner.plane((grad_b,))
        done = outer.cross(done)
        sum_b = Sum(where, make_chip_b(grad_a, grad_b))
        done = sum_b.split(done)
        done = sum_a.plane(done)
        theirs_part = input_back(grad_a, grad_b, qkv_w, (), done)
        done = inner.cross((theirs_part,))
        done = sum_b.plane(done)
        input_grad = input_back(
            grad_a, grad_b, qkv_w, (branch_grad, swap_cores(theirs_part)), done
        )
        done = sum_a.cross((input_grad,))
        done = outer.line(done)
        done = sum_b.cross(done)
        done = inner.line(done)
        outer_new = update(where, outer_states, [outer.shares], done)
        done = sum_a.line((outer_new[0],))
        inner_new = update(where, inner_states, [inner.shares], done)
        sum_b.line((inner_new[0],))
        attn_shares = [sum_a.shares, sum_b.shares]
        vector_shares = [
            jnp.concatenate(
                [
                    jnp.where(y == 0, sum_b.shares[at], sum_b.shares[at + 1])[0],
                    jnp.where(y == 0, sum_b.shares[at + 1], sum_b.shares[at])[0],
                ],
                0,
            )
            for at in (0, 2)
        ]
    else:
        grad_a = back(0, ())
        grad_b = back(pairs // 2, ())
        theirs_part = input_back(grad_a, grad_b, qkv_w, (), ())
        added = (branch_grad, swap_cores(theirs_part))
        input_grad = input_back(grad_a, grad_b, qkv_w, added, ())
        outer_new = update(where, outer_states, [sum_apart(outer_chip)])
        inner_new = update(where, inner_states, [sum_apart(inner_chip)])
        attn_shares = [sum_apart(make_chip_a(grad_a)), sum_apart(make_chip_b(grad_a, grad_b))]
        vector_shares = [share[0] for share in attn_shares[1]]
    attn_new = update(where, attn_states, attn_shares)
    cut = grad_b.shape[1]
    vector_sum = sum(share[: vec_low.shape[0], cut:].astype(F32) for share in vector_shares)
    vector_new = adamw(vector_sum, vector_moment, vector_square, vector_master, RATE_VECTOR)
    vector_new = vector_new + (vector_new[2].astype(BF16),)
    news = (attn_new, inner_new, outer_new, vector_new)
    updates = [[new[at] for new in news] for at in range(4)]
    return (
        result.reshape(seqs, half, width).astype(BF16),
        input_grad.reshape(seqs, half, width),
        *[item for kind in updates for item in kind],
    )


def solution(mesh):
    tokens = P(("replica", "shard"), "ctx", None)
    states = (P(None, "shard", None), P("shard", None), P("shard", None), P(None, "shard"))
    in_specs = (tokens, P(("replica", "shard"), None), tokens) + states * 3
    out_specs = (tokens, tokens) + states * 4
    return jax.shard_map(body, mesh=mesh, in_specs=in_specs, out_specs=out_specs, check_vma=False)
```

```python
import functools

import jax
import jax.numpy as jnp
from jax import lax
from jax.experimental import pallas as pl
from jax.experimental.pallas import tpu as pltpu
from jax.sharding import PartitionSpec as P

HD = 64
PAIR = 2 * HD
STEP = 5
OUTER = 4
EVERY = ("shard", "replica", "ctx")

EPS_NORM = 1e-05
BETA_ONE = 0.5
BETA_TWO = 0.6
RATE_MATRIX = 0.02
RATE_VECTOR = 0.1
DECAY = 0.01
EPS_ADAM = 1e-06
MASKED = -1e30
F32 = jnp.float32
BF16 = jnp.bfloat16
PARTS = 32
TILE = 32
VMEM = 56 * 1024 * 1024
SMALL_VMEM = 16 * 1024 * 1024
NT = (((1,), (1,)), ((), ()))
TN = (((0,), (0,)), ((), ()))


def contract_rows(left, right):
    return jnp.einsum("rd,re->de", left, right, preferred_element_type=F32)


def normalize(resid):
    centre = resid - jnp.mean(resid, -1, keepdims=True)
    scale = lax.rsqrt(jnp.mean(centre * centre, -1, keepdims=True) + EPS_NORM)
    return (centre * scale, scale)


def norm_back(grad, normed, scale):
    return scale * (
        grad
        - jnp.mean(grad, -1, keepdims=True)
        - normed * jnp.mean(grad * normed, -1, keepdims=True)
    )


def adamw(grad, moment, square, weight, rate):
    moment_new = BETA_ONE * moment + (1.0 - BETA_ONE) * grad
    square_new = BETA_TWO * square + (1.0 - BETA_TWO) * grad * grad
    stepped = (
        moment_new
        / (1.0 - BETA_ONE**STEP)
        / (jnp.sqrt(square_new / (1.0 - BETA_TWO**STEP)) + EPS_ADAM)
    )
    weight_new = weight - rate * (stepped + DECAY * weight)
    return (moment_new, square_new, weight_new)


def swap_cores(value):
    return lax.ppermute(value, "ctx", [(0, 1), (1, 0)])


def shift_outer(value, step):
    inner = lax.axis_size("shard") // OUTER
    pairs = [
        (o * inner + i, ((o + step) % OUTER) * inner + i) for o in range(OUTER) for i in range(inner)
    ]
    return lax.ppermute(value, "shard", pairs)


def shift_inner(value, step):
    inner = lax.axis_size("shard") // OUTER
    pairs = [
        (o * inner + i, o * inner + (i + step) % inner) for o in range(OUTER) for i in range(inner)
    ]
    return lax.ppermute(value, "shard", pairs)


def shift_replica(value, step):
    size = lax.axis_size("replica")
    return lax.ppermute(value, "replica", [(r, (r + step) % size) for r in range(size)])


def ring_gather(piece):
    inner = lax.axis_size("shard") // OUTER
    found = []
    held = piece
    for k in range(OUTER):
        if k:
            held = shift_outer(held, -1)
        found.append([held] + [shift_inner(held, -e) for e in range(1, inner)])
    return [item for group in found for item in group]


def slot_owners():
    inner = lax.axis_size("shard") // OUTER
    at = lax.axis_index("shard")
    o, i = at // inner, at % inner
    return [
        lax.rem(o + k, OUTER) * inner + lax.rem(i + e, inner)
        for k in range(OUTER)
        for e in range(inner)
    ]


def pick(array, index, axis):
    return lax.dynamic_index_in_dim(array, index, axis, keepdims=False)


def add_low(value, *others):
    total = value.astype(F32)
    for item in others:
        total = total + item.astype(F32)
    return total.astype(BF16)


def position():
    inner = lax.axis_size("shard") // OUTER
    at = lax.axis_index("shard")
    return at // inner, at % inner, lax.axis_index("replica"), inner


def is_square():
    return lax.axis_size("replica") == 2 and lax.axis_size("shard") == 2 * OUTER


def swap_cross(value):
    return lax.ppermute(value, ("replica", "ctx"), [(a, 3 - a) for a in range(4)])


def sum_apart(chip_sum):
    o, i, y, inner = position()
    grid = chip_sum.reshape(OUTER, inner, *chip_sum.shape[1:])
    got = [shift_inner(pick(grid, lax.rem(i + e, inner), 1), e) for e in range(1, inner)]
    line = add_low(pick(grid, i, 1), *got)
    got = [shift_outer(pick(line, lax.rem(o + d, OUTER), 0), d) for d in range(1, OUTER)]
    total = add_low(pick(line, o, 0), *got)
    got = [shift_replica(total, r) for r in range(1, lax.axis_size("replica"))]
    mine = add_low(total, *got)[None]
    return [mine, swap_cores(mine)]


def small_call(kernel, where, ins, outs, after, name):
    moved = sum(a.size * a.dtype.itemsize for a in ins)
    held = pl.BlockSpec(memory_space=pltpu.VMEM)
    return pl.pallas_call(
        functools.partial(kernel, len(ins), len(after)),
        in_specs=[pl.BlockSpec(memory_space=pltpu.SMEM)]
        + [held] * len(ins)
        + [pl.BlockSpec(memory_space=pl.ANY)] * len(after),
        out_specs=[held] * len(outs),
        out_shape=[pltpu.VMEM(shape, BF16) for shape in outs],
        compiler_params=pltpu.CompilerParams(vmem_limit_bytes=SMALL_VMEM),
        cost_estimate=pl.CostEstimate(flops=moved, bytes_accessed=moved, transcendentals=0),
        name=name,
    )(where, *[pltpu.with_memory_space_constraint(a, pltpu.VMEM) for a in ins], *after)


def fold_plane_kernel(count, after, where_ref, keep_p, got_p, keep_q, got_q, *rest):
    i, y = where_ref[1], where_ref[2]
    kept_p, send_p, kept_q, send_q = rest[after:]
    for o in range(OUTER):
        for out, at in ((kept_p, y), (send_p, 1 - y)):
            out[o] = add_low(keep_p[o, at], got_p[o, at])
        for out, at in ((kept_q, i), (send_q, 1 - i)):
            out[o] = add_low(keep_q[o, at], got_q[o, at])


def fold_cross_kernel(count, after, where_ref, keep_p, got_p, keep_q, got_q, *rest):
    for d, out in enumerate(rest[after:]):
        at = lax.rem(where_ref[0] + d, OUTER)
        out[0] = add_low(keep_p[at], got_p[at])
        out[1] = add_low(keep_q[at], got_q[at])


def fold_line_kernel(count, after, where_ref, *rest):
    for at in range(2):
        rest[count + after][at] = add_low(*(ref[at] for ref in rest[:count]))


def merge_kernel(chips, after, where_ref, *refs):
    send_p, send_q, keep_p, keep_q = refs[4 * chips + after :]
    for slot, out, lead in ((0, send_p, 0), (1, send_q, 1), (2, keep_p, 0), (3, keep_q, 1)):
        for at in range(2):
            pick_one = lambda ref: ref[0, 0, 0, at] if lead == 0 else ref[0, at, 0, 0]
            parts = [pick_one(refs[4 * chip + slot]) for chip in range(chips)]
            out[0, at] = parts[0] if chips == 1 else add_low(*parts)


class Sum:
    def __init__(self, where, *chips):
        rows, self.columns = chips[0].shape[1:]
        self.where, self.rows = where, rows // 4
        self.chips = [c.reshape(OUTER, 2, 2, 2, self.rows, self.columns) for c in chips]

    def shape(self, *lead):
        return lead + (self.rows, self.columns)

    def merge(self, after=()):
        block = (self.rows, self.columns)

        def spec(lead, flip):
            def place(o, w):
                at = w[1] if lead == 0 else w[2]
                at = 1 - at if flip else at
                return (o, at, 0, 0, 0, 0) if lead == 0 else (o, 0, 1, at, 0, 0)

            return pl.BlockSpec(((1, 1, 1, 2) if lead == 0 else (1, 2, 1, 1)) + block, place)

        specs = [spec(0, True), spec(1, True), spec(0, False), spec(1, False)]
        moved = 4 * sum(chip.size for chip in self.chips)
        out_spec = pl.BlockSpec((1, 2) + block, lambda o, w: (o, 0, 0, 0))
        *self.sent, keep_p, keep_q = pl.pallas_call(
            functools.partial(merge_kernel, len(self.chips), len(after)),
            grid_spec=pltpu.PrefetchScalarGridSpec(
                num_scalar_prefetch=1,
                grid=(OUTER,),
                in_specs=specs * len(self.chips)
                + [pl.BlockSpec(memory_space=pl.ANY)] * len(after),
                out_specs=[out_spec] * 4,
            ),
            out_shape=[jax.ShapeDtypeStruct(self.shape(OUTER, 2), BF16)] * 4,
            compiler_params=pltpu.CompilerParams(vmem_limit_bytes=SMALL_VMEM),
            cost_estimate=pl.CostEstimate(flops=moved, bytes_accessed=moved, transcendentals=0),
            name="merge",
        )(self.where, *[chip for chip in self.chips for _ in range(4)], *after)
        got_p, got_q = shift_inner(self.sent[0], 1), shift_replica(self.sent[1], 1)
        self.kept = [keep_p, got_p, keep_q, got_q]
        return tuple(self.sent)

    def plane(self, after=()):
        keep_p, send_p, keep_q, send_q = small_call(
            fold_plane_kernel, self.where, self.kept, [self.shape(OUTER)] * 4, after, "fold_plane"
        )
        self.kept = [keep_p, shift_replica(send_p, 1), keep_q, shift_inner(send_q, 1)]
        return (send_p, send_q)

    def cross(self, after=()):
        kept, *sent = small_call(
            fold_cross_kernel, self.where, self.kept, [self.shape(2)] * OUTER, after, "fold_cross"
        )
        self.kept = [kept] + [shift_outer(item, d + 1) for d, item in enumerate(sent)]
        return tuple(sent)

    def line(self, after=()):
        (total,) = small_call(
            fold_line_kernel, self.where, self.kept, [self.shape(2)], after, "fold_line"
        )
        self.shares = [total, shift_replica(total, 1), swap_cores(total), swap_cross(total)]
        return (total,)


def update_kernel(groups, after, where_ref, *refs):
    states, shares = refs[:3], refs[3 : 3 + sum(groups)]
    outs, grad_ref = refs[3 + sum(groups) + after : -1], refs[-1]
    rows = shares[0].shape[1]
    across = groups[0] // 2
    for core in range(2):

        @pl.when(pl.program_id(1) == core)
        def _():
            for n in range(across):
                line = where_ref[2] if n == 0 else 1 - where_ref[2]
                line = pl.ds(pl.multiple_of(line * rows, rows), rows) if across > 1 else slice(None)
                if len(groups) == 1:
                    grad_ref[line, :] = shares[across * core + n][0].astype(F32)
                    continue
                left, right = shares[across * core + n], shares[groups[0] + across * core + n]
                width = grad_ref.shape[2]
                pairs = width // PAIR
                for t in range(3):
                    for p in range(pairs):
                        side, at = (left, p) if 2 * p < pairs else (right, p - pairs // 2)
                        part = side[0, :, (3 * at + t) * PAIR : (3 * at + t + 1) * PAIR]
                        grad_ref[t, line, p * PAIR : (p + 1) * PAIR] = part.astype(F32)
                cut = 3 * PAIR * (pairs // 2)
                grad_ref[3, line, :] = left[0, :, cut : cut + width].astype(F32)

    new = adamw(grad_ref[...], states[1][...], states[2][...], states[0][...], RATE_MATRIX)
    for out, value in zip(outs, new + (new[2],)):
        out[...] = value.astype(out.dtype)


def update(where, states, groups, after=()):
    parts, rows = groups[0][0].shape[:2]
    rows = rows * (len(groups[0]) // 2)
    lead = states[0].shape[:-2]
    columns = states[0].shape[-1] // 2
    place = lambda p, v, w: (0,) * len(lead) + (p, w[3] + v - 2 * w[3] * v)
    block = pl.BlockSpec(lead + (rows, columns), place)
    shares = [share for group in groups for share in group]
    share_specs = [pl.BlockSpec((1,) + a.shape[1:], lambda p, v, w: (p, 0, 0)) for a in shares]
    kinds = (F32, F32, F32, BF16)
    return pl.pallas_call(
        functools.partial(update_kernel, [len(group) for group in groups], len(after)),
        grid_spec=pltpu.PrefetchScalarGridSpec(
            num_scalar_prefetch=1,
            grid=(parts, 2),
            in_specs=[block] * 3 + share_specs + [pl.BlockSpec(memory_space=pl.ANY)] * len(after),
            out_specs=[block] * 4,
            scratch_shapes=[pltpu.VMEM(lead + (rows, columns), F32)],
        ),
        out_shape=[jax.ShapeDtypeStruct(states[0].shape, kind) for kind in kinds],
        compiler_params=pltpu.CompilerParams(vmem_limit_bytes=SMALL_VMEM),
        cost_estimate=pl.CostEstimate(
            flops=20 * states[0].size, bytes_accessed=28 * states[0].size, transcendentals=0
        ),
        name="update",
    )(where, *states, *shares, *after)


def input_back_kernel(a_ref, b_ref, left_ref, right_ref, *rest):
    out_ref = rest[-1]
    total = lax.dot_general(a_ref[...], left_ref[...], NT, preferred_element_type=F32)
    total += lax.dot_general(b_ref[...], right_ref[...], NT, preferred_element_type=F32)
    if out_ref.dtype == F32:
        total += rest[0][...].astype(F32) + rest[1][...].astype(F32)
    out_ref[...] = total.astype(out_ref.dtype)


def input_back(grad_a, grad_b, weight, added, after):
    count, cut = grad_a.shape[0] // 2, grad_a.shape[1]
    width = weight.shape[0]
    tile = width // 4
    first = 0 if added else 1
    side = pl.BlockSpec((count, cut), lambda n: (first, 0))
    line = pl.BlockSpec((count, tile), lambda n: (0, n))
    return pl.pallas_call(
        input_back_kernel,
        grid=(width // tile,),
        in_specs=[side, side]
        + [pl.BlockSpec((tile, cut), lambda n, at=at: (n, at)) for at in range(2)]
        + [line] * len(added)
        + [pl.BlockSpec(memory_space=pl.ANY)] * len(after),
        out_specs=line,
        out_shape=jax.ShapeDtypeStruct((count, width), F32 if added else BF16),
        compiler_params=pltpu.CompilerParams(vmem_limit_bytes=SMALL_VMEM),
        cost_estimate=pl.CostEstimate(
            flops=4 * count * width * cut, bytes_accessed=8 * count * width, transcendentals=0
        ),
        name="input_back",
    )(grad_a, grad_b, weight, weight, *added, *after)


def gather_quarters(quarter):
    line = jnp.stack([quarter] + [shift_outer(quarter, -k) for k in range(1, OUTER)])
    near_x = shift_inner(line, 1)
    near_y = shift_replica(line, 1)
    far_x = shift_inner(near_y[: OUTER // 2], 1)
    far_y = shift_replica(near_x[OUTER // 2 :], 1)
    o, i, y, inner = position()
    row = lambda k, across: lax.rem(o + k, OUTER) * 2 + (1 - i if across else i)
    places = [(row(k, False), y) for k in range(OUTER)] + [(row(k, True), y) for k in range(OUTER)]
    places += [(row(k, False), 1 - y) for k in range(OUTER)]
    places += [(row(k, True), 1 - y) for k in range(OUTER)]
    return [line, near_x, near_y, far_x, far_y], places


def project_kernel(row_ref, column_ref, rows_ref, bias_ref, factor_ref, *rest):
    stacks, (out_ref, weight_ref) = rest[:-2], rest[-2:]
    columns = stacks[0].shape[2]
    part = weight_ref.shape[0] * weight_ref.shape[1] // columns
    part = part // sum(stack.shape[0] for stack in stacks)

    @pl.when(pl.program_id(0) == 0)
    def _():
        slot = 0
        for stack in stacks:
            for k in range(stack.shape[0]):
                start = pl.multiple_of(row_ref[slot] * part, part)
                left = pl.multiple_of(column_ref[slot] * columns, PAIR)
                weight_ref[pl.ds(start, part), pl.ds(left, columns)] = stack[k, :part, :]
                slot += 1

    acc = jnp.dot(rows_ref[...], weight_ref[...], preferred_element_type=F32)
    out_ref[...] = ((acc + bias_ref[...]) * factor_ref[...]).astype(BF16)


def project(rows, stacks, places, bias, factor):
    count, width = rows.shape
    columns = bias.shape[1]
    tile = 512
    whole = lambda shape: pl.BlockSpec(shape, lambda m, *_: (0,) * len(shape))
    tables = [jnp.stack([p[axis] for p in places]).astype(jnp.int32) for axis in range(2)]
    return pl.pallas_call(
        project_kernel,
        grid_spec=pltpu.PrefetchScalarGridSpec(
            num_scalar_prefetch=2,
            grid=(count // tile,),
            in_specs=[
                pl.BlockSpec((tile, width), lambda m, *_: (m, 0)),
                whole((1, columns)),
                whole((1, columns)),
            ]
            + [whole(stack.shape) for stack in stacks],
            out_specs=[
                pl.BlockSpec((tile, columns), lambda m, *_: (m, 0)),
                whole((width, columns)),
            ],
        ),
        out_shape=[
            jax.ShapeDtypeStruct((count, columns), BF16),
            jax.ShapeDtypeStruct((width, columns), BF16),
        ],
        compiler_params=pltpu.CompilerParams(vmem_limit_bytes=VMEM),
        cost_estimate=pl.CostEstimate(
            flops=2 * count * width * columns,
            bytes_accessed=2 * (count * width + count * columns + 2 * width * columns),
            transcendentals=0,
        ),
        name="project",
    )(*tables, rows, bias, factor, *stacks)


def gelu_and_slope(u):
    a = jnp.abs(u) * (0.5**0.5)
    d = 1.0 + 0.3275911 * a
    t = pl.reciprocal(d, approx=True)
    t = t * (2.0 - d * t)
    e = jnp.exp(-a * a)
    series = 1.061405429 * t - 1.453152027
    series = series * t + 1.421413741
    series = series * t - 0.284496736
    series = series * t + 0.254829592
    tail = 0.5 * series * t * e
    normal = jnp.where(u >= 0.0, 1.0 - tail, tail)
    return u * normal, normal + u * (0.3989422804014327 * e)


def total_rows(value):
    return jnp.sum(value, axis=0, keepdims=True)


def over_rows(count, step, work, unroll=2):
    def turn(at, carry):
        work(pl.ds(pl.multiple_of(at * step, step), step))
        return carry

    lax.fori_loop(0, count // step, turn, 0, unroll=unroll)


def ffn_kernel(
    mixed_ref,
    rows_ref,
    cotan_ref,
    vec_ref,
    out_w_ref,
    inner_w_ref,
    outer_w_ref,
    active_ref,
    slope_ref,
    hidden_ref,
    normed_ref,
    scale_ref,
    result_ref,
    grad_ref,
    sums_ref,
    resid,
    acc,
    pre,
):
    w = pl.program_id(0)
    count, width = acc.shape
    chunk = pre.shape[2]
    vec = lambda at: vec_ref[at : at + 1, :]

    @pl.when(w == 0)
    def _():
        acc[...] = jnp.dot(
            mixed_ref[...], out_w_ref[...].reshape(width, width), preferred_element_type=F32
        )

        def enter(part):
            normed, scale = normalize(acc[part, :] + vec(2) + rows_ref[part, :].astype(F32))
            normed_ref[part, :] = normed.astype(BF16)
            scale_ref[part, :] = scale
            hidden = normed * vec(3) + vec(4)
            resid[part, :] = hidden + vec(5)
            hidden_ref[part, :] = hidden.astype(BF16)
            acc[part, :] = jnp.zeros((TILE, width), F32)

        over_rows(count, TILE, enter)

    bias = vec_ref[pl.ds(8 + w, 1), :]

    def expand(n):
        cut = slice(n * chunk, (n + 1) * chunk)
        weight = inner_w_ref[:, :, cut].reshape(width, chunk)
        pre[n % 2] = jnp.dot(hidden_ref[...], weight, preferred_element_type=F32)

    def bend(n):
        cut = slice(n * chunk, (n + 1) * chunk)
        for at in range(0, count, TILE):
            part = slice(at, at + TILE)
            active, slope = gelu_and_slope(pre[n % 2, part, :] + bias[:, cut])
            active_ref[part, cut] = active.astype(BF16)
            slope_ref[part, cut] = slope.astype(BF16)

    def contract(first, last):
        cut = slice(first * chunk, last * chunk)
        weight = outer_w_ref[...].reshape(width, width)[cut]
        acc[...] += jnp.dot(active_ref[:, cut], weight, preferred_element_type=F32)

    chunks = width // chunk
    expand(0)
    for n in range(1, chunks):
        expand(n)
        bend(n - 1)
    contract(0, chunks - 1)
    bend(chunks - 1)
    contract(chunks - 1, chunks)

    @pl.when(w == pl.num_programs(0) - 1)
    def _():
        sums_ref[...] = jnp.zeros_like(sums_ref)

        def leave(part):
            normed, scale = normalize(resid[part, :] + acc[part, :])
            result_ref[part, :] = (normed * vec(6) + vec(7)).astype(BF16)
            cotan = cotan_ref[part, :].astype(F32)
            grad = norm_back(cotan * vec(6), normed, scale).astype(BF16)
            grad_ref[part, :] = grad
            sums_ref[0:1, :] += total_rows(cotan * normed)
            sums_ref[1:2, :] += total_rows(cotan)
            sums_ref[2:3, :] += total_rows(grad.astype(F32))

        over_rows(count, TILE, leave)


def ffn_back_kernel(
    grad_ref,
    slope_ref,
    normed_ref,
    scale_ref,
    vec_ref,
    out_w_ref,
    inner_w_ref,
    outer_w_ref,
    after_ref,
    pre_grad_ref,
    branch_ref,
    mixed_ref,
    sums_ref,
    acc,
    pre,
):
    w = pl.program_id(0)
    count, width = acc.shape
    chunk = pre.shape[2]
    vec = lambda at: vec_ref[at : at + 1, :]

    @pl.when(w == 0)
    def _():
        sums_ref[...] = jnp.zeros_like(sums_ref)

    def pull(n):
        each = outer_w_ref.shape[0] * chunk // width
        weight = outer_w_ref[n * each : (n + 1) * each].reshape(chunk, width)
        pre[n % 2] = lax.dot_general(grad_ref[...], weight, NT, preferred_element_type=F32)

    def bend(n):
        cut = slice(n * chunk, (n + 1) * chunk)
        sums = jnp.zeros((8, chunk), F32)
        for at in range(0, count, TILE):
            part = slice(at, at + TILE)
            back = pre[n % 2, part, :].astype(BF16).astype(F32) * slope_ref[part, cut].astype(F32)
            back = back.astype(BF16)
            pre_grad_ref[part, cut] = back
            sums += jnp.sum(back.astype(F32).reshape(TILE // 8, 8, chunk), axis=0)
        sums_ref[pl.ds(4 + w, 1), cut] += total_rows(sums)

    def contract(first, last):
        cut = slice(first * chunk, last * chunk)
        weight = inner_w_ref[:, :, cut].reshape(width, -1)
        return lax.dot_general(pre_grad_ref[:, cut], weight, NT, preferred_element_type=F32)

    chunks = width // chunk
    pull(0)
    for n in range(1, chunks):
        pull(n)
        bend(n - 1)
    more = contract(0, chunks - 1)

    @pl.when(w == 0)
    def _():
        acc[...] = more

    @pl.when(w > 0)
    def _():
        acc[...] += more

    bend(chunks - 1)
    acc[...] += contract(chunks - 1, chunks)

    @pl.when(w == pl.num_programs(0) - 1)
    def _():
        def leave(part):
            through = acc[part, :].astype(BF16).astype(F32) + grad_ref[part, :].astype(F32)
            normed = normed_ref[part, :].astype(F32)
            branch = norm_back(through * vec(3), normed, scale_ref[part, :]).astype(BF16)
            branch_ref[part, :] = branch
            sums_ref[0:1, :] += total_rows(through * normed)
            sums_ref[1:2, :] += total_rows(through)
            sums_ref[2:3, :] += total_rows(branch.astype(F32))

        over_rows(count, TILE, leave)
        mixed_ref[...] = lax.dot_general(
            branch_ref[...], out_w_ref[...].reshape(width, width), NT, preferred_element_type=F32
        ).astype(BF16)


def packed_specs(width):
    small = width // PARTS
    once = pl.Buffered(1)
    return [
        pl.BlockSpec((PARTS, small, width), lambda w: (0, 8, 0), pipeline_mode=once),
        pl.BlockSpec((PARTS, small, width), lambda w: (0, 4 + w, 0)),
        pl.BlockSpec((PARTS // 4, 4 * small, width), lambda w: (w, 0, 0)),
    ]


def ffn_call(kernel, ins, packed, after, wide_outs, outs, name):
    count, width = ins[0].shape
    steps = 4

    def spec(shape):
        if shape == (count, steps * width):
            return pl.BlockSpec((count, width), lambda w: (0, w))
        return pl.BlockSpec(shape, lambda w: (0, 0), pipeline_mode=pl.Buffered(1))

    shapes = [((count, steps * width), BF16)] * wide_outs + outs
    ffn_flops = 2 * count * width * (2 * steps + 1) * width
    return pl.pallas_call(
        kernel,
        grid=(steps,),
        in_specs=[spec(a.shape) for a in ins]
        + packed_specs(width)
        + [pl.BlockSpec(memory_space=pl.ANY)] * len(after),
        out_specs=[spec(shape) for shape, kind in shapes],
        out_shape=[jax.ShapeDtypeStruct(shape, kind) for shape, kind in shapes],
        scratch_shapes=[pltpu.VMEM((count, width), F32)] * wide_outs
        + [pltpu.VMEM((2, count, 256), F32)],
        compiler_params=pltpu.CompilerParams(vmem_limit_bytes=VMEM),
        cost_estimate=pl.CostEstimate(
            flops=ffn_flops,
            bytes_accessed=4 * count * (steps + 3) * width + 8 * steps * width * width,
            transcendentals=2 * count * steps * width * (wide_outs - 1),
        ),
        name=name,
    )(*ins, packed, packed, packed, *after)


def ffn(mixed, rows, cotan, vec, packed):
    low = (rows.shape, BF16)
    sums = ((8, rows.shape[1]), F32)
    outs = [low, low, ((rows.shape[0], 1), F32), low, low, sums]
    return ffn_call(ffn_kernel, [mixed, rows, cotan, vec], packed, (), 2, outs, "ffn")


def ffn_back(grad, slope, normed, scale, vec, packed, after):
    low = (grad.shape, BF16)
    outs = [low, low, ((8, grad.shape[1]), F32)]
    ins = [grad, slope, normed, scale, vec]
    return ffn_call(ffn_back_kernel, ins, packed, (after,), 1, outs, "ffn_back")


def attend_kernel(seg_row_ref, seg_col_ref, qkv_ref, out_ref, lse_ref, bias_ref, stat_ref, *more):
    score_ref, expo_ref = more
    pair = pl.program_id(1)
    length = bias_ref.shape[0]
    chunk = score_ref.shape[1]

    @pl.when(pair == 0)
    def _():
        bias_ref[...] = jnp.where(seg_col_ref[0] == seg_row_ref[0], 0.0, MASKED)
        stat_ref[...] = jnp.zeros_like(stat_ref)

    block = qkv_ref[:, 0].reshape(length, 3 * PAIR)
    q, k, v = (block[:, i * PAIR : (i + 1) * PAIR] for i in range(3))
    lane = lax.broadcasted_iota(jnp.int32, (length, PAIR), 1)
    low = lane < HD
    zero, one = jnp.zeros_like(q), jnp.ones_like(v)
    q_heads = [jnp.where(low, q, zero), jnp.where(low, zero, q)]
    v_heads = [jnp.where(low, v, one), jnp.where(low, one, v)]
    lane, low = lane[:chunk], low[:chunk]

    def score(step):
        c, h = divmod(step, 2)
        score_ref[step % 2] = lax.dot_general(
            q_heads[h][c * chunk : (c + 1) * chunk], k, NT, preferred_element_type=F32
        )

    def soften(step):
        c, h = divmod(step, 2)
        tops = []
        for at in range(0, chunk, TILE):
            rows = slice(c * chunk + at, c * chunk + at + TILE)
            s = score_ref[step % 2, at : at + TILE, :] + bias_ref[rows, :]
            top = jnp.max(s, axis=1, keepdims=True)
            expo_ref[step % 2, at : at + TILE, :] = jnp.exp(s - top).astype(BF16)
            tops.append(top)
        return jnp.concatenate(tops, 0)

    def mix(step):
        return jnp.dot(expo_ref[step % 2], v_heads[step % 2], preferred_element_type=F32)

    def finish(c, got, tops):
        rows = slice(c * chunk, (c + 1) * chunk)
        total = jnp.where(low, got[1], got[0])
        mixed = jnp.where(low, got[0], got[1]) / pltpu.roll(total, HD, 1)
        log = jnp.log(total)
        stat = stat_ref[rows, :]
        stat = jnp.where(lane == 2 * pair, tops[0] + log[:, HD : HD + 1], stat)
        stat_ref[rows, :] = jnp.where(lane == 2 * pair + 1, tops[1] + log[:, :1], stat)
        part = c * chunk // out_ref.shape[2]
        at = c * chunk % out_ref.shape[2]
        out_ref[part, 0, at : at + chunk, :] = mixed.astype(BF16)

    steps = 2 * length // chunk
    tops, got = [], []
    score(0)
    for step in range(steps):
        if step + 1 < steps:
            score(step + 1)
        tops.append(soften(step))
        got.append(mix(step))
        if step % 2:
            finish(step // 2, got[-2:], tops[-2:])

    @pl.when(pair == pl.num_programs(1) - 1)
    def _():
        lse_ref[0] = jnp.transpose(stat_ref[...])[: lse_ref.shape[1]]


def attend_back_kernel(first_pair, after, *refs):
    seg_row_ref, seg_col_ref, qkv_ref, out_ref, grad_ref, lse_ref = refs[:6]
    dqkv_ref, bias_ref, ds_ref, score_ref, slope_ref, prob_ref = refs[6 + after :]
    pair = pl.program_id(1)
    length = bias_ref.shape[0]
    half = qkv_ref.shape[2]
    chunk = score_ref.shape[1]

    @pl.when(pair == 0)
    def _():
        bias_ref[...] = jnp.where(seg_col_ref[0] == seg_row_ref[0], 0.0, MASKED)

    block = qkv_ref[:, 0].reshape(length, 3 * PAIR)
    q, k, v = (block[:, i * PAIR : (i + 1) * PAIR] for i in range(3))
    out = out_ref[:, 0].reshape(length, PAIR)
    grad = grad_ref[:, 0].reshape(length, PAIR)
    low = lax.broadcasted_iota(jnp.int32, (length, PAIR), 1) < HD
    zero = jnp.zeros_like(q)
    heads = lambda array: [jnp.where(low, array, zero), jnp.where(low, zero, array)]
    q_heads, k_heads, g_heads = heads(q), heads(k), heads(grad)
    product = jnp.transpose(out.astype(F32) * grad.astype(F32))
    chunks = length // chunk
    deltas = [total_rows(product[h * HD : (h + 1) * HD]) for h in range(2)]
    stats = [lse_ref[0, pl.ds(2 * (first_pair + pair) + h, 1), :] for h in range(2)]

    def score(step):
        h, c = divmod(step, chunks)
        rows = slice(c * chunk, (c + 1) * chunk)
        score_ref[step % 2] = lax.dot_general(k[rows], q_heads[h], NT, preferred_element_type=F32)
        slope_ref[step % 2] = lax.dot_general(v[rows], g_heads[h], NT, preferred_element_type=F32)

    def bend(step):
        h, c = divmod(step, chunks)
        for at in range(0, chunk, TILE):
            rows = slice(c * chunk + at, c * chunk + at + TILE)
            part = slice(at, at + TILE)
            p = jnp.exp(score_ref[step % 2, part, :] + bias_ref[rows, :] - stats[h])
            prob_ref[step % 2, part, :] = p.astype(BF16)
            ds_ref[h, rows, :] = (p * (slope_ref[step % 2, part, :] - deltas[h])).astype(BF16)

    steps = 2 * chunks
    dk, dv = [None] * chunks, [None] * chunks
    dq = None
    score(0)
    for step in range(steps):
        h, c = divmod(step, chunks)
        if step + 1 < steps:
            score(step + 1)
        bend(step)
        rows = slice(c * chunk, (c + 1) * chunk)
        v_part = jnp.dot(prob_ref[step % 2], g_heads[h], preferred_element_type=F32)
        k_part = jnp.dot(ds_ref[h, rows, :], q_heads[h], preferred_element_type=F32)
        if h == 0:
            dk[c], dv[c] = k_part, v_part
        else:
            part, at = c * chunk // half, c * chunk % half
            dqkv_ref[part, 0, at : at + chunk, PAIR : 2 * PAIR] = (dk[c] + k_part).astype(BF16)
            dqkv_ref[part, 0, at : at + chunk, 2 * PAIR :] = (dv[c] + v_part).astype(BF16)
        if c == chunks - 1:
            part = lax.dot_general(ds_ref[h], k_heads[h], TN, preferred_element_type=F32)
            dq = part if h == 0 else dq + part
    dqkv_ref[:, 0, :, :PAIR] = (dq * HD**-0.5).astype(BF16).reshape(-1, half, PAIR)


def attention_call(kernel, seg, arrays, outs, scratch, flops, name, first=0, after=()):
    parts, seqs, half, columns = arrays[0].shape
    length = parts * half

    def spec(array, first):
        shape = array.shape
        if len(shape) == 3:
            return pl.BlockSpec((1,) + shape[1:], lambda s, p: (s, 0, 0))
        size = 3 * PAIR if shape[3] % (3 * PAIR) == 0 else PAIR
        return pl.BlockSpec((parts, 1, half, size), lambda s, p: (0, s, 0, first + p))

    size = 3 * PAIR if outs[0].shape[3] % (3 * PAIR) == 0 else PAIR
    pairs = outs[0].shape[3] // size
    operands = [seg[:, None, :], seg[:, :, None]] + arrays
    moved = sum(a.size * a.dtype.itemsize for a in arrays + outs)
    return pl.pallas_call(
        kernel,
        grid=(seqs, pairs),
        in_specs=[spec(a, first) for a in operands]
        + [pl.BlockSpec(memory_space=pl.ANY)] * len(after),
        out_specs=[spec(a, 0) for a in outs],
        out_shape=outs,
        scratch_shapes=scratch(length),
        compiler_params=pltpu.CompilerParams(vmem_limit_bytes=SMALL_VMEM),
        cost_estimate=pl.CostEstimate(
            flops=flops * 2 * seqs * pairs * length * length * PAIR * 4,
            bytes_accessed=moved,
            transcendentals=seqs * pairs * 2 * length * length,
        ),
        name=name,
    )(*operands, *after)


def attend(qkv, seg):
    parts, seqs, half, columns = qkv.shape
    heads = columns // (3 * HD)
    outs = [
        jax.ShapeDtypeStruct((parts, seqs, half, columns // 3), BF16),
        jax.ShapeDtypeStruct((seqs, heads, parts * half), F32),
    ]
    scratch = lambda length: [
        pltpu.VMEM((length, length), F32),
        pltpu.VMEM((length, PAIR), F32),
        pltpu.VMEM((2, 128, length), F32),
        pltpu.VMEM((2, 128, length), BF16),
    ]
    return attention_call(attend_kernel, seg, [qkv], outs, scratch, 2, "attend")


def attend_back(qkv, seg, out, grad, lse, first, pairs, after):
    outs = [jax.ShapeDtypeStruct(qkv.shape[:3] + (3 * PAIR * pairs,), BF16)]
    scratch = lambda length: [
        pltpu.VMEM((length, length), F32),
        pltpu.VMEM((2, length, length), BF16),
        pltpu.VMEM((2, 128, length), F32),
        pltpu.VMEM((2, 128, length), F32),
        pltpu.VMEM((2, 128, length), BF16),
    ]
    kernel = functools.partial(attend_back_kernel, first, len(after))
    arrays = [qkv, out, grad, lse]
    name = "attend_back"
    return attention_call(kernel, seg, arrays, outs, scratch, 5, name, first, after)[0]


def body(
    layer_input,
    segment_ids,
    out_cotangent,
    attn_master,
    inner_master,
    outer_master,
    vector_master,
    attn_moment,
    inner_moment,
    outer_moment,
    vector_moment,
    attn_square,
    inner_square,
    outer_square,
    vector_square,
):
    seqs, half, width = layer_input.shape
    count = seqs * half
    hidden_units = inner_master.shape[1]
    pairs = width // (2 * PAIR)
    part_cols = width // 2
    shards = lax.axis_size("shard")
    owned_rows = attn_master.shape[1]
    core = lax.axis_index("ctx")
    first = core == 0

    def own_half(array, axis):
        size = array.shape[axis] // 2
        return lax.dynamic_slice_in_dim(array, core * size, size, axis)

    def other_half(array, axis):
        size = array.shape[axis] // 2
        return lax.dynamic_slice_in_dim(array, (1 - core) * size, size, axis)

    def in_order(mine, theirs, axis):
        return jnp.concatenate(
            [jnp.where(first, mine, theirs), jnp.where(first, theirs, mine)], axis
        )

    rows = layer_input.reshape(count, width)
    rows_chip = jnp.concatenate([rows, swap_cores(rows)], 0)
    square = is_square()

    piece = own_half(attn_master[:3], 2).astype(BF16).reshape(3, owned_rows, pairs, PAIR)
    piece = piece.transpose(1, 2, 0, 3).reshape(owned_rows, 3 * part_cols)
    vec_low = vector_master.astype(BF16)
    rider = vec_low[:2].reshape(1, -1)
    if square:
        piece = lax.dynamic_slice_in_dim(
            piece, lax.axis_index("replica") * (piece.shape[1] // 2), piece.shape[1] // 2, 1
        )
    rider = jnp.pad(rider, ((0, 15), (0, piece.shape[1] - rider.shape[1])))
    piece = jnp.concatenate([piece, rider], 0)
    if square:
        stacks, places = gather_quarters(piece)
    else:
        stacks = [item[None] for item in ring_gather(piece)]
        places = [(owner, 0) for owner in slot_owners()]
    riders = jnp.concatenate([stack[:, owned_rows] for stack in stacks], 0)[:shards]
    riders = riders[:, : 2 * width // shards].reshape(shards, 2, -1).astype(F32)
    slot_of = jnp.stack([place[0] for place in places[:shards]])
    chosen = (jnp.arange(shards)[:, None] == slot_of[None, :]).astype(F32)
    biases = jnp.einsum("ps,srw->rpw", chosen, riders).reshape(2, width)

    copies = lax.axis_size("replica") * 2
    copy_at = lax.axis_index("replica") * 2 + core
    quarter = lambda block: lax.dynamic_slice_in_dim(
        block, copy_at * (block.shape[0] // copies), block.shape[0] // copies, 0
    ).astype(BF16)
    out_q, inner_q, outer_q = quarter(attn_master[3]), quarter(inner_master), quarter(outer_master)
    wide = hidden_units // width
    small = out_q.shape[0]
    inner_q = inner_q.reshape(small, wide, width).transpose(1, 0, 2).reshape(-1, width)
    big = outer_q.shape[0]
    vec_q = vec_low.reshape(-1)
    vec_q = jnp.pad(vec_q, (0, 16 * width - vec_q.shape[0])).reshape(16, width)
    packed = lax.all_gather(jnp.concatenate([outer_q, inner_q, out_q, vec_q], 0), EVERY, axis=0)
    vec = packed[::copies, 2 * big + small :].reshape(shards, -1)[:, : vec_low.size]
    vec = vec.reshape((shards,) + vec_low.shape).transpose(1, 0, 2).reshape(-1, width).astype(F32)
    if packed.shape[0] != PARTS:
        outer_w = packed[:, :big].reshape(PARTS, -1, width)
        inner_w = packed[:, big : 2 * big].reshape(-1, wide, small, width).transpose(0, 2, 1, 3)
        inner_w = inner_w.reshape(PARTS, -1, wide, width).transpose(0, 2, 1, 3)
        out_w = packed[:, 2 * big : 2 * big + small].reshape(PARTS, -1, width)
        packed = jnp.concatenate([outer_w, inner_w.reshape(PARTS, -1, width), out_w], 1)

    halves = own_half(biases, 1).reshape(2, pairs, PAIR)
    bias = jnp.stack([halves[0], jnp.zeros_like(halves[0]), halves[1]], 1).reshape(1, -1)
    ones = jnp.ones((pairs, PAIR), F32)
    factor = jnp.stack([ones * HD**-0.5, ones, ones], 1).reshape(1, -1)
    qkv, qkv_w = project(rows_chip, stacks, places, bias, factor)
    qkv = qkv.reshape(2, seqs, half, 3 * part_cols)
    seg = jnp.concatenate([own_half(segment_ids, 1), other_half(segment_ids, 1)], 1)
    mixed, lse = attend(qkv, seg)
    mixed_back = swap_cores(mixed[1].reshape(count, part_cols))
    heads_out = in_order(mixed[0].reshape(count, part_cols), mixed_back, 1)

    cotan = out_cotangent.reshape(count, width)
    active, slope, hidden_low, normed, scale, result, ffn_grad, sums_two = ffn(
        heads_out, rows, cotan, vec, packed
    )

    def send_half(left, right):
        return contract_rows(left, other_half(right, 1)).astype(BF16)

    def own_part(left, right):
        return contract_rows(left, own_half(right, 1)).astype(BF16)

    def by_shard(array):
        return array.astype(BF16).reshape(shards, -1, array.shape[1])

    o, i, y, inner = position()
    where = jnp.stack([o, i, y, core]).astype(jnp.int32)
    outer_sent = send_half(active, ffn_grad)
    outer_chips = [by_shard(own_part(active, ffn_grad)), by_shard(swap_cores(outer_sent))]
    done = (outer_sent,)
    if square:
        outer = Sum(where, *outer_chips)
        done = outer.merge()
    pre_grad, branch_grad, mixed_grad, sums_one = ffn_back(
        ffn_grad, slope, normed, scale, vec, packed, done[0]
    )
    mixed_grad = jnp.stack(
        [own_half(mixed_grad, 1), swap_cores(other_half(mixed_grad, 1))], 0
    ).reshape(mixed.shape)
    inner_sent = send_half(hidden_low, pre_grad)
    out_sent = send_half(heads_out, branch_grad)
    inner_chips = [by_shard(own_part(hidden_low, pre_grad)), by_shard(swap_cores(inner_sent))]
    out_chip = add_low(
        by_shard(own_part(heads_out, branch_grad)), by_shard(swap_cores(out_sent))
    )

    def back(first, after):
        return attend_back(
            qkv, seg, mixed, mixed_grad, lse, first, pairs // 2, after
        ).reshape(2 * count, -1)

    def bias_sums(grad):
        sums = jnp.sum(grad.astype(F32), 0).reshape(-1, 3, PAIR)
        return sums[:, 0].reshape(-1), sums[:, 2].reshape(-1)

    def make_chip_a(grad):
        return jnp.concatenate([by_shard(contract_rows(rows_chip, grad)), out_chip], 2)

    def make_chip_b(grad_a, grad_b):
        bias_a, bias_b = bias_sums(grad_a), bias_sums(grad_b)
        blank = jnp.zeros((part_cols,), F32)
        attn_biases = [
            in_order(jnp.concatenate([bias_a[at], bias_b[at]]), blank, 0) for at in range(2)
        ]
        sums = [jnp.stack(attn_biases), sums_one[2:3], sums_one[:2], sums_two[2:3], sums_two[:2]]
        sums = jnp.concatenate(sums + [sums_one[4:8]], 0)
        sums = sums.reshape(-1, shards, width // shards).transpose(1, 0, 2)
        sums = jnp.pad(sums, ((0, 0), (0, owned_rows - sums.shape[1]), (0, 0)))
        return jnp.concatenate([by_shard(contract_rows(rows_chip, grad_b)), sums.astype(BF16)], 2)

    outer_states = (outer_master, outer_moment, outer_square)
    inner_states = (inner_master, inner_moment, inner_square)
    attn_states = (attn_master, attn_moment, attn_square)
    if square:
        done = outer.plane((pre_grad,))
        inner = Sum(where, *inner_chips)
        done = inner.merge(done)
        done = outer.cross(done)
        grad_a = back(0, done + (out_sent,))
        done = inner.plane((grad_a,))
        sum_a = Sum(where, make_chip_a(grad_a))
        done = sum_a.merge(done)
        done = outer.line(done)
        grad_b = back(pairs // 2, done)
        done = inner.cross((grad_b,))
        sum_b = Sum(where, make_chip_b(grad_a, grad_b))
        done = sum_b.merge(done)
        done = sum_a.plane(done)
        theirs_part = input_back(grad_a, grad_b, qkv_w, (), done)
        outer_new = update(where, outer_states, [outer.shares], (theirs_part,))
        done = sum_a.cross((outer_new[0],))
        done = sum_b.plane(done)
        done = inner.line(done)
        input_grad = input_back(
            grad_a, grad_b, qkv_w, (branch_grad, swap_cores(theirs_part)), done
        )
        done = sum_b.cross((input_grad,))
        done = sum_a.line(done)
        inner_new = update(where, inner_states, [inner.shares], done)
        sum_b.line((inner_new[0],))
        attn_shares = [sum_a.shares, sum_b.shares]
        vector_shares = [
            jnp.concatenate(
                [
                    jnp.where(y == 0, sum_b.shares[at], sum_b.shares[at + 1])[0],
                    jnp.where(y == 0, sum_b.shares[at + 1], sum_b.shares[at])[0],
                ],
                0,
            )
            for at in (0, 2)
        ]
    else:
        grad_a = back(0, ())
        grad_b = back(pairs // 2, ())
        theirs_part = input_back(grad_a, grad_b, qkv_w, (), ())
        added = (branch_grad, swap_cores(theirs_part))
        input_grad = input_back(grad_a, grad_b, qkv_w, added, ())
        outer_new = update(where, outer_states, [sum_apart(add_low(*outer_chips))])
        inner_new = update(where, inner_states, [sum_apart(add_low(*inner_chips))])
        attn_shares = [sum_apart(make_chip_a(grad_a)), sum_apart(make_chip_b(grad_a, grad_b))]
        vector_shares = [share[0] for share in attn_shares[1]]
    attn_new = update(where, attn_states, attn_shares)
    cut = grad_b.shape[1]
    vector_sum = sum(share[: vec_low.shape[0], cut:].astype(F32) for share in vector_shares)
    vector_new = adamw(vector_sum, vector_moment, vector_square, vector_master, RATE_VECTOR)
    vector_new = vector_new + (vector_new[2].astype(BF16),)
    news = (attn_new, inner_new, outer_new, vector_new)
    updates = [[new[at] for new in news] for at in range(4)]
    return (
        result.reshape(seqs, half, width).astype(BF16),
        input_grad.reshape(seqs, half, width),
        *[item for kind in updates for item in kind],
    )


def solution(mesh):
    tokens = P(("replica", "shard"), "ctx", None)
    states = (P(None, "shard", None), P("shard", None), P("shard", None), P(None, "shard"))
    in_specs = (tokens, P(("replica", "shard"), None), tokens) + states * 3
    out_specs = (tokens, tokens) + states * 4
    return jax.shard_map(body, mesh=mesh, in_specs=in_specs, out_specs=out_specs, check_vma=False)
```

```python
import functools

import jax
import jax.numpy as jnp
from jax import lax
from jax.experimental import pallas as pl
from jax.experimental.pallas import tpu as pltpu
from jax.sharding import PartitionSpec as P

HD = 64
PAIR = 2 * HD
STEP = 5
OUTER = 4
EVERY = ("shard", "replica", "ctx")

EPS_NORM = 1e-05
BETA_ONE = 0.5
BETA_TWO = 0.6
RATE_MATRIX = 0.02
RATE_VECTOR = 0.1
DECAY = 0.01
EPS_ADAM = 1e-06
MASKED = -1e30
F32 = jnp.float32
BF16 = jnp.bfloat16
PARTS = 32
TILE = 32
VMEM = 56 * 1024 * 1024
SMALL_VMEM = 16 * 1024 * 1024
LITTLE = pl.CostEstimate(flops=1, bytes_accessed=1, transcendentals=0)
GROUP = 256
NT = (((1,), (1,)), ((), ()))
TN = (((0,), (0,)), ((), ()))


def contract_rows(left, right):
    return jnp.einsum("rd,re->de", left, right, preferred_element_type=F32)


def normalize(resid):
    centre = resid - jnp.mean(resid, -1, keepdims=True)
    scale = lax.rsqrt(jnp.mean(centre * centre, -1, keepdims=True) + EPS_NORM)
    return (centre * scale, scale)


def norm_back(grad, normed, scale):
    return scale * (
        grad
        - jnp.mean(grad, -1, keepdims=True)
        - normed * jnp.mean(grad * normed, -1, keepdims=True)
    )


def adamw(grad, moment, square, weight, rate):
    moment_new = BETA_ONE * moment + (1.0 - BETA_ONE) * grad
    square_new = BETA_TWO * square + (1.0 - BETA_TWO) * grad * grad
    stepped = (
        moment_new
        / (1.0 - BETA_ONE**STEP)
        / (jnp.sqrt(square_new / (1.0 - BETA_TWO**STEP)) + EPS_ADAM)
    )
    weight_new = weight - rate * (stepped + DECAY * weight)
    return (moment_new, square_new, weight_new)


def swap_cores(value):
    return lax.ppermute(value, "ctx", [(0, 1), (1, 0)])


def shift_outer(value, step):
    inner = lax.axis_size("shard") // OUTER
    pairs = [
        (o * inner + i, ((o + step) % OUTER) * inner + i) for o in range(OUTER) for i in range(inner)
    ]
    return lax.ppermute(value, "shard", pairs)


def shift_inner(value, step):
    inner = lax.axis_size("shard") // OUTER
    pairs = [
        (o * inner + i, o * inner + (i + step) % inner) for o in range(OUTER) for i in range(inner)
    ]
    return lax.ppermute(value, "shard", pairs)


def shift_replica(value, step):
    size = lax.axis_size("replica")
    return lax.ppermute(value, "replica", [(r, (r + step) % size) for r in range(size)])


def ring_gather(piece):
    inner = lax.axis_size("shard") // OUTER
    found = []
    held = piece
    for k in range(OUTER):
        if k:
            held = shift_outer(held, -1)
        found.append([held] + [shift_inner(held, -e) for e in range(1, inner)])
    return [item for group in found for item in group]


def slot_owners():
    inner = lax.axis_size("shard") // OUTER
    at = lax.axis_index("shard")
    o, i = at // inner, at % inner
    return [
        lax.rem(o + k, OUTER) * inner + lax.rem(i + e, inner)
        for k in range(OUTER)
        for e in range(inner)
    ]


def pick(array, index, axis):
    return lax.dynamic_index_in_dim(array, index, axis, keepdims=False)


def add_low(value, *others):
    total = value.astype(F32)
    for item in others:
        total = total + item.astype(F32)
    return total.astype(BF16)


def position():
    inner = lax.axis_size("shard") // OUTER
    at = lax.axis_index("shard")
    return at // inner, at % inner, lax.axis_index("replica"), inner


def is_square():
    return lax.axis_size("replica") == 2 and lax.axis_size("shard") == 2 * OUTER


def swap_cross(value):
    return lax.ppermute(value, ("replica", "ctx"), [(a, 3 - a) for a in range(4)])


def sum_apart(chip_sum):
    o, i, y, inner = position()
    grid = chip_sum.reshape(OUTER, inner, *chip_sum.shape[1:])
    got = [shift_inner(pick(grid, lax.rem(i + e, inner), 1), e) for e in range(1, inner)]
    line = add_low(pick(grid, i, 1), *got)
    got = [shift_outer(pick(line, lax.rem(o + d, OUTER), 0), d) for d in range(1, OUTER)]
    total = add_low(pick(line, o, 0), *got)
    got = [shift_replica(total, r) for r in range(1, lax.axis_size("replica"))]
    mine = add_low(total, *got)[None]
    return [mine, swap_cores(mine)]


def small_call(kernel, where, ins, outs, after, name):
    held = pl.BlockSpec(memory_space=pltpu.VMEM)
    return pl.pallas_call(
        functools.partial(kernel, len(ins), len(after)),
        in_specs=[pl.BlockSpec(memory_space=pltpu.SMEM)]
        + [held] * len(ins)
        + [pl.BlockSpec(memory_space=pl.ANY)] * len(after),
        out_specs=[held] * len(outs),
        out_shape=[pltpu.VMEM(shape, BF16) for shape in outs],
        compiler_params=pltpu.CompilerParams(vmem_limit_bytes=SMALL_VMEM),
        cost_estimate=LITTLE,
        name=name,
    )(where, *[pltpu.with_memory_space_constraint(a, pltpu.VMEM) for a in ins], *after)


def fold_plane_kernel(count, after, where_ref, keep_p, got_p, keep_q, got_q, *rest):
    i, y = where_ref[1], where_ref[2]
    kept_p, send_p, kept_q, send_q = rest[after:]
    for o in range(OUTER):
        for out, at in ((kept_p, y), (send_p, 1 - y)):
            out[o] = add_low(keep_p[o, at], got_p[o, at])
        for out, at in ((kept_q, i), (send_q, 1 - i)):
            out[o] = add_low(keep_q[o, at], got_q[o, at])


def fold_cross_kernel(count, after, where_ref, keep_p, got_p, keep_q, got_q, *rest):
    for d, out in enumerate(rest[after:]):
        at = lax.rem(where_ref[0] + d, OUTER)
        out[0] = add_low(keep_p[at], got_p[at])
        out[1] = add_low(keep_q[at], got_q[at])


def fold_line_kernel(count, after, where_ref, *rest):
    for at in range(2):
        rest[count + after][at] = add_low(*(ref[at] for ref in rest[:count]))


def merge_kernel(chips, after, where_ref, *refs):
    send_p, send_q, keep_p, keep_q = refs[4 * chips + after :]
    for slot, out, lead in ((0, send_p, 0), (1, send_q, 1), (2, keep_p, 0), (3, keep_q, 1)):
        for at in range(2):
            pick_one = lambda ref: ref[0, 0, 0, at] if lead == 0 else ref[0, at, 0, 0]
            parts = [pick_one(refs[4 * chip + slot]) for chip in range(chips)]
            out[0, at] = parts[0] if chips == 1 else add_low(*parts)


class Sum:
    def __init__(self, where, *chips):
        rows, self.columns = chips[0].shape[1:]
        self.where, self.rows = where, rows // 4
        self.chips = [c.reshape(OUTER, 2, 2, 2, self.rows, self.columns) for c in chips]

    def shape(self, *lead):
        return lead + (self.rows, self.columns)

    def merge(self, after=()):
        block = (self.rows, self.columns)

        def spec(lead, flip):
            def place(o, w):
                at = w[1] if lead == 0 else w[2]
                at = 1 - at if flip else at
                return (o, at, 0, 0, 0, 0) if lead == 0 else (o, 0, 1, at, 0, 0)

            return pl.BlockSpec(((1, 1, 1, 2) if lead == 0 else (1, 2, 1, 1)) + block, place)

        specs = [spec(0, True), spec(1, True), spec(0, False), spec(1, False)]
        out_spec = pl.BlockSpec((1, 2) + block, lambda o, w: (o, 0, 0, 0))
        *self.sent, keep_p, keep_q = pl.pallas_call(
            functools.partial(merge_kernel, len(self.chips), len(after)),
            grid_spec=pltpu.PrefetchScalarGridSpec(
                num_scalar_prefetch=1,
                grid=(OUTER,),
                in_specs=specs * len(self.chips)
                + [pl.BlockSpec(memory_space=pl.ANY)] * len(after),
                out_specs=[out_spec] * 4,
            ),
            out_shape=[jax.ShapeDtypeStruct(self.shape(OUTER, 2), BF16)] * 4,
            compiler_params=pltpu.CompilerParams(vmem_limit_bytes=SMALL_VMEM),
            cost_estimate=LITTLE,
            name="merge",
        )(self.where, *[chip for chip in self.chips for _ in range(4)], *after)
        got_p, got_q = shift_inner(self.sent[0], 1), shift_replica(self.sent[1], 1)
        self.kept = [keep_p, got_p, keep_q, got_q]
        return tuple(self.sent)

    def plane(self, after=()):
        keep_p, send_p, keep_q, send_q = small_call(
            fold_plane_kernel, self.where, self.kept, [self.shape(OUTER)] * 4, after, "fold_plane"
        )
        self.kept = [keep_p, shift_replica(send_p, 1), keep_q, shift_inner(send_q, 1)]
        return (send_p, send_q)

    def cross(self, after=()):
        kept, *sent = small_call(
            fold_cross_kernel, self.where, self.kept, [self.shape(2)] * OUTER, after, "fold_cross"
        )
        self.kept = [kept] + [shift_outer(item, d + 1) for d, item in enumerate(sent)]
        return tuple(sent)

    def line(self, after=()):
        (total,) = small_call(
            fold_line_kernel, self.where, self.kept, [self.shape(2)], after, "fold_line"
        )
        self.shares = [total, shift_replica(total, 1), swap_cores(total), swap_cross(total)]
        return (total,)


def update_kernel(groups, after, where_ref, *refs):
    states, shares = refs[:3], refs[3 : 3 + sum(groups)]
    outs, grad_ref = refs[3 + sum(groups) + after : -1], refs[-1]
    rows = shares[0].shape[1]
    across = groups[0] // 2
    for core in range(2):

        @pl.when(pl.program_id(1) == core)
        def _():
            for n in range(across):
                line = where_ref[2] if n == 0 else 1 - where_ref[2]
                line = pl.ds(pl.multiple_of(line * rows, rows), rows) if across > 1 else slice(None)
                if len(groups) == 1:
                    grad_ref[line, :] = shares[across * core + n][0].astype(F32)
                    continue
                left, right = shares[across * core + n], shares[groups[0] + across * core + n]
                width = grad_ref.shape[2]
                pairs = width // PAIR
                for t in range(3):
                    for p in range(pairs):
                        side, at = (left, p) if 2 * p < pairs else (right, p - pairs // 2)
                        part = side[0, :, (3 * at + t) * PAIR : (3 * at + t + 1) * PAIR]
                        grad_ref[t, line, p * PAIR : (p + 1) * PAIR] = part.astype(F32)
                cut = 3 * PAIR * (pairs // 2)
                grad_ref[3, line, :] = left[0, :, cut : cut + width].astype(F32)

    new = adamw(grad_ref[...], states[1][...], states[2][...], states[0][...], RATE_MATRIX)
    for out, value in zip(outs, new + (new[2],)):
        out[...] = value.astype(out.dtype)


def update(where, states, groups, after=()):
    parts, rows = groups[0][0].shape[:2]
    rows = rows * (len(groups[0]) // 2)
    lead = states[0].shape[:-2]
    columns = states[0].shape[-1] // 2
    place = lambda p, v, w: (0,) * len(lead) + (p, w[3] + v - 2 * w[3] * v)
    block = pl.BlockSpec(lead + (rows, columns), place)
    shares = [share for group in groups for share in group]
    share_specs = [pl.BlockSpec((1,) + a.shape[1:], lambda p, v, w: (p, 0, 0)) for a in shares]
    kinds = (F32, F32, F32, BF16)
    return pl.pallas_call(
        functools.partial(update_kernel, [len(group) for group in groups], len(after)),
        grid_spec=pltpu.PrefetchScalarGridSpec(
            num_scalar_prefetch=1,
            grid=(parts, 2),
            in_specs=[block] * 3 + share_specs + [pl.BlockSpec(memory_space=pl.ANY)] * len(after),
            out_specs=[block] * 4,
            scratch_shapes=[pltpu.VMEM(lead + (rows, columns), F32)],
        ),
        out_shape=[jax.ShapeDtypeStruct(states[0].shape, kind) for kind in kinds],
        compiler_params=pltpu.CompilerParams(vmem_limit_bytes=SMALL_VMEM),
        cost_estimate=LITTLE,
        name="update",
    )(where, *states, *shares, *after)


def input_back_kernel(a_ref, b_ref, left_ref, right_ref, *rest):
    out_ref = rest[-1]
    total = lax.dot_general(a_ref[...], left_ref[...], NT, preferred_element_type=F32)
    total += lax.dot_general(b_ref[...], right_ref[...], NT, preferred_element_type=F32)
    if out_ref.dtype == F32:
        total += rest[0][...].astype(F32) + rest[1][...].astype(F32)
    out_ref[...] = total.astype(out_ref.dtype)


def input_back(grad_a, grad_b, weight, added, after):
    count, cut = grad_a.shape[0] // 2, grad_a.shape[1]
    width = weight.shape[0]
    tile = width // 4
    first = 0 if added else 1
    side = pl.BlockSpec((count, cut), lambda n: (first, 0))
    line = pl.BlockSpec((count, tile), lambda n: (0, n))
    return pl.pallas_call(
        input_back_kernel,
        grid=(width // tile,),
        in_specs=[side, side]
        + [pl.BlockSpec((tile, cut), lambda n, at=at: (n, at)) for at in range(2)]
        + [line] * len(added)
        + [pl.BlockSpec(memory_space=pl.ANY)] * len(after),
        out_specs=line,
        out_shape=jax.ShapeDtypeStruct((count, width), F32 if added else BF16),
        compiler_params=pltpu.CompilerParams(vmem_limit_bytes=SMALL_VMEM),
        cost_estimate=LITTLE,
        name="input_back",
    )(grad_a, grad_b, weight, weight, *added, *after)


def gather_quarters(quarter):
    line = jnp.stack([quarter] + [shift_outer(quarter, -k) for k in range(1, OUTER)])
    near_x = shift_inner(line, 1)
    near_y = shift_replica(line, 1)
    far_x = shift_inner(near_y[: OUTER // 2], 1)
    far_y = shift_replica(near_x[OUTER // 2 :], 1)
    o, i, y, inner = position()
    row = lambda k, across: lax.rem(o + k, OUTER) * 2 + (1 - i if across else i)
    places = [(row(k, False), y) for k in range(OUTER)] + [(row(k, True), y) for k in range(OUTER)]
    places += [(row(k, False), 1 - y) for k in range(OUTER)]
    places += [(row(k, True), 1 - y) for k in range(OUTER)]
    return [line, near_x, near_y, far_x, far_y], places


def project_kernel(row_ref, column_ref, rows_ref, bias_ref, factor_ref, *rest):
    stacks, (out_ref, weight_ref) = rest[:-2], rest[-2:]
    columns = stacks[0].shape[2]
    part = weight_ref.shape[0] * weight_ref.shape[1] // columns
    part = part // sum(stack.shape[0] for stack in stacks)

    @pl.when(pl.program_id(0) == 0)
    def _():
        slot = 0
        for stack in stacks:
            for k in range(stack.shape[0]):
                start = pl.multiple_of(row_ref[slot] * part, part)
                left = pl.multiple_of(column_ref[slot] * columns, PAIR)
                weight_ref[pl.ds(start, part), pl.ds(left, columns)] = stack[k, :part, :]
                slot += 1

    acc = jnp.dot(rows_ref[...], weight_ref[...], preferred_element_type=F32)
    out_ref[...] = ((acc + bias_ref[...]) * factor_ref[...]).astype(BF16)


def project(rows, stacks, places, bias, factor):
    count, width = rows.shape
    columns = bias.shape[1]
    tile = 512
    whole = lambda shape: pl.BlockSpec(shape, lambda m, *_: (0,) * len(shape))
    tables = [jnp.stack([p[axis] for p in places]).astype(jnp.int32) for axis in range(2)]
    return pl.pallas_call(
        project_kernel,
        grid_spec=pltpu.PrefetchScalarGridSpec(
            num_scalar_prefetch=2,
            grid=(count // tile,),
            in_specs=[
                pl.BlockSpec((tile, width), lambda m, *_: (m, 0)),
                whole((1, columns)),
                whole((1, columns)),
            ]
            + [whole(stack.shape) for stack in stacks],
            out_specs=[
                pl.BlockSpec((tile, columns), lambda m, *_: (m, 0)),
                whole((width, columns)),
            ],
        ),
        out_shape=[
            jax.ShapeDtypeStruct((count, columns), BF16),
            jax.ShapeDtypeStruct((width, columns), BF16),
        ],
        compiler_params=pltpu.CompilerParams(vmem_limit_bytes=VMEM),
        cost_estimate=LITTLE,
        name="project",
    )(*tables, rows, bias, factor, *stacks)


def gelu_and_slope(u):
    a = jnp.abs(u) * (0.5**0.5)
    d = 1.0 + 0.3275911 * a
    t = pl.reciprocal(d, approx=True)
    t = t * (2.0 - d * t)
    e = jnp.exp(-a * a)
    series = 1.061405429 * t - 1.453152027
    series = series * t + 1.421413741
    series = series * t - 0.284496736
    series = series * t + 0.254829592
    tail = 0.5 * series * t * e
    normal = jnp.where(u >= 0.0, 1.0 - tail, tail)
    return u * normal, normal + u * (0.3989422804014327 * e)


def total_rows(value):
    return jnp.sum(value, axis=0, keepdims=True)


def in_parts(count, work):
    def turn(at, carry):
        work(pl.ds(pl.multiple_of(at * 128, 128), 128))
        return carry

    lax.fori_loop(0, count // 128, turn, 0)


def in_units(units, begin, turn, other):
    if begin is not None:
        begin(0)
    for unit in range(units):
        if begin is not None and unit + 1 < units:
            begin(unit + 1)
        if other is not None:
            other(unit)
        if turn is not None:
            turn(unit)


def ffn_kernel(
    mixed_ref,
    rows_ref,
    cotan_ref,
    vec_ref,
    out_w_ref,
    inner_w_ref,
    outer_w_ref,
    active_ref,
    slope_ref,
    hidden_ref,
    normed_ref,
    scale_ref,
    result_ref,
    grad_ref,
    sums_ref,
    resid,
    acc,
    held,
    pre,
):
    w, last = pl.program_id(0), pl.num_programs(0) - 1
    count, width = acc.shape
    chunk = pre.shape[2]
    groups = count // GROUP
    units = groups * (width // chunk)
    vec = lambda at: vec_ref[at : at + 1, :]

    def where(unit):
        n, g = divmod(unit, groups)
        return slice(n * chunk, (n + 1) * chunk), slice(g * GROUP, (g + 1) * GROUP)

    @pl.when(w == 0)
    def _():
        acc[...] = jnp.dot(
            mixed_ref[...], out_w_ref[...].reshape(width, width), preferred_element_type=F32
        )

        def enter(part):
            normed, scale = normalize(acc[part, :] + vec(2) + rows_ref[part, :].astype(F32))
            normed_ref[part, :] = normed.astype(BF16)
            scale_ref[part, :] = scale
            hidden = normed * vec(3) + vec(4)
            resid[part, :] = hidden + vec(5)
            hidden_ref[part, :] = hidden.astype(BF16)

        in_parts(count, enter)
        acc[...] = jnp.zeros_like(acc)

    bias = vec_ref[pl.ds(8 + jnp.minimum(w, last - 1), 1), :]
    now, before = lax.rem(w, 2), lax.rem(w + 1, 2)

    def expand(unit):
        cut, group = where(unit)
        weight = inner_w_ref[:, :, cut].reshape(width, chunk)
        pre[unit % 2] = jnp.dot(hidden_ref[group, :], weight, preferred_element_type=F32)

    def bend(unit):
        cut, group = where(unit)
        for at in range(0, GROUP, TILE):
            part = slice(group.start + at, group.start + at + TILE)
            active, slope = gelu_and_slope(pre[unit % 2, at : at + TILE, :] + bias[:, cut])
            active = active.astype(BF16)
            active_ref[part, cut] = active
            held[now, part, cut] = active
            slope_ref[part, cut] = slope.astype(BF16)

    def contract(unit):
        cut, group = where(unit)
        weight = outer_w_ref[:, :, cut].reshape(width, chunk)
        acc[group, cut] += jnp.dot(held[before, group, :], weight, preferred_element_type=F32)

    @pl.when(w == 0)
    def _():
        in_units(units, expand, bend, None)

    @pl.when((w > 0) & (w < last))
    def _():
        in_units(units, expand, bend, contract)

    @pl.when(w == last)
    def _():
        in_units(units, None, None, contract)
        sums_ref[...] = jnp.zeros_like(sums_ref)

        def leave(part):
            normed, scale = normalize(resid[part, :] + acc[part, :])
            result_ref[part, :] = (normed * vec(6) + vec(7)).astype(BF16)
            cotan = cotan_ref[part, :].astype(F32)
            grad = norm_back(cotan * vec(6), normed, scale).astype(BF16)
            grad_ref[part, :] = grad
            sums_ref[0:1, :] += total_rows(cotan * normed)
            sums_ref[1:2, :] += total_rows(cotan)
            sums_ref[2:3, :] += total_rows(grad.astype(F32))

        in_parts(count, leave)


def ffn_back_kernel(
    grad_ref,
    slope_ref,
    normed_ref,
    scale_ref,
    vec_ref,
    out_w_ref,
    outer_w_ref,
    inner_w_ref,
    after_ref,
    pre_grad_ref,
    branch_ref,
    mixed_ref,
    sums_ref,
    acc,
    held,
    pre,
):
    w, last = pl.program_id(0), pl.num_programs(0) - 1
    count, width = acc.shape
    chunk = pre.shape[2]
    groups = count // GROUP
    units = groups * (width // chunk)
    vec = lambda at: vec_ref[at : at + 1, :]

    def where(unit):
        n, g = divmod(unit, groups)
        return slice(n * chunk, (n + 1) * chunk), slice(g * GROUP, (g + 1) * GROUP)

    @pl.when(w == 0)
    def _():
        sums_ref[...] = jnp.zeros_like(sums_ref)
        acc[...] = jnp.zeros_like(acc)

    now, before = lax.rem(w, 2), lax.rem(w + 1, 2)

    def pull(unit):
        cut, group = where(unit)
        each = outer_w_ref.shape[0] * chunk // width
        n = unit // groups
        weight = outer_w_ref[n * each : (n + 1) * each].reshape(chunk, width)
        pre[unit % 2] = lax.dot_general(
            grad_ref[group, :], weight, NT, preferred_element_type=F32
        )

    def bend(unit):
        cut, group = where(unit)
        sums = jnp.zeros((8, chunk), F32)
        for at in range(0, GROUP, TILE):
            part = slice(group.start + at, group.start + at + TILE)
            back = pre[unit % 2, at : at + TILE, :].astype(BF16).astype(F32)
            back = (back * slope_ref[part, cut].astype(F32)).astype(BF16)
            pre_grad_ref[part, cut] = back
            held[now, part, cut] = back
            sums += jnp.sum(back.astype(F32).reshape(TILE // 8, 8, chunk), axis=0)
        sums_ref[pl.ds(4 + w, 1), cut] += total_rows(sums)

    def contract(unit):
        cut, group = where(unit)
        each = inner_w_ref.shape[0] * chunk // width
        n = unit // groups
        weight = inner_w_ref[n * each : (n + 1) * each].reshape(chunk, width)
        acc[group, cut] += lax.dot_general(
            held[before, group, :], weight, NT, preferred_element_type=F32
        )

    @pl.when(w == 0)
    def _():
        in_units(units, pull, bend, None)

    @pl.when((w > 0) & (w < last))
    def _():
        in_units(units, pull, bend, contract)

    @pl.when(w == last)
    def _():
        in_units(units, None, None, contract)

        def leave(part):
            through = acc[part, :].astype(BF16).astype(F32) + grad_ref[part, :].astype(F32)
            normed = normed_ref[part, :].astype(F32)
            branch = norm_back(through * vec(3), normed, scale_ref[part, :]).astype(BF16)
            branch_ref[part, :] = branch
            sums_ref[0:1, :] += total_rows(through * normed)
            sums_ref[1:2, :] += total_rows(through)
            sums_ref[2:3, :] += total_rows(branch.astype(F32))

        in_parts(count, leave)
        mixed_ref[...] = lax.dot_general(
            branch_ref[...], out_w_ref[...].reshape(width, width), NT, preferred_element_type=F32
        ).astype(BF16)


def packed_specs(width, steps):
    small = width // PARTS
    inner = lambda at: pl.BlockSpec((PARTS, small, width), lambda w: (0, 4 + at(w), 0))
    outer = lambda at: pl.BlockSpec((PARTS // 4, 4 * small, width), lambda w: (at(w), 0, 0))
    out = pl.BlockSpec((PARTS, small, width), lambda w: (0, 8, 0), pipeline_mode=pl.Buffered(1))
    now = lambda w: jnp.minimum(w, steps - 1)
    before = lambda w: jnp.maximum(w - 1, 0)
    return out, inner, outer, now, before


def ffn_call(kernel, ins, packed, weights, after, wide_outs, outs, name):
    count, width = ins[0].shape
    steps = 4

    def spec(shape):
        if shape == (count, steps * width):
            return pl.BlockSpec((count, width), lambda w: (0, jnp.minimum(w, steps - 1)))
        return pl.BlockSpec(shape, lambda w: (0, 0), pipeline_mode=pl.Buffered(1))

    shapes = [((count, steps * width), BF16)] * wide_outs + outs
    return pl.pallas_call(
        kernel,
        grid=(steps + 1,),
        in_specs=[spec(a.shape) for a in ins]
        + weights(*packed_specs(width, steps))
        + [pl.BlockSpec(memory_space=pl.ANY)] * len(after),
        out_specs=[spec(shape) for shape, kind in shapes],
        out_shape=[jax.ShapeDtypeStruct(shape, kind) for shape, kind in shapes],
        scratch_shapes=[pltpu.VMEM((count, width), F32)] * wide_outs
        + [pltpu.VMEM((2, count, width), BF16), pltpu.VMEM((2, GROUP, 256), F32)],
        compiler_params=pltpu.CompilerParams(vmem_limit_bytes=VMEM),
        cost_estimate=LITTLE,
        name=name,
    )(*ins, packed, packed, packed, *after)


def ffn(mixed, rows, cotan, vec, packed):
    low = (rows.shape, BF16)
    sums = ((8, rows.shape[1]), F32)
    outs = [low, low, ((rows.shape[0], 1), F32), low, low, sums]
    weights = lambda out, inner, outer, now, before: [out, inner(now), outer(before)]
    return ffn_call(ffn_kernel, [mixed, rows, cotan, vec], packed, weights, (), 2, outs, "ffn")


def ffn_back(grad, slope, normed, scale, vec, packed, after):
    low = (grad.shape, BF16)
    outs = [low, low, ((8, grad.shape[1]), F32)]
    ins = [grad, slope, normed, scale, vec]
    weights = lambda out, inner, outer, now, before: [out, outer(now), inner(before)]
    return ffn_call(ffn_back_kernel, ins, packed, weights, (after,), 1, outs, "ffn_back")


def attend_kernel(seg_row_ref, seg_col_ref, qkv_ref, out_ref, lse_ref, bias_ref, stat_ref, *more):
    score_ref, expo_ref = more
    pair = pl.program_id(1)
    length = bias_ref.shape[0]
    chunk = score_ref.shape[1]

    @pl.when(pair == 0)
    def _():
        bias_ref[...] = jnp.where(seg_col_ref[0] == seg_row_ref[0], 0.0, MASKED)
        stat_ref[...] = jnp.zeros_like(stat_ref)

    block = qkv_ref[:, 0].reshape(length, 3 * PAIR)
    q, k, v = (block[:, i * PAIR : (i + 1) * PAIR] for i in range(3))
    lane = lax.broadcasted_iota(jnp.int32, (length, PAIR), 1)
    low = lane < HD
    zero, one = jnp.zeros_like(q), jnp.ones_like(v)
    q_heads = [jnp.where(low, q, zero), jnp.where(low, zero, q)]
    v_heads = [jnp.where(low, v, one), jnp.where(low, one, v)]
    lane, low = lane[:chunk], low[:chunk]

    def score(step):
        c, h = divmod(step, 2)
        score_ref[step % 2] = lax.dot_general(
            q_heads[h][c * chunk : (c + 1) * chunk], k, NT, preferred_element_type=F32
        )

    def soften(step):
        c, h = divmod(step, 2)
        tops = []
        for at in range(0, chunk, TILE):
            rows = slice(c * chunk + at, c * chunk + at + TILE)
            s = score_ref[step % 2, at : at + TILE, :] + bias_ref[rows, :]
            top = jnp.max(s, axis=1, keepdims=True)
            expo_ref[step % 2, at : at + TILE, :] = jnp.exp(s - top).astype(BF16)
            tops.append(top)
        return jnp.concatenate(tops, 0)

    def mix(step):
        return jnp.dot(expo_ref[step % 2], v_heads[step % 2], preferred_element_type=F32)

    def finish(c, got, tops):
        rows = slice(c * chunk, (c + 1) * chunk)
        total = jnp.where(low, got[1], got[0])
        mixed = jnp.where(low, got[0], got[1]) / pltpu.roll(total, HD, 1)
        log = jnp.log(total)
        stat = stat_ref[rows, :]
        stat = jnp.where(lane == 2 * pair, tops[0] + log[:, HD : HD + 1], stat)
        stat_ref[rows, :] = jnp.where(lane == 2 * pair + 1, tops[1] + log[:, :1], stat)
        part = c * chunk // out_ref.shape[2]
        at = c * chunk % out_ref.shape[2]
        out_ref[part, 0, at : at + chunk, :] = mixed.astype(BF16)

    steps = 2 * length // chunk
    tops, got = [], []
    score(0)
    for step in range(steps):
        if step + 1 < steps:
            score(step + 1)
        tops.append(soften(step))
        got.append(mix(step))
        if step % 2:
            finish(step // 2, got[-2:], tops[-2:])

    @pl.when(pair == pl.num_programs(1) - 1)
    def _():
        lse_ref[0] = jnp.transpose(stat_ref[...])[: lse_ref.shape[1]]


def attend_back_kernel(first_pair, after, *refs):
    seg_row_ref, seg_col_ref, qkv_ref, out_ref, grad_ref, lse_ref = refs[:6]
    dqkv_ref, bias_ref, ds_ref, score_ref, slope_ref, prob_ref = refs[6 + after :]
    pair = pl.program_id(1)
    length = bias_ref.shape[0]
    half = qkv_ref.shape[2]
    chunk = score_ref.shape[1]

    @pl.when(pair == 0)
    def _():
        bias_ref[...] = jnp.where(seg_col_ref[0] == seg_row_ref[0], 0.0, MASKED)

    block = qkv_ref[:, 0].reshape(length, 3 * PAIR)
    q, k, v = (block[:, i * PAIR : (i + 1) * PAIR] for i in range(3))
    out = out_ref[:, 0].reshape(length, PAIR)
    grad = grad_ref[:, 0].reshape(length, PAIR)
    low = lax.broadcasted_iota(jnp.int32, (length, PAIR), 1) < HD
    zero = jnp.zeros_like(q)
    heads = lambda array: [jnp.where(low, array, zero), jnp.where(low, zero, array)]
    q_heads, k_heads, g_heads = heads(q), heads(k), heads(grad)
    product = jnp.transpose(out.astype(F32) * grad.astype(F32))
    chunks = length // chunk
    deltas = [total_rows(product[h * HD : (h + 1) * HD]) for h in range(2)]
    stats = [lse_ref[0, pl.ds(2 * (first_pair + pair) + h, 1), :] for h in range(2)]

    def score(step):
        h, c = divmod(step, chunks)
        rows = slice(c * chunk, (c + 1) * chunk)
        score_ref[step % 2] = lax.dot_general(k[rows], q_heads[h], NT, preferred_element_type=F32)
        slope_ref[step % 2] = lax.dot_general(v[rows], g_heads[h], NT, preferred_element_type=F32)

    def bend(step):
        h, c = divmod(step, chunks)
        for at in range(0, chunk, TILE):
            rows = slice(c * chunk + at, c * chunk + at + TILE)
            part = slice(at, at + TILE)
            p = jnp.exp(score_ref[step % 2, part, :] + bias_ref[rows, :] - stats[h])
            prob_ref[step % 2, part, :] = p.astype(BF16)
            ds_ref[h, rows, :] = (p * (slope_ref[step % 2, part, :] - deltas[h])).astype(BF16)

    steps = 2 * chunks
    dk, dv = [None] * chunks, [None] * chunks
    dq = None
    score(0)
    for step in range(steps):
        h, c = divmod(step, chunks)
        if step + 1 < steps:
            score(step + 1)
        bend(step)
        rows = slice(c * chunk, (c + 1) * chunk)
        v_part = jnp.dot(prob_ref[step % 2], g_heads[h], preferred_element_type=F32)
        k_part = jnp.dot(ds_ref[h, rows, :], q_heads[h], preferred_element_type=F32)
        if h == 0:
            dk[c], dv[c] = k_part, v_part
        else:
            part, at = c * chunk // half, c * chunk % half
            dqkv_ref[part, 0, at : at + chunk, PAIR : 2 * PAIR] = (dk[c] + k_part).astype(BF16)
            dqkv_ref[part, 0, at : at + chunk, 2 * PAIR :] = (dv[c] + v_part).astype(BF16)
        if c == chunks - 1:
            part = lax.dot_general(ds_ref[h], k_heads[h], TN, preferred_element_type=F32)
            dq = part if h == 0 else dq + part
    dqkv_ref[:, 0, :, :PAIR] = (dq * HD**-0.5).astype(BF16).reshape(-1, half, PAIR)


def attention_call(kernel, seg, arrays, outs, scratch, name, first=0, after=()):
    parts, seqs, half, columns = arrays[0].shape
    length = parts * half

    def spec(array, first):
        shape = array.shape
        if len(shape) == 3:
            return pl.BlockSpec((1,) + shape[1:], lambda s, p: (s, 0, 0))
        size = 3 * PAIR if shape[3] % (3 * PAIR) == 0 else PAIR
        return pl.BlockSpec((parts, 1, half, size), lambda s, p: (0, s, 0, first + p))

    size = 3 * PAIR if outs[0].shape[3] % (3 * PAIR) == 0 else PAIR
    pairs = outs[0].shape[3] // size
    operands = [seg[:, None, :], seg[:, :, None]] + arrays
    return pl.pallas_call(
        kernel,
        grid=(seqs, pairs),
        in_specs=[spec(a, first) for a in operands]
        + [pl.BlockSpec(memory_space=pl.ANY)] * len(after),
        out_specs=[spec(a, 0) for a in outs],
        out_shape=outs,
        scratch_shapes=scratch(length),
        compiler_params=pltpu.CompilerParams(vmem_limit_bytes=SMALL_VMEM),
        cost_estimate=LITTLE,
        name=name,
    )(*operands, *after)


def attend(qkv, seg):
    parts, seqs, half, columns = qkv.shape
    heads = columns // (3 * HD)
    outs = [
        jax.ShapeDtypeStruct((parts, seqs, half, columns // 3), BF16),
        jax.ShapeDtypeStruct((seqs, heads, parts * half), F32),
    ]
    scratch = lambda length: [
        pltpu.VMEM((length, length), F32),
        pltpu.VMEM((length, PAIR), F32),
        pltpu.VMEM((2, 128, length), F32),
        pltpu.VMEM((2, 128, length), BF16),
    ]
    return attention_call(attend_kernel, seg, [qkv], outs, scratch, "attend")


def attend_back(qkv, seg, out, grad, lse, first, pairs, after):
    outs = [jax.ShapeDtypeStruct(qkv.shape[:3] + (3 * PAIR * pairs,), BF16)]
    scratch = lambda length: [
        pltpu.VMEM((length, length), F32),
        pltpu.VMEM((2, length, length), BF16),
        pltpu.VMEM((2, 128, length), F32),
        pltpu.VMEM((2, 128, length), F32),
        pltpu.VMEM((2, 128, length), BF16),
    ]
    kernel = functools.partial(attend_back_kernel, first, len(after))
    arrays = [qkv, out, grad, lse]
    name = "attend_back"
    return attention_call(kernel, seg, arrays, outs, scratch, name, first, after)[0]


def body(
    layer_input,
    segment_ids,
    out_cotangent,
    attn_master,
    inner_master,
    outer_master,
    vector_master,
    attn_moment,
    inner_moment,
    outer_moment,
    vector_moment,
    attn_square,
    inner_square,
    outer_square,
    vector_square,
):
    seqs, half, width = layer_input.shape
    count = seqs * half
    hidden_units = inner_master.shape[1]
    pairs = width // (2 * PAIR)
    part_cols = width // 2
    shards = lax.axis_size("shard")
    owned_rows = attn_master.shape[1]
    core = lax.axis_index("ctx")
    first = core == 0

    def own_half(array, axis):
        size = array.shape[axis] // 2
        return lax.dynamic_slice_in_dim(array, core * size, size, axis)

    def other_half(array, axis):
        size = array.shape[axis] // 2
        return lax.dynamic_slice_in_dim(array, (1 - core) * size, size, axis)

    def in_order(mine, theirs, axis):
        return jnp.concatenate(
            [jnp.where(first, mine, theirs), jnp.where(first, theirs, mine)], axis
        )

    rows = layer_input.reshape(count, width)
    rows_chip = jnp.concatenate([rows, swap_cores(rows)], 0)
    square = is_square()

    piece = own_half(attn_master[:3], 2).astype(BF16).reshape(3, owned_rows, pairs, PAIR)
    piece = piece.transpose(1, 2, 0, 3).reshape(owned_rows, 3 * part_cols)
    vec_low = vector_master.astype(BF16)
    rider = vec_low[:2].reshape(1, -1)
    if square:
        piece = lax.dynamic_slice_in_dim(
            piece, lax.axis_index("replica") * (piece.shape[1] // 2), piece.shape[1] // 2, 1
        )
    rider = jnp.pad(rider, ((0, 15), (0, piece.shape[1] - rider.shape[1])))
    piece = jnp.concatenate([piece, rider], 0)
    if square:
        stacks, places = gather_quarters(piece)
    else:
        stacks = [item[None] for item in ring_gather(piece)]
        places = [(owner, 0) for owner in slot_owners()]
    riders = jnp.concatenate([stack[:, owned_rows] for stack in stacks], 0)[:shards]
    riders = riders[:, : 2 * width // shards].reshape(shards, 2, -1).astype(F32)
    slot_of = jnp.stack([place[0] for place in places[:shards]])
    chosen = (jnp.arange(shards)[:, None] == slot_of[None, :]).astype(F32)
    biases = jnp.einsum("ps,srw->rpw", chosen, riders).reshape(2, width)

    copies = lax.axis_size("replica") * 2
    copy_at = lax.axis_index("replica") * 2 + core
    quarter = lambda block: lax.dynamic_slice_in_dim(
        block, copy_at * (block.shape[0] // copies), block.shape[0] // copies, 0
    ).astype(BF16)
    out_q, inner_q, outer_q = quarter(attn_master[3]), quarter(inner_master), quarter(outer_master)
    wide = hidden_units // width
    small = out_q.shape[0]
    inner_q = inner_q.reshape(small, wide, width).transpose(1, 0, 2).reshape(-1, width)
    big = outer_q.shape[0]
    vec_q = vec_low.reshape(-1)
    vec_q = jnp.pad(vec_q, (0, 16 * width - vec_q.shape[0])).reshape(16, width)
    packed = lax.all_gather(jnp.concatenate([outer_q, inner_q, out_q, vec_q], 0), EVERY, axis=0)
    vec = packed[::copies, 2 * big + small :].reshape(shards, -1)[:, : vec_low.size]
    vec = vec.reshape((shards,) + vec_low.shape).transpose(1, 0, 2).reshape(-1, width).astype(F32)
    if packed.shape[0] != PARTS:
        outer_w = packed[:, :big].reshape(PARTS, -1, width)
        inner_w = packed[:, big : 2 * big].reshape(-1, wide, small, width).transpose(0, 2, 1, 3)
        inner_w = inner_w.reshape(PARTS, -1, wide, width).transpose(0, 2, 1, 3)
        out_w = packed[:, 2 * big : 2 * big + small].reshape(PARTS, -1, width)
        packed = jnp.concatenate([outer_w, inner_w.reshape(PARTS, -1, width), out_w], 1)

    halves = own_half(biases, 1).reshape(2, pairs, PAIR)
    bias = jnp.stack([halves[0], jnp.zeros_like(halves[0]), halves[1]], 1).reshape(1, -1)
    ones = jnp.ones((pairs, PAIR), F32)
    factor = jnp.stack([ones * HD**-0.5, ones, ones], 1).reshape(1, -1)
    qkv, qkv_w = project(rows_chip, stacks, places, bias, factor)
    qkv = qkv.reshape(2, seqs, half, 3 * part_cols)
    seg = jnp.concatenate([own_half(segment_ids, 1), other_half(segment_ids, 1)], 1)
    mixed, lse = attend(qkv, seg)
    mixed_back = swap_cores(mixed[1].reshape(count, part_cols))
    heads_out = in_order(mixed[0].reshape(count, part_cols), mixed_back, 1)

    cotan = out_cotangent.reshape(count, width)
    active, slope, hidden_low, normed, scale, result, ffn_grad, sums_two = ffn(
        heads_out, rows, cotan, vec, packed
    )

    def send_half(left, right):
        return contract_rows(left, other_half(right, 1)).astype(BF16)

    def own_part(left, right):
        return contract_rows(left, own_half(right, 1)).astype(BF16)

    def by_shard(array):
        return array.astype(BF16).reshape(shards, -1, array.shape[1])

    o, i, y, inner = position()
    where = jnp.stack([o, i, y, core]).astype(jnp.int32)
    outer_sent = send_half(active, ffn_grad)
    outer_chips = [by_shard(own_part(active, ffn_grad)), by_shard(swap_cores(outer_sent))]
    done = (outer_sent,)
    if square:
        outer = Sum(where, *outer_chips)
        done = outer.merge()
    pre_grad, branch_grad, mixed_grad, sums_one = ffn_back(
        ffn_grad, slope, normed, scale, vec, packed, done[0]
    )
    mixed_grad = jnp.stack(
        [own_half(mixed_grad, 1), swap_cores(other_half(mixed_grad, 1))], 0
    ).reshape(mixed.shape)
    inner_sent = send_half(hidden_low, pre_grad)
    out_sent = send_half(heads_out, branch_grad)
    inner_chips = [by_shard(own_part(hidden_low, pre_grad)), by_shard(swap_cores(inner_sent))]
    out_chip = add_low(
        by_shard(own_part(heads_out, branch_grad)), by_shard(swap_cores(out_sent))
    )

    def back(first, after):
        return attend_back(
            qkv, seg, mixed, mixed_grad, lse, first, pairs // 2, after
        ).reshape(2 * count, -1)

    def bias_sums(grad):
        sums = jnp.sum(grad.astype(F32), 0).reshape(-1, 3, PAIR)
        return sums[:, 0].reshape(-1), sums[:, 2].reshape(-1)

    def make_chip_a(grad):
        return jnp.concatenate([by_shard(contract_rows(rows_chip, grad)), out_chip], 2)

    def make_chip_b(grad_a, grad_b):
        bias_a, bias_b = bias_sums(grad_a), bias_sums(grad_b)
        blank = jnp.zeros((part_cols,), F32)
        attn_biases = [
            in_order(jnp.concatenate([bias_a[at], bias_b[at]]), blank, 0) for at in range(2)
        ]
        sums = [jnp.stack(attn_biases), sums_one[2:3], sums_one[:2], sums_two[2:3], sums_two[:2]]
        sums = jnp.concatenate(sums + [sums_one[4:8]], 0)
        sums = sums.reshape(-1, shards, width // shards).transpose(1, 0, 2)
        sums = jnp.pad(sums, ((0, 0), (0, owned_rows - sums.shape[1]), (0, 0)))
        return jnp.concatenate([by_shard(contract_rows(rows_chip, grad_b)), sums.astype(BF16)], 2)

    outer_states = (outer_master, outer_moment, outer_square)
    inner_states = (inner_master, inner_moment, inner_square)
    attn_states = (attn_master, attn_moment, attn_square)
    if square:
        done = outer.plane((pre_grad,))
        inner = Sum(where, *inner_chips)
        done = inner.merge(done)
        done = outer.cross(done)
        grad_a = back(0, done + (out_sent,))
        done = inner.plane((grad_a,))
        sum_a = Sum(where, make_chip_a(grad_a))
        done = sum_a.merge(done)
        done = outer.line(done)
        grad_b = back(pairs // 2, done)
        done = inner.cross((grad_b,))
        sum_b = Sum(where, make_chip_b(grad_a, grad_b))
        done = sum_b.merge(done)
        done = sum_a.plane(done)
        theirs_part = input_back(grad_a, grad_b, qkv_w, (), done)
        outer_new = update(where, outer_states, [outer.shares], (theirs_part,))
        done = sum_a.cross((outer_new[0],))
        done = sum_b.plane(done)
        done = inner.line(done)
        input_grad = input_back(
            grad_a, grad_b, qkv_w, (branch_grad, swap_cores(theirs_part)), done
        )
        done = sum_b.cross((input_grad,))
        done = sum_a.line(done)
        inner_new = update(where, inner_states, [inner.shares], done)
        sum_b.line((inner_new[0],))
        attn_shares = [sum_a.shares, sum_b.shares]
        vector_shares = [
            jnp.concatenate(
                [
                    jnp.where(y == 0, sum_b.shares[at], sum_b.shares[at + 1])[0],
                    jnp.where(y == 0, sum_b.shares[at + 1], sum_b.shares[at])[0],
                ],
                0,
            )
            for at in (0, 2)
        ]
    else:
        grad_a = back(0, ())
        grad_b = back(pairs // 2, ())
        theirs_part = input_back(grad_a, grad_b, qkv_w, (), ())
        added = (branch_grad, swap_cores(theirs_part))
        input_grad = input_back(grad_a, grad_b, qkv_w, added, ())
        outer_new = update(where, outer_states, [sum_apart(add_low(*outer_chips))])
        inner_new = update(where, inner_states, [sum_apart(add_low(*inner_chips))])
        attn_shares = [sum_apart(make_chip_a(grad_a)), sum_apart(make_chip_b(grad_a, grad_b))]
        vector_shares = [share[0] for share in attn_shares[1]]
    attn_new = update(where, attn_states, attn_shares)
    cut = grad_b.shape[1]
    vector_sum = sum(share[: vec_low.shape[0], cut:].astype(F32) for share in vector_shares)
    vector_new = adamw(vector_sum, vector_moment, vector_square, vector_master, RATE_VECTOR)
    vector_new = vector_new + (vector_new[2].astype(BF16),)
    news = (attn_new, inner_new, outer_new, vector_new)
    updates = [[new[at] for new in news] for at in range(4)]
    return (
        result.reshape(seqs, half, width).astype(BF16),
        input_grad.reshape(seqs, half, width),
        *[item for kind in updates for item in kind],
    )


def solution(mesh):
    tokens = P(("replica", "shard"), "ctx", None)
    states = (P(None, "shard", None), P("shard", None), P("shard", None), P(None, "shard"))
    in_specs = (tokens, P(("replica", "shard"), None), tokens) + states * 3
    out_specs = (tokens, tokens) + states * 4
    return jax.shard_map(body, mesh=mesh, in_specs=in_specs, out_specs=out_specs, check_vma=False)
```

```python
import functools
import math

import jax
import jax.numpy as jnp
from jax import lax
from jax.experimental import pallas as pl
from jax.experimental.pallas import tpu as pltpu
from jax.sharding import PartitionSpec as P

HD = 64
PAIR = 2 * HD
STEP = 5
OUTER = 4
EVERY = ("shard", "replica", "ctx")

EPS_NORM = 1e-05
BETA_ONE = 0.5
BETA_TWO = 0.6
RATE_MATRIX = 0.02
RATE_VECTOR = 0.1
DECAY = 0.01
EPS_ADAM = 1e-06
MASKED = -1e30
F32 = jnp.float32
BF16 = jnp.bfloat16
PARTS = 32
TILE = 32
VMEM = 56 * 1024 * 1024
SMALL_VMEM = 16 * 1024 * 1024
GROUP = 256
NT = (((1,), (1,)), ((), ()))
TN = (((0,), (0,)), ((), ()))


def weight_of(micros):
    return pl.CostEstimate(
        flops=int(micros * 2.9e8), bytes_accessed=int(micros * 9.2e5), transcendentals=0
    )


def normalize(resid):
    centre = resid - jnp.mean(resid, -1, keepdims=True)
    scale = lax.rsqrt(jnp.mean(centre * centre, -1, keepdims=True) + EPS_NORM)
    return (centre * scale, scale)


def norm_back(grad, normed, scale):
    return scale * (
        grad
        - jnp.mean(grad, -1, keepdims=True)
        - normed * jnp.mean(grad * normed, -1, keepdims=True)
    )


def adamw(grad, moment, square, weight, rate):
    moment_new = BETA_ONE * moment + (1.0 - BETA_ONE) * grad
    square_new = BETA_TWO * square + (1.0 - BETA_TWO) * grad * grad
    stepped = (
        moment_new
        / (1.0 - BETA_ONE**STEP)
        / (jnp.sqrt(square_new / (1.0 - BETA_TWO**STEP)) + EPS_ADAM)
    )
    weight_new = weight - rate * (stepped + DECAY * weight)
    return (moment_new, square_new, weight_new)


def swap_cores(value):
    return lax.ppermute(value, "ctx", [(0, 1), (1, 0)])


def shift_outer(value, step):
    inner = lax.axis_size("shard") // OUTER
    pairs = [
        (o * inner + i, ((o + step) % OUTER) * inner + i) for o in range(OUTER) for i in range(inner)
    ]
    return lax.ppermute(value, "shard", pairs)


def shift_inner(value, step):
    inner = lax.axis_size("shard") // OUTER
    pairs = [
        (o * inner + i, o * inner + (i + step) % inner) for o in range(OUTER) for i in range(inner)
    ]
    return lax.ppermute(value, "shard", pairs)


def shift_replica(value, step):
    size = lax.axis_size("replica")
    return lax.ppermute(value, "replica", [(r, (r + step) % size) for r in range(size)])


def ring_gather(piece):
    inner = lax.axis_size("shard") // OUTER
    found = []
    held = piece
    for k in range(OUTER):
        if k:
            held = shift_outer(held, -1)
        found.append([held] + [shift_inner(held, -e) for e in range(1, inner)])
    return [item for group in found for item in group]


def slot_owners():
    inner = lax.axis_size("shard") // OUTER
    at = lax.axis_index("shard")
    o, i = at // inner, at % inner
    return [
        lax.rem(o + k, OUTER) * inner + lax.rem(i + e, inner)
        for k in range(OUTER)
        for e in range(inner)
    ]


def pick(array, index, axis):
    return lax.dynamic_index_in_dim(array, index, axis, keepdims=False)


def add_low(value, *others):
    total = value.astype(F32)
    for item in others:
        total = total + item.astype(F32)
    return total.astype(BF16)


def position():
    inner = lax.axis_size("shard") // OUTER
    at = lax.axis_index("shard")
    return at // inner, at % inner, lax.axis_index("replica"), inner


def is_square():
    return lax.axis_size("replica") == 2 and lax.axis_size("shard") == 2 * OUTER


def swap_outer(value, flip):
    inner = lax.axis_size("shard") // OUTER
    pairs = [(o * inner + i, (o ^ flip) * inner + i) for o in range(OUTER) for i in range(inner)]
    return lax.ppermute(value, "shard", pairs)


def swap_cross(value):
    return lax.ppermute(value, ("replica", "ctx"), [(a, 3 - a) for a in range(4)])


def sum_apart(chip_sum):
    o, i, y, inner = position()
    grid = chip_sum.reshape(OUTER, inner, *chip_sum.shape[1:])
    got = [shift_inner(pick(grid, lax.rem(i + e, inner), 1), e) for e in range(1, inner)]
    line = add_low(pick(grid, i, 1), *got)
    got = [shift_outer(pick(line, lax.rem(o + d, OUTER), 0), d) for d in range(1, OUTER)]
    total = add_low(pick(line, o, 0), *got)
    got = [shift_replica(total, r) for r in range(1, lax.axis_size("replica"))]
    mine = add_low(total, *got)[None]
    return [mine, swap_cores(mine)]


def small_call(kernel, where, ins, outs, after, name):
    held = pl.BlockSpec(memory_space=pltpu.VMEM)
    return pl.pallas_call(
        functools.partial(kernel, len(ins), len(after)),
        in_specs=[pl.BlockSpec(memory_space=pltpu.SMEM)]
        + [held] * len(ins)
        + [pl.BlockSpec(memory_space=pl.ANY)] * len(after),
        out_specs=[held] * len(outs),
        out_shape=[pltpu.VMEM(shape, BF16) for shape in outs],
        compiler_params=pltpu.CompilerParams(vmem_limit_bytes=SMALL_VMEM),
        cost_estimate=weight_of(1),
        name=name,
    )(where, *[pltpu.with_memory_space_constraint(a, pltpu.VMEM) for a in ins], *after)


def fold_plane_kernel(count, after, where_ref, keep_p, got_p, keep_q, got_q, *rest):
    i, y = where_ref[1], where_ref[2]
    kept_p, send_p, kept_q, send_q = rest[after:]
    for o in range(OUTER):
        for out, at in ((kept_p, y), (send_p, 1 - y)):
            out[o] = add_low(keep_p[o, at], got_p[o, at])
        for out, at in ((kept_q, i), (send_q, 1 - i)):
            out[o] = add_low(keep_q[o, at], got_q[o, at])


def line_order(o):
    near = o + 1 - 2 * lax.rem(o, 2)
    far = lambda at: lax.rem(at + 2, OUTER)
    return (o, far(o)), (near, far(near))


def fold_cross_kernel(count, after, where_ref, keep_p, got_p, keep_q, got_q, *rest):
    for out, order in zip(rest[after:], line_order(where_ref[0])):
        for n, at in enumerate(order):
            out[n, 0] = add_low(keep_p[at], got_p[at])
            out[n, 1] = add_low(keep_q[at], got_q[at])


def fold_turn_kernel(count, after, where_ref, keep, got, *rest):
    for n, out in enumerate(rest[after:]):
        out[...] = add_low(keep[n], got[n])


def fold_line_kernel(count, after, where_ref, *rest):
    rest[count + after][...] = add_low(*(ref[...] for ref in rest[:count]))


def merge_kernel(groups, after, where_ref, *refs):
    outs = refs[4 * sum(groups) + after :]
    for slot, out in enumerate(outs):
        left = chip = 0
        for group in groups:
            for at in range(2):
                parts = []
                for n in range(chip, chip + group):
                    ref = refs[4 * n + slot]
                    parts.append(ref[0, at, 0, 0] if slot % 2 else ref[0, 0, 0, at])
                cut = slice(left, left + parts[0].shape[1])
                out[0, at, :, cut] = parts[0] if group == 1 else add_low(*parts)
            left, chip = cut.stop, chip + group


class Sum:
    def __init__(self, where, *groups):
        self.where, self.rows = where, groups[0][0].shape[1] // 4
        self.columns = sum(group[0].shape[2] for group in groups)
        self.groups = [len(group) for group in groups]
        self.chips = [
            c.reshape(OUTER, 2, 2, 2, self.rows, c.shape[2]) for group in groups for c in group
        ]

    def shape(self, *lead):
        return lead + (self.rows, self.columns)

    def merge(self, after=()):
        def spec(chip, lead, flip):
            def place(o, w):
                at = w[1] if lead == 0 else w[2]
                at = 1 - at if flip else at
                return (o, at, 0, 0, 0, 0) if lead == 0 else (o, 0, 1, at, 0, 0)

            return pl.BlockSpec(((1, 1, 1, 2) if lead == 0 else (1, 2, 1, 1)) + chip.shape[4:], place)

        kinds = ((0, True), (1, True), (0, False), (1, False))
        out_spec = pl.BlockSpec((1, 2, self.rows, self.columns), lambda o, w: (o, 0, 0, 0))
        *sent, keep_p, keep_q = pl.pallas_call(
            functools.partial(merge_kernel, self.groups, len(after)),
            grid_spec=pltpu.PrefetchScalarGridSpec(
                num_scalar_prefetch=1,
                grid=(OUTER,),
                in_specs=[spec(chip, *kind) for chip in self.chips for kind in kinds]
                + [pl.BlockSpec(memory_space=pl.ANY)] * len(after),
                out_specs=[out_spec] * 4,
            ),
            out_shape=[jax.ShapeDtypeStruct(self.shape(OUTER, 2), BF16)] * 4,
            compiler_params=pltpu.CompilerParams(vmem_limit_bytes=SMALL_VMEM),
            cost_estimate=weight_of(4),
            name="merge",
        )(self.where, *[chip for chip in self.chips for _ in range(4)], *after)
        self.kept = [keep_p, shift_inner(sent[0], 1), keep_q, shift_replica(sent[1], 1)]
        return tuple(sent)

    def plane(self, after=()):
        keep_p, send_p, keep_q, send_q = small_call(
            fold_plane_kernel, self.where, self.kept, [self.shape(OUTER)] * 4, after, "fold_plane"
        )
        self.kept = [keep_p, shift_replica(send_p, 1), keep_q, shift_inner(send_q, 1)]
        return (send_p, send_q)

    def cross(self, after=()):
        keep, send = small_call(
            fold_cross_kernel, self.where, self.kept, [self.shape(2, 2)] * 2, after, "fold_cross"
        )
        self.kept = [keep, swap_outer(send, 1)]
        return (send,)

    def turn(self, after=()):
        shapes = [self.kept[0].shape[1:]] * 2
        keep, send = small_call(
            fold_turn_kernel, self.where, self.kept, shapes, after, "fold_turn"
        )
        self.kept = [keep, swap_outer(send, 2)]
        return (send,)

    def line(self, after=()):
        (total,) = small_call(
            fold_line_kernel, self.where, self.kept, [self.kept[0].shape], after, "fold_line"
        )
        self.shares = [total, shift_replica(total, 1), swap_cores(total), swap_cross(total)]
        return (total,)


def update_kernel(groups, after, where_ref, *refs):
    states, shares = refs[:3], refs[3 : 3 + sum(groups)]
    outs, grad_ref = refs[3 + sum(groups) + after : -1], refs[-1]
    rows = shares[0].shape[1]
    across = groups[0] // 2
    for core in range(2):

        @pl.when(pl.program_id(1) == core)
        def _():
            for n in range(across):
                line = where_ref[2] if n == 0 else 1 - where_ref[2]
                line = pl.ds(pl.multiple_of(line * rows, rows), rows) if across > 1 else slice(None)
                if len(groups) == 1:
                    grad_ref[line, :] = shares[across * core + n][0].astype(F32)
                    continue
                left, right = shares[across * core + n], shares[groups[0] + across * core + n]
                width = grad_ref.shape[2]
                pairs = width // PAIR
                for t in range(3):
                    for p in range(pairs):
                        side, at = (left, p) if 2 * p < pairs else (right, p - pairs // 2)
                        part = side[0, :, (3 * at + t) * PAIR : (3 * at + t + 1) * PAIR]
                        grad_ref[t, line, p * PAIR : (p + 1) * PAIR] = part.astype(F32)
                cut = 3 * PAIR * (pairs // 2)
                grad_ref[3, line, :] = left[0, :, cut : cut + width].astype(F32)

    new = adamw(grad_ref[...], states[1][...], states[2][...], states[0][...], RATE_MATRIX)
    for out, value in zip(outs, new + (new[2],)):
        out[...] = value.astype(out.dtype)


def update(where, states, groups, after=()):
    parts, rows = groups[0][0].shape[:2]
    rows = rows * (len(groups[0]) // 2)
    lead = states[0].shape[:-2]
    columns = states[0].shape[-1] // 2
    place = lambda p, v, w: (0,) * len(lead) + (p, w[3] + v - 2 * w[3] * v)
    block = pl.BlockSpec(lead + (rows, columns), place)
    shares = [share for group in groups for share in group]
    share_specs = [pl.BlockSpec((1,) + a.shape[1:], lambda p, v, w: (p, 0, 0)) for a in shares]
    kinds = (F32, F32, F32, BF16)
    return pl.pallas_call(
        functools.partial(update_kernel, [len(group) for group in groups], len(after)),
        grid_spec=pltpu.PrefetchScalarGridSpec(
            num_scalar_prefetch=1,
            grid=(parts, 2),
            in_specs=[block] * 3 + share_specs + [pl.BlockSpec(memory_space=pl.ANY)] * len(after),
            out_specs=[block] * 4,
            scratch_shapes=[pltpu.VMEM(lead + (rows, columns), F32)],
        ),
        out_shape=[jax.ShapeDtypeStruct(states[0].shape, kind) for kind in kinds],
        compiler_params=pltpu.CompilerParams(vmem_limit_bytes=SMALL_VMEM),
        cost_estimate=weight_of(5),
        name="update",
    )(where, *states, *shares, *after)


def input_back_kernel(a_ref, b_ref, left_ref, right_ref, *rest):
    out_ref = rest[-1]
    total = lax.dot_general(a_ref[...], left_ref[...], NT, preferred_element_type=F32)
    total += lax.dot_general(b_ref[...], right_ref[...], NT, preferred_element_type=F32)
    if out_ref.dtype == F32:
        total += rest[0][...].astype(F32) + rest[1][...].astype(F32)
    out_ref[...] = total.astype(out_ref.dtype)


def input_back(grad_a, grad_b, weight, added, after):
    count, cut = grad_a.shape[0] // 2, grad_a.shape[1]
    width = weight.shape[0]
    tile = width // 4
    first = 0 if added else 1
    side = pl.BlockSpec((count, cut), lambda n: (first, 0))
    line = pl.BlockSpec((count, tile), lambda n: (0, n))
    return pl.pallas_call(
        input_back_kernel,
        grid=(width // tile,),
        in_specs=[side, side]
        + [pl.BlockSpec((tile, cut), lambda n, at=at: (n, at)) for at in range(2)]
        + [line] * len(added)
        + [pl.BlockSpec(memory_space=pl.ANY)] * len(after),
        out_specs=line,
        out_shape=jax.ShapeDtypeStruct((count, width), F32 if added else BF16),
        compiler_params=pltpu.CompilerParams(vmem_limit_bytes=SMALL_VMEM),
        cost_estimate=weight_of(5),
        name="input_back",
    )(grad_a, grad_b, weight, weight, *added, *after)


def gather_quarters(quarter):
    line = jnp.stack([quarter] + [shift_outer(quarter, -k) for k in range(1, OUTER)])
    near_x = shift_inner(line, 1)
    near_y = shift_replica(line, 1)
    far_x = shift_inner(near_y[: OUTER // 2], 1)
    far_y = shift_replica(near_x[OUTER // 2 :], 1)
    o, i, y, inner = position()
    row = lambda k, across: lax.rem(o + k, OUTER) * 2 + (1 - i if across else i)
    places = [(row(k, False), y) for k in range(OUTER)] + [(row(k, True), y) for k in range(OUTER)]
    places += [(row(k, False), 1 - y) for k in range(OUTER)]
    places += [(row(k, True), 1 - y) for k in range(OUTER)]
    return [line, near_x, near_y, far_x, far_y], places


def project_kernel(row_ref, column_ref, rows_ref, bias_ref, factor_ref, *rest):
    stacks, (out_ref, weight_ref) = rest[:-2], rest[-2:]
    columns = stacks[0].shape[2]
    part = weight_ref.shape[0] * weight_ref.shape[1] // columns
    part = part // sum(stack.shape[0] for stack in stacks)

    @pl.when(pl.program_id(0) == 0)
    def _():
        slot = 0
        for stack in stacks:
            for k in range(stack.shape[0]):
                start = pl.multiple_of(row_ref[slot] * part, part)
                left = pl.multiple_of(column_ref[slot] * columns, PAIR)
                weight_ref[pl.ds(start, part), pl.ds(left, columns)] = stack[k, :part, :]
                slot += 1

    acc = jnp.dot(rows_ref[...], weight_ref[...], preferred_element_type=F32)
    out_ref[...] = ((acc + bias_ref[...]) * factor_ref[...]).astype(BF16)


def project(rows, stacks, places, bias, factor):
    count, width = rows.shape
    columns = bias.shape[1]
    tile = 512
    whole = lambda shape: pl.BlockSpec(shape, lambda m, *_: (0,) * len(shape))
    tables = [jnp.stack([p[axis] for p in places]).astype(jnp.int32) for axis in range(2)]
    return pl.pallas_call(
        project_kernel,
        grid_spec=pltpu.PrefetchScalarGridSpec(
            num_scalar_prefetch=2,
            grid=(count // tile,),
            in_specs=[
                pl.BlockSpec((tile, width), lambda m, *_: (m, 0)),
                whole((1, columns)),
                whole((1, columns)),
            ]
            + [whole(stack.shape) for stack in stacks],
            out_specs=[
                pl.BlockSpec((tile, columns), lambda m, *_: (m, 0)),
                whole((width, columns)),
            ],
        ),
        out_shape=[
            jax.ShapeDtypeStruct((count, columns), BF16),
            jax.ShapeDtypeStruct((width, columns), BF16),
        ],
        compiler_params=pltpu.CompilerParams(vmem_limit_bytes=VMEM),
        cost_estimate=weight_of(11),
        name="project",
    )(*tables, rows, bias, factor, *stacks)


def gelu_and_slope(u):
    a = jnp.abs(u)
    d = 1.0 + (0.3275911 * 0.5**0.5) * a
    t = pl.reciprocal(d, approx=True)
    t = t * (2.0 - d * t)
    e = jnp.exp2(u * u * (-0.5 * math.log2(math.e)))
    series = (0.5 * 1.061405429) * t - 0.5 * 1.453152027
    series = series * t + 0.5 * 1.421413741
    series = series * t - 0.5 * 0.284496736
    series = series * t + 0.5 * 0.254829592
    tail = series * t * e
    active = jnp.maximum(u, 0.0) - a * tail
    below = tail - a * (e * (1.0 / math.sqrt(2.0 * math.pi)))
    return active, jnp.where(u >= 0.0, 1.0 - below, below)


def total_rows(value):
    return jnp.sum(value, axis=0, keepdims=True)


def in_parts(count, work):
    def turn(at, carry):
        work(pl.ds(pl.multiple_of(at * 128, 128), 128))
        return carry

    lax.fori_loop(0, count // 128, turn, 0)


def ffn_kernel(
    core_ref,
    mine_ref,
    theirs_ref,
    rows_ref,
    cotan_ref,
    vec_ref,
    out_w_ref,
    inner_w_ref,
    outer_w_ref,
    active_ref,
    slope_ref,
    hidden_ref,
    normed_ref,
    scale_ref,
    result_ref,
    grad_ref,
    sums_ref,
    resid,
    acc,
    pre,
):
    w = pl.program_id(0)
    count, width = acc.shape
    chunk = pre.shape[2]
    vec = lambda at: vec_ref[at : at + 1, :]
    pieces = out_w_ref.shape[0] // 2
    half_of = lambda at: out_w_ref[pl.ds(at * pieces, pieces)].reshape(width // 2, width)

    @pl.when(w == 0)
    def _():
        acc[...] = jnp.dot(mine_ref[...], half_of(core_ref[0]), preferred_element_type=F32)
        acc[...] += jnp.dot(theirs_ref[...], half_of(1 - core_ref[0]), preferred_element_type=F32)

        def enter(part):
            normed, scale = normalize(acc[part, :] + vec(2) + rows_ref[part, :].astype(F32))
            normed_ref[part, :] = normed.astype(BF16)
            scale_ref[part, :] = scale
            hidden = normed * vec(3) + vec(4)
            resid[part, :] = hidden + vec(5)
            hidden_ref[part, :] = hidden.astype(BF16)

        in_parts(count, enter)

    bias = vec_ref[pl.ds(8 + w, 1), :]

    def expand(n):
        cut = slice(n * chunk, (n + 1) * chunk)
        weight = inner_w_ref[:, :, cut].reshape(width, chunk)
        pre[n % 2] = jnp.dot(hidden_ref[...], weight, preferred_element_type=F32)

    def bend(n):
        cut = slice(n * chunk, (n + 1) * chunk)
        for at in range(0, count, TILE):
            part = slice(at, at + TILE)
            active, slope = gelu_and_slope(pre[n % 2, part, :] + bias[:, cut])
            active_ref[part, cut] = active.astype(BF16)
            slope_ref[part, cut] = slope.astype(BF16)

    chunks = width // chunk
    expand(0)
    for n in range(1, chunks):
        expand(n)
        bend(n - 1)
    bend(chunks - 1)

    def contract():
        weight = outer_w_ref[...].reshape(width, width)
        return jnp.dot(active_ref[...], weight, preferred_element_type=F32)

    @pl.when(w == 0)
    def _():
        acc[...] = contract()

    @pl.when(w > 0)
    def _():
        acc[...] += contract()

    @pl.when(w == pl.num_programs(0) - 1)
    def _():
        sums_ref[...] = jnp.zeros_like(sums_ref)

        def leave(part):
            normed, scale = normalize(resid[part, :] + acc[part, :])
            result_ref[part, :] = (normed * vec(6) + vec(7)).astype(BF16)
            cotan = cotan_ref[part, :].astype(F32)
            grad = norm_back(cotan * vec(6), normed, scale).astype(BF16)
            grad_ref[part, :] = grad
            sums_ref[0:1, :] += total_rows(cotan * normed)
            sums_ref[1:2, :] += total_rows(cotan)
            sums_ref[2:3, :] += total_rows(grad.astype(F32))

        in_parts(count, leave)


def ffn_back_kernel(
    core_ref,
    grad_ref,
    slope_ref,
    normed_ref,
    scale_ref,
    vec_ref,
    out_w_ref,
    inner_w_ref,
    outer_w_ref,
    after_ref,
    pre_grad_ref,
    branch_ref,
    mine_ref,
    theirs_ref,
    sums_ref,
    acc,
    pre,
):
    w = pl.program_id(0)
    count, width = acc.shape
    chunk = pre.shape[2]
    vec = lambda at: vec_ref[at : at + 1, :]

    @pl.when(w == 0)
    def _():
        sums_ref[...] = jnp.zeros_like(sums_ref)

    def pull(n):
        each = outer_w_ref.shape[0] * chunk // width
        weight = outer_w_ref[n * each : (n + 1) * each].reshape(chunk, width)
        pre[n % 2] = lax.dot_general(grad_ref[...], weight, NT, preferred_element_type=F32)

    def bend(n):
        cut = slice(n * chunk, (n + 1) * chunk)
        sums = jnp.zeros((8, chunk), F32)
        for at in range(0, count, TILE):
            part = slice(at, at + TILE)
            back = pre[n % 2, part, :].astype(BF16).astype(F32) * slope_ref[part, cut].astype(F32)
            back = back.astype(BF16)
            pre_grad_ref[part, cut] = back
            sums += jnp.sum(back.astype(F32).reshape(TILE // 8, 8, chunk), axis=0)
        sums_ref[pl.ds(4 + w, 1), cut] += total_rows(sums)

    chunks = width // chunk
    pull(0)
    for n in range(1, chunks):
        pull(n)
        bend(n - 1)
    bend(chunks - 1)

    def contract():
        weight = inner_w_ref[...].reshape(width, width)
        return lax.dot_general(pre_grad_ref[...], weight, NT, preferred_element_type=F32)

    @pl.when(w == 0)
    def _():
        acc[...] = contract()

    @pl.when(w > 0)
    def _():
        acc[...] += contract()

    @pl.when(w == pl.num_programs(0) - 1)
    def _():
        def leave(part):
            through = acc[part, :].astype(BF16).astype(F32) + grad_ref[part, :].astype(F32)
            normed = normed_ref[part, :].astype(F32)
            branch = norm_back(through * vec(3), normed, scale_ref[part, :]).astype(BF16)
            branch_ref[part, :] = branch
            sums_ref[0:1, :] += total_rows(through * normed)
            sums_ref[1:2, :] += total_rows(through)
            sums_ref[2:3, :] += total_rows(branch.astype(F32))

        in_parts(count, leave)
        pieces = out_w_ref.shape[0] // 2
        for out, at in ((mine_ref, core_ref[0]), (theirs_ref, 1 - core_ref[0])):
            weight = out_w_ref[pl.ds(at * pieces, pieces)].reshape(width // 2, width)
            out[...] = lax.dot_general(
                branch_ref[...], weight, NT, preferred_element_type=F32
            ).astype(BF16)


def packed_specs(width):
    small = width // PARTS
    once = pl.Buffered(1)
    return [
        pl.BlockSpec((PARTS, small, width), lambda w: (0, 8, 0), pipeline_mode=once),
        pl.BlockSpec((PARTS, small, width), lambda w: (0, 4 + w, 0)),
        pl.BlockSpec((PARTS // 4, 4 * small, width), lambda w: (w, 0, 0)),
    ]


def ffn_call(kernel, core, ins, packed, after, wide_outs, outs, room, name):
    count, width = ins[0].shape[0], packed.shape[2]
    steps = 4

    def spec(shape):
        if shape == (count, steps * width):
            return pl.BlockSpec((count, width), lambda w: (0, w))
        return pl.BlockSpec(shape, lambda w: (0, 0), pipeline_mode=pl.Buffered(1))

    shapes = [((count, steps * width), BF16)] * wide_outs + outs
    return pl.pallas_call(
        kernel,
        grid=(steps,),
        in_specs=[pl.BlockSpec(memory_space=pltpu.SMEM)]
        + [spec(a.shape) for a in ins]
        + packed_specs(width)
        + [pl.BlockSpec(memory_space=pl.ANY)] * len(after),
        out_specs=[spec(shape) for shape, kind in shapes],
        out_shape=[jax.ShapeDtypeStruct(shape, kind) for shape, kind in shapes],
        scratch_shapes=[pltpu.VMEM((count, width), F32)] * wide_outs
        + [pltpu.VMEM((2, count, 256), F32)],
        compiler_params=pltpu.CompilerParams(vmem_limit_bytes=room * 1024 * 1024),
        cost_estimate=weight_of(40),
        name=name,
    )(core, *ins, packed, packed, packed, *after)


def ffn(core, mine, theirs, rows, cotan, vec, packed):
    low = (rows.shape, BF16)
    sums = ((8, rows.shape[1]), F32)
    outs = [low, low, ((rows.shape[0], 1), F32), low, low, sums]
    ins = [mine, theirs, rows, cotan, vec]
    return ffn_call(ffn_kernel, core, ins, packed, (), 2, outs, 54, "ffn")


def ffn_back(core, grad, slope, normed, scale, vec, packed, after):
    low, part = (grad.shape, BF16), ((grad.shape[0], grad.shape[1] // 2), BF16)
    outs = [low, part, part, ((8, grad.shape[1]), F32)]
    ins = [grad, slope, normed, scale, vec]
    return ffn_call(ffn_back_kernel, core, ins, packed, after, 1, outs, 44, "ffn_back")


def product_kernel(count, after, where_ref, *refs):
    lefts, right_ref, out_ref = refs[:count], refs[count], refs[count + 1 + after]
    for n, left_ref in enumerate(lefts):

        @pl.when((pl.program_id(0) == n) | (count == 1))
        def _():
            out_ref[...] = lax.dot_general(
                left_ref[...], right_ref[...], TN, preferred_element_type=F32
            ).astype(BF16)


def product(where, lefts, right, side, after=()):
    rows = right.shape[0]
    width = right.shape[1] // (1 if side is None else 2)
    tile = 512
    height = sum(left.shape[1] for left in lefts)
    micros = 2e-9 * height * width * rows + 1
    half = lambda a, w: (0, 0 if side is None else (w[3] if side else 1 - w[3]))
    if len(lefts) == 1:
        left_specs = [pl.BlockSpec((rows, tile), lambda a, w: (0, a))]
        place = lambda a, w: (a, 0)
    else:
        left_specs = [pl.BlockSpec((rows, tile), lambda a, w: (0, 0))] * 2
        place = lambda a, w: (a + w[3] - 2 * a * w[3], 0)
    return pl.pallas_call(
        functools.partial(product_kernel, len(lefts), len(after)),
        grid_spec=pltpu.PrefetchScalarGridSpec(
            num_scalar_prefetch=1,
            grid=(height // tile,),
            in_specs=left_specs
            + [pl.BlockSpec((rows, width), half, pipeline_mode=pl.Buffered(1))]
            + [pl.BlockSpec(memory_space=pl.ANY)] * len(after),
            out_specs=pl.BlockSpec((tile, width), place),
        ),
        out_shape=jax.ShapeDtypeStruct((height, width), BF16),
        compiler_params=pltpu.CompilerParams(vmem_limit_bytes=2 * SMALL_VMEM),
        cost_estimate=weight_of(micros),
        name="product",
    )(where, *lefts, right, *after)


def attend_kernel(seg_row_ref, seg_col_ref, qkv_ref, *rest):
    out_refs, (lse_ref, bias_ref, stat_ref, score_ref, expo_ref) = rest[:2], rest[2:]
    half = qkv_ref.shape[2]
    pair = pl.program_id(1)
    length = bias_ref.shape[0]
    chunk = score_ref.shape[1]

    @pl.when(pair == 0)
    def _():
        bias_ref[...] = jnp.where(seg_col_ref[0] == seg_row_ref[0], 0.0, MASKED)
        stat_ref[...] = jnp.zeros_like(stat_ref)

    block = qkv_ref[:, 0].reshape(length, 3 * PAIR)
    q, k, v = (block[:, i * PAIR : (i + 1) * PAIR] for i in range(3))
    lane = lax.broadcasted_iota(jnp.int32, (length, PAIR), 1)
    low = lane < HD
    zero, one = jnp.zeros_like(q), jnp.ones_like(v)
    q_heads = [jnp.where(low, q, zero), jnp.where(low, zero, q)]
    v_heads = [jnp.where(low, v, one), jnp.where(low, one, v)]
    lane, low = lane[:chunk], low[:chunk]

    def score(step):
        c, h = divmod(step, 2)
        score_ref[step % 2] = lax.dot_general(
            q_heads[h][c * chunk : (c + 1) * chunk], k, NT, preferred_element_type=F32
        )

    def soften(step):
        c, h = divmod(step, 2)
        tops = []
        for at in range(0, chunk, TILE):
            rows = slice(c * chunk + at, c * chunk + at + TILE)
            s = score_ref[step % 2, at : at + TILE, :] + bias_ref[rows, :]
            top = jnp.max(s, axis=1, keepdims=True)
            expo_ref[step % 2, at : at + TILE, :] = jnp.exp(s - top).astype(BF16)
            tops.append(top)
        return jnp.concatenate(tops, 0)

    def mix(step):
        return jnp.dot(expo_ref[step % 2], v_heads[step % 2], preferred_element_type=F32)

    def finish(c, got, tops):
        rows = slice(c * chunk, (c + 1) * chunk)
        total = jnp.where(low, got[1], got[0])
        mixed = jnp.where(low, got[0], got[1]) / pltpu.roll(total, HD, 1)
        log = jnp.log(total)
        stat = stat_ref[rows, :]
        stat = jnp.where(lane == 2 * pair, tops[0] + log[:, HD : HD + 1], stat)
        stat_ref[rows, :] = jnp.where(lane == 2 * pair + 1, tops[1] + log[:, :1], stat)
        part, at = divmod(c * chunk, half)
        out_refs[part][0, at : at + chunk, :] = mixed.astype(BF16)

    steps = 2 * length // chunk
    tops, got = [], []
    score(0)
    for step in range(steps):
        if step + 1 < steps:
            score(step + 1)
        tops.append(soften(step))
        got.append(mix(step))
        if step % 2:
            finish(step // 2, got[-2:], tops[-2:])

    @pl.when(pair == pl.num_programs(1) - 1)
    def _():
        lse_ref[0] = jnp.transpose(stat_ref[...])[: lse_ref.shape[1]]


def attend_back_kernel(first_pair, after, *refs):
    seg_row_ref, seg_col_ref, qkv_ref, out_a, out_b, grad_a, grad_b, lse_ref = refs[:8]
    dqkv_ref, sums_ref, bias_ref, ds_ref, score_ref, slope_ref, prob_ref = refs[8 + after :]
    pair = pl.program_id(1)
    length = bias_ref.shape[0]
    half = qkv_ref.shape[2]
    chunk = score_ref.shape[1]

    @pl.when(pair == 0)
    def _():
        bias_ref[...] = jnp.where(seg_col_ref[0] == seg_row_ref[0], 0.0, MASKED)

    @pl.when((pair == 0) & (pl.program_id(0) == 0))
    def _():
        sums_ref[...] = jnp.zeros_like(sums_ref)

    block = qkv_ref[:, 0].reshape(length, 3 * PAIR)
    q, k, v = (block[:, i * PAIR : (i + 1) * PAIR] for i in range(3))
    out = jnp.concatenate([out_a[0], out_b[0]], 0)
    grad = jnp.concatenate([grad_a[0], grad_b[0]], 0)
    low = lax.broadcasted_iota(jnp.int32, (length, PAIR), 1) < HD
    zero = jnp.zeros_like(q)
    heads = lambda array: [jnp.where(low, array, zero), jnp.where(low, zero, array)]
    q_heads, k_heads, g_heads = heads(q), heads(k), heads(grad)
    product = jnp.transpose(out.astype(F32) * grad.astype(F32))
    chunks = length // chunk
    deltas = [total_rows(product[h * HD : (h + 1) * HD]) for h in range(2)]
    stats = [lse_ref[0, pl.ds(2 * (first_pair + pair) + h, 1), :] for h in range(2)]

    def score(step):
        h, c = divmod(step, chunks)
        rows = slice(c * chunk, (c + 1) * chunk)
        score_ref[step % 2] = lax.dot_general(k[rows], q_heads[h], NT, preferred_element_type=F32)
        slope_ref[step % 2] = lax.dot_general(v[rows], g_heads[h], NT, preferred_element_type=F32)

    def bend(step):
        h, c = divmod(step, chunks)
        for at in range(0, chunk, TILE):
            rows = slice(c * chunk + at, c * chunk + at + TILE)
            part = slice(at, at + TILE)
            p = jnp.exp(score_ref[step % 2, part, :] + bias_ref[rows, :] - stats[h])
            prob_ref[step % 2, part, :] = p.astype(BF16)
            ds_ref[h, rows, :] = (p * (slope_ref[step % 2, part, :] - deltas[h])).astype(BF16)

    steps = 2 * chunks
    dk, dv = [None] * chunks, [None] * chunks
    dq = None
    score(0)
    for step in range(steps):
        h, c = divmod(step, chunks)
        if step + 1 < steps:
            score(step + 1)
        bend(step)
        rows = slice(c * chunk, (c + 1) * chunk)
        v_part = jnp.dot(prob_ref[step % 2], g_heads[h], preferred_element_type=F32)
        k_part = jnp.dot(ds_ref[h, rows, :], q_heads[h], preferred_element_type=F32)
        if h == 0:
            dk[c], dv[c] = k_part, v_part
        else:
            part, at = c * chunk // half, c * chunk % half
            dqkv_ref[part, 0, at : at + chunk, PAIR : 2 * PAIR] = (dk[c] + k_part).astype(BF16)
            dv[c] = (dv[c] + v_part).astype(BF16)
            dqkv_ref[part, 0, at : at + chunk, 2 * PAIR :] = dv[c]
        if c == chunks - 1:
            part = lax.dot_general(ds_ref[h], k_heads[h], TN, preferred_element_type=F32)
            dq = part if h == 0 else dq + part
    dq = (dq * HD**-0.5).astype(BF16)
    dqkv_ref[:, 0, :, :PAIR] = dq.reshape(-1, half, PAIR)
    sums = [total_rows(dq.astype(F32)), sum(total_rows(part.astype(F32)) for part in dv)]
    sums_ref[0:1, pl.ds(pl.multiple_of(pair * PAIR, PAIR), PAIR)] += sums[0]
    sums_ref[1:2, pl.ds(pl.multiple_of(pair * PAIR, PAIR), PAIR)] += sums[1]


def attention_call(kernel, seg, arrays, pairs, outs, scratch, name, first=0, after=()):
    micros = 26 if name == "attend" else 15
    parts, seqs, half, columns = arrays[0].shape
    length = parts * half

    def spec(array, first):
        shape = array.shape
        if len(shape) == 4:
            return pl.BlockSpec((parts, 1, half, 3 * PAIR), lambda s, p: (0, s, 0, first + p))
        if len(shape) == 3 and shape[1] == half:
            return pl.BlockSpec((1, half, PAIR), lambda s, p: (s, 0, first + p))
        if len(shape) == 3:
            return pl.BlockSpec((1,) + shape[1:], lambda s, p: (s, 0, 0))
        return pl.BlockSpec(shape, lambda s, p: (0, 0))

    operands = [seg[:, None, :], seg[:, :, None]] + arrays
    return pl.pallas_call(
        kernel,
        grid=(seqs, pairs),
        in_specs=[spec(a, first) for a in operands]
        + [pl.BlockSpec(memory_space=pl.ANY)] * len(after),
        out_specs=[spec(a, 0) for a in outs],
        out_shape=outs,
        scratch_shapes=scratch(length),
        compiler_params=pltpu.CompilerParams(vmem_limit_bytes=SMALL_VMEM),
        cost_estimate=weight_of(micros),
        name=name,
    )(*operands, *after)


def attend(qkv, seg):
    parts, seqs, half, columns = qkv.shape
    pairs = columns // (3 * PAIR)
    outs = [
        jax.ShapeDtypeStruct((seqs, half, columns // 3), BF16),
        jax.ShapeDtypeStruct((seqs, half, columns // 3), BF16),
        jax.ShapeDtypeStruct((seqs, 2 * pairs, parts * half), F32),
    ]
    scratch = lambda length: [
        pltpu.VMEM((length, length), F32),
        pltpu.VMEM((length, PAIR), F32),
        pltpu.VMEM((2, 128, length), F32),
        pltpu.VMEM((2, 128, length), BF16),
    ]
    return attention_call(attend_kernel, seg, [qkv], pairs, outs, scratch, "attend")


def attend_back(qkv, seg, out, grad, lse, first, pairs, after):
    outs = [
        jax.ShapeDtypeStruct(qkv.shape[:3] + (3 * PAIR * pairs,), BF16),
        jax.ShapeDtypeStruct((8, PAIR * pairs), F32),
    ]
    scratch = lambda length: [
        pltpu.VMEM((length, length), F32),
        pltpu.VMEM((2, length, length), BF16),
        pltpu.VMEM((2, 128, length), F32),
        pltpu.VMEM((2, 128, length), F32),
        pltpu.VMEM((2, 128, length), BF16),
    ]
    kernel = functools.partial(attend_back_kernel, first, len(after))
    arrays = [qkv, *out, *grad, lse]
    return attention_call(kernel, seg, arrays, pairs, outs, scratch, "attend_back", first, after)


def body(
    layer_input,
    segment_ids,
    out_cotangent,
    attn_master,
    inner_master,
    outer_master,
    vector_master,
    attn_moment,
    inner_moment,
    outer_moment,
    vector_moment,
    attn_square,
    inner_square,
    outer_square,
    vector_square,
):
    seqs, half, width = layer_input.shape
    count = seqs * half
    hidden_units = inner_master.shape[1]
    pairs = width // (2 * PAIR)
    part_cols = width // 2
    shards = lax.axis_size("shard")
    owned_rows = attn_master.shape[1]
    core = lax.axis_index("ctx")
    first = core == 0

    def own_half(array, axis):
        size = array.shape[axis] // 2
        return lax.dynamic_slice_in_dim(array, core * size, size, axis)

    def other_half(array, axis):
        size = array.shape[axis] // 2
        return lax.dynamic_slice_in_dim(array, (1 - core) * size, size, axis)

    def in_order(mine, theirs, axis):
        return jnp.concatenate(
            [jnp.where(first, mine, theirs), jnp.where(first, theirs, mine)], axis
        )

    rows = layer_input.reshape(count, width)
    rows_chip = jnp.concatenate([rows, swap_cores(rows)], 0)
    square = is_square()

    piece = own_half(attn_master[:3], 2).astype(BF16).reshape(3, owned_rows, pairs, PAIR)
    piece = piece.transpose(1, 2, 0, 3).reshape(owned_rows, 3 * part_cols)
    vec_low = vector_master.astype(BF16)
    rider = vec_low[:2].reshape(1, -1)
    if square:
        piece = lax.dynamic_slice_in_dim(
            piece, lax.axis_index("replica") * (piece.shape[1] // 2), piece.shape[1] // 2, 1
        )
    rider = jnp.pad(rider, ((0, 15), (0, piece.shape[1] - rider.shape[1])))
    piece = jnp.concatenate([piece, rider], 0)
    if square:
        stacks, places = gather_quarters(piece)
    else:
        stacks = [item[None] for item in ring_gather(piece)]
        places = [(owner, 0) for owner in slot_owners()]
    riders = jnp.concatenate([stack[:, owned_rows] for stack in stacks], 0)[:shards]
    riders = riders[:, : 2 * width // shards].reshape(shards, 2, -1).astype(F32)
    slot_of = jnp.stack([place[0] for place in places[:shards]])
    chosen = (jnp.arange(shards)[:, None] == slot_of[None, :]).astype(F32)
    biases = jnp.einsum("ps,srw->rpw", chosen, riders).reshape(2, width)

    copies = lax.axis_size("replica") * 2
    copy_at = lax.axis_index("replica") * 2 + core
    quarter = lambda block: lax.dynamic_slice_in_dim(
        block, copy_at * (block.shape[0] // copies), block.shape[0] // copies, 0
    ).astype(BF16)
    out_q, inner_q, outer_q = quarter(attn_master[3]), quarter(inner_master), quarter(outer_master)
    wide = hidden_units // width
    small = out_q.shape[0]
    inner_q = inner_q.reshape(small, wide, width).transpose(1, 0, 2).reshape(-1, width)
    big = outer_q.shape[0]
    vec_q = vec_low.reshape(-1)
    vec_q = jnp.pad(vec_q, (0, 16 * width - vec_q.shape[0])).reshape(16, width)
    packed = lax.all_gather(jnp.concatenate([outer_q, inner_q, out_q, vec_q], 0), EVERY, axis=0)
    vec = packed[::copies, 2 * big + small :].reshape(shards, -1)[:, : vec_low.size]
    vec = vec.reshape((shards,) + vec_low.shape).transpose(1, 0, 2).reshape(-1, width).astype(F32)
    if packed.shape[0] != PARTS:
        outer_w = packed[:, :big].reshape(PARTS, -1, width)
        inner_w = packed[:, big : 2 * big].reshape(-1, wide, small, width).transpose(0, 2, 1, 3)
        inner_w = inner_w.reshape(PARTS, -1, wide, width).transpose(0, 2, 1, 3)
        out_w = packed[:, 2 * big : 2 * big + small].reshape(PARTS, -1, width)
        packed = jnp.concatenate([outer_w, inner_w.reshape(PARTS, -1, width), out_w], 1)

    halves = own_half(biases, 1).reshape(2, pairs, PAIR)
    bias = jnp.stack([halves[0], jnp.zeros_like(halves[0]), halves[1]], 1).reshape(1, -1)
    ones = jnp.ones((pairs, PAIR), F32)
    factor = jnp.stack([ones * HD**-0.5, ones, ones], 1).reshape(1, -1)
    qkv, qkv_w = project(rows_chip, stacks, places, bias, factor)
    qkv = qkv.reshape(2, seqs, half, 3 * part_cols)
    seg = jnp.concatenate([own_half(segment_ids, 1), other_half(segment_ids, 1)], 1)
    mixed_mine, mixed_sent, lse = attend(qkv, seg)
    flat = lambda array: array.reshape(count, part_cols)
    deep = lambda array: array.reshape(seqs, half, part_cols)
    heads_mine, heads_theirs = flat(mixed_mine), swap_cores(flat(mixed_sent))

    cotan = out_cotangent.reshape(count, width)
    core_at = jnp.full((1,), core, jnp.int32)
    active, slope, hidden_low, normed, scale, result, ffn_grad, sums_two = ffn(
        core_at, heads_mine, heads_theirs, rows, cotan, vec, packed
    )

    o, i, y, inner = position()
    where = jnp.stack([o, i, y, core]).astype(jnp.int32)
    by_shard = lambda array: array.reshape(shards, -1, array.shape[1])

    outer_sent = product(where, [active], ffn_grad, 0)
    outer_kept = product(where, [active], ffn_grad, 1, (outer_sent,))
    outer_chips = [by_shard(outer_kept), by_shard(swap_cores(outer_sent))]
    done = (outer_kept,)
    if square:
        outer = Sum(where, outer_chips)
        done = outer.merge()
    pre_grad, branch_grad, mine, sent, sums_one = ffn_back(
        core_at, ffn_grad, slope, normed, scale, vec, packed, done[:1]
    )
    got = swap_cores(sent)
    mixed_grad = [deep(mine), deep(got)]
    done = outer.plane((pre_grad,)) if square else ()
    inner_sent = product(where, [hidden_low], pre_grad, 0, done)
    heads = [heads_mine, heads_theirs]
    done = outer.cross((inner_sent,)) if square else (inner_sent,)
    out_sent = product(where, heads, branch_grad, 0, done + (got,))
    inner_kept = product(where, [hidden_low], pre_grad, 1, (out_sent,))
    out_kept = product(where, heads, branch_grad, 1, (inner_kept,))
    inner_chips = [by_shard(inner_kept), by_shard(swap_cores(inner_sent))]
    out_chips = [by_shard(out_kept), by_shard(swap_cores(out_sent))]

    def back(first, after):
        grad, sums = attend_back(
            qkv, seg, (mixed_mine, mixed_sent), mixed_grad, lse, first, pairs // 2, after
        )
        return grad.reshape(2 * count, -1), sums

    def vector_chip(sums_a, sums_b):
        blank = jnp.zeros((part_cols,), F32)
        ours = jnp.concatenate([sums_a, sums_b], 1)
        attn_biases = jnp.stack([in_order(ours[at], blank, 0) for at in range(2)])
        sums = [attn_biases, sums_one[2:3], sums_one[:2], sums_two[2:3], sums_two[:2]]
        sums = jnp.concatenate(sums + [sums_one[4:8]], 0)
        sums = sums.reshape(-1, shards, width // shards).transpose(1, 0, 2)
        sums = jnp.pad(sums, ((0, 0), (0, owned_rows - sums.shape[1]), (0, 0)))
        return sums.astype(BF16)

    outer_states = (outer_master, outer_moment, outer_square)
    inner_states = (inner_master, inner_moment, inner_square)
    attn_states = (attn_master, attn_moment, attn_square)
    if square:
        inner = Sum(where, inner_chips)
        done = inner.merge((out_kept, out_chips[1]))
        grad_a, sums_a = back(0, done)
        done = outer.turn((grad_a,))
        done = inner.plane(done)
        ours = by_shard(product(where, [rows_chip], grad_a, None, done))
        sum_a = Sum(where, [ours], out_chips)
        done = sum_a.merge()
        grad_b, sums_b = back(pairs // 2, done)
        done = inner.cross((grad_b,))
        done = sum_a.plane(done)
        ours = by_shard(product(where, [rows_chip], grad_b, None, done))
        sum_b = Sum(where, [ours], [vector_chip(sums_a, sums_b)])
        done = outer.line((ours,))
        done = sum_a.cross(done)
        done = sum_b.merge(done)
        outer_new = update(where, outer_states, [outer.shares], done)
        done = inner.turn((outer_new[0],))
        theirs_part = input_back(grad_a, grad_b, qkv_w, (), done)
        done = sum_b.plane((theirs_part,))
        done = sum_a.turn(done)
        input_grad = input_back(
            grad_a, grad_b, qkv_w, (branch_grad, swap_cores(theirs_part)), done
        )
        done = sum_b.cross((input_grad,))
        done = inner.line(done)
        done = sum_a.line(done)
        done = sum_b.turn(done)
        inner_new = update(where, inner_states, [inner.shares], done)
        sum_b.line((inner_new[0],))
        attn_shares = [sum_a.shares, sum_b.shares]
        vector_shares = [
            jnp.concatenate(
                [
                    jnp.where(y == 0, sum_b.shares[at], sum_b.shares[at + 1])[0],
                    jnp.where(y == 0, sum_b.shares[at + 1], sum_b.shares[at])[0],
                ],
                0,
            )
            for at in (0, 2)
        ]
    else:
        grad_a, sums_a = back(0, ())
        grad_b, sums_b = back(pairs // 2, ())
        theirs_part = input_back(grad_a, grad_b, qkv_w, (), ())
        added = (branch_grad, swap_cores(theirs_part))
        input_grad = input_back(grad_a, grad_b, qkv_w, added, ())
        outer_new = update(where, outer_states, [sum_apart(add_low(*outer_chips))])
        inner_new = update(where, inner_states, [sum_apart(add_low(*inner_chips))])
        ours = [by_shard(product(where, [rows_chip], grad, None)) for grad in (grad_a, grad_b)]
        chip_a = jnp.concatenate([ours[0], add_low(*out_chips)], 2)
        chip_b = jnp.concatenate([ours[1], vector_chip(sums_a, sums_b)], 2)
        attn_shares = [sum_apart(chip_a), sum_apart(chip_b)]
        vector_shares = [share[0] for share in attn_shares[1]]
    attn_new = update(where, attn_states, attn_shares)
    cut = grad_b.shape[1]
    vector_sum = sum(share[: vec_low.shape[0], cut:].astype(F32) for share in vector_shares)
    vector_new = adamw(vector_sum, vector_moment, vector_square, vector_master, RATE_VECTOR)
    vector_new = vector_new + (vector_new[2].astype(BF16),)
    news = (attn_new, inner_new, outer_new, vector_new)
    updates = [[new[at] for new in news] for at in range(4)]
    return (
        result.reshape(seqs, half, width).astype(BF16),
        input_grad.reshape(seqs, half, width),
        *[item for kind in updates for item in kind],
    )


def solution(mesh):
    tokens = P(("replica", "shard"), "ctx", None)
    states = (P(None, "shard", None), P("shard", None), P("shard", None), P(None, "shard"))
    in_specs = (tokens, P(("replica", "shard"), None), tokens) + states * 3
    out_specs = (tokens, tokens) + states * 4
    return jax.shard_map(body, mesh=mesh, in_specs=in_specs, out_specs=out_specs, check_vma=False)
```

```python
import functools
import math

import jax
import jax.numpy as jnp
from jax import lax
from jax.experimental import pallas as pl
from jax.experimental.pallas import tpu as pltpu
from jax.sharding import PartitionSpec as P

HD = 64
PAIR = 2 * HD
STEP = 5
OUTER = 4
EVERY = ("shard", "replica", "ctx")

EPS_NORM = 1e-05
BETA_ONE = 0.5
BETA_TWO = 0.6
RATE_MATRIX = 0.02
RATE_VECTOR = 0.1
DECAY = 0.01
EPS_ADAM = 1e-06
MASKED = -1e30
F32 = jnp.float32
BF16 = jnp.bfloat16
PARTS = 32
TILE = 32
VMEM = 56 * 1024 * 1024
SMALL_VMEM = 16 * 1024 * 1024
GROUP = 256
NT = (((1,), (1,)), ((), ()))
TN = (((0,), (0,)), ((), ()))


def weight_of(micros):
    return pl.CostEstimate(
        flops=int(micros * 2.9e8), bytes_accessed=int(micros * 9.2e5), transcendentals=0
    )


def pinned(arrays):
    return [pltpu.with_memory_space_constraint(a, pltpu.HBM) for a in arrays]


def results(shapes):
    return [pltpu.HBM(s.shape, s.dtype) for s in shapes]


def normalize(resid):
    centre = resid - jnp.mean(resid, -1, keepdims=True)
    scale = lax.rsqrt(jnp.mean(centre * centre, -1, keepdims=True) + EPS_NORM)
    return (centre * scale, scale)


def norm_back(grad, normed, scale):
    return scale * (
        grad
        - jnp.mean(grad, -1, keepdims=True)
        - normed * jnp.mean(grad * normed, -1, keepdims=True)
    )


def adamw(grad, moment, square, weight, rate):
    moment_new = BETA_ONE * moment + (1.0 - BETA_ONE) * grad
    square_new = BETA_TWO * square + (1.0 - BETA_TWO) * grad * grad
    stepped = (
        moment_new
        / (1.0 - BETA_ONE**STEP)
        / (jnp.sqrt(square_new / (1.0 - BETA_TWO**STEP)) + EPS_ADAM)
    )
    weight_new = weight - rate * (stepped + DECAY * weight)
    return (moment_new, square_new, weight_new)


def swap_cores(value):
    return lax.ppermute(value, "ctx", [(0, 1), (1, 0)])


def shift_outer(value, step):
    inner = lax.axis_size("shard") // OUTER
    pairs = [
        (o * inner + i, ((o + step) % OUTER) * inner + i) for o in range(OUTER) for i in range(inner)
    ]
    return lax.ppermute(value, "shard", pairs)


def shift_inner(value, step):
    inner = lax.axis_size("shard") // OUTER
    pairs = [
        (o * inner + i, o * inner + (i + step) % inner) for o in range(OUTER) for i in range(inner)
    ]
    return lax.ppermute(value, "shard", pairs)


def shift_replica(value, step):
    size = lax.axis_size("replica")
    return lax.ppermute(value, "replica", [(r, (r + step) % size) for r in range(size)])


def ring_gather(piece):
    inner = lax.axis_size("shard") // OUTER
    found = []
    held = piece
    for k in range(OUTER):
        if k:
            held = shift_outer(held, -1)
        found.append([held] + [shift_inner(held, -e) for e in range(1, inner)])
    return [item for group in found for item in group]


def slot_owners():
    inner = lax.axis_size("shard") // OUTER
    at = lax.axis_index("shard")
    o, i = at // inner, at % inner
    return [
        lax.rem(o + k, OUTER) * inner + lax.rem(i + e, inner)
        for k in range(OUTER)
        for e in range(inner)
    ]


def pick(array, index, axis):
    return lax.dynamic_index_in_dim(array, index, axis, keepdims=False)


def add_low(value, *others):
    total = value.astype(F32)
    for item in others:
        total = total + item.astype(F32)
    return total.astype(BF16)


def position():
    inner = lax.axis_size("shard") // OUTER
    at = lax.axis_index("shard")
    return at // inner, at % inner, lax.axis_index("replica"), inner


def is_square():
    return lax.axis_size("replica") == 2 and lax.axis_size("shard") == 2 * OUTER


def swap_outer(value, flip):
    inner = lax.axis_size("shard") // OUTER
    pairs = [(o * inner + i, (o ^ flip) * inner + i) for o in range(OUTER) for i in range(inner)]
    return lax.ppermute(value, "shard", pairs)


def swap_cross(value):
    return lax.ppermute(value, ("replica", "ctx"), [(a, 3 - a) for a in range(4)])


def sum_apart(chip_sum):
    o, i, y, inner = position()
    grid = chip_sum.reshape(OUTER, inner, *chip_sum.shape[1:])
    got = [shift_inner(pick(grid, lax.rem(i + e, inner), 1), e) for e in range(1, inner)]
    line = add_low(pick(grid, i, 1), *got)
    got = [shift_outer(pick(line, lax.rem(o + d, OUTER), 0), d) for d in range(1, OUTER)]
    total = add_low(pick(line, o, 0), *got)
    got = [shift_replica(total, r) for r in range(1, lax.axis_size("replica"))]
    mine = add_low(total, *got)[None]
    return [mine, swap_cores(mine)]


def small_call(kernel, where, ins, outs, after, name):
    held = pl.BlockSpec(memory_space=pltpu.VMEM)
    return pl.pallas_call(
        functools.partial(kernel, len(ins), len(after)),
        in_specs=[pl.BlockSpec(memory_space=pltpu.SMEM)]
        + [held] * len(ins)
        + [pl.BlockSpec(memory_space=pl.ANY)] * len(after),
        out_specs=[held] * len(outs),
        out_shape=[pltpu.VMEM(shape, BF16) for shape in outs],
        compiler_params=pltpu.CompilerParams(vmem_limit_bytes=SMALL_VMEM),
        cost_estimate=weight_of(1),
        name=name,
    )(where, *[pltpu.with_memory_space_constraint(a, pltpu.VMEM) for a in ins], *after)


def fold_plane_kernel(count, after, where_ref, keep_p, got_p, keep_q, got_q, *rest):
    i, y = where_ref[1], where_ref[2]
    kept_p, send_p, kept_q, send_q = rest[after:]
    for o in range(OUTER):
        for out, at in ((kept_p, y), (send_p, 1 - y)):
            out[o] = add_low(keep_p[o, at], got_p[o, at])
        for out, at in ((kept_q, i), (send_q, 1 - i)):
            out[o] = add_low(keep_q[o, at], got_q[o, at])


def line_order(o):
    near = o + 1 - 2 * lax.rem(o, 2)
    far = lambda at: lax.rem(at + 2, OUTER)
    return (o, far(o)), (near, far(near))


def fold_cross_kernel(count, after, where_ref, keep_p, got_p, keep_q, got_q, *rest):
    for out, order in zip(rest[after:], line_order(where_ref[0])):
        for n, at in enumerate(order):
            out[n, 0] = add_low(keep_p[at], got_p[at])
            out[n, 1] = add_low(keep_q[at], got_q[at])


def fold_turn_kernel(count, after, where_ref, keep, got, *rest):
    for n, out in enumerate(rest[after:]):
        out[...] = add_low(keep[n], got[n])


def fold_line_kernel(count, after, where_ref, *rest):
    rest[count + after][...] = add_low(*(ref[...] for ref in rest[:count]))


def merge_kernel(groups, after, where_ref, *refs):
    outs = refs[4 * sum(groups) + after :]
    for slot, out in enumerate(outs):
        left = chip = 0
        for group in groups:
            for at in range(2):
                parts = []
                for n in range(chip, chip + group):
                    ref = refs[4 * n + slot]
                    parts.append(ref[0, at, 0, 0] if slot % 2 else ref[0, 0, 0, at])
                cut = slice(left, left + parts[0].shape[1])
                out[0, at, :, cut] = parts[0] if group == 1 else add_low(*parts)
            left, chip = cut.stop, chip + group


class Sum:
    def __init__(self, where, *groups):
        self.where, self.rows = where, groups[0][0].shape[1] // 4
        self.columns = sum(group[0].shape[2] for group in groups)
        self.groups = [len(group) for group in groups]
        self.chips = [
            c.reshape(OUTER, 2, 2, 2, self.rows, c.shape[2]) for group in groups for c in group
        ]

    def shape(self, *lead):
        return lead + (self.rows, self.columns)

    def merge(self, after=()):
        def spec(chip, lead, flip):
            def place(o, w):
                at = w[1] if lead == 0 else w[2]
                at = 1 - at if flip else at
                return (o, at, 0, 0, 0, 0) if lead == 0 else (o, 0, 1, at, 0, 0)

            return pl.BlockSpec(((1, 1, 1, 2) if lead == 0 else (1, 2, 1, 1)) + chip.shape[4:], place)

        kinds = ((0, True), (1, True), (0, False), (1, False))
        out_spec = pl.BlockSpec((1, 2, self.rows, self.columns), lambda o, w: (o, 0, 0, 0))
        *sent, keep_p, keep_q = pl.pallas_call(
            functools.partial(merge_kernel, self.groups, len(after)),
            grid_spec=pltpu.PrefetchScalarGridSpec(
                num_scalar_prefetch=1,
                grid=(OUTER,),
                in_specs=[spec(chip, *kind) for chip in self.chips for kind in kinds]
                + [pl.BlockSpec(memory_space=pl.ANY)] * len(after),
                out_specs=[out_spec] * 4,
            ),
            out_shape=[pltpu.HBM(self.shape(OUTER, 2), BF16)] * 4,
            compiler_params=pltpu.CompilerParams(vmem_limit_bytes=SMALL_VMEM),
            cost_estimate=weight_of(4),
            name="merge",
        )(self.where, *pinned(chip for chip in self.chips for _ in range(4)), *after)
        self.kept = [keep_p, shift_inner(sent[0], 1), keep_q, shift_replica(sent[1], 1)]
        return tuple(sent)

    def plane(self, after=()):
        keep_p, send_p, keep_q, send_q = small_call(
            fold_plane_kernel, self.where, self.kept, [self.shape(OUTER)] * 4, after, "fold_plane"
        )
        self.kept = [keep_p, shift_replica(send_p, 1), keep_q, shift_inner(send_q, 1)]
        return (send_p, send_q)

    def cross(self, after=()):
        keep, send = small_call(
            fold_cross_kernel, self.where, self.kept, [self.shape(2, 2)] * 2, after, "fold_cross"
        )
        self.kept = [keep, swap_outer(send, 1)]
        return (send,)

    def turn(self, after=()):
        shapes = [self.kept[0].shape[1:]] * 2
        keep, send = small_call(
            fold_turn_kernel, self.where, self.kept, shapes, after, "fold_turn"
        )
        self.kept = [keep, swap_outer(send, 2)]
        return (send,)

    def line(self, after=()):
        (total,) = small_call(
            fold_line_kernel, self.where, self.kept, [self.kept[0].shape], after, "fold_line"
        )
        self.shares = [total, shift_replica(total, 1), swap_cores(total), swap_cross(total)]
        return (total,)


def update_kernel(groups, after, where_ref, *refs):
    states, shares = refs[:3], refs[3 : 3 + sum(groups)]
    outs, grad_ref = refs[3 + sum(groups) + after : -1], refs[-1]
    rows = shares[0].shape[1]
    across = groups[0] // 2
    for core in range(2):

        @pl.when(pl.program_id(1) == core)
        def _():
            for n in range(across):
                line = where_ref[2] if n == 0 else 1 - where_ref[2]
                line = pl.ds(pl.multiple_of(line * rows, rows), rows) if across > 1 else slice(None)
                if len(groups) == 1:
                    grad_ref[line, :] = shares[across * core + n][0].astype(F32)
                    continue
                left, right = shares[across * core + n], shares[groups[0] + across * core + n]
                width = grad_ref.shape[2]
                pairs = width // PAIR
                for t in range(3):
                    for p in range(pairs):
                        side, at = (left, p) if 2 * p < pairs else (right, p - pairs // 2)
                        part = side[0, :, (3 * at + t) * PAIR : (3 * at + t + 1) * PAIR]
                        grad_ref[t, line, p * PAIR : (p + 1) * PAIR] = part.astype(F32)
                cut = 3 * PAIR * (pairs // 2)
                grad_ref[3, line, :] = left[0, :, cut : cut + width].astype(F32)

    new = adamw(grad_ref[...], states[1][...], states[2][...], states[0][...], RATE_MATRIX)
    for out, value in zip(outs, new + (new[2],)):
        out[...] = value.astype(out.dtype)


def update(where, states, groups, after=()):
    parts, rows = groups[0][0].shape[:2]
    rows = rows * (len(groups[0]) // 2)
    lead = states[0].shape[:-2]
    columns = states[0].shape[-1] // 2
    place = lambda p, v, w: (0,) * len(lead) + (p, w[3] + v - 2 * w[3] * v)
    block = pl.BlockSpec(lead + (rows, columns), place)
    shares = [share for group in groups for share in group]
    share_specs = [pl.BlockSpec((1,) + a.shape[1:], lambda p, v, w: (p, 0, 0)) for a in shares]
    kinds = (F32, F32, F32, BF16)
    return pl.pallas_call(
        functools.partial(update_kernel, [len(group) for group in groups], len(after)),
        grid_spec=pltpu.PrefetchScalarGridSpec(
            num_scalar_prefetch=1,
            grid=(parts, 2),
            in_specs=[block] * 3 + share_specs + [pl.BlockSpec(memory_space=pl.ANY)] * len(after),
            out_specs=[block] * 4,
            scratch_shapes=[pltpu.VMEM(lead + (rows, columns), F32)],
        ),
        out_shape=[pltpu.HBM(states[0].shape, kind) for kind in kinds],
        compiler_params=pltpu.CompilerParams(vmem_limit_bytes=SMALL_VMEM),
        cost_estimate=weight_of(5),
        name="update",
    )(where, *pinned(states), *pinned(shares), *after)


def input_back_kernel(a_ref, b_ref, left_ref, right_ref, *rest):
    out_ref = rest[-1]
    total = lax.dot_general(a_ref[...], left_ref[...], NT, preferred_element_type=F32)
    total += lax.dot_general(b_ref[...], right_ref[...], NT, preferred_element_type=F32)
    if out_ref.dtype == F32:
        total += rest[0][...].astype(F32) + rest[1][...].astype(F32)
    out_ref[...] = total.astype(out_ref.dtype)


def input_back(grad_a, grad_b, weight, added, after):
    count, cut = grad_a.shape[0] // 2, grad_a.shape[1]
    width = weight.shape[0]
    tile = width // 4
    first = 0 if added else 1
    side = pl.BlockSpec((count, cut), lambda n: (first, 0))
    line = pl.BlockSpec((count, tile), lambda n: (0, n))
    return pl.pallas_call(
        input_back_kernel,
        grid=(width // tile,),
        in_specs=[side, side]
        + [pl.BlockSpec((tile, cut), lambda n, at=at: (n, at)) for at in range(2)]
        + [line] * len(added)
        + [pl.BlockSpec(memory_space=pl.ANY)] * len(after),
        out_specs=line,
        out_shape=pltpu.HBM((count, width), F32 if added else BF16),
        compiler_params=pltpu.CompilerParams(vmem_limit_bytes=SMALL_VMEM),
        cost_estimate=weight_of(5),
        name="input_back",
    )(*pinned([grad_a, grad_b, weight, weight, *added]), *after)


def quarter_places(order):
    o, i, y, inner = position()
    kinds = ((i, y), (1 - i, y), (i, 1 - y), (1 - i, 1 - y))
    return [(row * 2 + across, side) for across, side in kinds for row in order]


def relay_kernel(count, after, where_ref, *rest):
    for source, out in zip(rest[:count], rest[count + after :]):
        out[...] = source[...]


def halves_kernel(count, after, where_ref, near_x, near_y, *rest):
    first, second = rest[after:]
    first[...] = near_y[: OUTER // 2]
    second[...] = near_x[OUTER // 2 :]


def pair_kernel(count, after, where_ref, own, other, *rest):
    rest[after][0] = own[...]
    rest[after][1] = other[...]


def relay(where, arrays, after):
    return small_call(relay_kernel, where, arrays, [a.shape for a in arrays], after, "relay")


def project_kernel(after, row_ref, column_ref, mine_ref, theirs_ref, bias_ref, factor_ref, *rest):
    stacks, (out_ref, weight_ref) = rest[: -2 - after], rest[-2:]
    columns = stacks[0].shape[2]
    part = weight_ref.shape[0] * weight_ref.shape[1] // columns
    part = part // sum(stack.shape[0] for stack in stacks)
    at = pl.program_id(0)

    @pl.when(at == 0)
    def _():
        slot = 0
        for stack in stacks:
            for k in range(stack.shape[0]):
                start = pl.multiple_of(row_ref[slot] * part, part)
                left = pl.multiple_of(column_ref[slot] * columns, PAIR)
                weight_ref[pl.ds(start, part), pl.ds(left, columns)] = stack[k, :part, :]
                slot += 1

    def fill(rows):
        acc = jnp.dot(rows, weight_ref[...], preferred_element_type=F32)
        out_ref[...] = ((acc + bias_ref[...]) * factor_ref[...]).astype(BF16)

    @pl.when(at < pl.num_programs(0) // 2)
    def _():
        fill(mine_ref[...])

    @pl.when(at >= pl.num_programs(0) // 2)
    def _():
        fill(theirs_ref[...])


def project(mine, theirs, stacks, places, bias, factor, after):
    count, width = mine.shape
    columns = bias.shape[1]
    tile = 512
    each = count // tile
    whole = lambda shape: pl.BlockSpec(shape, lambda m, *_: (0,) * len(shape))
    tables = [jnp.stack([p[axis] for p in places]).astype(jnp.int32) for axis in range(2)]
    return pl.pallas_call(
        functools.partial(project_kernel, len(after)),
        grid_spec=pltpu.PrefetchScalarGridSpec(
            num_scalar_prefetch=2,
            grid=(2 * each,),
            in_specs=[
                pl.BlockSpec((tile, width), lambda m, *_: (jnp.minimum(m, each - 1), 0)),
                pl.BlockSpec((tile, width), lambda m, *_: (jnp.maximum(m - each, 0), 0)),
                whole((1, columns)),
                whole((1, columns)),
            ]
            + [whole(stack.shape) for stack in stacks]
            + [pl.BlockSpec(memory_space=pl.ANY)] * len(after),
            out_specs=[
                pl.BlockSpec((tile, columns), lambda m, *_: (m, 0)),
                whole((width, columns)),
            ],
        ),
        out_shape=[pltpu.HBM((2 * count, columns), BF16), pltpu.HBM((width, columns), BF16)],
        compiler_params=pltpu.CompilerParams(vmem_limit_bytes=44 * 1024 * 1024),
        cost_estimate=weight_of(11),
        name="project",
    )(*tables, *pinned([mine, theirs, bias, factor, *stacks]), *after)


def gelu_and_slope(u):
    a = jnp.abs(u)
    d = 1.0 + (0.3275911 * 0.5**0.5) * a
    t = pl.reciprocal(d, approx=True)
    t = t * (2.0 - d * t)
    e = jnp.exp2(u * u * (-0.5 * math.log2(math.e)))
    series = (0.5 * 1.061405429) * t - 0.5 * 1.453152027
    series = series * t + 0.5 * 1.421413741
    series = series * t - 0.5 * 0.284496736
    series = series * t + 0.5 * 0.254829592
    tail = series * t * e
    active = jnp.maximum(u, 0.0) - a * tail
    below = tail - a * (e * (1.0 / math.sqrt(2.0 * math.pi)))
    return active, jnp.where(u >= 0.0, 1.0 - below, below)


def total_rows(value):
    return jnp.sum(value, axis=0, keepdims=True)


def in_parts(count, work):
    def turn(at, carry):
        work(pl.ds(pl.multiple_of(at * 128, 128), 128))
        return carry

    lax.fori_loop(0, count // 128, turn, 0)


def ffn_kernel(
    count_of,
    core_ref,
    row_ref,
    part_ref,
    mine_ref,
    theirs_ref,
    rows_ref,
    cotan_ref,
    vec_ref,
    outer_w_ref,
    *more,
):
    stacks, more = more[:count_of], more[count_of:]
    active_ref, slope_ref, inner_out_ref, hidden_ref, normed_ref, scale_ref = more[:6]
    result_ref, grad_ref, out_w_ref, sums_ref, resid, acc, pre, inner_w, sems = more[6:]
    w, last = pl.program_id(0), pl.num_programs(0) - 1
    count, width = acc.shape
    chunk = pre.shape[2]
    vec = lambda at: vec_ref[at : at + 1, :]
    half_of = lambda at: out_w_ref[pl.ds(pl.multiple_of(at * (width // 2), width // 2), width // 2), :]
    slots = [(stack, k) for stack in stacks for k in range(stack.shape[0])]
    deep = 4 * width // len(slots)
    thin = width // len(slots)

    def fetch(block):
        for slot, (stack, k) in enumerate(slots):

            @pl.when(part_ref[slot] == block)
            def _():
                start = pl.multiple_of(row_ref[slot] * deep, deep)
                pltpu.make_async_copy(
                    stack.at[k, pl.ds(0, deep), :],
                    inner_w.at[lax.rem(block, 2), pl.ds(start, deep), :],
                    sems.at[lax.rem(block, 2)],
                ).start()

    def arrived(block):
        target = inner_w.at[lax.rem(block, 2)]
        pltpu.make_async_copy(target, target, sems.at[lax.rem(block, 2)]).wait()

    @pl.when(w == 0)
    def _():
        for slot, (stack, k) in enumerate(slots):
            start = pl.multiple_of(row_ref[slot] * 4 * thin + part_ref[slot] * thin, thin)
            pltpu.make_async_copy(
                stack.at[k, pl.ds(deep, thin), :], out_w_ref.at[pl.ds(start, thin), :], sems.at[2]
            ).start()
        fetch(w)
        pltpu.make_async_copy(out_w_ref, out_w_ref, sems.at[2]).wait()
        acc[...] = jnp.dot(mine_ref[...], half_of(core_ref[0]), preferred_element_type=F32)
        acc[...] += jnp.dot(theirs_ref[...], half_of(1 - core_ref[0]), preferred_element_type=F32)

        def enter(part):
            normed, scale = normalize(acc[part, :] + vec(2) + rows_ref[part, :].astype(F32))
            normed_ref[part, :] = normed.astype(BF16)
            scale_ref[part, :] = scale
            hidden = normed * vec(3) + vec(4)
            resid[part, :] = hidden + vec(5)
            hidden_ref[part, :] = hidden.astype(BF16)

        in_parts(count, enter)

    arrived(w)

    @pl.when(w < last)
    def _():
        fetch(w + 1)

    now = lax.rem(w, 2)
    inner_out_ref[...] = inner_w[now]
    bias = vec_ref[pl.ds(8 + w, 1), :]

    def expand(n):
        cut = slice(n * chunk, (n + 1) * chunk)
        weight = inner_w[now, :, cut]
        pre[n % 2] = jnp.dot(hidden_ref[...], weight, preferred_element_type=F32)

    def bend(n):
        cut = slice(n * chunk, (n + 1) * chunk)
        for at in range(0, count, TILE):
            part = slice(at, at + TILE)
            active, slope = gelu_and_slope(pre[n % 2, part, :] + bias[:, cut])
            active_ref[part, cut] = active.astype(BF16)
            slope_ref[part, cut] = slope.astype(BF16)

    chunks = width // chunk
    expand(0)
    for n in range(1, chunks):
        expand(n)
        bend(n - 1)
    bend(chunks - 1)

    def contract():
        weight = outer_w_ref[...]
        return jnp.dot(active_ref[...], weight, preferred_element_type=F32)

    @pl.when(w == 0)
    def _():
        acc[...] = contract()

    @pl.when(w > 0)
    def _():
        acc[...] += contract()

    @pl.when(w == last)
    def _():
        sums_ref[...] = jnp.zeros_like(sums_ref)

        def leave(part):
            normed, scale = normalize(resid[part, :] + acc[part, :])
            result_ref[part, :] = (normed * vec(6) + vec(7)).astype(BF16)
            cotan = cotan_ref[part, :].astype(F32)
            grad = norm_back(cotan * vec(6), normed, scale).astype(BF16)
            grad_ref[part, :] = grad
            sums_ref[0:1, :] += total_rows(cotan * normed)
            sums_ref[1:2, :] += total_rows(cotan)
            sums_ref[2:3, :] += total_rows(grad.astype(F32))

        in_parts(count, leave)


def ffn_back_kernel(
    core_ref,
    grad_ref,
    slope_ref,
    normed_ref,
    scale_ref,
    vec_ref,
    out_w_ref,
    inner_w_ref,
    outer_w_ref,
    after_ref,
    pre_grad_ref,
    branch_ref,
    mine_ref,
    theirs_ref,
    sums_ref,
    acc,
    pre,
):
    w = pl.program_id(0)
    count, width = acc.shape
    chunk = pre.shape[2]
    vec = lambda at: vec_ref[at : at + 1, :]

    @pl.when(w == 0)
    def _():
        sums_ref[...] = jnp.zeros_like(sums_ref)

    def pull(n):
        weight = outer_w_ref[n * chunk : (n + 1) * chunk, :]
        pre[n % 2] = lax.dot_general(grad_ref[...], weight, NT, preferred_element_type=F32)

    def bend(n):
        cut = slice(n * chunk, (n + 1) * chunk)
        sums = jnp.zeros((8, chunk), F32)
        for at in range(0, count, TILE):
            part = slice(at, at + TILE)
            back = pre[n % 2, part, :].astype(BF16).astype(F32) * slope_ref[part, cut].astype(F32)
            back = back.astype(BF16)
            pre_grad_ref[part, cut] = back
            sums += jnp.sum(back.astype(F32).reshape(TILE // 8, 8, chunk), axis=0)
        sums_ref[pl.ds(4 + w, 1), cut] += total_rows(sums)

    chunks = width // chunk
    pull(0)
    for n in range(1, chunks):
        pull(n)
        bend(n - 1)
    bend(chunks - 1)

    def contract():
        weight = inner_w_ref[...]
        return lax.dot_general(pre_grad_ref[...], weight, NT, preferred_element_type=F32)

    @pl.when(w == 0)
    def _():
        acc[...] = contract()

    @pl.when(w > 0)
    def _():
        acc[...] += contract()

    @pl.when(w == pl.num_programs(0) - 1)
    def _():
        def leave(part):
            through = acc[part, :].astype(BF16).astype(F32) + grad_ref[part, :].astype(F32)
            normed = normed_ref[part, :].astype(F32)
            branch = norm_back(through * vec(3), normed, scale_ref[part, :]).astype(BF16)
            branch_ref[part, :] = branch
            sums_ref[0:1, :] += total_rows(through * normed)
            sums_ref[1:2, :] += total_rows(through)
            sums_ref[2:3, :] += total_rows(branch.astype(F32))

        in_parts(count, leave)
        part = width // 2
        for out, at in ((mine_ref, core_ref[0]), (theirs_ref, 1 - core_ref[0])):
            weight = out_w_ref[pl.ds(pl.multiple_of(at * part, part), part), :]
            out[...] = lax.dot_general(
                branch_ref[...], weight, NT, preferred_element_type=F32
            ).astype(BF16)


def ffn_call(kernel, scalars, ins, outer_w, anys, outs, scratch, room, name):
    width = outer_w.shape[1]
    steps = outer_w.shape[0] // width

    def spec(shape):
        if shape[1] == steps * width:
            return pl.BlockSpec((shape[0], width), lambda w: (0, w))
        if shape[0] == steps * width:
            return pl.BlockSpec((width, width), lambda w: (w, 0))
        return pl.BlockSpec(shape, lambda w: (0, 0), pipeline_mode=pl.Buffered(1))

    held = [*ins, outer_w]
    return pl.pallas_call(
        kernel,
        grid=(steps,),
        in_specs=[pl.BlockSpec(memory_space=pltpu.SMEM)] * len(scalars)
        + [spec(a.shape) for a in held]
        + [pl.BlockSpec(memory_space=pl.ANY)] * len(anys),
        out_specs=[spec(shape) for shape, kind in outs],
        out_shape=[pltpu.HBM(shape, kind) for shape, kind in outs],
        scratch_shapes=scratch,
        compiler_params=pltpu.CompilerParams(vmem_limit_bytes=room * 1024 * 1024),
        cost_estimate=weight_of(40),
        name=name,
    )(*scalars, *pinned(held), *anys)


def ffn(core, places, mine, theirs, rows, cotan, vec, outer_w, stacks):
    count, width = rows.shape
    units = outer_w.shape[0]
    low = (rows.shape, BF16)
    outs = [((count, units), BF16)] * 2 + [((width, units), BF16)]
    outs += [low, low, ((count, 1), F32), low, low, ((width, width), BF16), ((8, width), F32)]
    scratch = [
        pltpu.VMEM((count, width), F32),
        pltpu.VMEM((count, width), F32),
        pltpu.VMEM((2, count, 256), F32),
        pltpu.VMEM((2, width, width), BF16),
        pltpu.SemaphoreType.DMA((3,)),
    ]
    tables = [jnp.stack([p[axis] for p in places]).astype(jnp.int32) for axis in range(2)]
    kernel = functools.partial(ffn_kernel, len(stacks))
    ins = [mine, theirs, rows, cotan, vec]
    return ffn_call(
        kernel, [core, *tables], ins, outer_w, pinned(stacks), outs, scratch, 58, "ffn"
    )


def ffn_back(core, grad, slope, normed, scale, vec, out_w, inner_w, outer_w, after):
    count, width = grad.shape
    part = ((count, width // 2), BF16)
    outs = [(slope.shape, BF16), (grad.shape, BF16), part, part, ((8, width), F32)]
    scratch = [pltpu.VMEM((count, width), F32), pltpu.VMEM((2, count, 256), F32)]
    ins = [grad, slope, normed, scale, vec, out_w, inner_w]
    return ffn_call(
        ffn_back_kernel, [core], ins, outer_w, after, outs, scratch, 44, "ffn_back"
    )


def product_kernel(count, stacked, after, where_ref, *refs):
    lefts, right_ref, out_ref = refs[:count], refs[count], refs[count + 1 + after]
    if not stacked:
        total, rows = None, lefts[0].shape[0]
        for n, left_ref in enumerate(lefts):
            right = right_ref[n * rows : (n + 1) * rows, :]
            part = lax.dot_general(left_ref[...], right, TN, preferred_element_type=F32)
            total = part if n == 0 else total + part
        out_ref[...] = total.astype(BF16)
        return
    for n, left_ref in enumerate(lefts):

        @pl.when(pl.program_id(0) == n)
        def _():
            out_ref[...] = lax.dot_general(
                left_ref[...], right_ref[...], TN, preferred_element_type=F32
            ).astype(BF16)


def product(where, lefts, right, side, after=(), stacked=False):
    width = right.shape[1] // (1 if side is None else 2)
    tile = 512
    height = sum(left.shape[1] for left in lefts) if stacked else lefts[0].shape[1]
    micros = 2e-9 * height * width * right.shape[0] + 1
    half = lambda a, w: (0, 0 if side is None else (w[3] if side else 1 - w[3]))
    if stacked:
        left_place = lambda a, w: (0, 0)
        place = lambda a, w: (a + w[3] - 2 * a * w[3], 0)
    else:
        left_place = lambda a, w: (0, a)
        place = lambda a, w: (a, 0)
    return pl.pallas_call(
        functools.partial(product_kernel, len(lefts), stacked, len(after)),
        grid_spec=pltpu.PrefetchScalarGridSpec(
            num_scalar_prefetch=1,
            grid=(height // tile,),
            in_specs=[pl.BlockSpec((left.shape[0], tile), left_place) for left in lefts]
            + [pl.BlockSpec((right.shape[0], width), half, pipeline_mode=pl.Buffered(1))]
            + [pl.BlockSpec(memory_space=pl.ANY)] * len(after),
            out_specs=pl.BlockSpec((tile, width), place),
        ),
        out_shape=pltpu.HBM((height, width), BF16),
        compiler_params=pltpu.CompilerParams(vmem_limit_bytes=2 * SMALL_VMEM),
        cost_estimate=weight_of(micros),
        name="product",
    )(where, *pinned([*lefts, right]), *after)


def attend_kernel(held, seg_row_ref, seg_col_ref, qkv_ref, *rest):
    rest = rest[held:]
    out_refs, (lse_ref, bias_ref, stat_ref, score_ref, expo_ref) = rest[:2], rest[2:]
    half = qkv_ref.shape[2]
    pair = pl.program_id(1)
    length = bias_ref.shape[0]
    chunk = score_ref.shape[1]

    @pl.when(pair == 0)
    def _():
        bias_ref[...] = jnp.where(seg_col_ref[0] == seg_row_ref[0], 0.0, MASKED)
        stat_ref[...] = jnp.zeros_like(stat_ref)

    block = qkv_ref[:, 0].reshape(length, 3 * PAIR)
    q, k, v = (block[:, i * PAIR : (i + 1) * PAIR] for i in range(3))
    lane = lax.broadcasted_iota(jnp.int32, (length, PAIR), 1)
    low = lane < HD
    zero, one = jnp.zeros_like(q), jnp.ones_like(v)
    q_heads = [jnp.where(low, q, zero), jnp.where(low, zero, q)]
    v_heads = [jnp.where(low, v, one), jnp.where(low, one, v)]
    lane, low = lane[:chunk], low[:chunk]

    def score(step):
        c, h = divmod(step, 2)
        score_ref[step % 2] = lax.dot_general(
            q_heads[h][c * chunk : (c + 1) * chunk], k, NT, preferred_element_type=F32
        )

    def soften(step):
        c, h = divmod(step, 2)
        tops = []
        for at in range(0, chunk, TILE):
            rows = slice(c * chunk + at, c * chunk + at + TILE)
            s = score_ref[step % 2, at : at + TILE, :] + bias_ref[rows, :]
            top = jnp.max(s, axis=1, keepdims=True)
            expo_ref[step % 2, at : at + TILE, :] = jnp.exp(s - top).astype(BF16)
            tops.append(top)
        return jnp.concatenate(tops, 0)

    def mix(step):
        return jnp.dot(expo_ref[step % 2], v_heads[step % 2], preferred_element_type=F32)

    def finish(c, got, tops):
        rows = slice(c * chunk, (c + 1) * chunk)
        total = jnp.where(low, got[1], got[0])
        mixed = jnp.where(low, got[0], got[1]) / pltpu.roll(total, HD, 1)
        log = jnp.log(total)
        stat = stat_ref[rows, :]
        stat = jnp.where(lane == 2 * pair, tops[0] + log[:, HD : HD + 1], stat)
        stat_ref[rows, :] = jnp.where(lane == 2 * pair + 1, tops[1] + log[:, :1], stat)
        part, at = divmod(c * chunk, half)
        out_refs[part][0, at : at + chunk, :] = mixed.astype(BF16)

    steps = 2 * length // chunk
    tops, got = [], []
    score(0)
    for step in range(steps):
        if step + 1 < steps:
            score(step + 1)
        tops.append(soften(step))
        got.append(mix(step))
        if step % 2:
            finish(step // 2, got[-2:], tops[-2:])

    @pl.when(pair == pl.num_programs(1) - 1)
    def _():
        lse_ref[0] = jnp.transpose(stat_ref[...])[: lse_ref.shape[1]]


def attend_back_kernel(first_pair, after, *refs):
    seg_row_ref, seg_col_ref, qkv_ref, out_a, out_b, grad_a, grad_b, lse_ref = refs[:8]
    dqkv_ref, sums_ref, bias_ref, ds_ref, score_ref, slope_ref, prob_ref = refs[8 + after :]
    pair = pl.program_id(1)
    length = bias_ref.shape[0]
    half = qkv_ref.shape[2]
    chunk = score_ref.shape[1]

    @pl.when(pair == 0)
    def _():
        bias_ref[...] = jnp.where(seg_col_ref[0] == seg_row_ref[0], 0.0, MASKED)

    @pl.when((pair == 0) & (pl.program_id(0) == 0))
    def _():
        sums_ref[...] = jnp.zeros_like(sums_ref)

    block = qkv_ref[:, 0].reshape(length, 3 * PAIR)
    q, k, v = (block[:, i * PAIR : (i + 1) * PAIR] for i in range(3))
    out = jnp.concatenate([out_a[0], out_b[0]], 0)
    grad = jnp.concatenate([grad_a[0], grad_b[0]], 0)
    low = lax.broadcasted_iota(jnp.int32, (length, PAIR), 1) < HD
    zero = jnp.zeros_like(q)
    heads = lambda array: [jnp.where(low, array, zero), jnp.where(low, zero, array)]
    q_heads, k_heads, g_heads = heads(q), heads(k), heads(grad)
    product = jnp.transpose(out.astype(F32) * grad.astype(F32))
    chunks = length // chunk
    deltas = [total_rows(product[h * HD : (h + 1) * HD]) for h in range(2)]
    stats = [lse_ref[0, pl.ds(2 * (first_pair + pair) + h, 1), :] for h in range(2)]

    def score(step):
        h, c = divmod(step, chunks)
        rows = slice(c * chunk, (c + 1) * chunk)
        score_ref[step % 2] = lax.dot_general(k[rows], q_heads[h], NT, preferred_element_type=F32)
        slope_ref[step % 2] = lax.dot_general(v[rows], g_heads[h], NT, preferred_element_type=F32)

    def bend(step):
        h, c = divmod(step, chunks)
        for at in range(0, chunk, TILE):
            rows = slice(c * chunk + at, c * chunk + at + TILE)
            part = slice(at, at + TILE)
            p = jnp.exp(score_ref[step % 2, part, :] + bias_ref[rows, :] - stats[h])
            prob_ref[step % 2, part, :] = p.astype(BF16)
            ds_ref[h, rows, :] = (p * (slope_ref[step % 2, part, :] - deltas[h])).astype(BF16)

    steps = 2 * chunks
    dk, dv = [None] * chunks, [None] * chunks
    dq = None
    score(0)
    for step in range(steps):
        h, c = divmod(step, chunks)
        if step + 1 < steps:
            score(step + 1)
        bend(step)
        rows = slice(c * chunk, (c + 1) * chunk)
        v_part = jnp.dot(prob_ref[step % 2], g_heads[h], preferred_element_type=F32)
        k_part = jnp.dot(ds_ref[h, rows, :], q_heads[h], preferred_element_type=F32)
        if h == 0:
            dk[c], dv[c] = k_part, v_part
        else:
            part, at = c * chunk // half, c * chunk % half
            dqkv_ref[part, 0, at : at + chunk, PAIR : 2 * PAIR] = (dk[c] + k_part).astype(BF16)
            dv[c] = (dv[c] + v_part).astype(BF16)
            dqkv_ref[part, 0, at : at + chunk, 2 * PAIR :] = dv[c]
        if c == chunks - 1:
            part = lax.dot_general(ds_ref[h], k_heads[h], TN, preferred_element_type=F32)
            dq = part if h == 0 else dq + part
    dq = (dq * HD**-0.5).astype(BF16)
    dqkv_ref[:, 0, :, :PAIR] = dq.reshape(-1, half, PAIR)
    sums = [total_rows(dq.astype(F32)), sum(total_rows(part.astype(F32)) for part in dv)]
    sums_ref[0:1, pl.ds(pl.multiple_of(pair * PAIR, PAIR), PAIR)] += sums[0]
    sums_ref[1:2, pl.ds(pl.multiple_of(pair * PAIR, PAIR), PAIR)] += sums[1]


def attention_call(
    kernel, seg, arrays, pairs, outs, scratch, name, first=0, after=(), seqs=None, held=()
):
    parts, count, half, columns = arrays[0].shape
    start, seqs = seqs or (0, count)
    micros = 6.5 * seqs if name == "attend" else 3.7 * seqs
    length = parts * half

    def spec(array, first):
        shape = array.shape
        if len(shape) == 4:
            return pl.BlockSpec(
                (parts, 1, half, 3 * PAIR), lambda s, p: (0, start + s, 0, first + p)
            )
        if len(shape) == 3 and shape[1] == half:
            return pl.BlockSpec((1, half, PAIR), lambda s, p: (start + s, 0, first + p))
        if len(shape) == 3:
            return pl.BlockSpec((1,) + shape[1:], lambda s, p: (start + s, 0, 0))
        return pl.BlockSpec(shape, lambda s, p: (0, 0))

    operands = [seg[:, None, :], seg[:, :, None]] + arrays
    return pl.pallas_call(
        kernel,
        grid=(seqs, pairs),
        in_specs=[spec(a, first) for a in operands]
        + [pl.BlockSpec(memory_space=pl.ANY)] * (len(held) + len(after)),
        out_specs=[spec(a, 0) for a in outs],
        out_shape=results(outs),
        scratch_shapes=scratch(length),
        input_output_aliases={len(operands) + n: n for n in range(len(held))},
        compiler_params=pltpu.CompilerParams(vmem_limit_bytes=SMALL_VMEM),
        cost_estimate=weight_of(micros),
        name=name,
    )(*pinned(operands), *pinned(held), *after)


def attend(qkv, seg, seqs, held, after):
    parts, count, half, columns = qkv.shape
    pairs = columns // (3 * PAIR)
    outs = [
        jax.ShapeDtypeStruct((count, half, columns // 3), BF16),
        jax.ShapeDtypeStruct((count, half, columns // 3), BF16),
        jax.ShapeDtypeStruct((count, 2 * pairs, parts * half), F32),
    ]
    scratch = lambda length: [
        pltpu.VMEM((length, length), F32),
        pltpu.VMEM((length, PAIR), F32),
        pltpu.VMEM((2, 128, length), F32),
        pltpu.VMEM((2, 128, length), BF16),
    ]
    kernel = functools.partial(attend_kernel, len(held) + len(after))
    return attention_call(
        kernel, seg, [qkv], pairs, outs, scratch, "attend", 0, after, seqs, held
    )


def attend_back(qkv, seg, out, grad, lse, first, pairs, after):
    outs = [
        jax.ShapeDtypeStruct(qkv.shape[:3] + (3 * PAIR * pairs,), BF16),
        jax.ShapeDtypeStruct((8, PAIR * pairs), F32),
    ]
    scratch = lambda length: [
        pltpu.VMEM((length, length), F32),
        pltpu.VMEM((2, length, length), BF16),
        pltpu.VMEM((2, 128, length), F32),
        pltpu.VMEM((2, 128, length), F32),
        pltpu.VMEM((2, 128, length), BF16),
    ]
    kernel = functools.partial(attend_back_kernel, first, len(after))
    arrays = [qkv, *out, *grad, lse]
    return attention_call(kernel, seg, arrays, pairs, outs, scratch, "attend_back", first, after)


def body(
    layer_input,
    segment_ids,
    out_cotangent,
    attn_master,
    inner_master,
    outer_master,
    vector_master,
    attn_moment,
    inner_moment,
    outer_moment,
    vector_moment,
    attn_square,
    inner_square,
    outer_square,
    vector_square,
):
    seqs, half, width = layer_input.shape
    count = seqs * half
    hidden_units = inner_master.shape[1]
    pairs = width // (2 * PAIR)
    part_cols = width // 2
    shards = lax.axis_size("shard")
    owned_rows = attn_master.shape[1]
    core = lax.axis_index("ctx")
    first = core == 0

    def own_half(array, axis):
        size = array.shape[axis] // 2
        return lax.dynamic_slice_in_dim(array, core * size, size, axis)

    def other_half(array, axis):
        size = array.shape[axis] // 2
        return lax.dynamic_slice_in_dim(array, (1 - core) * size, size, axis)

    def in_order(mine, theirs, axis):
        return jnp.concatenate(
            [jnp.where(first, mine, theirs), jnp.where(first, theirs, mine)], axis
        )

    rows = layer_input.reshape(count, width)
    rows_theirs = swap_cores(rows)
    square = is_square()
    o, i, y, inner = position()
    where = jnp.stack([o, i, y, core]).astype(jnp.int32)

    piece = own_half(attn_master[:3], 2).astype(BF16).reshape(3, owned_rows, pairs, PAIR)
    piece = piece.transpose(1, 2, 0, 3).reshape(owned_rows, 3 * part_cols)
    vec_low = vector_master.astype(BF16)
    rider = vec_low[:2].reshape(1, -1)
    if square:
        piece = lax.dynamic_slice_in_dim(piece, y * (piece.shape[1] // 2), piece.shape[1] // 2, 1)
    rider = jnp.pad(rider, ((0, 15), (0, piece.shape[1] - rider.shape[1])))
    piece = jnp.concatenate([piece, rider], 0)

    def every_row(block):
        size = block.shape[0] // (lax.axis_size("replica") * 2)
        part = lax.dynamic_slice_in_dim(block, (2 * y + core) * size, size, 0)
        return lax.all_gather(part.astype(BF16), EVERY, axis=0, tiled=True)

    def placed(found, slots):
        chosen = jnp.stack([place[0] for place in slots[:shards]])
        chosen = (jnp.arange(shards)[:, None] == chosen[None, :]).astype(F32)
        return jnp.einsum("ps,srw->rpw", chosen, found.astype(F32)).reshape(-1, width)

    outer_w = every_row(outer_master)
    if square:
        q = 2 * core + y
        vec_rows = jnp.pad(vec_low.reshape(-1), (0, 16 * width - vec_low.size)).reshape(16, width)
        quarter = jnp.concatenate(
            [
                lax.dynamic_slice_in_dim(inner_master, q * width, width, 1).astype(BF16),
                lax.dynamic_slice_in_dim(
                    attn_master[3], q * (owned_rows // 4), owned_rows // 4, 0
                ).astype(BF16),
                vec_rows,
            ],
            0,
        )
        line = jnp.stack([piece] + [shift_outer(piece, -k) for k in range(1, OUTER)])
        near_x, near_y = shift_inner(line, 1), shift_replica(line, 1)
        (quarter,) = relay(where, [quarter], (line,))
        across = swap_outer(quarter, 2)
        two = (OUTER // 2,)
        far = small_call(
            halves_kernel, where, [near_x, near_y], [two + piece.shape] * 2, (), "halves"
        )
        (pair,) = small_call(
            pair_kernel, where, [quarter, across], [two + quarter.shape], (far[0],), "pair"
        )
        stacks = [line, near_x, near_y, shift_inner(far[0], 1), shift_replica(far[1], 1)]
        places = quarter_places([lax.rem(o + k, OUTER) for k in range(OUTER)])
        other_pair = swap_outer(pair, 1)
        pair_x, pair_y = shift_inner(pair, 1), shift_replica(pair, 1)
        done = (pair,)
    else:
        stacks = [item[None] for item in ring_gather(piece)]
        places = [(owner, 0) for owner in slot_owners()]
        wide = hidden_units // width
        inner_w = every_row(inner_master).reshape(8, -1, wide, width).transpose(0, 2, 1, 3)
        slots = [inner_w.reshape(PARTS, -1, width), every_row(attn_master[3]).reshape(PARTS, -1, width)]
        slots = jnp.pad(jnp.concatenate(slots, 1), ((0, 0), (0, 16), (0, 0)))
        wide_stacks = [slots[n : n + 2] for n in range(0, PARTS, 2)]
        wide_places = [(jnp.int32(n // 4), jnp.int32(n % 4)) for n in range(PARTS)]
        vec = lax.all_gather(vec_low, "shard", axis=1, tiled=True).astype(F32)
        done = ()
    riders = jnp.concatenate([stack[:, owned_rows] for stack in stacks], 0)[:shards]
    riders = riders[:, : 2 * width // shards].reshape(shards, 2, -1)
    biases = placed(riders, places)

    halves = own_half(biases, 1).reshape(2, pairs, PAIR)
    bias = jnp.stack([halves[0], jnp.zeros_like(halves[0]), halves[1]], 1).reshape(1, -1)
    ones = jnp.ones((pairs, PAIR), F32)
    factor = jnp.stack([ones * HD**-0.5, ones, ones], 1).reshape(1, -1)
    qkv, qkv_w = project(rows, rows_theirs, stacks, places, bias, factor, done)
    qkv = qkv.reshape(2, seqs, half, 3 * part_cols)
    seg = jnp.concatenate([own_half(segment_ids, 1), other_half(segment_ids, 1)], 1)
    if square:
        (other_pair,) = relay(where, [other_pair], (qkv_w,))
        other_x, other_y = shift_inner(other_pair, 1), shift_replica(other_pair, 1)
        early = attend(qkv, seg, (0, seqs // 2), (), (other_pair,))
        relayed = relay(where, [pair_y, other_x], (early[0],))
        wide_stacks = [pair, other_pair, pair_x, other_x, pair_y, other_y]
        wide_stacks += [shift_inner(relayed[0], 1), shift_replica(relayed[1], 1)]
        near_rows = jnp.concatenate([a[:, 160:162] for a in wide_stacks[:4]], 0)
        near_rows = near_rows.reshape(shards, -1)[:, : vec_low.size]
        wide_stacks += [swap_cores(a) for a in wide_stacks]
        both = line_order(o)
        places = quarter_places(both[0] + both[1])
        vec = placed(near_rows.reshape((shards,) + vec_low.shape), places)
        wide_places = [(row, 2 * core + side) for row, side in places]
        wide_places += [(row, 2 * (1 - core) + side) for row, side in places]
    else:
        early = attend(qkv, seg, (0, seqs // 2), (), ())
    mixed_mine, mixed_sent, lse = attend(qkv, seg, (seqs // 2, seqs - seqs // 2), early, ())
    flat = lambda array: array.reshape(count, part_cols)
    deep = lambda array: array.reshape(seqs, half, part_cols)
    heads_mine, heads_theirs = flat(mixed_mine), swap_cores(flat(mixed_sent))

    cotan = out_cotangent.reshape(count, width)
    core_at = jnp.full((1,), core, jnp.int32)
    active, slope, inner_w, hidden_low, normed, scale, result, ffn_grad, out_w, sums_two = ffn(
        core_at, wide_places, heads_mine, heads_theirs, rows, cotan, vec, outer_w, wide_stacks
    )

    by_shard = lambda array: array.reshape(shards, -1, array.shape[1])

    outer_sent = product(where, [active], ffn_grad, 0)
    outer_kept = product(where, [active], ffn_grad, 1, (outer_sent,))
    outer_chips = [by_shard(outer_kept), by_shard(swap_cores(outer_sent))]
    done = (outer_kept,)
    if square:
        outer = Sum(where, outer_chips)
        done = outer.merge()
    pre_grad, branch_grad, mine, sent, sums_one = ffn_back(
        core_at, ffn_grad, slope, normed, scale, vec, out_w, inner_w, outer_w, done[:1]
    )
    got = swap_cores(sent)
    mixed_grad = [deep(mine), deep(got)]
    done = outer.plane((pre_grad,)) if square else ()
    heads = [heads_mine, heads_theirs]
    inner_kept = product(where, [hidden_low], pre_grad, 1, done)
    done = outer.cross((inner_kept,)) if square else (inner_kept,)
    inner_sent = product(where, [hidden_low], pre_grad, 0, done)
    out_sent = product(where, heads, branch_grad, 0, (inner_sent, got), True)
    out_kept = product(where, heads, branch_grad, 1, (out_sent,), True)
    inner_chips = [by_shard(inner_kept), by_shard(swap_cores(inner_sent))]
    out_chips = [by_shard(out_kept), by_shard(swap_cores(out_sent))]

    def back(first, after):
        grad, sums = attend_back(
            qkv, seg, (mixed_mine, mixed_sent), mixed_grad, lse, first, pairs // 2, after
        )
        return grad.reshape(2 * count, -1), sums

    def vector_chip(sums_a, sums_b):
        blank = jnp.zeros((part_cols,), F32)
        ours = jnp.concatenate([sums_a, sums_b], 1)
        attn_biases = jnp.stack([in_order(ours[at], blank, 0) for at in range(2)])
        sums = [attn_biases, sums_one[2:3], sums_one[:2], sums_two[2:3], sums_two[:2]]
        sums = jnp.concatenate(sums + [sums_one[4:8]], 0)
        sums = sums.reshape(-1, shards, width // shards).transpose(1, 0, 2)
        sums = jnp.pad(sums, ((0, 0), (0, owned_rows - sums.shape[1]), (0, 0)))
        return sums.astype(BF16)

    outer_states = (outer_master, outer_moment, outer_square)
    inner_states = (inner_master, inner_moment, inner_square)
    attn_states = (attn_master, attn_moment, attn_square)
    if square:
        inner = Sum(where, inner_chips)
        done = inner.merge((out_kept, out_chips[1]))
        grad_a, sums_a = back(0, done)
        done = outer.turn((grad_a,))
        done = inner.plane(done)
        ours = by_shard(product(where, [rows, rows_theirs], grad_a, None, done))
        sum_a = Sum(where, [ours], out_chips)
        done = sum_a.merge()
        grad_b, sums_b = back(pairs // 2, done)
        done = inner.cross((grad_b,))
        done = sum_a.plane(done)
        ours = by_shard(product(where, [rows, rows_theirs], grad_b, None, done))
        sum_b = Sum(where, [ours], [vector_chip(sums_a, sums_b)])
        done = outer.line((ours,))
        done = sum_a.cross(done)
        done = sum_b.merge(done)
        done = inner.turn(done)
        theirs_part = input_back(grad_a, grad_b, qkv_w, (), done)
        outer_new = update(where, outer_states, [outer.shares], (theirs_part,))
        done = sum_b.plane((outer_new[0],))
        done = sum_a.turn(done)
        input_grad = input_back(
            grad_a, grad_b, qkv_w, (branch_grad, swap_cores(theirs_part)), done
        )
        done = sum_b.cross((input_grad,))
        done = inner.line(done)
        done = sum_a.line(done)
        done = sum_b.turn(done)
        inner_new = update(where, inner_states, [inner.shares], done)
        sum_b.line((inner_new[0],))
        attn_shares = [sum_a.shares, sum_b.shares]
        vector_shares = [
            jnp.concatenate(
                [
                    jnp.where(y == 0, sum_b.shares[at], sum_b.shares[at + 1])[0],
                    jnp.where(y == 0, sum_b.shares[at + 1], sum_b.shares[at])[0],
                ],
                0,
            )
            for at in (0, 2)
        ]
    else:
        grad_a, sums_a = back(0, ())
        grad_b, sums_b = back(pairs // 2, ())
        theirs_part = input_back(grad_a, grad_b, qkv_w, (), ())
        added = (branch_grad, swap_cores(theirs_part))
        input_grad = input_back(grad_a, grad_b, qkv_w, added, ())
        outer_new = update(where, outer_states, [sum_apart(add_low(*outer_chips))])
        inner_new = update(where, inner_states, [sum_apart(add_low(*inner_chips))])
        ours = [by_shard(product(where, [rows, rows_theirs], grad, None)) for grad in (grad_a, grad_b)]
        chip_a = jnp.concatenate([ours[0], add_low(*out_chips)], 2)
        chip_b = jnp.concatenate([ours[1], vector_chip(sums_a, sums_b)], 2)
        attn_shares = [sum_apart(chip_a), sum_apart(chip_b)]
        vector_shares = [share[0] for share in attn_shares[1]]
    attn_new = update(where, attn_states, attn_shares)
    cut = grad_b.shape[1]
    vector_sum = sum(share[: vec_low.shape[0], cut:].astype(F32) for share in vector_shares)
    vector_new = adamw(vector_sum, vector_moment, vector_square, vector_master, RATE_VECTOR)
    vector_new = vector_new + (vector_new[2].astype(BF16),)
    news = (attn_new, inner_new, outer_new, vector_new)
    updates = [[new[at] for new in news] for at in range(4)]
    return (
        result.reshape(seqs, half, width).astype(BF16),
        input_grad.reshape(seqs, half, width),
        *[item for kind in updates for item in kind],
    )


def solution(mesh):
    tokens = P(("replica", "shard"), "ctx", None)
    states = (P(None, "shard", None), P("shard", None), P("shard", None), P(None, "shard"))
    in_specs = (tokens, P(("replica", "shard"), None), tokens) + states * 3
    out_specs = (tokens, tokens) + states * 4
    return jax.shard_map(body, mesh=mesh, in_specs=in_specs, out_specs=out_specs, check_vma=False)
```

```python
import functools
import math

import jax
import jax.numpy as jnp
from jax import lax
from jax.experimental import pallas as pl
from jax.experimental.pallas import tpu as pltpu
from jax.sharding import PartitionSpec as P

HD = 64
PAIR = 2 * HD
STEP = 5
OUTER = 4
EVERY = ("shard", "replica", "ctx")

EPS_NORM = 1e-05
BETA_ONE = 0.5
BETA_TWO = 0.6
RATE_MATRIX = 0.02
RATE_VECTOR = 0.1
DECAY = 0.01
EPS_ADAM = 1e-06
MASKED = -1e30
F32 = jnp.float32
BF16 = jnp.bfloat16
PARTS = 32
TILE = 32
VMEM = 56 * 1024 * 1024
SMALL_VMEM = 16 * 1024 * 1024
GROUP = 256
NT = (((1,), (1,)), ((), ()))
TN = (((0,), (0,)), ((), ()))


def weight_of(micros):
    return pl.CostEstimate(
        flops=int(micros * 2.9e8), bytes_accessed=int(micros * 9.2e5), transcendentals=0
    )


def normalize(resid):
    centre = resid - jnp.mean(resid, -1, keepdims=True)
    scale = lax.rsqrt(jnp.mean(centre * centre, -1, keepdims=True) + EPS_NORM)
    return (centre * scale, scale)


def norm_back(grad, normed, scale):
    return scale * (
        grad
        - jnp.mean(grad, -1, keepdims=True)
        - normed * jnp.mean(grad * normed, -1, keepdims=True)
    )


def adamw(grad, moment, square, weight, rate):
    moment_new = BETA_ONE * moment + (1.0 - BETA_ONE) * grad
    square_new = BETA_TWO * square + (1.0 - BETA_TWO) * grad * grad
    stepped = (
        moment_new
        / (1.0 - BETA_ONE**STEP)
        / (jnp.sqrt(square_new / (1.0 - BETA_TWO**STEP)) + EPS_ADAM)
    )
    weight_new = weight - rate * (stepped + DECAY * weight)
    return (moment_new, square_new, weight_new)


def swap_cores(value):
    return lax.ppermute(value, "ctx", [(0, 1), (1, 0)])


def shift_outer(value, step):
    inner = lax.axis_size("shard") // OUTER
    pairs = [
        (o * inner + i, ((o + step) % OUTER) * inner + i) for o in range(OUTER) for i in range(inner)
    ]
    return lax.ppermute(value, "shard", pairs)


def shift_inner(value, step):
    inner = lax.axis_size("shard") // OUTER
    pairs = [
        (o * inner + i, o * inner + (i + step) % inner) for o in range(OUTER) for i in range(inner)
    ]
    return lax.ppermute(value, "shard", pairs)


def shift_replica(value, step):
    size = lax.axis_size("replica")
    return lax.ppermute(value, "replica", [(r, (r + step) % size) for r in range(size)])


def ring_gather(piece):
    inner = lax.axis_size("shard") // OUTER
    found = []
    held = piece
    for k in range(OUTER):
        if k:
            held = shift_outer(held, -1)
        found.append([held] + [shift_inner(held, -e) for e in range(1, inner)])
    return [item for group in found for item in group]


def slot_owners():
    inner = lax.axis_size("shard") // OUTER
    at = lax.axis_index("shard")
    o, i = at // inner, at % inner
    return [
        lax.rem(o + k, OUTER) * inner + lax.rem(i + e, inner)
        for k in range(OUTER)
        for e in range(inner)
    ]


def pick(array, index, axis):
    return lax.dynamic_index_in_dim(array, index, axis, keepdims=False)


def add_low(value, *others):
    total = value.astype(F32)
    for item in others:
        total = total + item.astype(F32)
    return total.astype(BF16)


def position():
    inner = lax.axis_size("shard") // OUTER
    at = lax.axis_index("shard")
    return at // inner, at % inner, lax.axis_index("replica"), inner


def is_square():
    return lax.axis_size("replica") == 2 and lax.axis_size("shard") == 2 * OUTER


def swap_outer(value, flip):
    inner = lax.axis_size("shard") // OUTER
    pairs = [(o * inner + i, (o ^ flip) * inner + i) for o in range(OUTER) for i in range(inner)]
    return lax.ppermute(value, "shard", pairs)


def swap_cross(value):
    return lax.ppermute(value, ("replica", "ctx"), [(a, 3 - a) for a in range(4)])


def sum_apart(chip_sum):
    o, i, y, inner = position()
    grid = chip_sum.reshape(OUTER, inner, *chip_sum.shape[1:])
    got = [shift_inner(pick(grid, lax.rem(i + e, inner), 1), e) for e in range(1, inner)]
    line = add_low(pick(grid, i, 1), *got)
    got = [shift_outer(pick(line, lax.rem(o + d, OUTER), 0), d) for d in range(1, OUTER)]
    total = add_low(pick(line, o, 0), *got)
    got = [shift_replica(total, r) for r in range(1, lax.axis_size("replica"))]
    mine = add_low(total, *got)[None]
    return [mine, swap_cores(mine)]


def small_call(kernel, where, ins, outs, after, name):
    held = pl.BlockSpec(memory_space=pltpu.VMEM)
    return pl.pallas_call(
        functools.partial(kernel, len(ins), len(after)),
        in_specs=[pl.BlockSpec(memory_space=pltpu.SMEM)]
        + [held] * len(ins)
        + [pl.BlockSpec(memory_space=pl.ANY)] * len(after),
        out_specs=[held] * len(outs),
        out_shape=[pltpu.VMEM(shape, BF16) for shape in outs],
        compiler_params=pltpu.CompilerParams(vmem_limit_bytes=SMALL_VMEM),
        cost_estimate=weight_of(1),
        name=name,
    )(where, *[pltpu.with_memory_space_constraint(a, pltpu.VMEM) for a in ins], *after)


def fold_plane_kernel(count, after, where_ref, keep_p, got_p, keep_q, got_q, *rest):
    i, y = where_ref[1], where_ref[2]
    kept_p, send_p, kept_q, send_q = rest[after:]
    for o in range(OUTER):
        for out, at in ((kept_p, y), (send_p, 1 - y)):
            out[o] = add_low(keep_p[o, at], got_p[o, at])
        for out, at in ((kept_q, i), (send_q, 1 - i)):
            out[o] = add_low(keep_q[o, at], got_q[o, at])


def line_order(o):
    near = o + 1 - 2 * lax.rem(o, 2)
    far = lambda at: lax.rem(at + 2, OUTER)
    return (o, far(o)), (near, far(near))


def fold_cross_kernel(count, after, where_ref, keep_p, got_p, keep_q, got_q, *rest):
    for out, order in zip(rest[after:], line_order(where_ref[0])):
        for n, at in enumerate(order):
            out[n, 0] = add_low(keep_p[at], got_p[at])
            out[n, 1] = add_low(keep_q[at], got_q[at])


def fold_turn_kernel(count, after, where_ref, keep, got, *rest):
    for n, out in enumerate(rest[after:]):
        out[...] = add_low(keep[n], got[n])


def fold_line_kernel(count, after, where_ref, *rest):
    rest[count + after][...] = add_low(*(ref[...] for ref in rest[:count]))


def merge_kernel(groups, after, where_ref, *refs):
    outs = refs[4 * sum(groups) + after :]
    for slot, out in enumerate(outs):
        left = chip = 0
        for group in groups:
            for at in range(2):
                parts = []
                for n in range(chip, chip + group):
                    ref = refs[4 * n + slot]
                    parts.append(ref[0, at, 0, 0] if slot % 2 else ref[0, 0, 0, at])
                cut = slice(left, left + parts[0].shape[1])
                out[0, at, :, cut] = parts[0] if group == 1 else add_low(*parts)
            left, chip = cut.stop, chip + group


class Sum:
    def __init__(self, where, *groups):
        self.where, self.rows = where, groups[0][0].shape[1] // 4
        self.columns = sum(group[0].shape[2] for group in groups)
        self.groups = [len(group) for group in groups]
        self.chips = [
            c.reshape(OUTER, 2, 2, 2, self.rows, c.shape[2]) for group in groups for c in group
        ]

    def shape(self, *lead):
        return lead + (self.rows, self.columns)

    def merge(self, after=()):
        def spec(chip, lead, flip):
            def place(o, w):
                at = w[1] if lead == 0 else w[2]
                at = 1 - at if flip else at
                return (o, at, 0, 0, 0, 0) if lead == 0 else (o, 0, 1, at, 0, 0)

            return pl.BlockSpec(((1, 1, 1, 2) if lead == 0 else (1, 2, 1, 1)) + chip.shape[4:], place)

        kinds = ((0, True), (1, True), (0, False), (1, False))
        out_spec = pl.BlockSpec((1, 2, self.rows, self.columns), lambda o, w: (o, 0, 0, 0))
        *sent, keep_p, keep_q = pl.pallas_call(
            functools.partial(merge_kernel, self.groups, len(after)),
            grid_spec=pltpu.PrefetchScalarGridSpec(
                num_scalar_prefetch=1,
                grid=(OUTER,),
                in_specs=[spec(chip, *kind) for chip in self.chips for kind in kinds]
                + [pl.BlockSpec(memory_space=pl.ANY)] * len(after),
                out_specs=[out_spec] * 4,
            ),
            out_shape=[jax.ShapeDtypeStruct(self.shape(OUTER, 2), BF16)] * 4,
            compiler_params=pltpu.CompilerParams(vmem_limit_bytes=SMALL_VMEM),
            cost_estimate=weight_of(4),
            name="merge",
        )(self.where, *[chip for chip in self.chips for _ in range(4)], *after)
        self.kept = [keep_p, shift_inner(sent[0], 1), keep_q, shift_replica(sent[1], 1)]
        return tuple(sent)

    def plane(self, after=()):
        keep_p, send_p, keep_q, send_q = small_call(
            fold_plane_kernel, self.where, self.kept, [self.shape(OUTER)] * 4, after, "fold_plane"
        )
        self.kept = [keep_p, shift_replica(send_p, 1), keep_q, shift_inner(send_q, 1)]
        return (send_p, send_q)

    def cross(self, after=()):
        keep, send = small_call(
            fold_cross_kernel, self.where, self.kept, [self.shape(2, 2)] * 2, after, "fold_cross"
        )
        self.kept = [keep, swap_outer(send, 1)]
        return (send,)

    def turn(self, after=()):
        shapes = [self.kept[0].shape[1:]] * 2
        keep, send = small_call(
            fold_turn_kernel, self.where, self.kept, shapes, after, "fold_turn"
        )
        self.kept = [keep, swap_outer(send, 2)]
        return (send,)

    def line(self, after=()):
        (total,) = small_call(
            fold_line_kernel, self.where, self.kept, [self.kept[0].shape], after, "fold_line"
        )
        self.shares = [total, shift_replica(total, 1), swap_cores(total), swap_cross(total)]
        return (total,)


def update_kernel(groups, after, where_ref, *refs):
    states, shares = refs[:3], refs[3 : 3 + sum(groups)]
    outs, grad_ref = refs[3 + sum(groups) + after : -1], refs[-1]
    rows = shares[0].shape[1]
    across = groups[0] // 2
    for core in range(2):

        @pl.when(pl.program_id(1) == core)
        def _():
            for n in range(across):
                line = where_ref[2] if n == 0 else 1 - where_ref[2]
                line = pl.ds(pl.multiple_of(line * rows, rows), rows) if across > 1 else slice(None)
                if len(groups) == 1:
                    grad_ref[line, :] = shares[across * core + n][0].astype(F32)
                    continue
                left, right = shares[across * core + n], shares[groups[0] + across * core + n]
                width = grad_ref.shape[2]
                pairs = width // PAIR
                for t in range(3):
                    for p in range(pairs):
                        side, at = (left, p) if 2 * p < pairs else (right, p - pairs // 2)
                        part = side[0, :, (3 * at + t) * PAIR : (3 * at + t + 1) * PAIR]
                        grad_ref[t, line, p * PAIR : (p + 1) * PAIR] = part.astype(F32)
                cut = 3 * PAIR * (pairs // 2)
                grad_ref[3, line, :] = left[0, :, cut : cut + width].astype(F32)

    new = adamw(grad_ref[...], states[1][...], states[2][...], states[0][...], RATE_MATRIX)
    for out, value in zip(outs, new + (new[2],)):
        out[...] = value.astype(out.dtype)


def update(where, states, groups, after=()):
    parts, rows = groups[0][0].shape[:2]
    rows = rows * (len(groups[0]) // 2)
    lead = states[0].shape[:-2]
    columns = states[0].shape[-1] // 2
    place = lambda p, v, w: (0,) * len(lead) + (p, w[3] + v - 2 * w[3] * v)
    block = pl.BlockSpec(lead + (rows, columns), place)
    shares = [share for group in groups for share in group]
    share_specs = [pl.BlockSpec((1,) + a.shape[1:], lambda p, v, w: (p, 0, 0)) for a in shares]
    kinds = (F32, F32, F32, BF16)
    return pl.pallas_call(
        functools.partial(update_kernel, [len(group) for group in groups], len(after)),
        grid_spec=pltpu.PrefetchScalarGridSpec(
            num_scalar_prefetch=1,
            grid=(parts, 2),
            in_specs=[block] * 3 + share_specs + [pl.BlockSpec(memory_space=pl.ANY)] * len(after),
            out_specs=[block] * 4,
            scratch_shapes=[pltpu.VMEM(lead + (rows, columns), F32)],
        ),
        out_shape=[jax.ShapeDtypeStruct(states[0].shape, kind) for kind in kinds],
        compiler_params=pltpu.CompilerParams(vmem_limit_bytes=SMALL_VMEM),
        cost_estimate=weight_of(5),
        name="update",
    )(where, *states, *shares, *after)


def input_back_kernel(a_ref, b_ref, left_ref, right_ref, *rest):
    out_ref = rest[-1]
    total = lax.dot_general(a_ref[...], left_ref[...], NT, preferred_element_type=F32)
    total += lax.dot_general(b_ref[...], right_ref[...], NT, preferred_element_type=F32)
    if out_ref.dtype == F32:
        total += rest[0][...].astype(F32) + rest[1][...].astype(F32)
    out_ref[...] = total.astype(out_ref.dtype)


def input_back(grad_a, grad_b, weight, added, after):
    count, cut = grad_a.shape[0] // 2, grad_a.shape[1]
    width = weight.shape[0]
    tile = width // 4
    first = 0 if added else 1
    side = pl.BlockSpec((count, cut), lambda n: (first, 0))
    line = pl.BlockSpec((count, tile), lambda n: (0, n))
    return pl.pallas_call(
        input_back_kernel,
        grid=(width // tile,),
        in_specs=[side, side]
        + [pl.BlockSpec((tile, cut), lambda n, at=at: (n, at)) for at in range(2)]
        + [line] * len(added)
        + [pl.BlockSpec(memory_space=pl.ANY)] * len(after),
        out_specs=line,
        out_shape=jax.ShapeDtypeStruct((count, width), F32 if added else BF16),
        compiler_params=pltpu.CompilerParams(vmem_limit_bytes=SMALL_VMEM),
        cost_estimate=weight_of(5),
        name="input_back",
    )(*[grad_a, grad_b, weight, weight, *added], *after)


def quarter_places(order):
    o, i, y, inner = position()
    kinds = ((i, y), (1 - i, y), (i, 1 - y), (1 - i, 1 - y))
    return [(row * 2 + across, side) for across, side in kinds for row in order]


def relay_kernel(count, after, where_ref, *rest):
    for source, out in zip(rest[:count], rest[count + after :]):
        out[...] = source[...]


def halves_kernel(count, after, where_ref, near_x, near_y, *rest):
    first, second = rest[after:]
    first[...] = near_y[: OUTER // 2]
    second[...] = near_x[OUTER // 2 :]


def pair_kernel(count, after, where_ref, own, other, *rest):
    rest[after][0] = own[...]
    rest[after][1] = other[...]


def relay(where, arrays, after):
    return small_call(relay_kernel, where, arrays, [a.shape for a in arrays], after, "relay")


def project_kernel(after, row_ref, column_ref, mine_ref, theirs_ref, bias_ref, factor_ref, *rest):
    stacks, (out_ref, weight_ref) = rest[: -2 - after], rest[-2:]
    columns = stacks[0].shape[2]
    part = weight_ref.shape[0] * weight_ref.shape[1] // columns
    part = part // sum(stack.shape[0] for stack in stacks)
    at = pl.program_id(0)

    @pl.when(at == 0)
    def _():
        slot = 0
        for stack in stacks:
            for k in range(stack.shape[0]):
                start = pl.multiple_of(row_ref[slot] * part, part)
                left = pl.multiple_of(column_ref[slot] * columns, PAIR)
                weight_ref[pl.ds(start, part), pl.ds(left, columns)] = stack[k, :part, :]
                slot += 1

    def fill(rows):
        acc = jnp.dot(rows, weight_ref[...], preferred_element_type=F32)
        out_ref[...] = ((acc + bias_ref[...]) * factor_ref[...]).astype(BF16)

    @pl.when(at < pl.num_programs(0) // 2)
    def _():
        fill(mine_ref[...])

    @pl.when(at >= pl.num_programs(0) // 2)
    def _():
        fill(theirs_ref[...])


def project(mine, theirs, stacks, places, bias, factor, after):
    count, width = mine.shape
    columns = bias.shape[1]
    tile = 512
    each = count // tile
    whole = lambda shape: pl.BlockSpec(shape, lambda m, *_: (0,) * len(shape))
    tables = [jnp.stack([p[axis] for p in places]).astype(jnp.int32) for axis in range(2)]
    return pl.pallas_call(
        functools.partial(project_kernel, len(after)),
        grid_spec=pltpu.PrefetchScalarGridSpec(
            num_scalar_prefetch=2,
            grid=(2 * each,),
            in_specs=[
                pl.BlockSpec((tile, width), lambda m, *_: (jnp.minimum(m, each - 1), 0)),
                pl.BlockSpec((tile, width), lambda m, *_: (jnp.maximum(m - each, 0), 0)),
                whole((1, columns)),
                whole((1, columns)),
            ]
            + [whole(stack.shape) for stack in stacks]
            + [pl.BlockSpec(memory_space=pl.ANY)] * len(after),
            out_specs=[
                pl.BlockSpec((tile, columns), lambda m, *_: (m, 0)),
                whole((width, columns)),
            ],
        ),
        out_shape=[jax.ShapeDtypeStruct((2 * count, columns), BF16), jax.ShapeDtypeStruct((width, columns), BF16)],
        compiler_params=pltpu.CompilerParams(vmem_limit_bytes=44 * 1024 * 1024),
        cost_estimate=weight_of(11),
        name="project",
    )(*tables, *[mine, theirs, bias, factor, *stacks], *after)


def gelu_and_slope(u):
    a = jnp.abs(u)
    d = 1.0 + (0.3275911 * 0.5**0.5) * a
    t = pl.reciprocal(d, approx=True)
    t = t * (2.0 - d * t)
    e = jnp.exp2(u * u * (-0.5 * math.log2(math.e)))
    series = (0.5 * 1.061405429) * t - 0.5 * 1.453152027
    series = series * t + 0.5 * 1.421413741
    series = series * t - 0.5 * 0.284496736
    series = series * t + 0.5 * 0.254829592
    tail = series * t * e
    active = jnp.maximum(u, 0.0) - a * tail
    below = tail - a * (e * (1.0 / math.sqrt(2.0 * math.pi)))
    return active, jnp.where(u >= 0.0, 1.0 - below, below)


def total_rows(value):
    return jnp.sum(value, axis=0, keepdims=True)


def in_parts(count, work):
    def turn(at, carry):
        work(pl.ds(pl.multiple_of(at * 128, 128), 128))
        return carry

    lax.fori_loop(0, count // 128, turn, 0)


def ffn_kernel(
    count_of,
    core_ref,
    row_ref,
    part_ref,
    mine_ref,
    theirs_ref,
    rows_ref,
    cotan_ref,
    vec_ref,
    outer_w_ref,
    *more,
):
    stacks, more = more[:count_of], more[count_of:]
    active_ref, slope_ref, inner_out_ref, hidden_ref, normed_ref, scale_ref = more[:6]
    result_ref, grad_ref, out_w_ref, sums_ref, resid, acc, pre, inner_w, sems = more[6:]
    w, last = pl.program_id(0), pl.num_programs(0) - 1
    count, width = acc.shape
    chunk = pre.shape[2]
    vec = lambda at: vec_ref[at : at + 1, :]
    half_of = lambda at: out_w_ref[pl.ds(pl.multiple_of(at * (width // 2), width // 2), width // 2), :]
    slots = [(stack, k) for stack in stacks for k in range(stack.shape[0])]
    deep = 4 * width // len(slots)
    thin = width // len(slots)

    def fetch(block):
        for slot, (stack, k) in enumerate(slots):

            @pl.when(part_ref[slot] == block)
            def _():
                start = pl.multiple_of(row_ref[slot] * deep, deep)
                pltpu.make_async_copy(
                    stack.at[k, pl.ds(0, deep), :],
                    inner_w.at[lax.rem(block, 2), pl.ds(start, deep), :],
                    sems.at[lax.rem(block, 2)],
                ).start()

    def arrived(block):
        target = inner_w.at[lax.rem(block, 2)]
        pltpu.make_async_copy(target, target, sems.at[lax.rem(block, 2)]).wait()

    @pl.when(w == 0)
    def _():
        for slot, (stack, k) in enumerate(slots):
            start = pl.multiple_of(row_ref[slot] * 4 * thin + part_ref[slot] * thin, thin)
            pltpu.make_async_copy(
                stack.at[k, pl.ds(deep, thin), :], out_w_ref.at[pl.ds(start, thin), :], sems.at[2]
            ).start()
        fetch(w)
        pltpu.make_async_copy(out_w_ref, out_w_ref, sems.at[2]).wait()
        acc[...] = jnp.dot(mine_ref[...], half_of(core_ref[0]), preferred_element_type=F32)
        acc[...] += jnp.dot(theirs_ref[...], half_of(1 - core_ref[0]), preferred_element_type=F32)

        def enter(part):
            normed, scale = normalize(acc[part, :] + vec(2) + rows_ref[part, :].astype(F32))
            normed_ref[part, :] = normed.astype(BF16)
            scale_ref[part, :] = scale
            hidden = normed * vec(3) + vec(4)
            resid[part, :] = hidden + vec(5)
            hidden_ref[part, :] = hidden.astype(BF16)

        in_parts(count, enter)

    arrived(w)

    @pl.when(w < last)
    def _():
        fetch(w + 1)

    now = lax.rem(w, 2)
    inner_out_ref[...] = inner_w[now]
    bias = vec_ref[pl.ds(8 + w, 1), :]

    def expand(n):
        cut = slice(n * chunk, (n + 1) * chunk)
        weight = inner_w[now, :, cut]
        pre[n % 2] = jnp.dot(hidden_ref[...], weight, preferred_element_type=F32)

    def bend(n):
        cut = slice(n * chunk, (n + 1) * chunk)
        for at in range(0, count, TILE):
            part = slice(at, at + TILE)
            active, slope = gelu_and_slope(pre[n % 2, part, :] + bias[:, cut])
            active_ref[part, cut] = active.astype(BF16)
            slope_ref[part, cut] = slope.astype(BF16)

    chunks = width // chunk
    expand(0)
    for n in range(1, chunks):
        expand(n)
        bend(n - 1)
    bend(chunks - 1)

    def contract():
        weight = outer_w_ref[...]
        return jnp.dot(active_ref[...], weight, preferred_element_type=F32)

    @pl.when(w == 0)
    def _():
        acc[...] = contract()

    @pl.when(w > 0)
    def _():
        acc[...] += contract()

    @pl.when(w == last)
    def _():
        sums_ref[...] = jnp.zeros_like(sums_ref)

        def leave(part):
            normed, scale = normalize(resid[part, :] + acc[part, :])
            result_ref[part, :] = (normed * vec(6) + vec(7)).astype(BF16)
            cotan = cotan_ref[part, :].astype(F32)
            grad = norm_back(cotan * vec(6), normed, scale).astype(BF16)
            grad_ref[part, :] = grad
            sums_ref[0:1, :] += total_rows(cotan * normed)
            sums_ref[1:2, :] += total_rows(cotan)
            sums_ref[2:3, :] += total_rows(grad.astype(F32))

        in_parts(count, leave)


def ffn_back_kernel(
    core_ref,
    grad_ref,
    slope_ref,
    normed_ref,
    scale_ref,
    vec_ref,
    out_w_ref,
    inner_w_ref,
    outer_w_ref,
    after_ref,
    pre_grad_ref,
    branch_ref,
    mine_ref,
    theirs_ref,
    sums_ref,
    acc,
    pre,
):
    w = pl.program_id(0)
    count, width = acc.shape
    chunk = pre.shape[2]
    vec = lambda at: vec_ref[at : at + 1, :]

    @pl.when(w == 0)
    def _():
        sums_ref[...] = jnp.zeros_like(sums_ref)

    def pull(n):
        weight = outer_w_ref[n * chunk : (n + 1) * chunk, :]
        pre[n % 2] = lax.dot_general(grad_ref[...], weight, NT, preferred_element_type=F32)

    def bend(n):
        cut = slice(n * chunk, (n + 1) * chunk)
        sums = jnp.zeros((8, chunk), F32)
        for at in range(0, count, TILE):
            part = slice(at, at + TILE)
            back = pre[n % 2, part, :].astype(BF16).astype(F32) * slope_ref[part, cut].astype(F32)
            back = back.astype(BF16)
            pre_grad_ref[part, cut] = back
            sums += jnp.sum(back.astype(F32).reshape(TILE // 8, 8, chunk), axis=0)
        sums_ref[pl.ds(4 + w, 1), cut] += total_rows(sums)

    chunks = width // chunk
    pull(0)
    for n in range(1, chunks):
        pull(n)
        bend(n - 1)
    bend(chunks - 1)

    def contract():
        weight = inner_w_ref[...]
        return lax.dot_general(pre_grad_ref[...], weight, NT, preferred_element_type=F32)

    @pl.when(w == 0)
    def _():
        acc[...] = contract()

    @pl.when(w > 0)
    def _():
        acc[...] += contract()

    @pl.when(w == pl.num_programs(0) - 1)
    def _():
        def leave(part):
            through = acc[part, :].astype(BF16).astype(F32) + grad_ref[part, :].astype(F32)
            normed = normed_ref[part, :].astype(F32)
            branch = norm_back(through * vec(3), normed, scale_ref[part, :]).astype(BF16)
            branch_ref[part, :] = branch
            sums_ref[0:1, :] += total_rows(through * normed)
            sums_ref[1:2, :] += total_rows(through)
            sums_ref[2:3, :] += total_rows(branch.astype(F32))

        in_parts(count, leave)
        part = width // 2
        for out, at in ((mine_ref, core_ref[0]), (theirs_ref, 1 - core_ref[0])):
            weight = out_w_ref[pl.ds(pl.multiple_of(at * part, part), part), :]
            out[...] = lax.dot_general(
                branch_ref[...], weight, NT, preferred_element_type=F32
            ).astype(BF16)


def ffn_call(kernel, scalars, ins, outer_w, anys, outs, scratch, room, name):
    width = outer_w.shape[1]
    steps = outer_w.shape[0] // width

    def spec(shape):
        if shape[1] == steps * width:
            return pl.BlockSpec((shape[0], width), lambda w: (0, w))
        if shape[0] == steps * width:
            return pl.BlockSpec((width, width), lambda w: (w, 0))
        return pl.BlockSpec(shape, lambda w: (0, 0), pipeline_mode=pl.Buffered(1))

    held = [*ins, outer_w]
    return pl.pallas_call(
        kernel,
        grid=(steps,),
        in_specs=[pl.BlockSpec(memory_space=pltpu.SMEM)] * len(scalars)
        + [spec(a.shape) for a in held]
        + [pl.BlockSpec(memory_space=pl.ANY)] * len(anys),
        out_specs=[spec(shape) for shape, kind in outs],
        out_shape=[jax.ShapeDtypeStruct(shape, kind) for shape, kind in outs],
        scratch_shapes=scratch,
        compiler_params=pltpu.CompilerParams(vmem_limit_bytes=room * 1024 * 1024),
        cost_estimate=weight_of(40),
        name=name,
    )(*scalars, *held, *anys)


def ffn(core, places, mine, theirs, rows, cotan, vec, outer_w, stacks):
    count, width = rows.shape
    units = outer_w.shape[0]
    low = (rows.shape, BF16)
    outs = [((count, units), BF16)] * 2 + [((width, units), BF16)]
    outs += [low, low, ((count, 1), F32), low, low, ((width, width), BF16), ((8, width), F32)]
    scratch = [
        pltpu.VMEM((count, width), F32),
        pltpu.VMEM((count, width), F32),
        pltpu.VMEM((2, count, 256), F32),
        pltpu.VMEM((2, width, width), BF16),
        pltpu.SemaphoreType.DMA((3,)),
    ]
    tables = [jnp.stack([p[axis] for p in places]).astype(jnp.int32) for axis in range(2)]
    kernel = functools.partial(ffn_kernel, len(stacks))
    ins = [mine, theirs, rows, cotan, vec]
    return ffn_call(
        kernel, [core, *tables], ins, outer_w, stacks, outs, scratch, 58, "ffn"
    )


def ffn_back(core, grad, slope, normed, scale, vec, out_w, inner_w, outer_w, after):
    count, width = grad.shape
    part = ((count, width // 2), BF16)
    outs = [(slope.shape, BF16), (grad.shape, BF16), part, part, ((8, width), F32)]
    scratch = [pltpu.VMEM((count, width), F32), pltpu.VMEM((2, count, 256), F32)]
    ins = [grad, slope, normed, scale, vec, out_w, inner_w]
    return ffn_call(
        ffn_back_kernel, [core], ins, outer_w, after, outs, scratch, 44, "ffn_back"
    )


def product_kernel(count, stacked, after, where_ref, *refs):
    lefts, right_ref, out_ref = refs[:count], refs[count], refs[count + 1 + after]
    if not stacked:
        total, rows = None, lefts[0].shape[0]
        for n, left_ref in enumerate(lefts):
            right = right_ref[n * rows : (n + 1) * rows, :]
            part = lax.dot_general(left_ref[...], right, TN, preferred_element_type=F32)
            total = part if n == 0 else total + part
        out_ref[...] = total.astype(BF16)
        return
    for n, left_ref in enumerate(lefts):

        @pl.when(pl.program_id(0) == n)
        def _():
            out_ref[...] = lax.dot_general(
                left_ref[...], right_ref[...], TN, preferred_element_type=F32
            ).astype(BF16)


def product(where, lefts, right, side, after=(), stacked=False):
    width = right.shape[1] // (1 if side is None else 2)
    tile = 512
    height = sum(left.shape[1] for left in lefts) if stacked else lefts[0].shape[1]
    micros = 2e-9 * height * width * right.shape[0] + 1
    half = lambda a, w: (0, 0 if side is None else (w[3] if side else 1 - w[3]))
    if stacked:
        left_place = lambda a, w: (0, 0)
        place = lambda a, w: (a + w[3] - 2 * a * w[3], 0)
    else:
        left_place = lambda a, w: (0, a)
        place = lambda a, w: (a, 0)
    return pl.pallas_call(
        functools.partial(product_kernel, len(lefts), stacked, len(after)),
        grid_spec=pltpu.PrefetchScalarGridSpec(
            num_scalar_prefetch=1,
            grid=(height // tile,),
            in_specs=[pl.BlockSpec((left.shape[0], tile), left_place) for left in lefts]
            + [pl.BlockSpec((right.shape[0], width), half, pipeline_mode=pl.Buffered(1))]
            + [pl.BlockSpec(memory_space=pl.ANY)] * len(after),
            out_specs=pl.BlockSpec((tile, width), place),
        ),
        out_shape=jax.ShapeDtypeStruct((height, width), BF16),
        compiler_params=pltpu.CompilerParams(vmem_limit_bytes=2 * SMALL_VMEM),
        cost_estimate=weight_of(micros),
        name="product",
    )(where, *[*lefts, right], *after)


def attend_kernel(held, seg_row_ref, seg_col_ref, qkv_ref, *rest):
    rest = rest[held:]
    out_refs, (lse_ref, bias_ref, stat_ref, score_ref, expo_ref) = rest[:2], rest[2:]
    half = qkv_ref.shape[2]
    pair = pl.program_id(1)
    length = bias_ref.shape[0]
    chunk = score_ref.shape[1]

    @pl.when(pair == 0)
    def _():
        bias_ref[...] = jnp.where(seg_col_ref[0] == seg_row_ref[0], 0.0, MASKED)
        stat_ref[...] = jnp.zeros_like(stat_ref)

    block = qkv_ref[:, 0].reshape(length, 3 * PAIR)
    q, k, v = (block[:, i * PAIR : (i + 1) * PAIR] for i in range(3))
    lane = lax.broadcasted_iota(jnp.int32, (length, PAIR), 1)
    low = lane < HD
    zero, one = jnp.zeros_like(q), jnp.ones_like(v)
    q_heads = [jnp.where(low, q, zero), jnp.where(low, zero, q)]
    v_heads = [jnp.where(low, v, one), jnp.where(low, one, v)]
    lane, low = lane[:chunk], low[:chunk]

    def score(step):
        c, h = divmod(step, 2)
        score_ref[step % 2] = lax.dot_general(
            q_heads[h][c * chunk : (c + 1) * chunk], k, NT, preferred_element_type=F32
        )

    def soften(step):
        c, h = divmod(step, 2)
        tops = []
        for at in range(0, chunk, TILE):
            rows = slice(c * chunk + at, c * chunk + at + TILE)
            s = score_ref[step % 2, at : at + TILE, :] + bias_ref[rows, :]
            top = jnp.max(s, axis=1, keepdims=True)
            expo_ref[step % 2, at : at + TILE, :] = jnp.exp(s - top).astype(BF16)
            tops.append(top)
        return jnp.concatenate(tops, 0)

    def mix(step):
        return jnp.dot(expo_ref[step % 2], v_heads[step % 2], preferred_element_type=F32)

    def finish(c, got, tops):
        rows = slice(c * chunk, (c + 1) * chunk)
        total = jnp.where(low, got[1], got[0])
        mixed = jnp.where(low, got[0], got[1]) / pltpu.roll(total, HD, 1)
        log = jnp.log(total)
        stat = stat_ref[rows, :]
        stat = jnp.where(lane == 2 * pair, tops[0] + log[:, HD : HD + 1], stat)
        stat_ref[rows, :] = jnp.where(lane == 2 * pair + 1, tops[1] + log[:, :1], stat)
        part, at = divmod(c * chunk, half)
        out_refs[part][0, at : at + chunk, :] = mixed.astype(BF16)

    steps = 2 * length // chunk
    tops, got = [], []
    score(0)
    for step in range(steps):
        if step + 1 < steps:
            score(step + 1)
        tops.append(soften(step))
        got.append(mix(step))
        if step % 2:
            finish(step // 2, got[-2:], tops[-2:])

    @pl.when(pair == pl.num_programs(1) - 1)
    def _():
        lse_ref[0] = jnp.transpose(stat_ref[...])[: lse_ref.shape[1]]


def attend_back_kernel(first_pair, after, *refs):
    seg_row_ref, seg_col_ref, qkv_ref, out_a, out_b, grad_a, grad_b, lse_ref = refs[:8]
    dqkv_ref, sums_ref, bias_ref, ds_ref, score_ref, slope_ref, prob_ref = refs[8 + after :]
    pair = pl.program_id(1)
    length = bias_ref.shape[0]
    half = qkv_ref.shape[2]
    chunk = score_ref.shape[1]

    @pl.when(pair == 0)
    def _():
        bias_ref[...] = jnp.where(seg_col_ref[0] == seg_row_ref[0], 0.0, MASKED)

    @pl.when((pair == 0) & (pl.program_id(0) == 0))
    def _():
        sums_ref[...] = jnp.zeros_like(sums_ref)

    block = qkv_ref[:, 0].reshape(length, 3 * PAIR)
    q, k, v = (block[:, i * PAIR : (i + 1) * PAIR] for i in range(3))
    out = jnp.concatenate([out_a[0], out_b[0]], 0)
    grad = jnp.concatenate([grad_a[0], grad_b[0]], 0)
    low = lax.broadcasted_iota(jnp.int32, (length, PAIR), 1) < HD
    zero = jnp.zeros_like(q)
    heads = lambda array: [jnp.where(low, array, zero), jnp.where(low, zero, array)]
    q_heads, k_heads, g_heads = heads(q), heads(k), heads(grad)
    product = jnp.transpose(out.astype(F32) * grad.astype(F32))
    chunks = length // chunk
    deltas = [total_rows(product[h * HD : (h + 1) * HD]) for h in range(2)]
    stats = [lse_ref[0, pl.ds(2 * (first_pair + pair) + h, 1), :] for h in range(2)]

    def score(step):
        h, c = divmod(step, chunks)
        rows = slice(c * chunk, (c + 1) * chunk)
        score_ref[step % 2] = lax.dot_general(k[rows], q_heads[h], NT, preferred_element_type=F32)
        slope_ref[step % 2] = lax.dot_general(v[rows], g_heads[h], NT, preferred_element_type=F32)

    def bend(step):
        h, c = divmod(step, chunks)
        for at in range(0, chunk, TILE):
            rows = slice(c * chunk + at, c * chunk + at + TILE)
            part = slice(at, at + TILE)
            p = jnp.exp(score_ref[step % 2, part, :] + bias_ref[rows, :] - stats[h])
            prob_ref[step % 2, part, :] = p.astype(BF16)
            ds_ref[h, rows, :] = (p * (slope_ref[step % 2, part, :] - deltas[h])).astype(BF16)

    steps = 2 * chunks
    dk, dv = [None] * chunks, [None] * chunks
    dq = None
    score(0)
    for step in range(steps):
        h, c = divmod(step, chunks)
        if step + 1 < steps:
            score(step + 1)
        bend(step)
        rows = slice(c * chunk, (c + 1) * chunk)
        v_part = jnp.dot(prob_ref[step % 2], g_heads[h], preferred_element_type=F32)
        k_part = jnp.dot(ds_ref[h, rows, :], q_heads[h], preferred_element_type=F32)
        if h == 0:
            dk[c], dv[c] = k_part, v_part
        else:
            part, at = c * chunk // half, c * chunk % half
            dqkv_ref[part, 0, at : at + chunk, PAIR : 2 * PAIR] = (dk[c] + k_part).astype(BF16)
            dv[c] = (dv[c] + v_part).astype(BF16)
            dqkv_ref[part, 0, at : at + chunk, 2 * PAIR :] = dv[c]
        if c == chunks - 1:
            part = lax.dot_general(ds_ref[h], k_heads[h], TN, preferred_element_type=F32)
            dq = part if h == 0 else dq + part
    dq = (dq * HD**-0.5).astype(BF16)
    dqkv_ref[:, 0, :, :PAIR] = dq.reshape(-1, half, PAIR)
    sums = [total_rows(dq.astype(F32)), sum(total_rows(part.astype(F32)) for part in dv)]
    sums_ref[0:1, pl.ds(pl.multiple_of(pair * PAIR, PAIR), PAIR)] += sums[0]
    sums_ref[1:2, pl.ds(pl.multiple_of(pair * PAIR, PAIR), PAIR)] += sums[1]


def attention_call(
    kernel, seg, arrays, pairs, outs, scratch, name, first=0, after=(), seqs=None, held=()
):
    parts, count, half, columns = arrays[0].shape
    start, seqs = seqs or (0, count)
    micros = 6.5 * seqs if name == "attend" else 3.7 * seqs
    length = parts * half

    def spec(array, first):
        shape = array.shape
        if len(shape) == 4:
            return pl.BlockSpec(
                (parts, 1, half, 3 * PAIR), lambda s, p: (0, start + s, 0, first + p)
            )
        if len(shape) == 3 and shape[1] == half:
            return pl.BlockSpec((1, half, PAIR), lambda s, p: (start + s, 0, first + p))
        if len(shape) == 3:
            return pl.BlockSpec((1,) + shape[1:], lambda s, p: (start + s, 0, 0))
        return pl.BlockSpec(shape, lambda s, p: (0, 0))

    operands = [seg[:, None, :], seg[:, :, None]] + arrays
    return pl.pallas_call(
        kernel,
        grid=(seqs, pairs),
        in_specs=[spec(a, first) for a in operands]
        + [pl.BlockSpec(memory_space=pl.ANY)] * (len(held) + len(after)),
        out_specs=[spec(a, 0) for a in outs],
        out_shape=outs,
        scratch_shapes=scratch(length),
        input_output_aliases={len(operands) + n: n for n in range(len(held))},
        compiler_params=pltpu.CompilerParams(vmem_limit_bytes=SMALL_VMEM),
        cost_estimate=weight_of(micros),
        name=name,
    )(*operands, *held, *after)


def attend(qkv, seg, seqs, held, after):
    parts, count, half, columns = qkv.shape
    pairs = columns // (3 * PAIR)
    outs = [
        jax.ShapeDtypeStruct((count, half, columns // 3), BF16),
        jax.ShapeDtypeStruct((count, half, columns // 3), BF16),
        jax.ShapeDtypeStruct((count, 2 * pairs, parts * half), F32),
    ]
    scratch = lambda length: [
        pltpu.VMEM((length, length), F32),
        pltpu.VMEM((length, PAIR), F32),
        pltpu.VMEM((2, 128, length), F32),
        pltpu.VMEM((2, 128, length), BF16),
    ]
    kernel = functools.partial(attend_kernel, len(held) + len(after))
    return attention_call(
        kernel, seg, [qkv], pairs, outs, scratch, "attend", 0, after, seqs, held
    )


def attend_back(qkv, seg, out, grad, lse, first, pairs, after):
    outs = [
        jax.ShapeDtypeStruct(qkv.shape[:3] + (3 * PAIR * pairs,), BF16),
        jax.ShapeDtypeStruct((8, PAIR * pairs), F32),
    ]
    scratch = lambda length: [
        pltpu.VMEM((length, length), F32),
        pltpu.VMEM((2, length, length), BF16),
        pltpu.VMEM((2, 128, length), F32),
        pltpu.VMEM((2, 128, length), F32),
        pltpu.VMEM((2, 128, length), BF16),
    ]
    kernel = functools.partial(attend_back_kernel, first, len(after))
    arrays = [qkv, *out, *grad, lse]
    return attention_call(kernel, seg, arrays, pairs, outs, scratch, "attend_back", first, after)


def body(
    layer_input,
    segment_ids,
    out_cotangent,
    attn_master,
    inner_master,
    outer_master,
    vector_master,
    attn_moment,
    inner_moment,
    outer_moment,
    vector_moment,
    attn_square,
    inner_square,
    outer_square,
    vector_square,
):
    seqs, half, width = layer_input.shape
    count = seqs * half
    hidden_units = inner_master.shape[1]
    pairs = width // (2 * PAIR)
    part_cols = width // 2
    shards = lax.axis_size("shard")
    owned_rows = attn_master.shape[1]
    core = lax.axis_index("ctx")
    first = core == 0

    def own_half(array, axis):
        size = array.shape[axis] // 2
        return lax.dynamic_slice_in_dim(array, core * size, size, axis)

    def other_half(array, axis):
        size = array.shape[axis] // 2
        return lax.dynamic_slice_in_dim(array, (1 - core) * size, size, axis)

    def in_order(mine, theirs, axis):
        return jnp.concatenate(
            [jnp.where(first, mine, theirs), jnp.where(first, theirs, mine)], axis
        )

    rows = layer_input.reshape(count, width)
    rows_theirs = swap_cores(rows)
    square = is_square()
    o, i, y, inner = position()
    where = jnp.stack([o, i, y, core]).astype(jnp.int32)

    piece = own_half(attn_master[:3], 2).astype(BF16).reshape(3, owned_rows, pairs, PAIR)
    piece = piece.transpose(1, 2, 0, 3).reshape(owned_rows, 3 * part_cols)
    vec_low = vector_master.astype(BF16)
    rider = vec_low[:2].reshape(1, -1)
    if square:
        piece = lax.dynamic_slice_in_dim(piece, y * (piece.shape[1] // 2), piece.shape[1] // 2, 1)
    rider = jnp.pad(rider, ((0, 15), (0, piece.shape[1] - rider.shape[1])))
    piece = jnp.concatenate([piece, rider], 0)

    def every_row(block):
        size = block.shape[0] // (lax.axis_size("replica") * 2)
        part = lax.dynamic_slice_in_dim(block, (2 * y + core) * size, size, 0)
        return lax.all_gather(part.astype(BF16), EVERY, axis=0, tiled=True)

    def placed(found, slots):
        chosen = jnp.stack([place[0] for place in slots[:shards]])
        chosen = (jnp.arange(shards)[:, None] == chosen[None, :]).astype(F32)
        return jnp.einsum("ps,srw->rpw", chosen, found.astype(F32)).reshape(-1, width)

    outer_w = every_row(outer_master)
    if square:
        q = 2 * core + y
        vec_rows = jnp.pad(vec_low.reshape(-1), (0, 16 * width - vec_low.size)).reshape(16, width)
        quarter = jnp.concatenate(
            [
                lax.dynamic_slice_in_dim(inner_master, q * width, width, 1).astype(BF16),
                lax.dynamic_slice_in_dim(
                    attn_master[3], q * (owned_rows // 4), owned_rows // 4, 0
                ).astype(BF16),
                vec_rows,
            ],
            0,
        )
        line = jnp.stack([piece] + [shift_outer(piece, -k) for k in range(1, OUTER)])
        near_x, near_y = shift_inner(line, 1), shift_replica(line, 1)
        (quarter,) = relay(where, [quarter], (line,))
        across = swap_outer(quarter, 2)
        two = (OUTER // 2,)
        far = small_call(
            halves_kernel, where, [near_x, near_y], [two + piece.shape] * 2, (), "halves"
        )
        (pair,) = small_call(
            pair_kernel, where, [quarter, across], [two + quarter.shape], (far[0],), "pair"
        )
        stacks = [line, near_x, near_y, shift_inner(far[0], 1), shift_replica(far[1], 1)]
        places = quarter_places([lax.rem(o + k, OUTER) for k in range(OUTER)])
        other_pair = swap_outer(pair, 1)
        pair_x, pair_y = shift_inner(pair, 1), shift_replica(pair, 1)
        done = (pair,)
    else:
        stacks = [item[None] for item in ring_gather(piece)]
        places = [(owner, 0) for owner in slot_owners()]
        wide = hidden_units // width
        inner_w = every_row(inner_master).reshape(8, -1, wide, width).transpose(0, 2, 1, 3)
        slots = [inner_w.reshape(PARTS, -1, width), every_row(attn_master[3]).reshape(PARTS, -1, width)]
        slots = jnp.pad(jnp.concatenate(slots, 1), ((0, 0), (0, 16), (0, 0)))
        wide_stacks = [slots[n : n + 2] for n in range(0, PARTS, 2)]
        wide_places = [(jnp.int32(n // 4), jnp.int32(n % 4)) for n in range(PARTS)]
        vec = lax.all_gather(vec_low, "shard", axis=1, tiled=True).astype(F32)
        done = ()
    riders = jnp.concatenate([stack[:, owned_rows] for stack in stacks], 0)[:shards]
    riders = riders[:, : 2 * width // shards].reshape(shards, 2, -1)
    biases = placed(riders, places)

    halves = own_half(biases, 1).reshape(2, pairs, PAIR)
    bias = jnp.stack([halves[0], jnp.zeros_like(halves[0]), halves[1]], 1).reshape(1, -1)
    ones = jnp.ones((pairs, PAIR), F32)
    factor = jnp.stack([ones * HD**-0.5, ones, ones], 1).reshape(1, -1)
    qkv, qkv_w = project(rows, rows_theirs, stacks, places, bias, factor, done)
    qkv = qkv.reshape(2, seqs, half, 3 * part_cols)
    seg = jnp.concatenate([own_half(segment_ids, 1), other_half(segment_ids, 1)], 1)
    if square:
        (other_pair,) = relay(where, [other_pair], (qkv_w,))
        other_x, other_y = shift_inner(other_pair, 1), shift_replica(other_pair, 1)
        early = attend(qkv, seg, (0, seqs // 2), (), (other_pair,))
        relayed = relay(where, [pair_y, other_x], (early[0],))
        wide_stacks = [pair, other_pair, pair_x, other_x, pair_y, other_y]
        wide_stacks += [shift_inner(relayed[0], 1), shift_replica(relayed[1], 1)]
        near_rows = jnp.concatenate([a[:, 160:162] for a in wide_stacks[:4]], 0)
        near_rows = near_rows.reshape(shards, -1)[:, : vec_low.size]
        wide_stacks += [swap_cores(a) for a in wide_stacks]
        both = line_order(o)
        places = quarter_places(both[0] + both[1])
        vec = placed(near_rows.reshape((shards,) + vec_low.shape), places)
        wide_places = [(row, 2 * core + side) for row, side in places]
        wide_places += [(row, 2 * (1 - core) + side) for row, side in places]
    else:
        early = attend(qkv, seg, (0, seqs // 2), (), ())
    mixed_mine, mixed_sent, lse = attend(qkv, seg, (seqs // 2, seqs - seqs // 2), early, ())
    flat = lambda array: array.reshape(count, part_cols)
    deep = lambda array: array.reshape(seqs, half, part_cols)
    heads_mine, heads_theirs = flat(mixed_mine), swap_cores(flat(mixed_sent))

    cotan = out_cotangent.reshape(count, width)
    core_at = jnp.full((1,), core, jnp.int32)
    active, slope, inner_w, hidden_low, normed, scale, result, ffn_grad, out_w, sums_two = ffn(
        core_at, wide_places, heads_mine, heads_theirs, rows, cotan, vec, outer_w, wide_stacks
    )

    by_shard = lambda array: array.reshape(shards, -1, array.shape[1])

    outer_sent = product(where, [active], ffn_grad, 0)
    outer_kept = product(where, [active], ffn_grad, 1, (outer_sent,))
    outer_chips = [by_shard(outer_kept), by_shard(swap_cores(outer_sent))]
    done = (outer_kept,)
    if square:
        outer = Sum(where, outer_chips)
        done = outer.merge()
    pre_grad, branch_grad, mine, sent, sums_one = ffn_back(
        core_at, ffn_grad, slope, normed, scale, vec, out_w, inner_w, outer_w, done[:1]
    )
    got = swap_cores(sent)
    mixed_grad = [deep(mine), deep(got)]
    done = outer.plane((pre_grad,)) if square else ()
    heads = [heads_mine, heads_theirs]
    inner_kept = product(where, [hidden_low], pre_grad, 1, done)
    done = outer.cross((inner_kept,)) if square else (inner_kept,)
    inner_sent = product(where, [hidden_low], pre_grad, 0, done)
    out_sent = product(where, heads, branch_grad, 0, (inner_sent, got), True)
    out_kept = product(where, heads, branch_grad, 1, (out_sent,), True)
    inner_chips = [by_shard(inner_kept), by_shard(swap_cores(inner_sent))]
    out_chips = [by_shard(out_kept), by_shard(swap_cores(out_sent))]

    def back(first, after):
        grad, sums = attend_back(
            qkv, seg, (mixed_mine, mixed_sent), mixed_grad, lse, first, pairs // 2, after
        )
        return grad.reshape(2 * count, -1), sums

    def vector_chip(sums_a, sums_b):
        blank = jnp.zeros((part_cols,), F32)
        ours = jnp.concatenate([sums_a, sums_b], 1)
        attn_biases = jnp.stack([in_order(ours[at], blank, 0) for at in range(2)])
        sums = [attn_biases, sums_one[2:3], sums_one[:2], sums_two[2:3], sums_two[:2]]
        sums = jnp.concatenate(sums + [sums_one[4:8]], 0)
        sums = sums.reshape(-1, shards, width // shards).transpose(1, 0, 2)
        sums = jnp.pad(sums, ((0, 0), (0, owned_rows - sums.shape[1]), (0, 0)))
        return sums.astype(BF16)

    outer_states = (outer_master, outer_moment, outer_square)
    inner_states = (inner_master, inner_moment, inner_square)
    attn_states = (attn_master, attn_moment, attn_square)
    if square:
        inner = Sum(where, inner_chips)
        done = outer.turn((out_kept,))
        done = inner.merge(done)
        grad_a, sums_a = back(0, done)
        done = outer.line((grad_a,))
        done = inner.plane(done)
        ours = by_shard(product(where, [rows, rows_theirs], grad_a, None, done))
        sum_a = Sum(where, [ours], out_chips)
        done = sum_a.merge()
        grad_b, sums_b = back(pairs // 2, done)
        done = inner.cross((grad_b,))
        done = sum_a.plane(done)
        theirs_part = input_back(grad_a, grad_b, qkv_w, (), done)
        ours = by_shard(product(where, [rows, rows_theirs], grad_b, None, (theirs_part,)))
        sum_b = Sum(where, [ours], [vector_chip(sums_a, sums_b)])
        done = sum_a.cross((ours,))
        done = sum_b.merge(done)
        outer_new = update(where, outer_states, [outer.shares], done)
        input_grad = input_back(
            grad_a, grad_b, qkv_w, (branch_grad, swap_cores(theirs_part)), (outer_new[0],)
        )
        done = sum_b.plane((input_grad,))
        done = inner.turn(done)
        done = sum_a.turn(done)
        done = sum_b.cross(done)
        done = inner.line(done)
        done = sum_b.turn(done)
        done = sum_a.line(done)
        inner_new = update(where, inner_states, [inner.shares], done)
        sum_b.line((inner_new[0],))
        attn_shares = [sum_a.shares, sum_b.shares]
        vector_shares = [
            jnp.concatenate(
                [
                    jnp.where(y == 0, sum_b.shares[at], sum_b.shares[at + 1])[0],
                    jnp.where(y == 0, sum_b.shares[at + 1], sum_b.shares[at])[0],
                ],
                0,
            )
            for at in (0, 2)
        ]
    else:
        grad_a, sums_a = back(0, ())
        grad_b, sums_b = back(pairs // 2, ())
        theirs_part = input_back(grad_a, grad_b, qkv_w, (), ())
        added = (branch_grad, swap_cores(theirs_part))
        input_grad = input_back(grad_a, grad_b, qkv_w, added, ())
        outer_new = update(where, outer_states, [sum_apart(add_low(*outer_chips))])
        inner_new = update(where, inner_states, [sum_apart(add_low(*inner_chips))])
        ours = [by_shard(product(where, [rows, rows_theirs], grad, None)) for grad in (grad_a, grad_b)]
        chip_a = jnp.concatenate([ours[0], add_low(*out_chips)], 2)
        chip_b = jnp.concatenate([ours[1], vector_chip(sums_a, sums_b)], 2)
        attn_shares = [sum_apart(chip_a), sum_apart(chip_b)]
        vector_shares = [share[0] for share in attn_shares[1]]
    attn_new = update(where, attn_states, attn_shares)
    cut = grad_b.shape[1]
    vector_sum = sum(share[: vec_low.shape[0], cut:].astype(F32) for share in vector_shares)
    vector_new = adamw(vector_sum, vector_moment, vector_square, vector_master, RATE_VECTOR)
    vector_new = vector_new + (vector_new[2].astype(BF16),)
    news = (attn_new, inner_new, outer_new, vector_new)
    updates = [[new[at] for new in news] for at in range(4)]
    return (
        result.reshape(seqs, half, width).astype(BF16),
        input_grad.reshape(seqs, half, width),
        *[item for kind in updates for item in kind],
    )


def solution(mesh):
    tokens = P(("replica", "shard"), "ctx", None)
    states = (P(None, "shard", None), P("shard", None), P("shard", None), P(None, "shard"))
    in_specs = (tokens, P(("replica", "shard"), None), tokens) + states * 3
    out_specs = (tokens, tokens) + states * 4
    return jax.shard_map(body, mesh=mesh, in_specs=in_specs, out_specs=out_specs, check_vma=False)
```

```python
import functools
import math

import jax
import jax.numpy as jnp
from jax import lax
from jax.experimental import pallas as pl
from jax.experimental.pallas import tpu as pltpu
from jax.sharding import PartitionSpec as P

HD = 64
PAIR = 2 * HD
STEP = 5
OUTER = 4
EVERY = ("shard", "replica", "ctx")

EPS_NORM = 1e-05
BETA_ONE = 0.5
BETA_TWO = 0.6
RATE_MATRIX = 0.02
RATE_VECTOR = 0.1
DECAY = 0.01
EPS_ADAM = 1e-06
MASKED = -1e30
F32 = jnp.float32
BF16 = jnp.bfloat16
PARTS = 32
TILE = 32
VMEM = 56 * 1024 * 1024
SMALL_VMEM = 16 * 1024 * 1024
GROUP = 256
NT = (((1,), (1,)), ((), ()))
TN = (((0,), (0,)), ((), ()))


def weight_of(micros):
    return pl.CostEstimate(
        flops=int(micros * 2.9e8), bytes_accessed=int(micros * 9.2e5), transcendentals=0
    )


def normalize(resid):
    centre = resid - jnp.mean(resid, -1, keepdims=True)
    scale = lax.rsqrt(jnp.mean(centre * centre, -1, keepdims=True) + EPS_NORM)
    return (centre * scale, scale)


def norm_back(grad, normed, scale):
    return scale * (
        grad
        - jnp.mean(grad, -1, keepdims=True)
        - normed * jnp.mean(grad * normed, -1, keepdims=True)
    )


def adamw(grad, moment, square, weight, rate):
    moment_new = BETA_ONE * moment + (1.0 - BETA_ONE) * grad
    square_new = BETA_TWO * square + (1.0 - BETA_TWO) * grad * grad
    stepped = (
        moment_new
        / (1.0 - BETA_ONE**STEP)
        / (jnp.sqrt(square_new / (1.0 - BETA_TWO**STEP)) + EPS_ADAM)
    )
    weight_new = weight - rate * (stepped + DECAY * weight)
    return (moment_new, square_new, weight_new)


def swap_cores(value):
    return lax.ppermute(value, "ctx", [(0, 1), (1, 0)])


def shift_outer(value, step):
    inner = lax.axis_size("shard") // OUTER
    pairs = [
        (o * inner + i, ((o + step) % OUTER) * inner + i) for o in range(OUTER) for i in range(inner)
    ]
    return lax.ppermute(value, "shard", pairs)


def shift_inner(value, step):
    inner = lax.axis_size("shard") // OUTER
    pairs = [
        (o * inner + i, o * inner + (i + step) % inner) for o in range(OUTER) for i in range(inner)
    ]
    return lax.ppermute(value, "shard", pairs)


def shift_replica(value, step):
    size = lax.axis_size("replica")
    return lax.ppermute(value, "replica", [(r, (r + step) % size) for r in range(size)])


def ring_gather(piece):
    inner = lax.axis_size("shard") // OUTER
    found = []
    held = piece
    for k in range(OUTER):
        if k:
            held = shift_outer(held, -1)
        found.append([held] + [shift_inner(held, -e) for e in range(1, inner)])
    return [item for group in found for item in group]


def slot_owners():
    inner = lax.axis_size("shard") // OUTER
    at = lax.axis_index("shard")
    o, i = at // inner, at % inner
    return [
        lax.rem(o + k, OUTER) * inner + lax.rem(i + e, inner)
        for k in range(OUTER)
        for e in range(inner)
    ]


def pick(array, index, axis):
    return lax.dynamic_index_in_dim(array, index, axis, keepdims=False)


def add_low(value, *others):
    total = value.astype(F32)
    for item in others:
        total = total + item.astype(F32)
    return total.astype(BF16)


def position():
    inner = lax.axis_size("shard") // OUTER
    at = lax.axis_index("shard")
    return at // inner, at % inner, lax.axis_index("replica"), inner


def is_square():
    return lax.axis_size("replica") == 2 and lax.axis_size("shard") == 2 * OUTER


def swap_outer(value, flip):
    inner = lax.axis_size("shard") // OUTER
    pairs = [(o * inner + i, (o ^ flip) * inner + i) for o in range(OUTER) for i in range(inner)]
    return lax.ppermute(value, "shard", pairs)


def swap_cross(value):
    return lax.ppermute(value, ("replica", "ctx"), [(a, 3 - a) for a in range(4)])


def sum_apart(chip_sum):
    o, i, y, inner = position()
    grid = chip_sum.reshape(OUTER, inner, *chip_sum.shape[1:])
    got = [shift_inner(pick(grid, lax.rem(i + e, inner), 1), e) for e in range(1, inner)]
    line = add_low(pick(grid, i, 1), *got)
    got = [shift_outer(pick(line, lax.rem(o + d, OUTER), 0), d) for d in range(1, OUTER)]
    total = add_low(pick(line, o, 0), *got)
    got = [shift_replica(total, r) for r in range(1, lax.axis_size("replica"))]
    mine = add_low(total, *got)[None]
    return [mine, swap_cores(mine)]


def small_call(kernel, where, ins, outs, after, name):
    held = pl.BlockSpec(memory_space=pltpu.VMEM)
    return pl.pallas_call(
        functools.partial(kernel, len(ins), len(after)),
        in_specs=[pl.BlockSpec(memory_space=pltpu.SMEM)]
        + [held] * len(ins)
        + [pl.BlockSpec(memory_space=pl.ANY)] * len(after),
        out_specs=[held] * len(outs),
        out_shape=[pltpu.VMEM(shape, BF16) for shape in outs],
        compiler_params=pltpu.CompilerParams(vmem_limit_bytes=SMALL_VMEM),
        cost_estimate=weight_of(1),
        name=name,
    )(where, *[pltpu.with_memory_space_constraint(a, pltpu.VMEM) for a in ins], *after)


def fold_plane_kernel(count, after, where_ref, keep_p, got_p, keep_q, got_q, *rest):
    i, y = where_ref[1], where_ref[2]
    kept_p, send_p, kept_q, send_q = rest[after:]
    for o in range(OUTER):
        for out, at in ((kept_p, y), (send_p, 1 - y)):
            out[o] = add_low(keep_p[o, at], got_p[o, at])
        for out, at in ((kept_q, i), (send_q, 1 - i)):
            out[o] = add_low(keep_q[o, at], got_q[o, at])


def line_order(o):
    near = o + 1 - 2 * lax.rem(o, 2)
    far = lambda at: lax.rem(at + 2, OUTER)
    return (o, far(o)), (near, far(near))


def fold_cross_kernel(count, after, where_ref, keep_p, got_p, keep_q, got_q, *rest):
    for out, order in zip(rest[after:], line_order(where_ref[0])):
        for n, at in enumerate(order):
            out[n, 0] = add_low(keep_p[at], got_p[at])
            out[n, 1] = add_low(keep_q[at], got_q[at])


def fold_turn_kernel(count, after, where_ref, keep, got, *rest):
    for n, out in enumerate(rest[after:]):
        out[...] = add_low(keep[n], got[n])


def fold_line_kernel(count, after, where_ref, *rest):
    rest[count + after][...] = add_low(*(ref[...] for ref in rest[:count]))


def merge_kernel(groups, after, where_ref, *refs):
    outs = refs[4 * sum(groups) + after :]
    for slot, out in enumerate(outs):
        left = chip = 0
        for group in groups:
            for at in range(2):
                parts = []
                for n in range(chip, chip + group):
                    ref = refs[4 * n + slot]
                    parts.append(ref[0, at, 0, 0] if slot % 2 else ref[0, 0, 0, at])
                cut = slice(left, left + parts[0].shape[1])
                out[0, at, :, cut] = parts[0] if group == 1 else add_low(*parts)
            left, chip = cut.stop, chip + group


class Sum:
    def __init__(self, where, *groups):
        self.where, self.rows = where, groups[0][0].shape[1] // 4
        self.columns = sum(group[0].shape[2] for group in groups)
        self.groups = [len(group) for group in groups]
        self.chips = [
            c.reshape(OUTER, 2, 2, 2, self.rows, c.shape[2]) for group in groups for c in group
        ]

    def shape(self, *lead):
        return lead + (self.rows, self.columns)

    def merge(self, after=()):
        def spec(chip, lead, flip):
            def place(o, w):
                at = w[1] if lead == 0 else w[2]
                at = 1 - at if flip else at
                return (o, at, 0, 0, 0, 0) if lead == 0 else (o, 0, 1, at, 0, 0)

            return pl.BlockSpec(((1, 1, 1, 2) if lead == 0 else (1, 2, 1, 1)) + chip.shape[4:], place)

        kinds = ((0, True), (1, True), (0, False), (1, False))
        out_spec = pl.BlockSpec((1, 2, self.rows, self.columns), lambda o, w: (o, 0, 0, 0))
        *sent, keep_p, keep_q = pl.pallas_call(
            functools.partial(merge_kernel, self.groups, len(after)),
            grid_spec=pltpu.PrefetchScalarGridSpec(
                num_scalar_prefetch=1,
                grid=(OUTER,),
                in_specs=[spec(chip, *kind) for chip in self.chips for kind in kinds]
                + [pl.BlockSpec(memory_space=pl.ANY)] * len(after),
                out_specs=[out_spec] * 4,
            ),
            out_shape=[jax.ShapeDtypeStruct(self.shape(OUTER, 2), BF16)] * 4,
            compiler_params=pltpu.CompilerParams(vmem_limit_bytes=SMALL_VMEM),
            cost_estimate=weight_of(4),
            name="merge",
        )(self.where, *[chip for chip in self.chips for _ in range(4)], *after)
        self.kept = [keep_p, shift_inner(sent[0], 1), keep_q, shift_replica(sent[1], 1)]
        return tuple(sent)

    def plane(self, after=()):
        keep_p, send_p, keep_q, send_q = small_call(
            fold_plane_kernel, self.where, self.kept, [self.shape(OUTER)] * 4, after, "fold_plane"
        )
        self.kept = [keep_p, shift_replica(send_p, 1), keep_q, shift_inner(send_q, 1)]
        return (send_p, send_q)

    def cross(self, after=()):
        keep, send = small_call(
            fold_cross_kernel, self.where, self.kept, [self.shape(2, 2)] * 2, after, "fold_cross"
        )
        self.kept = [keep, swap_outer(send, 1)]
        return (send,)

    def turn(self, after=()):
        shapes = [self.kept[0].shape[1:]] * 2
        keep, send = small_call(
            fold_turn_kernel, self.where, self.kept, shapes, after, "fold_turn"
        )
        self.kept = [keep, swap_outer(send, 2)]
        return (send,)

    def line(self, after=()):
        (total,) = small_call(
            fold_line_kernel, self.where, self.kept, [self.kept[0].shape], after, "fold_line"
        )
        self.shares = [total, shift_replica(total, 1), swap_cores(total), swap_cross(total)]
        return (total,)


def update_kernel(groups, after, where_ref, *refs):
    states, shares = refs[:3], refs[3 : 3 + sum(groups)]
    outs, grad_ref = refs[3 + sum(groups) + after : -1], refs[-1]
    rows = shares[0].shape[1]
    across = groups[0] // 2
    for core in range(2):

        @pl.when(pl.program_id(1) == core)
        def _():
            for n in range(across):
                line = where_ref[2] if n == 0 else 1 - where_ref[2]
                line = pl.ds(pl.multiple_of(line * rows, rows), rows) if across > 1 else slice(None)
                if len(groups) == 1:
                    grad_ref[line, :] = shares[across * core + n][0].astype(F32)
                    continue
                left, right = shares[across * core + n], shares[groups[0] + across * core + n]
                width = grad_ref.shape[2]
                pairs = width // PAIR
                for t in range(3):
                    for p in range(pairs):
                        side, at = (left, p) if 2 * p < pairs else (right, p - pairs // 2)
                        part = side[0, :, (3 * at + t) * PAIR : (3 * at + t + 1) * PAIR]
                        grad_ref[t, line, p * PAIR : (p + 1) * PAIR] = part.astype(F32)
                cut = 3 * PAIR * (pairs // 2)
                grad_ref[3, line, :] = left[0, :, cut : cut + width].astype(F32)

    new = adamw(grad_ref[...], states[1][...], states[2][...], states[0][...], RATE_MATRIX)
    for out, value in zip(outs, new + (new[2],)):
        out[...] = value.astype(out.dtype)


def update(where, states, groups, after=()):
    parts, rows = groups[0][0].shape[:2]
    rows = rows * (len(groups[0]) // 2)
    lead = states[0].shape[:-2]
    columns = states[0].shape[-1] // 2
    place = lambda p, v, w: (0,) * len(lead) + (p, w[3] + v - 2 * w[3] * v)
    block = pl.BlockSpec(lead + (rows, columns), place)
    shares = [share for group in groups for share in group]
    share_specs = [pl.BlockSpec((1,) + a.shape[1:], lambda p, v, w: (p, 0, 0)) for a in shares]
    kinds = (F32, F32, F32, BF16)
    return pl.pallas_call(
        functools.partial(update_kernel, [len(group) for group in groups], len(after)),
        grid_spec=pltpu.PrefetchScalarGridSpec(
            num_scalar_prefetch=1,
            grid=(parts, 2),
            in_specs=[block] * 3 + share_specs + [pl.BlockSpec(memory_space=pl.ANY)] * len(after),
            out_specs=[block] * 4,
            scratch_shapes=[pltpu.VMEM(lead + (rows, columns), F32)],
        ),
        out_shape=[jax.ShapeDtypeStruct(states[0].shape, kind) for kind in kinds],
        compiler_params=pltpu.CompilerParams(vmem_limit_bytes=SMALL_VMEM),
        cost_estimate=weight_of(5),
        name="update",
    )(where, *states, *shares, *after)


def input_back_kernel(a_ref, b_ref, left_ref, right_ref, *rest):
    out_ref = rest[-1]
    total = lax.dot_general(a_ref[...], left_ref[...], NT, preferred_element_type=F32)
    total += lax.dot_general(b_ref[...], right_ref[...], NT, preferred_element_type=F32)
    if out_ref.dtype == F32:
        total += rest[0][...].astype(F32) + rest[1][...].astype(F32)
    out_ref[...] = total.astype(out_ref.dtype)


def input_back(grad_a, grad_b, weight, added, after):
    count, cut = grad_a.shape[0] // 2, grad_a.shape[1]
    width = weight.shape[0]
    tile = width // 4
    first = 0 if added else 1
    side = pl.BlockSpec((count, cut), lambda n: (first, 0))
    line = pl.BlockSpec((count, tile), lambda n: (0, n))
    return pl.pallas_call(
        input_back_kernel,
        grid=(width // tile,),
        in_specs=[side, side]
        + [pl.BlockSpec((tile, cut), lambda n, at=at: (n, at)) for at in range(2)]
        + [line] * len(added)
        + [pl.BlockSpec(memory_space=pl.ANY)] * len(after),
        out_specs=line,
        out_shape=jax.ShapeDtypeStruct((count, width), F32 if added else BF16),
        compiler_params=pltpu.CompilerParams(vmem_limit_bytes=SMALL_VMEM),
        cost_estimate=weight_of(5),
        name="input_back",
    )(*[grad_a, grad_b, weight, weight, *added], *after)


def quarter_places(order):
    o, i, y, inner = position()
    kinds = ((i, y), (1 - i, y), (i, 1 - y), (1 - i, 1 - y))
    return [(row * 2 + across, side) for across, side in kinds for row in order]


def relay_kernel(count, after, where_ref, *rest):
    for source, out in zip(rest[:count], rest[count + after :]):
        out[...] = source[...]


def halves_kernel(count, after, where_ref, near_x, near_y, *rest):
    first, second = rest[after:]
    first[...] = near_y[: OUTER // 2]
    second[...] = near_x[OUTER // 2 :]


def pair_kernel(count, after, where_ref, own, other, *rest):
    rest[after][0] = own[...]
    rest[after][1] = other[...]


def relay(where, arrays, after):
    return small_call(relay_kernel, where, arrays, [a.shape for a in arrays], after, "relay")


def project_kernel(after, row_ref, column_ref, mine_ref, theirs_ref, bias_ref, factor_ref, *rest):
    stacks, (out_ref, weight_ref) = rest[: -2 - after], rest[-2:]
    columns = stacks[0].shape[2]
    part = weight_ref.shape[0] * weight_ref.shape[1] // columns
    part = part // sum(stack.shape[0] for stack in stacks)
    at = pl.program_id(0)

    @pl.when(at == 0)
    def _():
        slot = 0
        for stack in stacks:
            for k in range(stack.shape[0]):
                start = pl.multiple_of(row_ref[slot] * part, part)
                left = pl.multiple_of(column_ref[slot] * columns, PAIR)
                weight_ref[pl.ds(start, part), pl.ds(left, columns)] = stack[k, :part, :]
                slot += 1

    def fill(rows):
        acc = jnp.dot(rows, weight_ref[...], preferred_element_type=F32)
        out_ref[...] = ((acc + bias_ref[...]) * factor_ref[...]).astype(BF16)

    @pl.when(at < pl.num_programs(0) // 2)
    def _():
        fill(mine_ref[...])

    @pl.when(at >= pl.num_programs(0) // 2)
    def _():
        fill(theirs_ref[...])


def project(mine, theirs, stacks, places, bias, factor, after):
    count, width = mine.shape
    columns = bias.shape[1]
    tile = 512
    each = count // tile
    whole = lambda shape: pl.BlockSpec(shape, lambda m, *_: (0,) * len(shape))
    tables = [jnp.stack([p[axis] for p in places]).astype(jnp.int32) for axis in range(2)]
    return pl.pallas_call(
        functools.partial(project_kernel, len(after)),
        grid_spec=pltpu.PrefetchScalarGridSpec(
            num_scalar_prefetch=2,
            grid=(2 * each,),
            in_specs=[
                pl.BlockSpec((tile, width), lambda m, *_: (jnp.minimum(m, each - 1), 0)),
                pl.BlockSpec((tile, width), lambda m, *_: (jnp.maximum(m - each, 0), 0)),
                whole((1, columns)),
                whole((1, columns)),
            ]
            + [whole(stack.shape) for stack in stacks]
            + [pl.BlockSpec(memory_space=pl.ANY)] * len(after),
            out_specs=[
                pl.BlockSpec((tile, columns), lambda m, *_: (m, 0)),
                whole((width, columns)),
            ],
        ),
        out_shape=[jax.ShapeDtypeStruct((2 * count, columns), BF16), jax.ShapeDtypeStruct((width, columns), BF16)],
        compiler_params=pltpu.CompilerParams(vmem_limit_bytes=44 * 1024 * 1024),
        cost_estimate=weight_of(11),
        name="project",
    )(*tables, *[mine, theirs, bias, factor, *stacks], *after)


def gelu_and_slope(u):
    a = jnp.abs(u)
    d = 1.0 + (0.3275911 * 0.5**0.5) * a
    t = pl.reciprocal(d, approx=True)
    t = t * (2.0 - d * t)
    e = jnp.exp2(u * u * (-0.5 * math.log2(math.e)))
    series = (0.5 * 1.061405429) * t - 0.5 * 1.453152027
    series = series * t + 0.5 * 1.421413741
    series = series * t - 0.5 * 0.284496736
    series = series * t + 0.5 * 0.254829592
    tail = series * t * e
    active = jnp.maximum(u, 0.0) - a * tail
    below = tail - a * (e * (1.0 / math.sqrt(2.0 * math.pi)))
    return active, jnp.where(u >= 0.0, 1.0 - below, below)


def total_rows(value):
    return jnp.sum(value, axis=0, keepdims=True)


def in_parts(count, work):
    def turn(at, carry):
        work(pl.ds(pl.multiple_of(at * 128, 128), 128))
        return carry

    lax.fori_loop(0, count // 128, turn, 0)


def ffn_kernel(
    count_of,
    core_ref,
    row_ref,
    part_ref,
    mine_ref,
    theirs_ref,
    rows_ref,
    cotan_ref,
    vec_ref,
    outer_w_ref,
    *more,
):
    stacks, more = more[:count_of], more[count_of:]
    active_ref, slope_ref, inner_out_ref, hidden_ref, normed_ref, scale_ref = more[:6]
    result_ref, grad_ref, out_w_ref, sums_ref, resid, acc, pre, inner_w, sems = more[6:]
    w, last = pl.program_id(0), pl.num_programs(0) - 1
    count, width = acc.shape
    chunk = pre.shape[2]
    vec = lambda at: vec_ref[at : at + 1, :]
    half_of = lambda at: out_w_ref[pl.ds(pl.multiple_of(at * (width // 2), width // 2), width // 2), :]
    slots = [(stack, k) for stack in stacks for k in range(stack.shape[0])]
    deep = 4 * width // len(slots)
    thin = width // len(slots)

    def fetch(block):
        for slot, (stack, k) in enumerate(slots):

            @pl.when(part_ref[slot] == block)
            def _():
                start = pl.multiple_of(row_ref[slot] * deep, deep)
                pltpu.make_async_copy(
                    stack.at[k, pl.ds(0, deep), :],
                    inner_w.at[lax.rem(block, 2), pl.ds(start, deep), :],
                    sems.at[lax.rem(block, 2)],
                ).start()

    def arrived(block):
        target = inner_w.at[lax.rem(block, 2)]
        pltpu.make_async_copy(target, target, sems.at[lax.rem(block, 2)]).wait()

    @pl.when(w == 0)
    def _():
        for slot, (stack, k) in enumerate(slots):
            start = pl.multiple_of(row_ref[slot] * 4 * thin + part_ref[slot] * thin, thin)
            pltpu.make_async_copy(
                stack.at[k, pl.ds(deep, thin), :], out_w_ref.at[pl.ds(start, thin), :], sems.at[2]
            ).start()
        fetch(w)
        pltpu.make_async_copy(out_w_ref, out_w_ref, sems.at[2]).wait()
        acc[...] = jnp.dot(mine_ref[...], half_of(core_ref[0]), preferred_element_type=F32)
        acc[...] += jnp.dot(theirs_ref[...], half_of(1 - core_ref[0]), preferred_element_type=F32)

        def enter(part):
            normed, scale = normalize(acc[part, :] + vec(2) + rows_ref[part, :].astype(F32))
            normed_ref[part, :] = normed.astype(BF16)
            scale_ref[part, :] = scale
            hidden = normed * vec(3) + vec(4)
            resid[part, :] = hidden + vec(5)
            hidden_ref[part, :] = hidden.astype(BF16)

        in_parts(count, enter)

    arrived(w)

    @pl.when(w < last)
    def _():
        fetch(w + 1)

    now = lax.rem(w, 2)
    inner_out_ref[...] = inner_w[now]
    bias = vec_ref[pl.ds(8 + w, 1), :]

    def expand(n):
        cut = slice(n * chunk, (n + 1) * chunk)
        weight = inner_w[now, :, cut]
        pre[n % 2] = jnp.dot(hidden_ref[...], weight, preferred_element_type=F32)

    def bend(n):
        cut = slice(n * chunk, (n + 1) * chunk)
        for at in range(0, count, TILE):
            part = slice(at, at + TILE)
            active, slope = gelu_and_slope(pre[n % 2, part, :] + bias[:, cut])
            active_ref[part, cut] = active.astype(BF16)
            slope_ref[part, cut] = slope.astype(BF16)

    chunks = width // chunk
    expand(0)
    for n in range(1, chunks):
        expand(n)
        bend(n - 1)
    bend(chunks - 1)

    def contract():
        weight = outer_w_ref[...]
        return jnp.dot(active_ref[...], weight, preferred_element_type=F32)

    @pl.when(w == 0)
    def _():
        acc[...] = contract()

    @pl.when(w > 0)
    def _():
        acc[...] += contract()

    @pl.when(w == last)
    def _():
        sums_ref[...] = jnp.zeros_like(sums_ref)

        def leave(part):
            normed, scale = normalize(resid[part, :] + acc[part, :])
            result_ref[part, :] = (normed * vec(6) + vec(7)).astype(BF16)
            cotan = cotan_ref[part, :].astype(F32)
            grad = norm_back(cotan * vec(6), normed, scale).astype(BF16)
            grad_ref[part, :] = grad
            sums_ref[0:1, :] += total_rows(cotan * normed)
            sums_ref[1:2, :] += total_rows(cotan)
            sums_ref[2:3, :] += total_rows(grad.astype(F32))

        in_parts(count, leave)


def ffn_back_kernel(
    core_ref,
    grad_ref,
    slope_ref,
    normed_ref,
    scale_ref,
    vec_ref,
    out_w_ref,
    inner_w_ref,
    outer_w_ref,
    after_ref,
    pre_grad_ref,
    branch_ref,
    mine_ref,
    theirs_ref,
    sums_ref,
    acc,
    pre,
):
    w = pl.program_id(0)
    count, width = acc.shape
    chunk = pre.shape[2]
    vec = lambda at: vec_ref[at : at + 1, :]

    @pl.when(w == 0)
    def _():
        sums_ref[...] = jnp.zeros_like(sums_ref)

    def pull(n):
        weight = outer_w_ref[n * chunk : (n + 1) * chunk, :]
        pre[n % 2] = lax.dot_general(grad_ref[...], weight, NT, preferred_element_type=F32)

    def bend(n):
        cut = slice(n * chunk, (n + 1) * chunk)
        sums = jnp.zeros((8, chunk), F32)
        for at in range(0, count, TILE):
            part = slice(at, at + TILE)
            back = pre[n % 2, part, :].astype(BF16).astype(F32) * slope_ref[part, cut].astype(F32)
            back = back.astype(BF16)
            pre_grad_ref[part, cut] = back
            sums += jnp.sum(back.astype(F32).reshape(TILE // 8, 8, chunk), axis=0)
        sums_ref[pl.ds(4 + w, 1), cut] += total_rows(sums)

    chunks = width // chunk
    pull(0)
    for n in range(1, chunks):
        pull(n)
        bend(n - 1)
    bend(chunks - 1)

    def contract():
        weight = inner_w_ref[...]
        return lax.dot_general(pre_grad_ref[...], weight, NT, preferred_element_type=F32)

    @pl.when(w == 0)
    def _():
        acc[...] = contract()

    @pl.when(w > 0)
    def _():
        acc[...] += contract()

    @pl.when(w == pl.num_programs(0) - 1)
    def _():
        def leave(part):
            through = acc[part, :].astype(BF16).astype(F32) + grad_ref[part, :].astype(F32)
            normed = normed_ref[part, :].astype(F32)
            branch = norm_back(through * vec(3), normed, scale_ref[part, :]).astype(BF16)
            branch_ref[part, :] = branch
            sums_ref[0:1, :] += total_rows(through * normed)
            sums_ref[1:2, :] += total_rows(through)
            sums_ref[2:3, :] += total_rows(branch.astype(F32))

        in_parts(count, leave)
        part = width // 2
        for out, at in ((mine_ref, core_ref[0]), (theirs_ref, 1 - core_ref[0])):
            weight = out_w_ref[pl.ds(pl.multiple_of(at * part, part), part), :]
            out[...] = lax.dot_general(
                branch_ref[...], weight, NT, preferred_element_type=F32
            ).astype(BF16)


def ffn_call(kernel, scalars, ins, outer_w, anys, outs, scratch, room, name):
    width = outer_w.shape[1]
    steps = outer_w.shape[0] // width

    def spec(shape):
        if shape[1] == steps * width:
            return pl.BlockSpec((shape[0], width), lambda w: (0, w))
        if shape[0] == steps * width:
            return pl.BlockSpec((width, width), lambda w: (w, 0))
        return pl.BlockSpec(shape, lambda w: (0, 0), pipeline_mode=pl.Buffered(1))

    held = [*ins, outer_w]
    return pl.pallas_call(
        kernel,
        grid=(steps,),
        in_specs=[pl.BlockSpec(memory_space=pltpu.SMEM)] * len(scalars)
        + [spec(a.shape) for a in held]
        + [pl.BlockSpec(memory_space=pl.ANY)] * len(anys),
        out_specs=[spec(shape) for shape, kind in outs],
        out_shape=[jax.ShapeDtypeStruct(shape, kind) for shape, kind in outs],
        scratch_shapes=scratch,
        compiler_params=pltpu.CompilerParams(vmem_limit_bytes=room * 1024 * 1024),
        cost_estimate=weight_of(40),
        name=name,
    )(*scalars, *held, *anys)


def ffn(core, places, mine, theirs, rows, cotan, vec, outer_w, stacks):
    count, width = rows.shape
    units = outer_w.shape[0]
    low = (rows.shape, BF16)
    outs = [((count, units), BF16)] * 2 + [((width, units), BF16)]
    outs += [low, low, ((count, 1), F32), low, low, ((width, width), BF16), ((8, width), F32)]
    scratch = [
        pltpu.VMEM((count, width), F32),
        pltpu.VMEM((count, width), F32),
        pltpu.VMEM((2, count, 256), F32),
        pltpu.VMEM((2, width, width), BF16),
        pltpu.SemaphoreType.DMA((3,)),
    ]
    tables = [jnp.stack([p[axis] for p in places]).astype(jnp.int32) for axis in range(2)]
    kernel = functools.partial(ffn_kernel, len(stacks))
    ins = [mine, theirs, rows, cotan, vec]
    return ffn_call(
        kernel, [core, *tables], ins, outer_w, stacks, outs, scratch, 58, "ffn"
    )


def ffn_back(core, grad, slope, normed, scale, vec, out_w, inner_w, outer_w, after):
    count, width = grad.shape
    part = ((count, width // 2), BF16)
    outs = [(slope.shape, BF16), (grad.shape, BF16), part, part, ((8, width), F32)]
    scratch = [pltpu.VMEM((count, width), F32), pltpu.VMEM((2, count, 256), F32)]
    ins = [grad, slope, normed, scale, vec, out_w, inner_w]
    return ffn_call(
        ffn_back_kernel, [core], ins, outer_w, after, outs, scratch, 44, "ffn_back"
    )


def product_kernel(count, stacked, after, where_ref, *refs):
    lefts, right_ref, out_ref = refs[:count], refs[count], refs[count + 1 + after]
    if not stacked:
        total, rows = None, lefts[0].shape[0]
        for n, left_ref in enumerate(lefts):
            right = right_ref[n * rows : (n + 1) * rows, :]
            part = lax.dot_general(left_ref[...], right, TN, preferred_element_type=F32)
            total = part if n == 0 else total + part
        out_ref[...] = total.astype(BF16)
        return
    for n, left_ref in enumerate(lefts):

        @pl.when(pl.program_id(0) == n)
        def _():
            out_ref[...] = lax.dot_general(
                left_ref[...], right_ref[...], TN, preferred_element_type=F32
            ).astype(BF16)


def product(where, lefts, right, side, after=(), stacked=False):
    width = right.shape[1] // (1 if side is None else 2)
    tile = 512
    height = sum(left.shape[1] for left in lefts) if stacked else lefts[0].shape[1]
    micros = 2e-9 * height * width * right.shape[0] + 1
    half = lambda a, w: (0, 0 if side is None else (w[3] if side else 1 - w[3]))
    if stacked:
        left_place = lambda a, w: (0, 0)
        place = lambda a, w: (a + w[3] - 2 * a * w[3], 0)
    else:
        left_place = lambda a, w: (0, a)
        place = lambda a, w: (a, 0)
    return pl.pallas_call(
        functools.partial(product_kernel, len(lefts), stacked, len(after)),
        grid_spec=pltpu.PrefetchScalarGridSpec(
            num_scalar_prefetch=1,
            grid=(height // tile,),
            in_specs=[pl.BlockSpec((left.shape[0], tile), left_place) for left in lefts]
            + [pl.BlockSpec((right.shape[0], width), half, pipeline_mode=pl.Buffered(1))]
            + [pl.BlockSpec(memory_space=pl.ANY)] * len(after),
            out_specs=pl.BlockSpec((tile, width), place),
        ),
        out_shape=jax.ShapeDtypeStruct((height, width), BF16),
        compiler_params=pltpu.CompilerParams(vmem_limit_bytes=2 * SMALL_VMEM),
        cost_estimate=weight_of(micros),
        name="product",
    )(where, *[*lefts, right], *after)


def attend_kernel(held, seg_row_ref, seg_col_ref, qkv_ref, *rest):
    rest = rest[held:]
    out_refs, (lse_ref, bias_ref, stat_ref, score_ref, expo_ref) = rest[:2], rest[2:]
    half = qkv_ref.shape[2]
    pair = pl.program_id(1)
    length = bias_ref.shape[0]
    chunk = score_ref.shape[1]

    @pl.when(pair == 0)
    def _():
        bias_ref[...] = jnp.where(seg_col_ref[0] == seg_row_ref[0], 0.0, MASKED)
        stat_ref[...] = jnp.zeros_like(stat_ref)

    block = qkv_ref[:, 0].reshape(length, 3 * PAIR)
    q, k, v = (block[:, i * PAIR : (i + 1) * PAIR] for i in range(3))
    lane = lax.broadcasted_iota(jnp.int32, (length, PAIR), 1)
    low = lane < HD
    zero, one = jnp.zeros_like(q), jnp.ones_like(v)
    q_heads = [jnp.where(low, q, zero), jnp.where(low, zero, q)]
    v_heads = [jnp.where(low, v, one), jnp.where(low, one, v)]
    lane, low = lane[:chunk], low[:chunk]

    def score(step):
        c, h = divmod(step, 2)
        score_ref[step % 2] = lax.dot_general(
            q_heads[h][c * chunk : (c + 1) * chunk], k, NT, preferred_element_type=F32
        )

    def soften(step):
        c, h = divmod(step, 2)
        tops = []
        for at in range(0, chunk, TILE):
            rows = slice(c * chunk + at, c * chunk + at + TILE)
            s = score_ref[step % 2, at : at + TILE, :] + bias_ref[rows, :]
            top = jnp.max(s, axis=1, keepdims=True)
            expo_ref[step % 2, at : at + TILE, :] = jnp.exp(s - top).astype(BF16)
            tops.append(top)
        return jnp.concatenate(tops, 0)

    def mix(step):
        return jnp.dot(expo_ref[step % 2], v_heads[step % 2], preferred_element_type=F32)

    def finish(c, got, tops):
        rows = slice(c * chunk, (c + 1) * chunk)
        total = jnp.where(low, got[1], got[0])
        mixed = jnp.where(low, got[0], got[1]) / pltpu.roll(total, HD, 1)
        log = jnp.log(total)
        stat = stat_ref[rows, :]
        stat = jnp.where(lane == 2 * pair, tops[0] + log[:, HD : HD + 1], stat)
        stat_ref[rows, :] = jnp.where(lane == 2 * pair + 1, tops[1] + log[:, :1], stat)
        part, at = divmod(c * chunk, half)
        out_refs[part][0, at : at + chunk, :] = mixed.astype(BF16)

    steps = 2 * length // chunk
    tops, got = [], []
    score(0)
    for step in range(steps):
        if step + 1 < steps:
            score(step + 1)
        tops.append(soften(step))
        got.append(mix(step))
        if step % 2:
            finish(step // 2, got[-2:], tops[-2:])

    @pl.when(pair == pl.num_programs(1) - 1)
    def _():
        lse_ref[0] = jnp.transpose(stat_ref[...])[: lse_ref.shape[1]]


def attend_back_kernel(first_pair, after, *refs):
    seg_row_ref, seg_col_ref, qkv_ref, out_a, out_b, grad_a, grad_b, lse_ref = refs[:8]
    dqkv_ref, sums_ref, bias_ref, ds_ref, score_ref, slope_ref, prob_ref = refs[8 + after :]
    pair = pl.program_id(1)
    length = bias_ref.shape[0]
    half = qkv_ref.shape[2]
    chunk = score_ref.shape[1]

    @pl.when(pair == 0)
    def _():
        bias_ref[...] = jnp.where(seg_col_ref[0] == seg_row_ref[0], 0.0, MASKED)

    @pl.when((pair == 0) & (pl.program_id(0) == 0))
    def _():
        sums_ref[...] = jnp.zeros_like(sums_ref)

    block = qkv_ref[:, 0].reshape(length, 3 * PAIR)
    q, k, v = (block[:, i * PAIR : (i + 1) * PAIR] for i in range(3))
    out = jnp.concatenate([out_a[0], out_b[0]], 0)
    grad = jnp.concatenate([grad_a[0], grad_b[0]], 0)
    low = lax.broadcasted_iota(jnp.int32, (length, PAIR), 1) < HD
    zero = jnp.zeros_like(q)
    heads = lambda array: [jnp.where(low, array, zero), jnp.where(low, zero, array)]
    q_heads, k_heads, g_heads = heads(q), heads(k), heads(grad)
    product = jnp.transpose(out.astype(F32) * grad.astype(F32))
    chunks = length // chunk
    deltas = [total_rows(product[h * HD : (h + 1) * HD]) for h in range(2)]
    stats = [lse_ref[0, pl.ds(2 * (first_pair + pair) + h, 1), :] for h in range(2)]

    def score(step):
        h, c = divmod(step, chunks)
        rows = slice(c * chunk, (c + 1) * chunk)
        score_ref[step % 2] = lax.dot_general(k[rows], q_heads[h], NT, preferred_element_type=F32)
        slope_ref[step % 2] = lax.dot_general(v[rows], g_heads[h], NT, preferred_element_type=F32)

    def bend(step):
        h, c = divmod(step, chunks)
        for at in range(0, chunk, TILE):
            rows = slice(c * chunk + at, c * chunk + at + TILE)
            part = slice(at, at + TILE)
            p = jnp.exp(score_ref[step % 2, part, :] + bias_ref[rows, :] - stats[h])
            prob_ref[step % 2, part, :] = p.astype(BF16)
            ds_ref[h, rows, :] = (p * (slope_ref[step % 2, part, :] - deltas[h])).astype(BF16)

    steps = 2 * chunks
    dk, dv = [None] * chunks, [None] * chunks
    dq = None
    score(0)
    for step in range(steps):
        h, c = divmod(step, chunks)
        if step + 1 < steps:
            score(step + 1)
        bend(step)
        rows = slice(c * chunk, (c + 1) * chunk)
        v_part = jnp.dot(prob_ref[step % 2], g_heads[h], preferred_element_type=F32)
        k_part = jnp.dot(ds_ref[h, rows, :], q_heads[h], preferred_element_type=F32)
        if h == 0:
            dk[c], dv[c] = k_part, v_part
        else:
            part, at = c * chunk // half, c * chunk % half
            dqkv_ref[part, 0, at : at + chunk, PAIR : 2 * PAIR] = (dk[c] + k_part).astype(BF16)
            dv[c] = (dv[c] + v_part).astype(BF16)
            dqkv_ref[part, 0, at : at + chunk, 2 * PAIR :] = dv[c]
        if c == chunks - 1:
            part = lax.dot_general(ds_ref[h], k_heads[h], TN, preferred_element_type=F32)
            dq = part if h == 0 else dq + part
    dq = (dq * HD**-0.5).astype(BF16)
    dqkv_ref[:, 0, :, :PAIR] = dq.reshape(-1, half, PAIR)
    sums = [total_rows(dq.astype(F32)), sum(total_rows(part.astype(F32)) for part in dv)]
    sums_ref[0:1, pl.ds(pl.multiple_of(pair * PAIR, PAIR), PAIR)] += sums[0]
    sums_ref[1:2, pl.ds(pl.multiple_of(pair * PAIR, PAIR), PAIR)] += sums[1]


def attention_call(
    kernel, seg, arrays, pairs, outs, scratch, name, first=0, after=(), seqs=None, held=()
):
    parts, count, half, columns = arrays[0].shape
    start, seqs = seqs or (0, count)
    micros = 6.5 * seqs if name == "attend" else 3.7 * seqs
    length = parts * half

    def spec(array, first):
        shape = array.shape
        if len(shape) == 4:
            return pl.BlockSpec(
                (parts, 1, half, 3 * PAIR), lambda s, p: (0, start + s, 0, first + p)
            )
        if len(shape) == 3 and shape[1] == half:
            return pl.BlockSpec((1, half, PAIR), lambda s, p: (start + s, 0, first + p))
        if len(shape) == 3:
            return pl.BlockSpec((1,) + shape[1:], lambda s, p: (start + s, 0, 0))
        return pl.BlockSpec(shape, lambda s, p: (0, 0))

    operands = [seg[:, None, :], seg[:, :, None]] + arrays
    return pl.pallas_call(
        kernel,
        grid=(seqs, pairs),
        in_specs=[spec(a, first) for a in operands]
        + [pl.BlockSpec(memory_space=pl.ANY)] * (len(held) + len(after)),
        out_specs=[spec(a, 0) for a in outs],
        out_shape=outs,
        scratch_shapes=scratch(length),
        input_output_aliases={len(operands) + n: n for n in range(len(held))},
        compiler_params=pltpu.CompilerParams(vmem_limit_bytes=SMALL_VMEM),
        cost_estimate=weight_of(micros),
        name=name,
    )(*operands, *held, *after)


def attend(qkv, seg, seqs, held, after):
    parts, count, half, columns = qkv.shape
    pairs = columns // (3 * PAIR)
    outs = [
        jax.ShapeDtypeStruct((count, half, columns // 3), BF16),
        jax.ShapeDtypeStruct((count, half, columns // 3), BF16),
        jax.ShapeDtypeStruct((count, 2 * pairs, parts * half), F32),
    ]
    scratch = lambda length: [
        pltpu.VMEM((length, length), F32),
        pltpu.VMEM((length, PAIR), F32),
        pltpu.VMEM((2, 128, length), F32),
        pltpu.VMEM((2, 128, length), BF16),
    ]
    kernel = functools.partial(attend_kernel, len(held) + len(after))
    return attention_call(
        kernel, seg, [qkv], pairs, outs, scratch, "attend", 0, after, seqs, held
    )


def attend_back(qkv, seg, out, grad, lse, first, pairs, after):
    outs = [
        jax.ShapeDtypeStruct(qkv.shape[:3] + (3 * PAIR * pairs,), BF16),
        jax.ShapeDtypeStruct((8, PAIR * pairs), F32),
    ]
    scratch = lambda length: [
        pltpu.VMEM((length, length), F32),
        pltpu.VMEM((2, length, length), BF16),
        pltpu.VMEM((2, 128, length), F32),
        pltpu.VMEM((2, 128, length), F32),
        pltpu.VMEM((2, 128, length), BF16),
    ]
    kernel = functools.partial(attend_back_kernel, first, len(after))
    arrays = [qkv, *out, *grad, lse]
    return attention_call(kernel, seg, arrays, pairs, outs, scratch, "attend_back", first, after)


def body(
    layer_input,
    segment_ids,
    out_cotangent,
    attn_master,
    inner_master,
    outer_master,
    vector_master,
    attn_moment,
    inner_moment,
    outer_moment,
    vector_moment,
    attn_square,
    inner_square,
    outer_square,
    vector_square,
):
    seqs, half, width = layer_input.shape
    count = seqs * half
    hidden_units = inner_master.shape[1]
    pairs = width // (2 * PAIR)
    part_cols = width // 2
    shards = lax.axis_size("shard")
    owned_rows = attn_master.shape[1]
    core = lax.axis_index("ctx")
    first = core == 0

    def own_half(array, axis):
        size = array.shape[axis] // 2
        return lax.dynamic_slice_in_dim(array, core * size, size, axis)

    def other_half(array, axis):
        size = array.shape[axis] // 2
        return lax.dynamic_slice_in_dim(array, (1 - core) * size, size, axis)

    def in_order(mine, theirs, axis):
        return jnp.concatenate(
            [jnp.where(first, mine, theirs), jnp.where(first, theirs, mine)], axis
        )

    rows = layer_input.reshape(count, width)
    rows_theirs = swap_cores(rows)
    square = is_square()
    o, i, y, inner = position()
    where = jnp.stack([o, i, y, core]).astype(jnp.int32)

    piece = own_half(attn_master[:3], 2).astype(BF16).reshape(3, owned_rows, pairs, PAIR)
    piece = piece.transpose(1, 2, 0, 3).reshape(owned_rows, 3 * part_cols)
    vec_low = vector_master.astype(BF16)
    rider = vec_low[:2].reshape(1, -1)
    if square:
        piece = lax.dynamic_slice_in_dim(piece, y * (piece.shape[1] // 2), piece.shape[1] // 2, 1)
    rider = jnp.pad(rider, ((0, 15), (0, piece.shape[1] - rider.shape[1])))
    piece = jnp.concatenate([piece, rider], 0)

    def every_row(block, after=()):
        size = block.shape[0] // (lax.axis_size("replica") * 2)
        part = lax.dynamic_slice_in_dim(block, (2 * y + core) * size, size, 0).astype(BF16)
        if after:
            (part,) = relay(where, [part], after)
        return lax.all_gather(part, EVERY, axis=0, tiled=True)

    def placed(found, slots):
        chosen = jnp.stack([place[0] for place in slots[:shards]])
        chosen = (jnp.arange(shards)[:, None] == chosen[None, :]).astype(F32)
        return jnp.einsum("ps,srw->rpw", chosen, found.astype(F32)).reshape(-1, width)

    if square:
        q = 2 * core + y
        vec_rows = jnp.pad(vec_low.reshape(-1), (0, 16 * width - vec_low.size)).reshape(16, width)
        quarter = jnp.concatenate(
            [
                lax.dynamic_slice_in_dim(inner_master, q * width, width, 1).astype(BF16),
                lax.dynamic_slice_in_dim(
                    attn_master[3], q * (owned_rows // 4), owned_rows // 4, 0
                ).astype(BF16),
                vec_rows,
            ],
            0,
        )
        line = jnp.stack([piece] + [shift_outer(piece, -k) for k in range(1, OUTER)])
        near_x, near_y = shift_inner(line, 1), shift_replica(line, 1)
        (quarter,) = relay(where, [quarter], (line,))
        across = swap_outer(quarter, 2)
        two = (OUTER // 2,)
        far = small_call(
            halves_kernel, where, [near_x, near_y], [two + piece.shape] * 2, (), "halves"
        )
        outer_w = every_row(outer_master, (far[0],))
        stacks = [line, near_x, near_y, shift_inner(far[0], 1), shift_replica(far[1], 1)]
        (pair,) = small_call(
            pair_kernel, where, [quarter, across], [two + quarter.shape], tuple(stacks[3:]), "pair"
        )
        places = quarter_places([lax.rem(o + k, OUTER) for k in range(OUTER)])
        other_pair = swap_outer(pair, 1)
        pair_x, pair_y = shift_inner(pair, 1), shift_replica(pair, 1)
        done = (pair,)
    else:
        stacks = [item[None] for item in ring_gather(piece)]
        places = [(owner, 0) for owner in slot_owners()]
        wide = hidden_units // width
        inner_w = every_row(inner_master).reshape(8, -1, wide, width).transpose(0, 2, 1, 3)
        slots = [inner_w.reshape(PARTS, -1, width), every_row(attn_master[3]).reshape(PARTS, -1, width)]
        slots = jnp.pad(jnp.concatenate(slots, 1), ((0, 0), (0, 16), (0, 0)))
        wide_stacks = [slots[n : n + 2] for n in range(0, PARTS, 2)]
        wide_places = [(jnp.int32(n // 4), jnp.int32(n % 4)) for n in range(PARTS)]
        vec = lax.all_gather(vec_low, "shard", axis=1, tiled=True).astype(F32)
        outer_w = every_row(outer_master)
        done = ()
    riders = jnp.concatenate([stack[:, owned_rows] for stack in stacks], 0)[:shards]
    riders = riders[:, : 2 * width // shards].reshape(shards, 2, -1)
    biases = placed(riders, places)

    halves = own_half(biases, 1).reshape(2, pairs, PAIR)
    bias = jnp.stack([halves[0], jnp.zeros_like(halves[0]), halves[1]], 1).reshape(1, -1)
    ones = jnp.ones((pairs, PAIR), F32)
    factor = jnp.stack([ones * HD**-0.5, ones, ones], 1).reshape(1, -1)
    qkv, qkv_w = project(rows, rows_theirs, stacks, places, bias, factor, done)
    qkv = qkv.reshape(2, seqs, half, 3 * part_cols)
    seg = jnp.concatenate([own_half(segment_ids, 1), other_half(segment_ids, 1)], 1)
    if square:
        (other_pair,) = relay(where, [other_pair], (qkv_w,))
        other_x, other_y = shift_inner(other_pair, 1), shift_replica(other_pair, 1)
        early = attend(qkv, seg, (0, seqs // 2), (), (other_pair,))
        relayed = relay(where, [pair_y, other_x], (early[0],))
        wide_stacks = [pair, other_pair, pair_x, other_x, pair_y, other_y]
        wide_stacks += [shift_inner(relayed[0], 1), shift_replica(relayed[1], 1)]
        near_rows = jnp.concatenate([a[:, 160:162] for a in wide_stacks[:4]], 0)
        near_rows = near_rows.reshape(shards, -1)[:, : vec_low.size]
        wide_stacks += [swap_cores(a) for a in wide_stacks]
        both = line_order(o)
        places = quarter_places(both[0] + both[1])
        vec = placed(near_rows.reshape((shards,) + vec_low.shape), places)
        wide_places = [(row, 2 * core + side) for row, side in places]
        wide_places += [(row, 2 * (1 - core) + side) for row, side in places]
    else:
        early = attend(qkv, seg, (0, seqs // 2), (), ())
    mixed_mine, mixed_sent, lse = attend(qkv, seg, (seqs // 2, seqs - seqs // 2), early, ())
    flat = lambda array: array.reshape(count, part_cols)
    deep = lambda array: array.reshape(seqs, half, part_cols)
    heads_mine, heads_theirs = flat(mixed_mine), swap_cores(flat(mixed_sent))

    cotan = out_cotangent.reshape(count, width)
    core_at = jnp.full((1,), core, jnp.int32)
    active, slope, inner_w, hidden_low, normed, scale, result, ffn_grad, out_w, sums_two = ffn(
        core_at, wide_places, heads_mine, heads_theirs, rows, cotan, vec, outer_w, wide_stacks
    )

    by_shard = lambda array: array.reshape(shards, -1, array.shape[1])

    outer_sent = product(where, [active], ffn_grad, 0)
    outer_kept = product(where, [active], ffn_grad, 1, (outer_sent,))
    outer_chips = [by_shard(outer_kept), by_shard(swap_cores(outer_sent))]
    done = (outer_kept,)
    if square:
        outer = Sum(where, outer_chips)
        done = outer.merge()
    pre_grad, branch_grad, mine, sent, sums_one = ffn_back(
        core_at, ffn_grad, slope, normed, scale, vec, out_w, inner_w, outer_w, done[:1]
    )
    got = swap_cores(sent)
    mixed_grad = [deep(mine), deep(got)]
    done = outer.plane((pre_grad,)) if square else ()
    heads = [heads_mine, heads_theirs]
    inner_kept = product(where, [hidden_low], pre_grad, 1, done)
    done = outer.cross((inner_kept,)) if square else (inner_kept,)
    inner_sent = product(where, [hidden_low], pre_grad, 0, done)
    out_sent = product(where, heads, branch_grad, 0, (inner_sent,), True)
    out_kept = product(where, heads, branch_grad, 1, (out_sent,), True)
    inner_chips = [by_shard(inner_kept), by_shard(swap_cores(inner_sent))]
    out_chips = [by_shard(out_kept), by_shard(swap_cores(out_sent))]

    def back(first, after):
        grad, sums = attend_back(
            qkv, seg, (mixed_mine, mixed_sent), mixed_grad, lse, first, pairs // 2, after
        )
        return grad.reshape(2 * count, -1), sums

    def vector_chip(sums_a, sums_b):
        blank = jnp.zeros((part_cols,), F32)
        ours = jnp.concatenate([sums_a, sums_b], 1)
        attn_biases = jnp.stack([in_order(ours[at], blank, 0) for at in range(2)])
        sums = [attn_biases, sums_one[2:3], sums_one[:2], sums_two[2:3], sums_two[:2]]
        sums = jnp.concatenate(sums + [sums_one[4:8]], 0)
        sums = sums.reshape(-1, shards, width // shards).transpose(1, 0, 2)
        sums = jnp.pad(sums, ((0, 0), (0, owned_rows - sums.shape[1]), (0, 0)))
        return sums.astype(BF16)

    outer_states = (outer_master, outer_moment, outer_square)
    inner_states = (inner_master, inner_moment, inner_square)
    attn_states = (attn_master, attn_moment, attn_square)
    if square:
        inner = Sum(where, inner_chips)
        done = outer.turn((out_kept,))
        done = inner.merge(done)
        grad_a, sums_a = back(0, done)
        done = outer.line((grad_a,))
        ours = by_shard(product(where, [rows, rows_theirs], grad_a, None, done))
        done = inner.plane((ours,))
        sum_a = Sum(where, [ours], out_chips)
        done = sum_a.merge(done)
        grad_b, sums_b = back(pairs // 2, done)
        done = inner.cross((grad_b,))
        done = sum_a.plane(done)
        theirs_part = input_back(grad_a, grad_b, qkv_w, (), done)
        ours = by_shard(product(where, [rows, rows_theirs], grad_b, None, (theirs_part,)))
        sum_b = Sum(where, [ours], [vector_chip(sums_a, sums_b)])
        done = sum_a.cross((ours,))
        done = sum_b.merge(done)
        outer_new = update(where, outer_states, [outer.shares], done)
        input_grad = input_back(
            grad_a, grad_b, qkv_w, (branch_grad, swap_cores(theirs_part)), (outer_new[0],)
        )
        done = sum_b.plane((input_grad,))
        done = inner.turn(done)
        done = sum_a.turn(done)
        done = sum_b.cross(done)
        done = inner.line(done)
        done = sum_b.turn(done)
        inner_new = update(where, inner_states, [inner.shares], done)
        done = sum_a.line((inner_new[0],))
        sum_b.line(done)
        attn_shares = [sum_a.shares, sum_b.shares]
        vector_shares = [
            jnp.concatenate(
                [
                    jnp.where(y == 0, sum_b.shares[at], sum_b.shares[at + 1])[0],
                    jnp.where(y == 0, sum_b.shares[at + 1], sum_b.shares[at])[0],
                ],
                0,
            )
            for at in (0, 2)
        ]
    else:
        grad_a, sums_a = back(0, ())
        grad_b, sums_b = back(pairs // 2, ())
        theirs_part = input_back(grad_a, grad_b, qkv_w, (), ())
        added = (branch_grad, swap_cores(theirs_part))
        input_grad = input_back(grad_a, grad_b, qkv_w, added, ())
        outer_new = update(where, outer_states, [sum_apart(add_low(*outer_chips))])
        inner_new = update(where, inner_states, [sum_apart(add_low(*inner_chips))])
        ours = [by_shard(product(where, [rows, rows_theirs], grad, None)) for grad in (grad_a, grad_b)]
        chip_a = jnp.concatenate([ours[0], add_low(*out_chips)], 2)
        chip_b = jnp.concatenate([ours[1], vector_chip(sums_a, sums_b)], 2)
        attn_shares = [sum_apart(chip_a), sum_apart(chip_b)]
        vector_shares = [share[0] for share in attn_shares[1]]
    attn_new = update(where, attn_states, attn_shares)
    cut = grad_b.shape[1]
    vector_sum = sum(share[: vec_low.shape[0], cut:].astype(F32) for share in vector_shares)
    vector_new = adamw(vector_sum, vector_moment, vector_square, vector_master, RATE_VECTOR)
    vector_new = vector_new + (vector_new[2].astype(BF16),)
    news = (attn_new, inner_new, outer_new, vector_new)
    updates = [[new[at] for new in news] for at in range(4)]
    return (
        result.reshape(seqs, half, width).astype(BF16),
        input_grad.reshape(seqs, half, width),
        *[item for kind in updates for item in kind],
    )


def solution(mesh):
    tokens = P(("replica", "shard"), "ctx", None)
    states = (P(None, "shard", None), P("shard", None), P("shard", None), P(None, "shard"))
    in_specs = (tokens, P(("replica", "shard"), None), tokens) + states * 3
    out_specs = (tokens, tokens) + states * 4
    return jax.shard_map(body, mesh=mesh, in_specs=in_specs, out_specs=out_specs, check_vma=False)
```

```python
import functools
import math

import jax
import jax.numpy as jnp
from jax import lax
from jax.experimental import pallas as pl
from jax.experimental.pallas import tpu as pltpu
from jax.sharding import PartitionSpec as P

HD = 64
PAIR = 2 * HD
STEP = 5
OUTER = 4
EVERY = ("shard", "replica", "ctx")

EPS_NORM = 1e-05
BETA_ONE = 0.5
BETA_TWO = 0.6
RATE_MATRIX = 0.02
RATE_VECTOR = 0.1
DECAY = 0.01
EPS_ADAM = 1e-06
MASKED = -1e30
F32 = jnp.float32
BF16 = jnp.bfloat16
PARTS = 32
TILE = 32
VMEM = 56 * 1024 * 1024
SMALL_VMEM = 16 * 1024 * 1024
GROUP = 256
NT = (((1,), (1,)), ((), ()))
TN = (((0,), (0,)), ((), ()))


def weight_of(micros):
    return pl.CostEstimate(
        flops=int(micros * 2.9e8), bytes_accessed=int(micros * 9.2e5), transcendentals=0
    )


def normalize(resid):
    centre = resid - jnp.mean(resid, -1, keepdims=True)
    scale = lax.rsqrt(jnp.mean(centre * centre, -1, keepdims=True) + EPS_NORM)
    return (centre * scale, scale)


def norm_back(grad, normed, scale):
    return scale * (
        grad
        - jnp.mean(grad, -1, keepdims=True)
        - normed * jnp.mean(grad * normed, -1, keepdims=True)
    )


def adamw(grad, moment, square, weight, rate):
    moment_new = BETA_ONE * moment + (1.0 - BETA_ONE) * grad
    square_new = BETA_TWO * square + (1.0 - BETA_TWO) * grad * grad
    stepped = (
        moment_new
        / (1.0 - BETA_ONE**STEP)
        / (jnp.sqrt(square_new / (1.0 - BETA_TWO**STEP)) + EPS_ADAM)
    )
    weight_new = weight - rate * (stepped + DECAY * weight)
    return (moment_new, square_new, weight_new)


def swap_cores(value):
    return lax.ppermute(value, "ctx", [(0, 1), (1, 0)])


def shift_outer(value, step):
    inner = lax.axis_size("shard") // OUTER
    pairs = [
        (o * inner + i, ((o + step) % OUTER) * inner + i) for o in range(OUTER) for i in range(inner)
    ]
    return lax.ppermute(value, "shard", pairs)


def shift_inner(value, step):
    inner = lax.axis_size("shard") // OUTER
    pairs = [
        (o * inner + i, o * inner + (i + step) % inner) for o in range(OUTER) for i in range(inner)
    ]
    return lax.ppermute(value, "shard", pairs)


def shift_replica(value, step):
    size = lax.axis_size("replica")
    return lax.ppermute(value, "replica", [(r, (r + step) % size) for r in range(size)])


def ring_gather(piece):
    inner = lax.axis_size("shard") // OUTER
    found = []
    held = piece
    for k in range(OUTER):
        if k:
            held = shift_outer(held, -1)
        found.append([held] + [shift_inner(held, -e) for e in range(1, inner)])
    return [item for group in found for item in group]


def slot_owners():
    inner = lax.axis_size("shard") // OUTER
    at = lax.axis_index("shard")
    o, i = at // inner, at % inner
    return [
        lax.rem(o + k, OUTER) * inner + lax.rem(i + e, inner)
        for k in range(OUTER)
        for e in range(inner)
    ]


def pick(array, index, axis):
    return lax.dynamic_index_in_dim(array, index, axis, keepdims=False)


def add_low(value, *others):
    total = value.astype(F32)
    for item in others:
        total = total + item.astype(F32)
    return total.astype(BF16)


def position():
    inner = lax.axis_size("shard") // OUTER
    at = lax.axis_index("shard")
    return at // inner, at % inner, lax.axis_index("replica"), inner


def is_square():
    return lax.axis_size("replica") == 2 and lax.axis_size("shard") == 2 * OUTER


def swap_outer(value, flip):
    inner = lax.axis_size("shard") // OUTER
    pairs = [(o * inner + i, (o ^ flip) * inner + i) for o in range(OUTER) for i in range(inner)]
    return lax.ppermute(value, "shard", pairs)


def swap_cross(value):
    return lax.ppermute(value, ("replica", "ctx"), [(a, 3 - a) for a in range(4)])


def sum_apart(chip_sum):
    o, i, y, inner = position()
    grid = chip_sum.reshape(OUTER, inner, *chip_sum.shape[1:])
    got = [shift_inner(pick(grid, lax.rem(i + e, inner), 1), e) for e in range(1, inner)]
    line = add_low(pick(grid, i, 1), *got)
    got = [shift_outer(pick(line, lax.rem(o + d, OUTER), 0), d) for d in range(1, OUTER)]
    total = add_low(pick(line, o, 0), *got)
    got = [shift_replica(total, r) for r in range(1, lax.axis_size("replica"))]
    mine = add_low(total, *got)[None]
    return [mine, swap_cores(mine)]


def small_call(kernel, where, ins, outs, after, name):
    held = pl.BlockSpec(memory_space=pltpu.VMEM)
    return pl.pallas_call(
        functools.partial(kernel, len(ins), len(after)),
        in_specs=[pl.BlockSpec(memory_space=pltpu.SMEM)]
        + [held] * len(ins)
        + [pl.BlockSpec(memory_space=pl.ANY)] * len(after),
        out_specs=[held] * len(outs),
        out_shape=[pltpu.VMEM(shape, BF16) for shape in outs],
        compiler_params=pltpu.CompilerParams(vmem_limit_bytes=SMALL_VMEM),
        cost_estimate=weight_of(1),
        name=name,
    )(where, *[pltpu.with_memory_space_constraint(a, pltpu.VMEM) for a in ins], *after)


def fold_plane_kernel(count, after, where_ref, keep_p, got_p, keep_q, got_q, *rest):
    i, y = where_ref[1], where_ref[2]
    kept_p, send_p, kept_q, send_q = rest[after:]
    for o in range(OUTER):
        for out, at in ((kept_p, y), (send_p, 1 - y)):
            out[o] = add_low(keep_p[o, at], got_p[o, at])
        for out, at in ((kept_q, i), (send_q, 1 - i)):
            out[o] = add_low(keep_q[o, at], got_q[o, at])


def line_order(o):
    near = o + 1 - 2 * lax.rem(o, 2)
    far = lambda at: lax.rem(at + 2, OUTER)
    return (o, far(o)), (near, far(near))


def fold_cross_kernel(count, after, where_ref, keep_p, got_p, keep_q, got_q, *rest):
    for out, order in zip(rest[after:], line_order(where_ref[0])):
        for n, at in enumerate(order):
            out[n, 0] = add_low(keep_p[at], got_p[at])
            out[n, 1] = add_low(keep_q[at], got_q[at])


def fold_turn_kernel(count, after, where_ref, keep, got, *rest):
    for n, out in enumerate(rest[after:]):
        out[...] = add_low(keep[n], got[n])


def fold_line_kernel(count, after, where_ref, *rest):
    rest[count + after][...] = add_low(*(ref[...] for ref in rest[:count]))


def merge_kernel(groups, after, where_ref, *refs):
    outs = refs[4 * sum(groups) + after :]
    for slot, out in enumerate(outs):
        left = chip = 0
        for group in groups:
            for at in range(2):
                parts = []
                for n in range(chip, chip + group):
                    ref = refs[4 * n + slot]
                    parts.append(ref[0, at, 0, 0] if slot % 2 else ref[0, 0, 0, at])
                cut = slice(left, left + parts[0].shape[1])
                out[0, at, :, cut] = parts[0] if group == 1 else add_low(*parts)
            left, chip = cut.stop, chip + group


class Sum:
    def __init__(self, where, *groups):
        self.where, self.rows = where, groups[0][0].shape[1] // 4
        self.columns = sum(group[0].shape[2] for group in groups)
        self.groups = [len(group) for group in groups]
        self.chips = [
            c.reshape(OUTER, 2, 2, 2, self.rows, c.shape[2]) for group in groups for c in group
        ]

    def shape(self, *lead):
        return lead + (self.rows, self.columns)

    def merge(self, after=()):
        def spec(chip, lead, flip):
            def place(o, w):
                at = w[1] if lead == 0 else w[2]
                at = 1 - at if flip else at
                return (o, at, 0, 0, 0, 0) if lead == 0 else (o, 0, 1, at, 0, 0)

            return pl.BlockSpec(((1, 1, 1, 2) if lead == 0 else (1, 2, 1, 1)) + chip.shape[4:], place)

        kinds = ((0, True), (1, True), (0, False), (1, False))
        out_spec = pl.BlockSpec((1, 2, self.rows, self.columns), lambda o, w: (o, 0, 0, 0))
        *sent, keep_p, keep_q = pl.pallas_call(
            functools.partial(merge_kernel, self.groups, len(after)),
            grid_spec=pltpu.PrefetchScalarGridSpec(
                num_scalar_prefetch=1,
                grid=(OUTER,),
                in_specs=[spec(chip, *kind) for chip in self.chips for kind in kinds]
                + [pl.BlockSpec(memory_space=pl.ANY)] * len(after),
                out_specs=[out_spec] * 4,
            ),
            out_shape=[jax.ShapeDtypeStruct(self.shape(OUTER, 2), BF16)] * 4,
            compiler_params=pltpu.CompilerParams(vmem_limit_bytes=SMALL_VMEM),
            cost_estimate=weight_of(4),
            name="merge",
        )(self.where, *[chip for chip in self.chips for _ in range(4)], *after)
        self.kept = [keep_p, shift_inner(sent[0], 1), keep_q, shift_replica(sent[1], 1)]
        return tuple(sent)

    def plane(self, after=()):
        keep_p, send_p, keep_q, send_q = small_call(
            fold_plane_kernel, self.where, self.kept, [self.shape(OUTER)] * 4, after, "fold_plane"
        )
        self.kept = [keep_p, shift_replica(send_p, 1), keep_q, shift_inner(send_q, 1)]
        return (send_p, send_q)

    def cross(self, after=()):
        keep, send = small_call(
            fold_cross_kernel, self.where, self.kept, [self.shape(2, 2)] * 2, after, "fold_cross"
        )
        self.kept = [keep, swap_outer(send, 1)]
        return (send,)

    def turn(self, after=()):
        shapes = [self.kept[0].shape[1:]] * 2
        keep, send = small_call(
            fold_turn_kernel, self.where, self.kept, shapes, after, "fold_turn"
        )
        self.kept = [keep, swap_outer(send, 2)]
        return (send,)

    def line(self, after=()):
        (total,) = small_call(
            fold_line_kernel, self.where, self.kept, [self.kept[0].shape], after, "fold_line"
        )
        self.shares = [total, shift_replica(total, 1), swap_cores(total), swap_cross(total)]
        return (total,)


def update_kernel(groups, after, where_ref, *refs):
    states, shares = refs[:3], refs[3 : 3 + sum(groups)]
    outs, grad_ref = refs[3 + sum(groups) + after : -1], refs[-1]
    rows = shares[0].shape[1]
    across = groups[0] // 2
    for core in range(2):

        @pl.when(pl.program_id(1) == core)
        def _():
            for n in range(across):
                line = where_ref[2] if n == 0 else 1 - where_ref[2]
                line = pl.ds(pl.multiple_of(line * rows, rows), rows) if across > 1 else slice(None)
                if len(groups) == 1:
                    grad_ref[line, :] = shares[across * core + n][0].astype(F32)
                    continue
                left, right = shares[across * core + n], shares[groups[0] + across * core + n]
                width = grad_ref.shape[2]
                pairs = width // PAIR
                for t in range(3):
                    for p in range(pairs):
                        side, at = (left, p) if 2 * p < pairs else (right, p - pairs // 2)
                        part = side[0, :, (3 * at + t) * PAIR : (3 * at + t + 1) * PAIR]
                        grad_ref[t, line, p * PAIR : (p + 1) * PAIR] = part.astype(F32)
                cut = 3 * PAIR * (pairs // 2)
                grad_ref[3, line, :] = left[0, :, cut : cut + width].astype(F32)

    new = adamw(grad_ref[...], states[1][...], states[2][...], states[0][...], RATE_MATRIX)
    for out, value in zip(outs, new + (new[2],)):
        out[...] = value.astype(out.dtype)


def update(where, states, groups, after=()):
    parts, rows = groups[0][0].shape[:2]
    rows = rows * (len(groups[0]) // 2)
    lead = states[0].shape[:-2]
    columns = states[0].shape[-1] // 2
    place = lambda p, v, w: (0,) * len(lead) + (p, w[3] + v - 2 * w[3] * v)
    block = pl.BlockSpec(lead + (rows, columns), place)
    shares = [share for group in groups for share in group]
    share_specs = [pl.BlockSpec((1,) + a.shape[1:], lambda p, v, w: (p, 0, 0)) for a in shares]
    kinds = (F32, F32, F32, BF16)
    return pl.pallas_call(
        functools.partial(update_kernel, [len(group) for group in groups], len(after)),
        grid_spec=pltpu.PrefetchScalarGridSpec(
            num_scalar_prefetch=1,
            grid=(parts, 2),
            in_specs=[block] * 3 + share_specs + [pl.BlockSpec(memory_space=pl.ANY)] * len(after),
            out_specs=[block] * 4,
            scratch_shapes=[pltpu.VMEM(lead + (rows, columns), F32)],
        ),
        out_shape=[jax.ShapeDtypeStruct(states[0].shape, kind) for kind in kinds],
        compiler_params=pltpu.CompilerParams(vmem_limit_bytes=SMALL_VMEM),
        cost_estimate=weight_of(5),
        name="update",
    )(where, *states, *shares, *after)


def input_back_kernel(a_ref, b_ref, left_ref, right_ref, *rest):
    out_ref = rest[-1]
    total = lax.dot_general(a_ref[...], left_ref[...], NT, preferred_element_type=F32)
    total += lax.dot_general(b_ref[...], right_ref[...], NT, preferred_element_type=F32)
    if out_ref.dtype == F32:
        total += rest[0][...].astype(F32) + rest[1][...].astype(F32)
    out_ref[...] = total.astype(out_ref.dtype)


def input_back(grad_a, grad_b, weight, added, after):
    count, cut = grad_a.shape[0] // 2, grad_a.shape[1]
    width = weight.shape[0]
    tile = width // 4
    first = 0 if added else 1
    side = pl.BlockSpec((count, cut), lambda n: (first, 0))
    line = pl.BlockSpec((count, tile), lambda n: (0, n))
    return pl.pallas_call(
        input_back_kernel,
        grid=(width // tile,),
        in_specs=[side, side]
        + [pl.BlockSpec((tile, cut), lambda n, at=at: (n, at)) for at in range(2)]
        + [line] * len(added)
        + [pl.BlockSpec(memory_space=pl.ANY)] * len(after),
        out_specs=line,
        out_shape=jax.ShapeDtypeStruct((count, width), F32 if added else BF16),
        compiler_params=pltpu.CompilerParams(vmem_limit_bytes=SMALL_VMEM),
        cost_estimate=weight_of(5),
        name="input_back",
    )(*[grad_a, grad_b, weight, weight, *added], *after)


def quarter_places(order):
    o, i, y, inner = position()
    kinds = ((i, y), (1 - i, y), (i, 1 - y), (1 - i, 1 - y))
    return [(row * 2 + across, side) for across, side in kinds for row in order]


def relay_kernel(count, after, where_ref, *rest):
    for source, out in zip(rest[:count], rest[count + after :]):
        out[...] = source[...]


def halves_kernel(count, after, where_ref, near_x, near_y, *rest):
    first, second = rest[after:]
    first[...] = near_y[: OUTER // 2]
    second[...] = near_x[OUTER // 2 :]


def pair_kernel(count, after, where_ref, own, other, *rest):
    rest[after][0] = own[...]
    rest[after][1] = other[...]


def bulk_kernel(count, after, where_ref, *rest):
    ins, (bulk, *far) = rest[:count], rest[count + after :]
    at = 0
    for source in ins:
        bulk[at : at + source.shape[0]] = source[...]
        at += source.shape[0]
    for out, source in zip(far, (4, 3)):
        out[...] = ins[source][...]


def relay(where, arrays, after):
    return small_call(relay_kernel, where, arrays, [a.shape for a in arrays], after, "relay")


def project_kernel(after, row_ref, column_ref, mine_ref, theirs_ref, bias_ref, factor_ref, *rest):
    stacks, (out_ref, weight_ref) = rest[: -2 - after], rest[-2:]
    columns = stacks[0].shape[2]
    part = weight_ref.shape[0] * weight_ref.shape[1] // columns
    part = part // sum(stack.shape[0] for stack in stacks)
    at = pl.program_id(0)

    @pl.when(at == 0)
    def _():
        slot = 0
        for stack in stacks:
            for k in range(stack.shape[0]):
                start = pl.multiple_of(row_ref[slot] * part, part)
                left = pl.multiple_of(column_ref[slot] * columns, PAIR)
                weight_ref[pl.ds(start, part), pl.ds(left, columns)] = stack[k, :part, :]
                slot += 1

    def fill(rows):
        acc = jnp.dot(rows, weight_ref[...], preferred_element_type=F32)
        out_ref[...] = ((acc + bias_ref[...]) * factor_ref[...]).astype(BF16)

    @pl.when(at < pl.num_programs(0) // 2)
    def _():
        fill(mine_ref[...])

    @pl.when(at >= pl.num_programs(0) // 2)
    def _():
        fill(theirs_ref[...])


def project(mine, theirs, stacks, places, bias, factor, after):
    count, width = mine.shape
    columns = bias.shape[1]
    tile = 512
    each = count // tile
    whole = lambda shape: pl.BlockSpec(shape, lambda m, *_: (0,) * len(shape))
    tables = [jnp.stack([p[axis] for p in places]).astype(jnp.int32) for axis in range(2)]
    return pl.pallas_call(
        functools.partial(project_kernel, len(after)),
        grid_spec=pltpu.PrefetchScalarGridSpec(
            num_scalar_prefetch=2,
            grid=(2 * each,),
            in_specs=[
                pl.BlockSpec((tile, width), lambda m, *_: (jnp.minimum(m, each - 1), 0)),
                pl.BlockSpec((tile, width), lambda m, *_: (jnp.maximum(m - each, 0), 0)),
                whole((1, columns)),
                whole((1, columns)),
            ]
            + [whole(stack.shape) for stack in stacks]
            + [pl.BlockSpec(memory_space=pl.ANY)] * len(after),
            out_specs=[
                pl.BlockSpec((tile, columns), lambda m, *_: (m, 0)),
                whole((width, columns)),
            ],
        ),
        out_shape=[jax.ShapeDtypeStruct((2 * count, columns), BF16), jax.ShapeDtypeStruct((width, columns), BF16)],
        compiler_params=pltpu.CompilerParams(vmem_limit_bytes=44 * 1024 * 1024),
        cost_estimate=weight_of(11),
        name="project",
    )(*tables, *[mine, theirs, bias, factor, *stacks], *after)


def gelu_and_slope(u):
    a = jnp.abs(u)
    d = 1.0 + (0.3275911 * 0.5**0.5) * a
    t = pl.reciprocal(d, approx=True)
    t = t * (2.0 - d * t)
    e = jnp.exp2(u * u * (-0.5 * math.log2(math.e)))
    series = (0.5 * 1.061405429) * t - 0.5 * 1.453152027
    series = series * t + 0.5 * 1.421413741
    series = series * t - 0.5 * 0.284496736
    series = series * t + 0.5 * 0.254829592
    tail = series * t * e
    active = jnp.maximum(u, 0.0) - a * tail
    below = tail - a * (e * (1.0 / math.sqrt(2.0 * math.pi)))
    return active, jnp.where(u >= 0.0, 1.0 - below, below)


def total_rows(value):
    return jnp.sum(value, axis=0, keepdims=True)


def in_parts(count, work):
    def turn(at, carry):
        work(pl.ds(pl.multiple_of(at * 128, 128), 128))
        return carry

    lax.fori_loop(0, count // 128, turn, 0)


def ffn_kernel(
    count_of,
    core_ref,
    row_ref,
    part_ref,
    mine_ref,
    theirs_ref,
    rows_ref,
    cotan_ref,
    vec_ref,
    *more,
):
    stacks, more = more[:count_of], more[count_of:]
    active_ref, slope_ref, inner_out_ref, outer_w_ref, hidden_ref, normed_ref = more[:6]
    scale_ref, result_ref, grad_ref, out_w_ref, sums_ref, resid, acc, pre, inner_w, sems = more[6:]
    w, last = pl.program_id(0), pl.num_programs(0) - 1
    count, width = acc.shape
    chunk = pre.shape[2]
    vec = lambda at: vec_ref[at : at + 1, :]
    half_of = lambda at: out_w_ref[pl.ds(pl.multiple_of(at * (width // 2), width // 2), width // 2), :]
    slots = [(stack, k) for stack in stacks for k in range(stack.shape[0])]
    deep = 4 * width // len(slots)
    thin = width // len(slots)

    def fetch(block):
        for slot, (stack, k) in enumerate(slots):

            @pl.when(part_ref[slot] == block)
            def _():
                start = pl.multiple_of(row_ref[slot] * deep, deep)
                pltpu.make_async_copy(
                    stack.at[k, pl.ds(0, deep), :],
                    inner_w.at[lax.rem(block, 2), pl.ds(start, deep), :],
                    sems.at[lax.rem(block, 2)],
                ).start()

    def fetch_outer(block):
        for slot, (stack, k) in enumerate(slots):

            @pl.when(row_ref[slot] // 2 == block)
            def _():
                start = lax.rem(row_ref[slot], 2) * 4 * deep + part_ref[slot] * deep
                pltpu.make_async_copy(
                    stack.at[k, pl.ds(stack.shape[1] - deep, deep), :],
                    outer_w_ref.at[pl.ds(pl.multiple_of(start, deep), deep), :],
                    sems.at[3],
                ).start()

    def arrived(block):
        target = inner_w.at[lax.rem(block, 2)]
        pltpu.make_async_copy(target, target, sems.at[lax.rem(block, 2)]).wait()

    @pl.when(w == 0)
    def _():
        for slot, (stack, k) in enumerate(slots):
            start = pl.multiple_of(row_ref[slot] * 4 * thin + part_ref[slot] * thin, thin)
            pltpu.make_async_copy(
                stack.at[k, pl.ds(deep, thin), :], out_w_ref.at[pl.ds(start, thin), :], sems.at[2]
            ).start()
        fetch(w)
        pltpu.make_async_copy(out_w_ref, out_w_ref, sems.at[2]).wait()
        acc[...] = jnp.dot(mine_ref[...], half_of(core_ref[0]), preferred_element_type=F32)
        acc[...] += jnp.dot(theirs_ref[...], half_of(1 - core_ref[0]), preferred_element_type=F32)

        def enter(part):
            normed, scale = normalize(acc[part, :] + vec(2) + rows_ref[part, :].astype(F32))
            normed_ref[part, :] = normed.astype(BF16)
            scale_ref[part, :] = scale
            hidden = normed * vec(3) + vec(4)
            resid[part, :] = hidden + vec(5)
            hidden_ref[part, :] = hidden.astype(BF16)

        in_parts(count, enter)

    fetch_outer(w)
    arrived(w)

    @pl.when(w < last)
    def _():
        fetch(w + 1)

    now = lax.rem(w, 2)
    inner_out_ref[...] = inner_w[now]
    bias = vec_ref[pl.ds(8 + w, 1), :]

    def expand(n):
        cut = slice(n * chunk, (n + 1) * chunk)
        weight = inner_w[now, :, cut]
        pre[n % 2] = jnp.dot(hidden_ref[...], weight, preferred_element_type=F32)

    def bend(n):
        cut = slice(n * chunk, (n + 1) * chunk)
        for at in range(0, count, TILE):
            part = slice(at, at + TILE)
            active, slope = gelu_and_slope(pre[n % 2, part, :] + bias[:, cut])
            active_ref[part, cut] = active.astype(BF16)
            slope_ref[part, cut] = slope.astype(BF16)

    chunks = width // chunk
    expand(0)
    for n in range(1, chunks):
        expand(n)
        bend(n - 1)
    bend(chunks - 1)
    pltpu.make_async_copy(outer_w_ref, outer_w_ref, sems.at[3]).wait()

    def contract():
        weight = outer_w_ref[...]
        return jnp.dot(active_ref[...], weight, preferred_element_type=F32)

    @pl.when(w == 0)
    def _():
        acc[...] = contract()

    @pl.when(w > 0)
    def _():
        acc[...] += contract()

    @pl.when(w == last)
    def _():
        sums_ref[...] = jnp.zeros_like(sums_ref)

        def leave(part):
            normed, scale = normalize(resid[part, :] + acc[part, :])
            result_ref[part, :] = (normed * vec(6) + vec(7)).astype(BF16)
            cotan = cotan_ref[part, :].astype(F32)
            grad = norm_back(cotan * vec(6), normed, scale).astype(BF16)
            grad_ref[part, :] = grad
            sums_ref[0:1, :] += total_rows(cotan * normed)
            sums_ref[1:2, :] += total_rows(cotan)
            sums_ref[2:3, :] += total_rows(grad.astype(F32))

        in_parts(count, leave)


def ffn_back_kernel(
    core_ref,
    grad_ref,
    slope_ref,
    normed_ref,
    scale_ref,
    vec_ref,
    out_w_ref,
    inner_w_ref,
    outer_w_ref,
    after_ref,
    pre_grad_ref,
    branch_ref,
    mine_ref,
    theirs_ref,
    sums_ref,
    acc,
    pre,
):
    w = pl.program_id(0)
    count, width = acc.shape
    chunk = pre.shape[2]
    vec = lambda at: vec_ref[at : at + 1, :]

    @pl.when(w == 0)
    def _():
        sums_ref[...] = jnp.zeros_like(sums_ref)

    def pull(n):
        weight = outer_w_ref[n * chunk : (n + 1) * chunk, :]
        pre[n % 2] = lax.dot_general(grad_ref[...], weight, NT, preferred_element_type=F32)

    def bend(n):
        cut = slice(n * chunk, (n + 1) * chunk)
        sums = jnp.zeros((8, chunk), F32)
        for at in range(0, count, TILE):
            part = slice(at, at + TILE)
            back = pre[n % 2, part, :].astype(BF16).astype(F32) * slope_ref[part, cut].astype(F32)
            back = back.astype(BF16)
            pre_grad_ref[part, cut] = back
            sums += jnp.sum(back.astype(F32).reshape(TILE // 8, 8, chunk), axis=0)
        sums_ref[pl.ds(4 + w, 1), cut] += total_rows(sums)

    chunks = width // chunk
    pull(0)
    for n in range(1, chunks):
        pull(n)
        bend(n - 1)
    bend(chunks - 1)

    def contract():
        weight = inner_w_ref[...]
        return lax.dot_general(pre_grad_ref[...], weight, NT, preferred_element_type=F32)

    @pl.when(w == 0)
    def _():
        acc[...] = contract()

    @pl.when(w > 0)
    def _():
        acc[...] += contract()

    @pl.when(w == pl.num_programs(0) - 1)
    def _():
        def leave(part):
            through = acc[part, :].astype(BF16).astype(F32) + grad_ref[part, :].astype(F32)
            normed = normed_ref[part, :].astype(F32)
            branch = norm_back(through * vec(3), normed, scale_ref[part, :]).astype(BF16)
            branch_ref[part, :] = branch
            sums_ref[0:1, :] += total_rows(through * normed)
            sums_ref[1:2, :] += total_rows(through)
            sums_ref[2:3, :] += total_rows(branch.astype(F32))

        in_parts(count, leave)
        part = width // 2
        for out, at in ((mine_ref, core_ref[0]), (theirs_ref, 1 - core_ref[0])):
            weight = out_w_ref[pl.ds(pl.multiple_of(at * part, part), part), :]
            out[...] = lax.dot_general(
                branch_ref[...], weight, NT, preferred_element_type=F32
            ).astype(BF16)


def ffn_call(kernel, scalars, ins, anys, outs, scratch, width, steps, room, name):
    def spec(shape):
        if shape[1] == steps * width:
            return pl.BlockSpec((shape[0], width), lambda w: (0, w))
        if shape[0] == steps * width:
            return pl.BlockSpec((width, width), lambda w: (w, 0))
        return pl.BlockSpec(shape, lambda w: (0, 0), pipeline_mode=pl.Buffered(1))

    return pl.pallas_call(
        kernel,
        grid=(steps,),
        in_specs=[pl.BlockSpec(memory_space=pltpu.SMEM)] * len(scalars)
        + [spec(a.shape) for a in ins]
        + [pl.BlockSpec(memory_space=pl.ANY)] * len(anys),
        out_specs=[spec(shape) for shape, kind in outs],
        out_shape=[jax.ShapeDtypeStruct(shape, kind) for shape, kind in outs],
        scratch_shapes=scratch,
        compiler_params=pltpu.CompilerParams(vmem_limit_bytes=room * 1024 * 1024),
        cost_estimate=weight_of(40),
        name=name,
    )(*scalars, *ins, *anys)


def ffn(core, places, mine, theirs, rows, cotan, vec, stacks):
    count, width = rows.shape
    units = 4 * width
    low = (rows.shape, BF16)
    outs = [((count, units), BF16)] * 2 + [((width, units), BF16), ((units, width), BF16)]
    outs += [low, low, ((count, 1), F32), low, low, ((width, width), BF16), ((8, width), F32)]
    scratch = [
        pltpu.VMEM((count, width), F32),
        pltpu.VMEM((count, width), F32),
        pltpu.VMEM((2, count, 256), F32),
        pltpu.VMEM((2, width, width), BF16),
        pltpu.SemaphoreType.DMA((4,)),
    ]
    tables = [jnp.stack([p[axis] for p in places]).astype(jnp.int32) for axis in range(2)]
    kernel = functools.partial(ffn_kernel, len(stacks))
    ins = [mine, theirs, rows, cotan, vec]
    return ffn_call(kernel, [core, *tables], ins, stacks, outs, scratch, width, 4, 58, "ffn")


def ffn_back(core, grad, slope, normed, scale, vec, out_w, inner_w, outer_w, after):
    count, width = grad.shape
    part = ((count, width // 2), BF16)
    outs = [(slope.shape, BF16), (grad.shape, BF16), part, part, ((8, width), F32)]
    scratch = [pltpu.VMEM((count, width), F32), pltpu.VMEM((2, count, 256), F32)]
    ins = [grad, slope, normed, scale, vec, out_w, inner_w, outer_w]
    return ffn_call(
        ffn_back_kernel, [core], ins, after, outs, scratch, width, 4, 44, "ffn_back"
    )


def product_kernel(count, stacked, after, where_ref, *refs):
    lefts, right_ref, out_ref = refs[:count], refs[count], refs[count + 1 + after]
    if not stacked:
        total, rows = None, lefts[0].shape[0]
        for n, left_ref in enumerate(lefts):
            right = right_ref[n * rows : (n + 1) * rows, :]
            part = lax.dot_general(left_ref[...], right, TN, preferred_element_type=F32)
            total = part if n == 0 else total + part
        out_ref[...] = total.astype(BF16)
        return
    for n, left_ref in enumerate(lefts):

        @pl.when(pl.program_id(0) == n)
        def _():
            out_ref[...] = lax.dot_general(
                left_ref[...], right_ref[...], TN, preferred_element_type=F32
            ).astype(BF16)


def product(where, lefts, right, side, after=(), stacked=False):
    width = right.shape[1] // (1 if side is None else 2)
    tile = 512
    height = sum(left.shape[1] for left in lefts) if stacked else lefts[0].shape[1]
    micros = 2e-9 * height * width * right.shape[0] + 1
    half = lambda a, w: (0, 0 if side is None else (w[3] if side else 1 - w[3]))
    if stacked:
        left_place = lambda a, w: (0, 0)
        place = lambda a, w: (a + w[3] - 2 * a * w[3], 0)
    else:
        left_place = lambda a, w: (0, a)
        place = lambda a, w: (a, 0)
    return pl.pallas_call(
        functools.partial(product_kernel, len(lefts), stacked, len(after)),
        grid_spec=pltpu.PrefetchScalarGridSpec(
            num_scalar_prefetch=1,
            grid=(height // tile,),
            in_specs=[pl.BlockSpec((left.shape[0], tile), left_place) for left in lefts]
            + [pl.BlockSpec((right.shape[0], width), half, pipeline_mode=pl.Buffered(1))]
            + [pl.BlockSpec(memory_space=pl.ANY)] * len(after),
            out_specs=pl.BlockSpec((tile, width), place),
        ),
        out_shape=jax.ShapeDtypeStruct((height, width), BF16),
        compiler_params=pltpu.CompilerParams(vmem_limit_bytes=2 * SMALL_VMEM),
        cost_estimate=weight_of(micros),
        name="product",
    )(where, *[*lefts, right], *after)


def attend_kernel(held, seg_row_ref, seg_col_ref, qkv_ref, *rest):
    rest = rest[held:]
    out_refs, (lse_ref, bias_ref, stat_ref, score_ref, expo_ref) = rest[:2], rest[2:]
    half = qkv_ref.shape[2]
    pair = pl.program_id(1)
    length = bias_ref.shape[0]
    chunk = score_ref.shape[1]

    @pl.when(pair == 0)
    def _():
        bias_ref[...] = jnp.where(seg_col_ref[0] == seg_row_ref[0], 0.0, MASKED)
        stat_ref[...] = jnp.zeros_like(stat_ref)

    block = qkv_ref[:, 0].reshape(length, 3 * PAIR)
    q, k, v = (block[:, i * PAIR : (i + 1) * PAIR] for i in range(3))
    lane = lax.broadcasted_iota(jnp.int32, (length, PAIR), 1)
    low = lane < HD
    zero, one = jnp.zeros_like(q), jnp.ones_like(v)
    q_heads = [jnp.where(low, q, zero), jnp.where(low, zero, q)]
    v_heads = [jnp.where(low, v, one), jnp.where(low, one, v)]
    lane, low = lane[:chunk], low[:chunk]

    def score(step):
        c, h = divmod(step, 2)
        score_ref[step % 2] = lax.dot_general(
            q_heads[h][c * chunk : (c + 1) * chunk], k, NT, preferred_element_type=F32
        )

    def soften(step):
        c, h = divmod(step, 2)
        tops = []
        for at in range(0, chunk, TILE):
            rows = slice(c * chunk + at, c * chunk + at + TILE)
            s = score_ref[step % 2, at : at + TILE, :] + bias_ref[rows, :]
            top = jnp.max(s, axis=1, keepdims=True)
            expo_ref[step % 2, at : at + TILE, :] = jnp.exp(s - top).astype(BF16)
            tops.append(top)
        return jnp.concatenate(tops, 0)

    def mix(step):
        return jnp.dot(expo_ref[step % 2], v_heads[step % 2], preferred_element_type=F32)

    def finish(c, got, tops):
        rows = slice(c * chunk, (c + 1) * chunk)
        total = jnp.where(low, got[1], got[0])
        mixed = jnp.where(low, got[0], got[1]) / pltpu.roll(total, HD, 1)
        log = jnp.log(total)
        stat = stat_ref[rows, :]
        stat = jnp.where(lane == 2 * pair, tops[0] + log[:, HD : HD + 1], stat)
        stat_ref[rows, :] = jnp.where(lane == 2 * pair + 1, tops[1] + log[:, :1], stat)
        part, at = divmod(c * chunk, half)
        out_refs[part][0, at : at + chunk, :] = mixed.astype(BF16)

    steps = 2 * length // chunk
    tops, got = [], []
    score(0)
    for step in range(steps):
        if step + 1 < steps:
            score(step + 1)
        tops.append(soften(step))
        got.append(mix(step))
        if step % 2:
            finish(step // 2, got[-2:], tops[-2:])

    @pl.when(pair == pl.num_programs(1) - 1)
    def _():
        lse_ref[0] = jnp.transpose(stat_ref[...])[: lse_ref.shape[1]]


def attend_back_kernel(first_pair, after, *refs):
    seg_row_ref, seg_col_ref, qkv_ref, out_a, out_b, grad_a, grad_b, lse_ref = refs[:8]
    dqkv_ref, sums_ref, bias_ref, ds_ref, score_ref, slope_ref, prob_ref = refs[8 + after :]
    pair = pl.program_id(1)
    length = bias_ref.shape[0]
    half = qkv_ref.shape[2]
    chunk = score_ref.shape[1]

    @pl.when(pair == 0)
    def _():
        bias_ref[...] = jnp.where(seg_col_ref[0] == seg_row_ref[0], 0.0, MASKED)

    @pl.when((pair == 0) & (pl.program_id(0) == 0))
    def _():
        sums_ref[...] = jnp.zeros_like(sums_ref)

    block = qkv_ref[:, 0].reshape(length, 3 * PAIR)
    q, k, v = (block[:, i * PAIR : (i + 1) * PAIR] for i in range(3))
    out = jnp.concatenate([out_a[0], out_b[0]], 0)
    grad = jnp.concatenate([grad_a[0], grad_b[0]], 0)
    low = lax.broadcasted_iota(jnp.int32, (length, PAIR), 1) < HD
    zero = jnp.zeros_like(q)
    heads = lambda array: [jnp.where(low, array, zero), jnp.where(low, zero, array)]
    q_heads, k_heads, g_heads = heads(q), heads(k), heads(grad)
    product = jnp.transpose(out.astype(F32) * grad.astype(F32))
    chunks = length // chunk
    deltas = [total_rows(product[h * HD : (h + 1) * HD]) for h in range(2)]
    stats = [lse_ref[0, pl.ds(2 * (first_pair + pair) + h, 1), :] for h in range(2)]

    def score(step):
        h, c = divmod(step, chunks)
        rows = slice(c * chunk, (c + 1) * chunk)
        score_ref[step % 2] = lax.dot_general(k[rows], q_heads[h], NT, preferred_element_type=F32)
        slope_ref[step % 2] = lax.dot_general(v[rows], g_heads[h], NT, preferred_element_type=F32)

    def bend(step):
        h, c = divmod(step, chunks)
        for at in range(0, chunk, TILE):
            rows = slice(c * chunk + at, c * chunk + at + TILE)
            part = slice(at, at + TILE)
            p = jnp.exp(score_ref[step % 2, part, :] + bias_ref[rows, :] - stats[h])
            prob_ref[step % 2, part, :] = p.astype(BF16)
            ds_ref[h, rows, :] = (p * (slope_ref[step % 2, part, :] - deltas[h])).astype(BF16)

    steps = 2 * chunks
    dk, dv = [None] * chunks, [None] * chunks
    dq = None
    score(0)
    for step in range(steps):
        h, c = divmod(step, chunks)
        if step + 1 < steps:
            score(step + 1)
        bend(step)
        rows = slice(c * chunk, (c + 1) * chunk)
        v_part = jnp.dot(prob_ref[step % 2], g_heads[h], preferred_element_type=F32)
        k_part = jnp.dot(ds_ref[h, rows, :], q_heads[h], preferred_element_type=F32)
        if h == 0:
            dk[c], dv[c] = k_part, v_part
        else:
            part, at = c * chunk // half, c * chunk % half
            dqkv_ref[part, 0, at : at + chunk, PAIR : 2 * PAIR] = (dk[c] + k_part).astype(BF16)
            dv[c] = (dv[c] + v_part).astype(BF16)
            dqkv_ref[part, 0, at : at + chunk, 2 * PAIR :] = dv[c]
        if c == chunks - 1:
            part = lax.dot_general(ds_ref[h], k_heads[h], TN, preferred_element_type=F32)
            dq = part if h == 0 else dq + part
    dq = (dq * HD**-0.5).astype(BF16)
    dqkv_ref[:, 0, :, :PAIR] = dq.reshape(-1, half, PAIR)
    sums = [total_rows(dq.astype(F32)), sum(total_rows(part.astype(F32)) for part in dv)]
    sums_ref[0:1, pl.ds(pl.multiple_of(pair * PAIR, PAIR), PAIR)] += sums[0]
    sums_ref[1:2, pl.ds(pl.multiple_of(pair * PAIR, PAIR), PAIR)] += sums[1]


def attention_call(
    kernel, seg, arrays, pairs, outs, scratch, name, first=0, after=(), seqs=None, held=()
):
    parts, count, half, columns = arrays[0].shape
    start, seqs = seqs or (0, count)
    micros = 6.5 * seqs if name == "attend" else 3.7 * seqs
    length = parts * half

    def spec(array, first):
        shape = array.shape
        if len(shape) == 4:
            return pl.BlockSpec(
                (parts, 1, half, 3 * PAIR), lambda s, p: (0, start + s, 0, first + p)
            )
        if len(shape) == 3 and shape[1] == half:
            return pl.BlockSpec((1, half, PAIR), lambda s, p: (start + s, 0, first + p))
        if len(shape) == 3:
            return pl.BlockSpec((1,) + shape[1:], lambda s, p: (start + s, 0, 0))
        return pl.BlockSpec(shape, lambda s, p: (0, 0))

    operands = [seg[:, None, :], seg[:, :, None]] + arrays
    return pl.pallas_call(
        kernel,
        grid=(seqs, pairs),
        in_specs=[spec(a, first) for a in operands]
        + [pl.BlockSpec(memory_space=pl.ANY)] * (len(held) + len(after)),
        out_specs=[spec(a, 0) for a in outs],
        out_shape=outs,
        scratch_shapes=scratch(length),
        input_output_aliases={len(operands) + n: n for n in range(len(held))},
        compiler_params=pltpu.CompilerParams(vmem_limit_bytes=SMALL_VMEM),
        cost_estimate=weight_of(micros),
        name=name,
    )(*operands, *held, *after)


def attend(qkv, seg, seqs, held, after):
    parts, count, half, columns = qkv.shape
    pairs = columns // (3 * PAIR)
    outs = [
        jax.ShapeDtypeStruct((count, half, columns // 3), BF16),
        jax.ShapeDtypeStruct((count, half, columns // 3), BF16),
        jax.ShapeDtypeStruct((count, 2 * pairs, parts * half), F32),
    ]
    scratch = lambda length: [
        pltpu.VMEM((length, length), F32),
        pltpu.VMEM((length, PAIR), F32),
        pltpu.VMEM((2, 128, length), F32),
        pltpu.VMEM((2, 128, length), BF16),
    ]
    kernel = functools.partial(attend_kernel, len(held) + len(after))
    return attention_call(
        kernel, seg, [qkv], pairs, outs, scratch, "attend", 0, after, seqs, held
    )


def attend_back(qkv, seg, out, grad, lse, first, pairs, after):
    outs = [
        jax.ShapeDtypeStruct(qkv.shape[:3] + (3 * PAIR * pairs,), BF16),
        jax.ShapeDtypeStruct((8, PAIR * pairs), F32),
    ]
    scratch = lambda length: [
        pltpu.VMEM((length, length), F32),
        pltpu.VMEM((2, length, length), BF16),
        pltpu.VMEM((2, 128, length), F32),
        pltpu.VMEM((2, 128, length), F32),
        pltpu.VMEM((2, 128, length), BF16),
    ]
    kernel = functools.partial(attend_back_kernel, first, len(after))
    arrays = [qkv, *out, *grad, lse]
    return attention_call(kernel, seg, arrays, pairs, outs, scratch, "attend_back", first, after)


def body(
    layer_input,
    segment_ids,
    out_cotangent,
    attn_master,
    inner_master,
    outer_master,
    vector_master,
    attn_moment,
    inner_moment,
    outer_moment,
    vector_moment,
    attn_square,
    inner_square,
    outer_square,
    vector_square,
):
    seqs, half, width = layer_input.shape
    count = seqs * half
    hidden_units = inner_master.shape[1]
    pairs = width // (2 * PAIR)
    part_cols = width // 2
    shards = lax.axis_size("shard")
    owned_rows = attn_master.shape[1]
    core = lax.axis_index("ctx")
    first = core == 0

    def own_half(array, axis):
        size = array.shape[axis] // 2
        return lax.dynamic_slice_in_dim(array, core * size, size, axis)

    def other_half(array, axis):
        size = array.shape[axis] // 2
        return lax.dynamic_slice_in_dim(array, (1 - core) * size, size, axis)

    def in_order(mine, theirs, axis):
        return jnp.concatenate(
            [jnp.where(first, mine, theirs), jnp.where(first, theirs, mine)], axis
        )

    rows = layer_input.reshape(count, width)
    rows_theirs = swap_cores(rows)
    square = is_square()
    o, i, y, inner = position()
    where = jnp.stack([o, i, y, core]).astype(jnp.int32)

    piece = own_half(attn_master[:3], 2).astype(BF16).reshape(3, owned_rows, pairs, PAIR)
    piece = piece.transpose(1, 2, 0, 3).reshape(owned_rows, 3 * part_cols)
    vec_low = vector_master.astype(BF16)
    rider = vec_low[:2].reshape(1, -1)
    if square:
        piece = lax.dynamic_slice_in_dim(piece, y * (piece.shape[1] // 2), piece.shape[1] // 2, 1)
    rider = jnp.pad(rider, ((0, 15), (0, piece.shape[1] - rider.shape[1])))
    piece = jnp.concatenate([piece, rider], 0)

    def every_row(block):
        size = block.shape[0] // (lax.axis_size("replica") * 2)
        part = lax.dynamic_slice_in_dim(block, (2 * y + core) * size, size, 0).astype(BF16)
        return lax.all_gather(part, EVERY, axis=0, tiled=True)

    def placed(found, slots):
        chosen = jnp.stack([place[0] for place in slots[:shards]])
        chosen = (jnp.arange(shards)[:, None] == chosen[None, :]).astype(F32)
        return jnp.einsum("ps,srw->rpw", chosen, found.astype(F32)).reshape(-1, width)

    if square:
        q = 2 * core + y
        vec_rows = jnp.pad(vec_low.reshape(-1), (0, 16 * width - vec_low.size)).reshape(16, width)
        quarter = jnp.concatenate(
            [
                lax.dynamic_slice_in_dim(inner_master, q * width, width, 1).astype(BF16),
                lax.dynamic_slice_in_dim(
                    attn_master[3], q * (owned_rows // 4), owned_rows // 4, 0
                ).astype(BF16),
                vec_rows,
                lax.dynamic_slice_in_dim(
                    outer_master, q * (outer_master.shape[0] // 4), outer_master.shape[0] // 4, 0
                ).astype(BF16),
            ],
            0,
        )
        line = jnp.stack([piece] + [shift_outer(piece, -k) for k in range(1, OUTER)])
        near_x, near_y = shift_inner(line, 1), shift_replica(line, 1)
        (quarter,) = relay(where, [quarter], (line,))
        across = swap_outer(quarter, 2)
        two = (OUTER // 2,)
        far = small_call(
            halves_kernel, where, [near_x, near_y], [two + piece.shape] * 2, (), "halves"
        )
        stacks = [line, near_x, near_y, shift_inner(far[0], 1), shift_replica(far[1], 1)]
        (pair,) = small_call(
            pair_kernel, where, [quarter, across], [two + quarter.shape], tuple(stacks[3:]), "pair"
        )
        places = quarter_places([lax.rem(o + k, OUTER) for k in range(OUTER)])
        other_pair = swap_outer(pair, 1)
        pair_x, pair_y = shift_inner(pair, 1), shift_replica(pair, 1)
        done = (pair,)
    else:
        stacks = [item[None] for item in ring_gather(piece)]
        places = [(owner, 0) for owner in slot_owners()]
        wide = hidden_units // width
        inner_w = every_row(inner_master).reshape(8, -1, wide, width).transpose(0, 2, 1, 3)
        slots = [inner_w.reshape(PARTS, -1, width), every_row(attn_master[3]).reshape(PARTS, -1, width)]
        slots = jnp.pad(jnp.concatenate(slots, 1), ((0, 0), (0, 16), (0, 0)))
        outer_w = every_row(outer_master).reshape(PARTS, -1, width)
        slots = jnp.concatenate([slots, outer_w], 1)
        wide_stacks = [slots[n : n + 2] for n in range(0, PARTS, 2)]
        wide_places = [(jnp.int32(n // 4), jnp.int32(n % 4)) for n in range(PARTS)]
        vec = lax.all_gather(vec_low, "shard", axis=1, tiled=True).astype(F32)
        done = ()
    riders = jnp.concatenate([stack[:, owned_rows] for stack in stacks], 0)[:shards]
    riders = riders[:, : 2 * width // shards].reshape(shards, 2, -1)
    biases = placed(riders, places)

    halves = own_half(biases, 1).reshape(2, pairs, PAIR)
    bias = jnp.stack([halves[0], jnp.zeros_like(halves[0]), halves[1]], 1).reshape(1, -1)
    ones = jnp.ones((pairs, PAIR), F32)
    factor = jnp.stack([ones * HD**-0.5, ones, ones], 1).reshape(1, -1)
    qkv, qkv_w = project(rows, rows_theirs, stacks, places, bias, factor, done)
    qkv = qkv.reshape(2, seqs, half, 3 * part_cols)
    seg = jnp.concatenate([own_half(segment_ids, 1), other_half(segment_ids, 1)], 1)
    if square:
        (other_pair,) = relay(where, [other_pair], (qkv_w,))
        other_x, other_y = shift_inner(other_pair, 1), shift_replica(other_pair, 1)
        early = attend(qkv, seg, (0, seqs // 2), (), (other_pair,))
        near = [pair, other_pair, pair_x, other_x, pair_y, other_y]
        bulk, *relayed = small_call(
            bulk_kernel,
            where,
            near,
            [(12,) + quarter.shape, pair.shape, pair.shape],
            (early[0],),
            "bulk",
        )
        far_pair = [shift_inner(relayed[0], 1), shift_replica(relayed[1], 1)]
        near_rows = bulk[:8, 160:162].reshape(shards, -1)[:, : vec_low.size]
        both = line_order(o)
        places = quarter_places(both[0] + both[1])
        vec = placed(near_rows.reshape((shards,) + vec_low.shape), places)
        wide_places = [(row, 2 * core + side) for row, side in places]
        wide_places += [(row, 2 * (1 - core) + side) for row, side in places]
    else:
        early = attend(qkv, seg, (0, seqs // 2), (), ())
    mixed_mine, mixed_sent, lse = attend(qkv, seg, (seqs // 2, seqs - seqs // 2), early, ())
    if square:
        (far_bulk,) = small_call(
            bulk_kernel, where, far_pair, [(4,) + quarter.shape], (mixed_mine,), "bulk"
        )
        wide_stacks = [bulk, far_bulk, swap_cores(bulk), swap_cores(far_bulk)]
    flat = lambda array: array.reshape(count, part_cols)
    deep = lambda array: array.reshape(seqs, half, part_cols)
    heads_mine, heads_theirs = flat(mixed_mine), swap_cores(flat(mixed_sent))

    cotan = out_cotangent.reshape(count, width)
    core_at = jnp.full((1,), core, jnp.int32)
    forward = ffn(core_at, wide_places, heads_mine, heads_theirs, rows, cotan, vec, wide_stacks)
    active, slope, inner_w, outer_w, hidden_low, normed, scale, result = forward[:8]
    ffn_grad, out_w, sums_two = forward[8:]

    by_shard = lambda array: array.reshape(shards, -1, array.shape[1])

    outer_sent = product(where, [active], ffn_grad, 0)
    outer_kept = product(where, [active], ffn_grad, 1, (outer_sent,))
    outer_chips = [by_shard(outer_kept), by_shard(swap_cores(outer_sent))]
    done = (outer_kept,)
    if square:
        outer = Sum(where, outer_chips)
        done = outer.merge()
    pre_grad, branch_grad, mine, sent, sums_one = ffn_back(
        core_at, ffn_grad, slope, normed, scale, vec, out_w, inner_w, outer_w, done[:1]
    )
    got = swap_cores(sent)
    mixed_grad = [deep(mine), deep(got)]
    done = outer.plane((pre_grad,)) if square else ()
    heads = [heads_mine, heads_theirs]
    inner_kept = product(where, [hidden_low], pre_grad, 1, done)
    done = outer.cross((inner_kept,)) if square else (inner_kept,)
    inner_sent = product(where, [hidden_low], pre_grad, 0, done)
    out_sent = product(where, heads, branch_grad, 0, (inner_sent,), True)
    out_kept = product(where, heads, branch_grad, 1, (out_sent,), True)
    inner_chips = [by_shard(inner_kept), by_shard(swap_cores(inner_sent))]
    out_chips = [by_shard(out_kept), by_shard(swap_cores(out_sent))]

    def back(first, after):
        grad, sums = attend_back(
            qkv, seg, (mixed_mine, mixed_sent), mixed_grad, lse, first, pairs // 2, after
        )
        return grad.reshape(2 * count, -1), sums

    def vector_chip(sums_a, sums_b):
        blank = jnp.zeros((part_cols,), F32)
        ours = jnp.concatenate([sums_a, sums_b], 1)
        attn_biases = jnp.stack([in_order(ours[at], blank, 0) for at in range(2)])
        sums = [attn_biases, sums_one[2:3], sums_one[:2], sums_two[2:3], sums_two[:2]]
        sums = jnp.concatenate(sums + [sums_one[4:8]], 0)
        sums = sums.reshape(-1, shards, width // shards).transpose(1, 0, 2)
        sums = jnp.pad(sums, ((0, 0), (0, owned_rows - sums.shape[1]), (0, 0)))
        return sums.astype(BF16)

    outer_states = (outer_master, outer_moment, outer_square)
    inner_states = (inner_master, inner_moment, inner_square)
    attn_states = (attn_master, attn_moment, attn_square)
    if square:
        inner = Sum(where, inner_chips)
        done = outer.turn((out_kept,))
        done = inner.merge(done)
        grad_a, sums_a = back(0, done)
        done = outer.line((grad_a,))
        ours = by_shard(product(where, [rows, rows_theirs], grad_a, None, done))
        done = inner.plane((ours,))
        sum_a = Sum(where, [ours], out_chips)
        done = sum_a.merge(done)
        grad_b, sums_b = back(pairs // 2, done)
        done = inner.cross((grad_b,))
        done = sum_a.plane(done)
        theirs_part = input_back(grad_a, grad_b, qkv_w, (), done)
        ours = by_shard(product(where, [rows, rows_theirs], grad_b, None, (theirs_part,)))
        sum_b = Sum(where, [ours], [vector_chip(sums_a, sums_b)])
        done = sum_a.cross((ours,))
        done = sum_b.merge(done)
        outer_new = update(where, outer_states, [outer.shares], done)
        input_grad = input_back(
            grad_a, grad_b, qkv_w, (branch_grad, swap_cores(theirs_part)), (outer_new[0],)
        )
        done = sum_b.plane((input_grad,))
        done = inner.turn(done)
        done = sum_a.turn(done)
        done = sum_b.cross(done)
        done = inner.line(done)
        done = sum_b.turn(done)
        inner_new = update(where, inner_states, [inner.shares], done)
        done = sum_a.line((inner_new[0],))
        sum_b.line(done)
        attn_shares = [sum_a.shares, sum_b.shares]
        vector_shares = [
            jnp.concatenate(
                [
                    jnp.where(y == 0, sum_b.shares[at], sum_b.shares[at + 1])[0],
                    jnp.where(y == 0, sum_b.shares[at + 1], sum_b.shares[at])[0],
                ],
                0,
            )
            for at in (0, 2)
        ]
    else:
        grad_a, sums_a = back(0, ())
        grad_b, sums_b = back(pairs // 2, ())
        theirs_part = input_back(grad_a, grad_b, qkv_w, (), ())
        added = (branch_grad, swap_cores(theirs_part))
        input_grad = input_back(grad_a, grad_b, qkv_w, added, ())
        outer_new = update(where, outer_states, [sum_apart(add_low(*outer_chips))])
        inner_new = update(where, inner_states, [sum_apart(add_low(*inner_chips))])
        ours = [by_shard(product(where, [rows, rows_theirs], grad, None)) for grad in (grad_a, grad_b)]
        chip_a = jnp.concatenate([ours[0], add_low(*out_chips)], 2)
        chip_b = jnp.concatenate([ours[1], vector_chip(sums_a, sums_b)], 2)
        attn_shares = [sum_apart(chip_a), sum_apart(chip_b)]
        vector_shares = [share[0] for share in attn_shares[1]]
    attn_new = update(where, attn_states, attn_shares)
    cut = grad_b.shape[1]
    vector_sum = sum(share[: vec_low.shape[0], cut:].astype(F32) for share in vector_shares)
    vector_new = adamw(vector_sum, vector_moment, vector_square, vector_master, RATE_VECTOR)
    vector_new = vector_new + (vector_new[2].astype(BF16),)
    news = (attn_new, inner_new, outer_new, vector_new)
    updates = [[new[at] for new in news] for at in range(4)]
    return (
        result.reshape(seqs, half, width).astype(BF16),
        input_grad.reshape(seqs, half, width),
        *[item for kind in updates for item in kind],
    )


def solution(mesh):
    tokens = P(("replica", "shard"), "ctx", None)
    states = (P(None, "shard", None), P("shard", None), P("shard", None), P(None, "shard"))
    in_specs = (tokens, P(("replica", "shard"), None), tokens) + states * 3
    out_specs = (tokens, tokens) + states * 4
    return jax.shard_map(body, mesh=mesh, in_specs=in_specs, out_specs=out_specs, check_vma=False)
```

```python
import functools
import math

import jax
import jax.numpy as jnp
from jax import lax
from jax.experimental import pallas as pl
from jax.experimental.pallas import tpu as pltpu
from jax.sharding import PartitionSpec as P

HD = 64
PAIR = 2 * HD
STEP = 5
OUTER = 4
EVERY = ("shard", "replica", "ctx")

EPS_NORM = 1e-05
BETA_ONE = 0.5
BETA_TWO = 0.6
RATE_MATRIX = 0.02
RATE_VECTOR = 0.1
DECAY = 0.01
EPS_ADAM = 1e-06
MASKED = -1e30
F32 = jnp.float32
BF16 = jnp.bfloat16
PARTS = 32
TILE = 32
VMEM = 56 * 1024 * 1024
SMALL_VMEM = 16 * 1024 * 1024
GROUP = 256
NT = (((1,), (1,)), ((), ()))
TN = (((0,), (0,)), ((), ()))


def weight_of(micros):
    return pl.CostEstimate(
        flops=int(micros * 2.9e8), bytes_accessed=int(micros * 9.2e5), transcendentals=0
    )


def normalize(resid):
    centre = resid - jnp.mean(resid, -1, keepdims=True)
    scale = lax.rsqrt(jnp.mean(centre * centre, -1, keepdims=True) + EPS_NORM)
    return (centre * scale, scale)


def norm_back(grad, normed, scale):
    return scale * (
        grad
        - jnp.mean(grad, -1, keepdims=True)
        - normed * jnp.mean(grad * normed, -1, keepdims=True)
    )


def adamw(grad, moment, square, weight, rate):
    moment_new = BETA_ONE * moment + (1.0 - BETA_ONE) * grad
    square_new = BETA_TWO * square + (1.0 - BETA_TWO) * grad * grad
    stepped = (
        moment_new
        / (1.0 - BETA_ONE**STEP)
        / (jnp.sqrt(square_new / (1.0 - BETA_TWO**STEP)) + EPS_ADAM)
    )
    weight_new = weight - rate * (stepped + DECAY * weight)
    return (moment_new, square_new, weight_new)


def swap_cores(value):
    return lax.ppermute(value, "ctx", [(0, 1), (1, 0)])


def shift_outer(value, step):
    inner = lax.axis_size("shard") // OUTER
    pairs = [
        (o * inner + i, ((o + step) % OUTER) * inner + i) for o in range(OUTER) for i in range(inner)
    ]
    return lax.ppermute(value, "shard", pairs)


def shift_inner(value, step):
    inner = lax.axis_size("shard") // OUTER
    pairs = [
        (o * inner + i, o * inner + (i + step) % inner) for o in range(OUTER) for i in range(inner)
    ]
    return lax.ppermute(value, "shard", pairs)


def shift_replica(value, step):
    size = lax.axis_size("replica")
    return lax.ppermute(value, "replica", [(r, (r + step) % size) for r in range(size)])


def ring_gather(piece):
    inner = lax.axis_size("shard") // OUTER
    found = []
    held = piece
    for k in range(OUTER):
        if k:
            held = shift_outer(held, -1)
        found.append([held] + [shift_inner(held, -e) for e in range(1, inner)])
    return [item for group in found for item in group]


def slot_owners():
    inner = lax.axis_size("shard") // OUTER
    at = lax.axis_index("shard")
    o, i = at // inner, at % inner
    return [
        lax.rem(o + k, OUTER) * inner + lax.rem(i + e, inner)
        for k in range(OUTER)
        for e in range(inner)
    ]


def pick(array, index, axis):
    return lax.dynamic_index_in_dim(array, index, axis, keepdims=False)


def add_low(value, *others):
    total = value.astype(F32)
    for item in others:
        total = total + item.astype(F32)
    return total.astype(BF16)


def position():
    inner = lax.axis_size("shard") // OUTER
    at = lax.axis_index("shard")
    return at // inner, at % inner, lax.axis_index("replica"), inner


def is_square():
    return lax.axis_size("replica") == 2 and lax.axis_size("shard") == 2 * OUTER


def swap_outer(value, flip):
    inner = lax.axis_size("shard") // OUTER
    pairs = [(o * inner + i, (o ^ flip) * inner + i) for o in range(OUTER) for i in range(inner)]
    return lax.ppermute(value, "shard", pairs)


def swap_cross(value):
    return lax.ppermute(value, ("replica", "ctx"), [(a, 3 - a) for a in range(4)])


def sum_apart(chip_sum):
    o, i, y, inner = position()
    grid = chip_sum.reshape(OUTER, inner, *chip_sum.shape[1:])
    got = [shift_inner(pick(grid, lax.rem(i + e, inner), 1), e) for e in range(1, inner)]
    line = add_low(pick(grid, i, 1), *got)
    got = [shift_outer(pick(line, lax.rem(o + d, OUTER), 0), d) for d in range(1, OUTER)]
    total = add_low(pick(line, o, 0), *got)
    got = [shift_replica(total, r) for r in range(1, lax.axis_size("replica"))]
    mine = add_low(total, *got)[None]
    return [mine, swap_cores(mine)]


def small_call(kernel, where, ins, outs, after, name):
    held = pl.BlockSpec(memory_space=pltpu.VMEM)
    return pl.pallas_call(
        functools.partial(kernel, len(ins), len(after)),
        in_specs=[pl.BlockSpec(memory_space=pltpu.SMEM)]
        + [held] * len(ins)
        + [pl.BlockSpec(memory_space=pl.ANY)] * len(after),
        out_specs=[held] * len(outs),
        out_shape=[pltpu.VMEM(shape, BF16) for shape in outs],
        compiler_params=pltpu.CompilerParams(vmem_limit_bytes=SMALL_VMEM),
        cost_estimate=weight_of(1),
        name=name,
    )(where, *[pltpu.with_memory_space_constraint(a, pltpu.VMEM) for a in ins], *after)


def fold_plane_kernel(count, after, where_ref, keep_p, got_p, keep_q, got_q, *rest):
    i, y = where_ref[1], where_ref[2]
    kept_p, send_p, kept_q, send_q = rest[after:]
    for o in range(OUTER):
        for out, at in ((kept_p, y), (send_p, 1 - y)):
            out[o] = add_low(keep_p[o, at], got_p[o, at])
        for out, at in ((kept_q, i), (send_q, 1 - i)):
            out[o] = add_low(keep_q[o, at], got_q[o, at])


def line_order(o):
    near = o + 1 - 2 * lax.rem(o, 2)
    far = lambda at: lax.rem(at + 2, OUTER)
    return (o, far(o)), (near, far(near))


def fold_cross_kernel(count, after, where_ref, keep_p, got_p, keep_q, got_q, *rest):
    for out, order in zip(rest[after:], line_order(where_ref[0])):
        for n, at in enumerate(order):
            out[n, 0] = add_low(keep_p[at], got_p[at])
            out[n, 1] = add_low(keep_q[at], got_q[at])


def fold_turn_kernel(count, after, where_ref, keep, got, *rest):
    for n, out in enumerate(rest[after:]):
        out[...] = add_low(keep[n], got[n])


def fold_line_kernel(count, after, where_ref, *rest):
    rest[count + after][...] = add_low(*(ref[...] for ref in rest[:count]))


def merge_kernel(groups, after, where_ref, *refs):
    outs = refs[4 * sum(groups) + after :]
    for slot, out in enumerate(outs):
        left = chip = 0
        for group in groups:
            for at in range(2):
                parts = []
                for n in range(chip, chip + group):
                    ref = refs[4 * n + slot]
                    parts.append(ref[0, at, 0, 0] if slot % 2 else ref[0, 0, 0, at])
                cut = slice(left, left + parts[0].shape[1])
                out[0, at, :, cut] = parts[0] if group == 1 else add_low(*parts)
            left, chip = cut.stop, chip + group


class Sum:
    def __init__(self, where, *groups):
        self.where, self.rows = where, groups[0][0].shape[1] // 4
        self.columns = sum(group[0].shape[2] for group in groups)
        self.groups = [len(group) for group in groups]
        self.chips = [
            c.reshape(OUTER, 2, 2, 2, self.rows, c.shape[2]) for group in groups for c in group
        ]

    def shape(self, *lead):
        return lead + (self.rows, self.columns)

    def merge(self, after=()):
        def spec(chip, lead, flip):
            def place(o, w):
                at = w[1] if lead == 0 else w[2]
                at = 1 - at if flip else at
                return (o, at, 0, 0, 0, 0) if lead == 0 else (o, 0, 1, at, 0, 0)

            return pl.BlockSpec(((1, 1, 1, 2) if lead == 0 else (1, 2, 1, 1)) + chip.shape[4:], place)

        kinds = ((0, True), (1, True), (0, False), (1, False))
        out_spec = pl.BlockSpec((1, 2, self.rows, self.columns), lambda o, w: (o, 0, 0, 0))
        *sent, keep_p, keep_q = pl.pallas_call(
            functools.partial(merge_kernel, self.groups, len(after)),
            grid_spec=pltpu.PrefetchScalarGridSpec(
                num_scalar_prefetch=1,
                grid=(OUTER,),
                in_specs=[spec(chip, *kind) for chip in self.chips for kind in kinds]
                + [pl.BlockSpec(memory_space=pl.ANY)] * len(after),
                out_specs=[out_spec] * 4,
            ),
            out_shape=[jax.ShapeDtypeStruct(self.shape(OUTER, 2), BF16)] * 4,
            compiler_params=pltpu.CompilerParams(vmem_limit_bytes=SMALL_VMEM),
            cost_estimate=weight_of(4),
            name="merge",
        )(self.where, *[chip for chip in self.chips for _ in range(4)], *after)
        self.kept = [keep_p, shift_inner(sent[0], 1), keep_q, shift_replica(sent[1], 1)]
        return tuple(sent)

    def plane(self, after=()):
        keep_p, send_p, keep_q, send_q = small_call(
            fold_plane_kernel, self.where, self.kept, [self.shape(OUTER)] * 4, after, "fold_plane"
        )
        self.kept = [keep_p, shift_replica(send_p, 1), keep_q, shift_inner(send_q, 1)]
        return (send_p, send_q)

    def cross(self, after=()):
        keep, send = small_call(
            fold_cross_kernel, self.where, self.kept, [self.shape(2, 2)] * 2, after, "fold_cross"
        )
        self.kept = [keep, swap_outer(send, 1)]
        return (send,)

    def turn(self, after=()):
        shapes = [self.kept[0].shape[1:]] * 2
        keep, send = small_call(
            fold_turn_kernel, self.where, self.kept, shapes, after, "fold_turn"
        )
        self.kept = [keep, swap_outer(send, 2)]
        return (send,)

    def line(self, after=()):
        (total,) = small_call(
            fold_line_kernel, self.where, self.kept, [self.kept[0].shape], after, "fold_line"
        )
        self.shares = [total, shift_replica(total, 1), swap_cores(total), swap_cross(total)]
        return (total,)


def update_kernel(groups, after, where_ref, *refs):
    states, shares = refs[:3], refs[3 : 3 + sum(groups)]
    outs, grad_ref = refs[3 + sum(groups) + after : -1], refs[-1]
    rows = shares[0].shape[1]
    across = groups[0] // 2
    for core in range(2):

        @pl.when(pl.program_id(1) == core)
        def _():
            for n in range(across):
                line = where_ref[2] if n == 0 else 1 - where_ref[2]
                line = pl.ds(pl.multiple_of(line * rows, rows), rows) if across > 1 else slice(None)
                if len(groups) == 1:
                    grad_ref[line, :] = shares[across * core + n][0].astype(F32)
                    continue
                left, right = shares[across * core + n], shares[groups[0] + across * core + n]
                width = grad_ref.shape[2]
                pairs = width // PAIR
                for t in range(3):
                    for p in range(pairs):
                        side, at = (left, p) if 2 * p < pairs else (right, p - pairs // 2)
                        part = side[0, :, (3 * at + t) * PAIR : (3 * at + t + 1) * PAIR]
                        grad_ref[t, line, p * PAIR : (p + 1) * PAIR] = part.astype(F32)
                cut = 3 * PAIR * (pairs // 2)
                grad_ref[3, line, :] = left[0, :, cut : cut + width].astype(F32)

    new = adamw(grad_ref[...], states[1][...], states[2][...], states[0][...], RATE_MATRIX)
    for out, value in zip(outs, new + (new[2],)):
        out[...] = value.astype(out.dtype)


def update(where, states, groups, after=()):
    parts, rows = groups[0][0].shape[:2]
    rows = rows * (len(groups[0]) // 2)
    lead = states[0].shape[:-2]
    columns = states[0].shape[-1] // 2
    place = lambda p, v, w: (0,) * len(lead) + (p, w[3] + v - 2 * w[3] * v)
    block = pl.BlockSpec(lead + (rows, columns), place)
    shares = [share for group in groups for share in group]
    share_specs = [pl.BlockSpec((1,) + a.shape[1:], lambda p, v, w: (p, 0, 0)) for a in shares]
    kinds = (F32, F32, F32, BF16)
    return pl.pallas_call(
        functools.partial(update_kernel, [len(group) for group in groups], len(after)),
        grid_spec=pltpu.PrefetchScalarGridSpec(
            num_scalar_prefetch=1,
            grid=(parts, 2),
            in_specs=[block] * 3 + share_specs + [pl.BlockSpec(memory_space=pl.ANY)] * len(after),
            out_specs=[block] * 4,
            scratch_shapes=[pltpu.VMEM(lead + (rows, columns), F32)],
        ),
        out_shape=[jax.ShapeDtypeStruct(states[0].shape, kind) for kind in kinds],
        compiler_params=pltpu.CompilerParams(vmem_limit_bytes=SMALL_VMEM),
        cost_estimate=weight_of(5),
        name="update",
    )(where, *states, *shares, *after)


def input_back_kernel(a_ref, b_ref, left_ref, right_ref, *rest):
    out_ref = rest[-1]
    total = lax.dot_general(a_ref[...], left_ref[...], NT, preferred_element_type=F32)
    total += lax.dot_general(b_ref[...], right_ref[...], NT, preferred_element_type=F32)
    if out_ref.dtype == F32:
        total += rest[0][...].astype(F32) + rest[1][...].astype(F32)
    out_ref[...] = total.astype(out_ref.dtype)


def input_back(grad_a, grad_b, weight, added, after):
    count, cut = grad_a.shape[0] // 2, grad_a.shape[1]
    width = weight.shape[0]
    tile = width // 4
    first = 0 if added else 1
    side = pl.BlockSpec((count, cut), lambda n: (first, 0))
    line = pl.BlockSpec((count, tile), lambda n: (0, n))
    return pl.pallas_call(
        input_back_kernel,
        grid=(width // tile,),
        in_specs=[side, side]
        + [pl.BlockSpec((tile, cut), lambda n, at=at: (n, at)) for at in range(2)]
        + [line] * len(added)
        + [pl.BlockSpec(memory_space=pl.ANY)] * len(after),
        out_specs=line,
        out_shape=jax.ShapeDtypeStruct((count, width), F32 if added else BF16),
        compiler_params=pltpu.CompilerParams(vmem_limit_bytes=SMALL_VMEM),
        cost_estimate=weight_of(5),
        name="input_back",
    )(*[grad_a, grad_b, weight, weight, *added], *after)


def quarter_places(order):
    o, i, y, inner = position()
    kinds = ((i, y), (1 - i, y), (i, 1 - y), (1 - i, 1 - y))
    return [(row * 2 + across, side) for across, side in kinds for row in order]


def relay_kernel(count, after, where_ref, *rest):
    for source, out in zip(rest[:count], rest[count + after :]):
        out[...] = source[...]


def halves_kernel(count, after, where_ref, near_x, near_y, *rest):
    first, second = rest[after:]
    first[...] = near_y[: OUTER // 2]
    second[...] = near_x[OUTER // 2 :]


def pair_kernel(count, after, where_ref, own, other, *rest):
    rest[after][0] = own[...]
    rest[after][1] = other[...]


def bulk_kernel(count, after, where_ref, *rest):
    ins, (bulk, *far) = rest[:count], rest[count + after :]
    at = 0
    for source in ins:
        bulk[at : at + source.shape[0]] = source[...]
        at += source.shape[0]
    for out, source in zip(far, (4, 3)):
        out[...] = ins[source][...]


def relay(where, arrays, after):
    return small_call(relay_kernel, where, arrays, [a.shape for a in arrays], after, "relay")


def project_kernel(after, row_ref, column_ref, mine_ref, theirs_ref, bias_ref, factor_ref, *rest):
    stacks, (out_ref, weight_ref) = rest[: -2 - after], rest[-2:]
    columns = stacks[0].shape[2]
    part = weight_ref.shape[0] * weight_ref.shape[1] // columns
    part = part // sum(stack.shape[0] for stack in stacks)
    at = pl.program_id(0)

    @pl.when(at == 0)
    def _():
        slot = 0
        for stack in stacks:
            for k in range(stack.shape[0]):
                start = pl.multiple_of(row_ref[slot] * part, part)
                left = pl.multiple_of(column_ref[slot] * columns, PAIR)
                weight_ref[pl.ds(start, part), pl.ds(left, columns)] = stack[k, :part, :]
                slot += 1

    def fill(rows):
        acc = jnp.dot(rows, weight_ref[...], preferred_element_type=F32)
        out_ref[...] = ((acc + bias_ref[...]) * factor_ref[...]).astype(BF16)

    @pl.when(at < pl.num_programs(0) // 2)
    def _():
        fill(mine_ref[...])

    @pl.when(at >= pl.num_programs(0) // 2)
    def _():
        fill(theirs_ref[...])


def project(mine, theirs, stacks, places, bias, factor, after):
    count, width = mine.shape
    columns = bias.shape[1]
    tile = 512
    each = count // tile
    whole = lambda shape: pl.BlockSpec(shape, lambda m, *_: (0,) * len(shape))
    tables = [jnp.stack([p[axis] for p in places]).astype(jnp.int32) for axis in range(2)]
    return pl.pallas_call(
        functools.partial(project_kernel, len(after)),
        grid_spec=pltpu.PrefetchScalarGridSpec(
            num_scalar_prefetch=2,
            grid=(2 * each,),
            in_specs=[
                pl.BlockSpec((tile, width), lambda m, *_: (jnp.minimum(m, each - 1), 0)),
                pl.BlockSpec((tile, width), lambda m, *_: (jnp.maximum(m - each, 0), 0)),
                whole((1, columns)),
                whole((1, columns)),
            ]
            + [whole(stack.shape) for stack in stacks]
            + [pl.BlockSpec(memory_space=pl.ANY)] * len(after),
            out_specs=[
                pl.BlockSpec((tile, columns), lambda m, *_: (m, 0)),
                whole((width, columns)),
            ],
        ),
        out_shape=[jax.ShapeDtypeStruct((2 * count, columns), BF16), jax.ShapeDtypeStruct((width, columns), BF16)],
        compiler_params=pltpu.CompilerParams(vmem_limit_bytes=44 * 1024 * 1024),
        cost_estimate=weight_of(11),
        name="project",
    )(*tables, *[mine, theirs, bias, factor, *stacks], *after)


def gelu_and_slope(u):
    d = 1.0 + (0.3275911 * 0.5**0.5) * jnp.abs(u)
    t = pl.reciprocal(d, approx=True).astype(BF16)
    e = jnp.exp2(u * u * (-0.5 * math.log2(math.e))).astype(BF16)
    u = u.astype(BF16)
    a = jnp.abs(u)
    low = lambda value: jnp.asarray(value, BF16)
    series = low(0.5 * 1.061405429) * t - low(0.5 * 1.453152027)
    series = series * t + low(0.5 * 1.421413741)
    series = series * t - low(0.5 * 0.284496736)
    series = series * t + low(0.5 * 0.254829592)
    tail = series * t * e
    active = jnp.maximum(u, low(0.0)) - a * tail
    below = tail - a * (e * low(1.0 / math.sqrt(2.0 * math.pi)))
    return active, jnp.where(u >= low(0.0), low(1.0) - below, below)


def total_rows(value):
    return jnp.sum(value, axis=0, keepdims=True)


def in_parts(count, work):
    def turn(at, carry):
        work(pl.ds(pl.multiple_of(at * 128, 128), 128))
        return carry

    lax.fori_loop(0, count // 128, turn, 0)


def ffn_kernel(
    count_of,
    core_ref,
    row_ref,
    part_ref,
    mine_ref,
    theirs_ref,
    rows_ref,
    cotan_ref,
    vec_ref,
    *more,
):
    stacks, more = more[:count_of], more[count_of:]
    active_ref, slope_ref, inner_out_ref, outer_w_ref, hidden_ref, normed_ref = more[:6]
    scale_ref, result_ref, grad_ref, out_w_ref, sums_ref, resid, acc, pre, inner_w, sems = more[6:]
    w, last = pl.program_id(0), pl.num_programs(0) - 1
    count, width = acc.shape
    chunk = pre.shape[2]
    vec = lambda at: vec_ref[at : at + 1, :]
    half_of = lambda at: out_w_ref[pl.ds(pl.multiple_of(at * (width // 2), width // 2), width // 2), :]
    slots = [(stack, k) for stack in stacks for k in range(stack.shape[0])]
    deep = 4 * width // len(slots)
    thin = width // len(slots)

    def fetch(block):
        for slot, (stack, k) in enumerate(slots):

            @pl.when(part_ref[slot] == block)
            def _():
                start = pl.multiple_of(row_ref[slot] * deep, deep)
                pltpu.make_async_copy(
                    stack.at[k, pl.ds(0, deep), :],
                    inner_w.at[lax.rem(block, 2), pl.ds(start, deep), :],
                    sems.at[lax.rem(block, 2)],
                ).start()

    def fetch_outer(block):
        for slot, (stack, k) in enumerate(slots):

            @pl.when(row_ref[slot] // 2 == block)
            def _():
                start = lax.rem(row_ref[slot], 2) * 4 * deep + part_ref[slot] * deep
                pltpu.make_async_copy(
                    stack.at[k, pl.ds(stack.shape[1] - deep, deep), :],
                    outer_w_ref.at[pl.ds(pl.multiple_of(start, deep), deep), :],
                    sems.at[3],
                ).start()

    def arrived(block):
        target = inner_w.at[lax.rem(block, 2)]
        pltpu.make_async_copy(target, target, sems.at[lax.rem(block, 2)]).wait()

    @pl.when(w == 0)
    def _():
        for slot, (stack, k) in enumerate(slots):
            start = pl.multiple_of(row_ref[slot] * 4 * thin + part_ref[slot] * thin, thin)
            pltpu.make_async_copy(
                stack.at[k, pl.ds(deep, thin), :], out_w_ref.at[pl.ds(start, thin), :], sems.at[2]
            ).start()
        fetch(w)
        pltpu.make_async_copy(out_w_ref, out_w_ref, sems.at[2]).wait()
        acc[...] = jnp.dot(mine_ref[...], half_of(core_ref[0]), preferred_element_type=F32)
        acc[...] += jnp.dot(theirs_ref[...], half_of(1 - core_ref[0]), preferred_element_type=F32)

        def enter(part):
            normed, scale = normalize(acc[part, :] + vec(2) + rows_ref[part, :].astype(F32))
            normed_ref[part, :] = normed.astype(BF16)
            scale_ref[part, :] = scale
            hidden = normed * vec(3) + vec(4)
            resid[part, :] = hidden + vec(5)
            hidden_ref[part, :] = hidden.astype(BF16)

        in_parts(count, enter)

    fetch_outer(w)
    arrived(w)

    @pl.when(w < last)
    def _():
        fetch(w + 1)

    now = lax.rem(w, 2)
    inner_out_ref[...] = inner_w[now]
    bias = vec_ref[pl.ds(8 + w, 1), :]

    def expand(n):
        cut = slice(n * chunk, (n + 1) * chunk)
        weight = inner_w[now, :, cut]
        pre[n % 2] = jnp.dot(hidden_ref[...], weight, preferred_element_type=F32)

    def bend(n):
        cut = slice(n * chunk, (n + 1) * chunk)
        for at in range(0, count, TILE):
            part = slice(at, at + TILE)
            active, slope = gelu_and_slope(pre[n % 2, part, :] + bias[:, cut])
            active_ref[part, cut] = active.astype(BF16)
            slope_ref[part, cut] = slope.astype(BF16)

    chunks = width // chunk
    expand(0)
    for n in range(1, chunks):
        expand(n)
        bend(n - 1)
    bend(chunks - 1)
    pltpu.make_async_copy(outer_w_ref, outer_w_ref, sems.at[3]).wait()

    def contract():
        weight = outer_w_ref[...]
        return jnp.dot(active_ref[...], weight, preferred_element_type=F32)

    @pl.when(w == 0)
    def _():
        acc[...] = contract()

    @pl.when(w > 0)
    def _():
        acc[...] += contract()

    @pl.when(w == last)
    def _():
        sums_ref[...] = jnp.zeros_like(sums_ref)

        def leave(part):
            normed, scale = normalize(resid[part, :] + acc[part, :])
            result_ref[part, :] = (normed * vec(6) + vec(7)).astype(BF16)
            cotan = cotan_ref[part, :].astype(F32)
            grad = norm_back(cotan * vec(6), normed, scale).astype(BF16)
            grad_ref[part, :] = grad
            sums_ref[0:1, :] += total_rows(cotan * normed)
            sums_ref[1:2, :] += total_rows(cotan)
            sums_ref[2:3, :] += total_rows(grad.astype(F32))

        in_parts(count, leave)


def ffn_back_kernel(
    core_ref,
    grad_ref,
    slope_ref,
    normed_ref,
    scale_ref,
    vec_ref,
    out_w_ref,
    inner_w_ref,
    outer_w_ref,
    after_ref,
    pre_grad_ref,
    branch_ref,
    mine_ref,
    theirs_ref,
    sums_ref,
    acc,
    pre,
):
    w = pl.program_id(0)
    count, width = acc.shape
    chunk = pre.shape[2]
    vec = lambda at: vec_ref[at : at + 1, :]

    @pl.when(w == 0)
    def _():
        sums_ref[...] = jnp.zeros_like(sums_ref)

    def pull(n):
        weight = outer_w_ref[n * chunk : (n + 1) * chunk, :]
        pre[n % 2] = lax.dot_general(grad_ref[...], weight, NT, preferred_element_type=F32)

    def bend(n):
        cut = slice(n * chunk, (n + 1) * chunk)
        sums = jnp.zeros((8, chunk), F32)
        for at in range(0, count, TILE):
            part = slice(at, at + TILE)
            back = pre[n % 2, part, :].astype(BF16).astype(F32) * slope_ref[part, cut].astype(F32)
            back = back.astype(BF16)
            pre_grad_ref[part, cut] = back
            sums += jnp.sum(back.astype(F32).reshape(TILE // 8, 8, chunk), axis=0)
        sums_ref[pl.ds(4 + w, 1), cut] += total_rows(sums)

    chunks = width // chunk
    pull(0)
    for n in range(1, chunks):
        pull(n)
        bend(n - 1)
    bend(chunks - 1)

    def contract():
        weight = inner_w_ref[...]
        return lax.dot_general(pre_grad_ref[...], weight, NT, preferred_element_type=F32)

    @pl.when(w == 0)
    def _():
        acc[...] = contract()

    @pl.when(w > 0)
    def _():
        acc[...] += contract()

    @pl.when(w == pl.num_programs(0) - 1)
    def _():
        def leave(part):
            through = acc[part, :].astype(BF16).astype(F32) + grad_ref[part, :].astype(F32)
            normed = normed_ref[part, :].astype(F32)
            branch = norm_back(through * vec(3), normed, scale_ref[part, :]).astype(BF16)
            branch_ref[part, :] = branch
            sums_ref[0:1, :] += total_rows(through * normed)
            sums_ref[1:2, :] += total_rows(through)
            sums_ref[2:3, :] += total_rows(branch.astype(F32))

        in_parts(count, leave)
        part = width // 2
        for out, at in ((mine_ref, core_ref[0]), (theirs_ref, 1 - core_ref[0])):
            weight = out_w_ref[pl.ds(pl.multiple_of(at * part, part), part), :]
            out[...] = lax.dot_general(
                branch_ref[...], weight, NT, preferred_element_type=F32
            ).astype(BF16)


def ffn_call(kernel, scalars, ins, anys, outs, scratch, width, steps, room, name):
    def spec(shape):
        if shape[1] == steps * width:
            return pl.BlockSpec((shape[0], width), lambda w: (0, w))
        if shape[0] == steps * width:
            return pl.BlockSpec((width, width), lambda w: (w, 0))
        return pl.BlockSpec(shape, lambda w: (0, 0), pipeline_mode=pl.Buffered(1))

    return pl.pallas_call(
        kernel,
        grid=(steps,),
        in_specs=[pl.BlockSpec(memory_space=pltpu.SMEM)] * len(scalars)
        + [spec(a.shape) for a in ins]
        + [pl.BlockSpec(memory_space=pl.ANY)] * len(anys),
        out_specs=[spec(shape) for shape, kind in outs],
        out_shape=[jax.ShapeDtypeStruct(shape, kind) for shape, kind in outs],
        scratch_shapes=scratch,
        compiler_params=pltpu.CompilerParams(vmem_limit_bytes=room * 1024 * 1024),
        cost_estimate=weight_of(40),
        name=name,
    )(*scalars, *ins, *anys)


def ffn(core, places, mine, theirs, rows, cotan, vec, stacks):
    count, width = rows.shape
    units = 4 * width
    low = (rows.shape, BF16)
    outs = [((count, units), BF16)] * 2 + [((width, units), BF16), ((units, width), BF16)]
    outs += [low, low, ((count, 1), F32), low, low, ((width, width), BF16), ((8, width), F32)]
    scratch = [
        pltpu.VMEM((count, width), F32),
        pltpu.VMEM((count, width), F32),
        pltpu.VMEM((2, count, 256), F32),
        pltpu.VMEM((2, width, width), BF16),
        pltpu.SemaphoreType.DMA((4,)),
    ]
    tables = [jnp.stack([p[axis] for p in places]).astype(jnp.int32) for axis in range(2)]
    kernel = functools.partial(ffn_kernel, len(stacks))
    ins = [mine, theirs, rows, cotan, vec]
    return ffn_call(kernel, [core, *tables], ins, stacks, outs, scratch, width, 4, 58, "ffn")


def ffn_back(core, grad, slope, normed, scale, vec, out_w, inner_w, outer_w, after):
    count, width = grad.shape
    part = ((count, width // 2), BF16)
    outs = [(slope.shape, BF16), (grad.shape, BF16), part, part, ((8, width), F32)]
    scratch = [pltpu.VMEM((count, width), F32), pltpu.VMEM((2, count, 256), F32)]
    ins = [grad, slope, normed, scale, vec, out_w, inner_w, outer_w]
    return ffn_call(
        ffn_back_kernel, [core], ins, after, outs, scratch, width, 4, 44, "ffn_back"
    )


def product_kernel(count, stacked, after, where_ref, *refs):
    lefts, right_ref, out_ref = refs[:count], refs[count], refs[count + 1 + after]
    if not stacked:
        total, rows = None, lefts[0].shape[0]
        for n, left_ref in enumerate(lefts):
            right = right_ref[n * rows : (n + 1) * rows, :]
            part = lax.dot_general(left_ref[...], right, TN, preferred_element_type=F32)
            total = part if n == 0 else total + part
        out_ref[...] = total.astype(BF16)
        return
    for n, left_ref in enumerate(lefts):

        @pl.when(pl.program_id(0) == n)
        def _():
            out_ref[...] = lax.dot_general(
                left_ref[...], right_ref[...], TN, preferred_element_type=F32
            ).astype(BF16)


def product(where, lefts, right, side, after=(), stacked=False):
    width = right.shape[1] // (1 if side is None else 2)
    tile = 512
    height = sum(left.shape[1] for left in lefts) if stacked else lefts[0].shape[1]
    micros = 2e-9 * height * width * right.shape[0] + 1
    half = lambda a, w: (0, 0 if side is None else (w[3] if side else 1 - w[3]))
    if stacked:
        left_place = lambda a, w: (0, 0)
        place = lambda a, w: (a + w[3] - 2 * a * w[3], 0)
    else:
        left_place = lambda a, w: (0, a)
        place = lambda a, w: (a, 0)
    return pl.pallas_call(
        functools.partial(product_kernel, len(lefts), stacked, len(after)),
        grid_spec=pltpu.PrefetchScalarGridSpec(
            num_scalar_prefetch=1,
            grid=(height // tile,),
            in_specs=[pl.BlockSpec((left.shape[0], tile), left_place) for left in lefts]
            + [pl.BlockSpec((right.shape[0], width), half, pipeline_mode=pl.Buffered(1))]
            + [pl.BlockSpec(memory_space=pl.ANY)] * len(after),
            out_specs=pl.BlockSpec((tile, width), place),
        ),
        out_shape=jax.ShapeDtypeStruct((height, width), BF16),
        compiler_params=pltpu.CompilerParams(vmem_limit_bytes=2 * SMALL_VMEM),
        cost_estimate=weight_of(micros),
        name="product",
    )(where, *[*lefts, right], *after)


def attend_kernel(held, seg_row_ref, seg_col_ref, qkv_ref, *rest):
    rest = rest[held:]
    out_refs, (lse_ref, bias_ref, stat_ref, score_ref, expo_ref) = rest[:2], rest[2:]
    half = qkv_ref.shape[2]
    pair = pl.program_id(1)
    length = bias_ref.shape[0]
    chunk = score_ref.shape[1]

    @pl.when(pair == 0)
    def _():
        bias_ref[...] = jnp.where(seg_col_ref[0] == seg_row_ref[0], 0.0, MASKED)
        stat_ref[...] = jnp.zeros_like(stat_ref)

    block = qkv_ref[:, 0].reshape(length, 3 * PAIR)
    q, k, v = (block[:, i * PAIR : (i + 1) * PAIR] for i in range(3))
    lane = lax.broadcasted_iota(jnp.int32, (length, PAIR), 1)
    low = lane < HD
    zero, one = jnp.zeros_like(q), jnp.ones_like(v)
    q_heads = [jnp.where(low, q, zero), jnp.where(low, zero, q)]
    v_heads = [jnp.where(low, v, one), jnp.where(low, one, v)]
    lane, low = lane[:chunk], low[:chunk]

    def score(step):
        c, h = divmod(step, 2)
        score_ref[step % 2] = lax.dot_general(
            q_heads[h][c * chunk : (c + 1) * chunk], k, NT, preferred_element_type=F32
        )

    def soften(step):
        c, h = divmod(step, 2)
        tops = []
        for at in range(0, chunk, TILE):
            rows = slice(c * chunk + at, c * chunk + at + TILE)
            s = score_ref[step % 2, at : at + TILE, :] + bias_ref[rows, :]
            top = jnp.max(s, axis=1, keepdims=True)
            expo_ref[step % 2, at : at + TILE, :] = jnp.exp(s - top).astype(BF16)
            tops.append(top)
        return jnp.concatenate(tops, 0)

    def mix(step):
        return jnp.dot(expo_ref[step % 2], v_heads[step % 2], preferred_element_type=F32)

    def finish(c, got, tops):
        rows = slice(c * chunk, (c + 1) * chunk)
        total = jnp.where(low, got[1], got[0])
        mixed = jnp.where(low, got[0], got[1]) / pltpu.roll(total, HD, 1)
        log = jnp.log(total)
        stat = stat_ref[rows, :]
        stat = jnp.where(lane == 2 * pair, tops[0] + log[:, HD : HD + 1], stat)
        stat_ref[rows, :] = jnp.where(lane == 2 * pair + 1, tops[1] + log[:, :1], stat)
        part, at = divmod(c * chunk, half)
        out_refs[part][0, at : at + chunk, :] = mixed.astype(BF16)

    steps = 2 * length // chunk
    tops, got = [], []
    score(0)
    for step in range(steps):
        if step + 1 < steps:
            score(step + 1)
        tops.append(soften(step))
        got.append(mix(step))
        if step % 2:
            finish(step // 2, got[-2:], tops[-2:])

    @pl.when(pair == pl.num_programs(1) - 1)
    def _():
        lse_ref[0] = jnp.transpose(stat_ref[...])[: lse_ref.shape[1]]


def attend_back_kernel(first_pair, after, *refs):
    seg_row_ref, seg_col_ref, qkv_ref, out_a, out_b, grad_a, grad_b, lse_ref = refs[:8]
    dqkv_ref, sums_ref, bias_ref, ds_ref, score_ref, slope_ref, prob_ref = refs[8 + after :]
    pair = pl.program_id(1)
    length = bias_ref.shape[0]
    half = qkv_ref.shape[2]
    chunk = score_ref.shape[1]

    @pl.when(pair == 0)
    def _():
        bias_ref[...] = jnp.where(seg_col_ref[0] == seg_row_ref[0], 0.0, MASKED)

    @pl.when((pair == 0) & (pl.program_id(0) == 0))
    def _():
        sums_ref[...] = jnp.zeros_like(sums_ref)

    block = qkv_ref[:, 0].reshape(length, 3 * PAIR)
    q, k, v = (block[:, i * PAIR : (i + 1) * PAIR] for i in range(3))
    out = jnp.concatenate([out_a[0], out_b[0]], 0)
    grad = jnp.concatenate([grad_a[0], grad_b[0]], 0)
    low = lax.broadcasted_iota(jnp.int32, (length, PAIR), 1) < HD
    zero = jnp.zeros_like(q)
    heads = lambda array: [jnp.where(low, array, zero), jnp.where(low, zero, array)]
    q_heads, k_heads, g_heads = heads(q), heads(k), heads(grad)
    product = jnp.transpose(out.astype(F32) * grad.astype(F32))
    chunks = length // chunk
    deltas = [total_rows(product[h * HD : (h + 1) * HD]) for h in range(2)]
    stats = [lse_ref[0, pl.ds(2 * (first_pair + pair) + h, 1), :] for h in range(2)]

    def score(step):
        h, c = divmod(step, chunks)
        rows = slice(c * chunk, (c + 1) * chunk)
        score_ref[step % 2] = lax.dot_general(k[rows], q_heads[h], NT, preferred_element_type=F32)
        slope_ref[step % 2] = lax.dot_general(v[rows], g_heads[h], NT, preferred_element_type=F32)

    def bend(step):
        h, c = divmod(step, chunks)
        for at in range(0, chunk, TILE):
            rows = slice(c * chunk + at, c * chunk + at + TILE)
            part = slice(at, at + TILE)
            p = jnp.exp(score_ref[step % 2, part, :] + bias_ref[rows, :] - stats[h])
            prob_ref[step % 2, part, :] = p.astype(BF16)
            ds_ref[h, rows, :] = (p * (slope_ref[step % 2, part, :] - deltas[h])).astype(BF16)

    steps = 2 * chunks
    dk, dv = [None] * chunks, [None] * chunks
    dq = None
    score(0)
    for step in range(steps):
        h, c = divmod(step, chunks)
        if step + 1 < steps:
            score(step + 1)
        bend(step)
        rows = slice(c * chunk, (c + 1) * chunk)
        v_part = jnp.dot(prob_ref[step % 2], g_heads[h], preferred_element_type=F32)
        k_part = jnp.dot(ds_ref[h, rows, :], q_heads[h], preferred_element_type=F32)
        if h == 0:
            dk[c], dv[c] = k_part, v_part
        else:
            part, at = c * chunk // half, c * chunk % half
            dqkv_ref[part, 0, at : at + chunk, PAIR : 2 * PAIR] = (dk[c] + k_part).astype(BF16)
            dv[c] = (dv[c] + v_part).astype(BF16)
            dqkv_ref[part, 0, at : at + chunk, 2 * PAIR :] = dv[c]
        if c == chunks - 1:
            part = lax.dot_general(ds_ref[h], k_heads[h], TN, preferred_element_type=F32)
            dq = part if h == 0 else dq + part
    dq = (dq * HD**-0.5).astype(BF16)
    dqkv_ref[:, 0, :, :PAIR] = dq.reshape(-1, half, PAIR)
    sums = [total_rows(dq.astype(F32)), sum(total_rows(part.astype(F32)) for part in dv)]
    sums_ref[0:1, pl.ds(pl.multiple_of(pair * PAIR, PAIR), PAIR)] += sums[0]
    sums_ref[1:2, pl.ds(pl.multiple_of(pair * PAIR, PAIR), PAIR)] += sums[1]


def attention_call(
    kernel, seg, arrays, pairs, outs, scratch, name, first=0, after=(), seqs=None, held=()
):
    parts, count, half, columns = arrays[0].shape
    start, seqs = seqs or (0, count)
    micros = 6.5 * seqs if name == "attend" else 3.7 * seqs
    length = parts * half

    def spec(array, first):
        shape = array.shape
        if len(shape) == 4:
            return pl.BlockSpec(
                (parts, 1, half, 3 * PAIR), lambda s, p: (0, start + s, 0, first + p)
            )
        if len(shape) == 3 and shape[1] == half:
            return pl.BlockSpec((1, half, PAIR), lambda s, p: (start + s, 0, first + p))
        if len(shape) == 3:
            return pl.BlockSpec((1,) + shape[1:], lambda s, p: (start + s, 0, 0))
        return pl.BlockSpec(shape, lambda s, p: (0, 0))

    operands = [seg[:, None, :], seg[:, :, None]] + arrays
    return pl.pallas_call(
        kernel,
        grid=(seqs, pairs),
        in_specs=[spec(a, first) for a in operands]
        + [pl.BlockSpec(memory_space=pl.ANY)] * (len(held) + len(after)),
        out_specs=[spec(a, 0) for a in outs],
        out_shape=outs,
        scratch_shapes=scratch(length),
        input_output_aliases={len(operands) + n: n for n in range(len(held))},
        compiler_params=pltpu.CompilerParams(vmem_limit_bytes=SMALL_VMEM),
        cost_estimate=weight_of(micros),
        name=name,
    )(*operands, *held, *after)


def attend(qkv, seg, seqs, held, after):
    parts, count, half, columns = qkv.shape
    pairs = columns // (3 * PAIR)
    outs = [
        jax.ShapeDtypeStruct((count, half, columns // 3), BF16),
        jax.ShapeDtypeStruct((count, half, columns // 3), BF16),
        jax.ShapeDtypeStruct((count, 2 * pairs, parts * half), F32),
    ]
    scratch = lambda length: [
        pltpu.VMEM((length, length), F32),
        pltpu.VMEM((length, PAIR), F32),
        pltpu.VMEM((2, 128, length), F32),
        pltpu.VMEM((2, 128, length), BF16),
    ]
    kernel = functools.partial(attend_kernel, len(held) + len(after))
    return attention_call(
        kernel, seg, [qkv], pairs, outs, scratch, "attend", 0, after, seqs, held
    )


def attend_back(qkv, seg, out, grad, lse, first, pairs, after):
    outs = [
        jax.ShapeDtypeStruct(qkv.shape[:3] + (3 * PAIR * pairs,), BF16),
        jax.ShapeDtypeStruct((8, PAIR * pairs), F32),
    ]
    scratch = lambda length: [
        pltpu.VMEM((length, length), F32),
        pltpu.VMEM((2, length, length), BF16),
        pltpu.VMEM((2, 128, length), F32),
        pltpu.VMEM((2, 128, length), F32),
        pltpu.VMEM((2, 128, length), BF16),
    ]
    kernel = functools.partial(attend_back_kernel, first, len(after))
    arrays = [qkv, *out, *grad, lse]
    return attention_call(kernel, seg, arrays, pairs, outs, scratch, "attend_back", first, after)


def body(
    layer_input,
    segment_ids,
    out_cotangent,
    attn_master,
    inner_master,
    outer_master,
    vector_master,
    attn_moment,
    inner_moment,
    outer_moment,
    vector_moment,
    attn_square,
    inner_square,
    outer_square,
    vector_square,
):
    seqs, half, width = layer_input.shape
    count = seqs * half
    hidden_units = inner_master.shape[1]
    pairs = width // (2 * PAIR)
    part_cols = width // 2
    shards = lax.axis_size("shard")
    owned_rows = attn_master.shape[1]
    core = lax.axis_index("ctx")
    first = core == 0

    def own_half(array, axis):
        size = array.shape[axis] // 2
        return lax.dynamic_slice_in_dim(array, core * size, size, axis)

    def other_half(array, axis):
        size = array.shape[axis] // 2
        return lax.dynamic_slice_in_dim(array, (1 - core) * size, size, axis)

    def in_order(mine, theirs, axis):
        return jnp.concatenate(
            [jnp.where(first, mine, theirs), jnp.where(first, theirs, mine)], axis
        )

    rows = layer_input.reshape(count, width)
    rows_theirs = swap_cores(rows)
    square = is_square()
    o, i, y, inner = position()
    where = jnp.stack([o, i, y, core]).astype(jnp.int32)

    piece = own_half(attn_master[:3], 2).astype(BF16).reshape(3, owned_rows, pairs, PAIR)
    piece = piece.transpose(1, 2, 0, 3).reshape(owned_rows, 3 * part_cols)
    vec_low = vector_master.astype(BF16)
    rider = vec_low[:2].reshape(1, -1)
    if square:
        piece = lax.dynamic_slice_in_dim(piece, y * (piece.shape[1] // 2), piece.shape[1] // 2, 1)
    rider = jnp.pad(rider, ((0, 15), (0, piece.shape[1] - rider.shape[1])))
    piece = jnp.concatenate([piece, rider], 0)

    def every_row(block):
        size = block.shape[0] // (lax.axis_size("replica") * 2)
        part = lax.dynamic_slice_in_dim(block, (2 * y + core) * size, size, 0).astype(BF16)
        return lax.all_gather(part, EVERY, axis=0, tiled=True)

    def placed(found, slots):
        chosen = jnp.stack([place[0] for place in slots[:shards]])
        chosen = (jnp.arange(shards)[:, None] == chosen[None, :]).astype(F32)
        return jnp.einsum("ps,srw->rpw", chosen, found.astype(F32)).reshape(-1, width)

    if square:
        q = 2 * core + y
        vec_rows = jnp.pad(vec_low.reshape(-1), (0, 16 * width - vec_low.size)).reshape(16, width)
        quarter = jnp.concatenate(
            [
                lax.dynamic_slice_in_dim(inner_master, q * width, width, 1).astype(BF16),
                lax.dynamic_slice_in_dim(
                    attn_master[3], q * (owned_rows // 4), owned_rows // 4, 0
                ).astype(BF16),
                vec_rows,
                lax.dynamic_slice_in_dim(
                    outer_master, q * (outer_master.shape[0] // 4), outer_master.shape[0] // 4, 0
                ).astype(BF16),
            ],
            0,
        )
        line = jnp.stack([piece] + [shift_outer(piece, -k) for k in range(1, OUTER)])
        near_x, near_y = shift_inner(line, 1), shift_replica(line, 1)
        (quarter,) = relay(where, [quarter], (line,))
        across = swap_outer(quarter, 2)
        two = (OUTER // 2,)
        far = small_call(
            halves_kernel, where, [near_x, near_y], [two + piece.shape] * 2, (), "halves"
        )
        stacks = [line, near_x, near_y, shift_inner(far[0], 1), shift_replica(far[1], 1)]
        (pair,) = small_call(
            pair_kernel, where, [quarter, across], [two + quarter.shape], tuple(stacks[3:]), "pair"
        )
        places = quarter_places([lax.rem(o + k, OUTER) for k in range(OUTER)])
        other_pair = swap_outer(pair, 1)
        pair_x, pair_y = shift_inner(pair, 1), shift_replica(pair, 1)
        done = (pair,)
    else:
        stacks = [item[None] for item in ring_gather(piece)]
        places = [(owner, 0) for owner in slot_owners()]
        wide = hidden_units // width
        inner_w = every_row(inner_master).reshape(8, -1, wide, width).transpose(0, 2, 1, 3)
        slots = [inner_w.reshape(PARTS, -1, width), every_row(attn_master[3]).reshape(PARTS, -1, width)]
        slots = jnp.pad(jnp.concatenate(slots, 1), ((0, 0), (0, 16), (0, 0)))
        outer_w = every_row(outer_master).reshape(PARTS, -1, width)
        slots = jnp.concatenate([slots, outer_w], 1)
        wide_stacks = [slots[n : n + 2] for n in range(0, PARTS, 2)]
        wide_places = [(jnp.int32(n // 4), jnp.int32(n % 4)) for n in range(PARTS)]
        vec = lax.all_gather(vec_low, "shard", axis=1, tiled=True).astype(F32)
        done = ()
    riders = jnp.concatenate([stack[:, owned_rows] for stack in stacks], 0)[:shards]
    riders = riders[:, : 2 * width // shards].reshape(shards, 2, -1)
    biases = placed(riders, places)

    halves = own_half(biases, 1).reshape(2, pairs, PAIR)
    bias = jnp.stack([halves[0], jnp.zeros_like(halves[0]), halves[1]], 1).reshape(1, -1)
    ones = jnp.ones((pairs, PAIR), F32)
    factor = jnp.stack([ones * HD**-0.5, ones, ones], 1).reshape(1, -1)
    qkv, qkv_w = project(rows, rows_theirs, stacks, places, bias, factor, done)
    qkv = qkv.reshape(2, seqs, half, 3 * part_cols)
    seg = jnp.concatenate([own_half(segment_ids, 1), other_half(segment_ids, 1)], 1)
    if square:
        (other_pair,) = relay(where, [other_pair], (qkv_w,))
        other_x, other_y = shift_inner(other_pair, 1), shift_replica(other_pair, 1)
        early = attend(qkv, seg, (0, seqs // 2), (), (other_pair,))
        near = [pair, other_pair, pair_x, other_x, pair_y, other_y]
        bulk, *relayed = small_call(
            bulk_kernel,
            where,
            near,
            [(12,) + quarter.shape, pair.shape, pair.shape],
            (early[0],),
            "bulk",
        )
        far_pair = [shift_inner(relayed[0], 1), shift_replica(relayed[1], 1)]
        near_rows = bulk[:8, 160:162].reshape(shards, -1)[:, : vec_low.size]
        both = line_order(o)
        places = quarter_places(both[0] + both[1])
        vec = placed(near_rows.reshape((shards,) + vec_low.shape), places)
        wide_places = [(row, 2 * core + side) for row, side in places]
        wide_places += [(row, 2 * (1 - core) + side) for row, side in places]
    else:
        early = attend(qkv, seg, (0, seqs // 2), (), ())
    mixed_mine, mixed_sent, lse = attend(qkv, seg, (seqs // 2, seqs - seqs // 2), early, ())
    if square:
        (far_bulk,) = small_call(
            bulk_kernel, where, far_pair, [(4,) + quarter.shape], (mixed_mine,), "bulk"
        )
        wide_stacks = [bulk, far_bulk, swap_cores(bulk), swap_cores(far_bulk)]
    flat = lambda array: array.reshape(count, part_cols)
    deep = lambda array: array.reshape(seqs, half, part_cols)
    heads_mine, heads_theirs = flat(mixed_mine), swap_cores(flat(mixed_sent))

    cotan = out_cotangent.reshape(count, width)
    core_at = jnp.full((1,), core, jnp.int32)
    forward = ffn(core_at, wide_places, heads_mine, heads_theirs, rows, cotan, vec, wide_stacks)
    active, slope, inner_w, outer_w, hidden_low, normed, scale, result = forward[:8]
    ffn_grad, out_w, sums_two = forward[8:]

    by_shard = lambda array: array.reshape(shards, -1, array.shape[1])

    outer_sent = product(where, [active], ffn_grad, 0)
    outer_kept = product(where, [active], ffn_grad, 1, (outer_sent,))
    outer_chips = [by_shard(outer_kept), by_shard(swap_cores(outer_sent))]
    done = (outer_kept,)
    if square:
        outer = Sum(where, outer_chips)
        done = outer.merge()
    pre_grad, branch_grad, mine, sent, sums_one = ffn_back(
        core_at, ffn_grad, slope, normed, scale, vec, out_w, inner_w, outer_w, done[:1]
    )
    got = swap_cores(sent)
    mixed_grad = [deep(mine), deep(got)]
    done = outer.plane((pre_grad,)) if square else ()
    heads = [heads_mine, heads_theirs]
    inner_kept = product(where, [hidden_low], pre_grad, 1, done)
    done = outer.cross((inner_kept,)) if square else (inner_kept,)
    inner_sent = product(where, [hidden_low], pre_grad, 0, done)
    out_sent = product(where, heads, branch_grad, 0, (inner_sent,), True)
    out_kept = product(where, heads, branch_grad, 1, (out_sent,), True)
    inner_chips = [by_shard(inner_kept), by_shard(swap_cores(inner_sent))]
    out_chips = [by_shard(out_kept), by_shard(swap_cores(out_sent))]

    def back(first, after):
        grad, sums = attend_back(
            qkv, seg, (mixed_mine, mixed_sent), mixed_grad, lse, first, pairs // 2, after
        )
        return grad.reshape(2 * count, -1), sums

    def vector_chip(sums_a, sums_b):
        blank = jnp.zeros((part_cols,), F32)
        ours = jnp.concatenate([sums_a, sums_b], 1)
        attn_biases = jnp.stack([in_order(ours[at], blank, 0) for at in range(2)])
        sums = [attn_biases, sums_one[2:3], sums_one[:2], sums_two[2:3], sums_two[:2]]
        sums = jnp.concatenate(sums + [sums_one[4:8]], 0)
        sums = sums.reshape(-1, shards, width // shards).transpose(1, 0, 2)
        sums = jnp.pad(sums, ((0, 0), (0, owned_rows - sums.shape[1]), (0, 0)))
        return sums.astype(BF16)

    outer_states = (outer_master, outer_moment, outer_square)
    inner_states = (inner_master, inner_moment, inner_square)
    attn_states = (attn_master, attn_moment, attn_square)
    if square:
        inner = Sum(where, inner_chips)
        done = outer.turn((out_kept,))
        done = inner.merge(done)
        grad_a, sums_a = back(0, done)
        done = outer.line((grad_a,))
        ours = by_shard(product(where, [rows, rows_theirs], grad_a, None, done))
        done = inner.plane((ours,))
        sum_a = Sum(where, [ours], out_chips)
        done = sum_a.merge(done)
        grad_b, sums_b = back(pairs // 2, done)
        done = inner.cross((grad_b,))
        done = sum_a.plane(done)
        theirs_part = input_back(grad_a, grad_b, qkv_w, (), done)
        ours = by_shard(product(where, [rows, rows_theirs], grad_b, None, (theirs_part,)))
        sum_b = Sum(where, [ours], [vector_chip(sums_a, sums_b)])
        done = sum_a.cross((ours,))
        done = sum_b.merge(done)
        outer_new = update(where, outer_states, [outer.shares], done)
        input_grad = input_back(
            grad_a, grad_b, qkv_w, (branch_grad, swap_cores(theirs_part)), (outer_new[0],)
        )
        done = sum_b.plane((input_grad,))
        done = inner.turn(done)
        done = sum_a.turn(done)
        done = sum_b.cross(done)
        done = inner.line(done)
        done = sum_b.turn(done)
        inner_new = update(where, inner_states, [inner.shares], done)
        done = sum_a.line((inner_new[0],))
        sum_b.line(done)
        attn_shares = [sum_a.shares, sum_b.shares]
        vector_shares = [
            jnp.concatenate(
                [
                    jnp.where(y == 0, sum_b.shares[at], sum_b.shares[at + 1])[0],
                    jnp.where(y == 0, sum_b.shares[at + 1], sum_b.shares[at])[0],
                ],
                0,
            )
            for at in (0, 2)
        ]
    else:
        grad_a, sums_a = back(0, ())
        grad_b, sums_b = back(pairs // 2, ())
        theirs_part = input_back(grad_a, grad_b, qkv_w, (), ())
        added = (branch_grad, swap_cores(theirs_part))
        input_grad = input_back(grad_a, grad_b, qkv_w, added, ())
        outer_new = update(where, outer_states, [sum_apart(add_low(*outer_chips))])
        inner_new = update(where, inner_states, [sum_apart(add_low(*inner_chips))])
        ours = [by_shard(product(where, [rows, rows_theirs], grad, None)) for grad in (grad_a, grad_b)]
        chip_a = jnp.concatenate([ours[0], add_low(*out_chips)], 2)
        chip_b = jnp.concatenate([ours[1], vector_chip(sums_a, sums_b)], 2)
        attn_shares = [sum_apart(chip_a), sum_apart(chip_b)]
        vector_shares = [share[0] for share in attn_shares[1]]
    attn_new = update(where, attn_states, attn_shares)
    cut = grad_b.shape[1]
    vector_sum = sum(share[: vec_low.shape[0], cut:].astype(F32) for share in vector_shares)
    vector_new = adamw(vector_sum, vector_moment, vector_square, vector_master, RATE_VECTOR)
    vector_new = vector_new + (vector_new[2].astype(BF16),)
    news = (attn_new, inner_new, outer_new, vector_new)
    updates = [[new[at] for new in news] for at in range(4)]
    return (
        result.reshape(seqs, half, width).astype(BF16),
        input_grad.reshape(seqs, half, width),
        *[item for kind in updates for item in kind],
    )


def solution(mesh):
    tokens = P(("replica", "shard"), "ctx", None)
    states = (P(None, "shard", None), P("shard", None), P("shard", None), P(None, "shard"))
    in_specs = (tokens, P(("replica", "shard"), None), tokens) + states * 3
    out_specs = (tokens, tokens) + states * 4
    return jax.shard_map(body, mesh=mesh, in_specs=in_specs, out_specs=out_specs, check_vma=False)
```

```python
import functools
import math

import jax
import jax.numpy as jnp
from jax import lax
from jax.experimental import pallas as pl
from jax.experimental.pallas import tpu as pltpu
from jax.sharding import PartitionSpec as P

HD = 64
PAIR = 2 * HD
STEP = 5
OUTER = 4
EVERY = ("shard", "replica", "ctx")

EPS_NORM = 1e-05
BETA_ONE = 0.5
BETA_TWO = 0.6
RATE_MATRIX = 0.02
RATE_VECTOR = 0.1
DECAY = 0.01
EPS_ADAM = 1e-06
MASKED = -1e30
F32 = jnp.float32
BF16 = jnp.bfloat16
PARTS = 32
TILE = 32
VMEM = 56 * 1024 * 1024
SMALL_VMEM = 16 * 1024 * 1024
GROUP = 256
NT = (((1,), (1,)), ((), ()))
TN = (((0,), (0,)), ((), ()))


def weight_of(micros):
    return pl.CostEstimate(
        flops=int(micros * 2.9e8), bytes_accessed=int(micros * 9.2e5), transcendentals=0
    )


def normalize(resid):
    centre = resid - jnp.mean(resid, -1, keepdims=True)
    scale = lax.rsqrt(jnp.mean(centre * centre, -1, keepdims=True) + EPS_NORM)
    return (centre * scale, scale)


def norm_back(grad, normed, scale):
    return scale * (
        grad
        - jnp.mean(grad, -1, keepdims=True)
        - normed * jnp.mean(grad * normed, -1, keepdims=True)
    )


def adamw(grad, moment, square, weight, rate):
    moment_new = BETA_ONE * moment + (1.0 - BETA_ONE) * grad
    square_new = BETA_TWO * square + (1.0 - BETA_TWO) * grad * grad
    stepped = (
        moment_new
        / (1.0 - BETA_ONE**STEP)
        / (jnp.sqrt(square_new / (1.0 - BETA_TWO**STEP)) + EPS_ADAM)
    )
    weight_new = weight - rate * (stepped + DECAY * weight)
    return (moment_new, square_new, weight_new)


def swap_cores(value):
    return lax.ppermute(value, "ctx", [(0, 1), (1, 0)])


def shift_outer(value, step):
    inner = lax.axis_size("shard") // OUTER
    pairs = [
        (o * inner + i, ((o + step) % OUTER) * inner + i) for o in range(OUTER) for i in range(inner)
    ]
    return lax.ppermute(value, "shard", pairs)


def shift_inner(value, step):
    inner = lax.axis_size("shard") // OUTER
    pairs = [
        (o * inner + i, o * inner + (i + step) % inner) for o in range(OUTER) for i in range(inner)
    ]
    return lax.ppermute(value, "shard", pairs)


def shift_replica(value, step):
    size = lax.axis_size("replica")
    return lax.ppermute(value, "replica", [(r, (r + step) % size) for r in range(size)])


def ring_gather(piece):
    inner = lax.axis_size("shard") // OUTER
    found = []
    held = piece
    for k in range(OUTER):
        if k:
            held = shift_outer(held, -1)
        found.append([held] + [shift_inner(held, -e) for e in range(1, inner)])
    return [item for group in found for item in group]


def slot_owners():
    inner = lax.axis_size("shard") // OUTER
    at = lax.axis_index("shard")
    o, i = at // inner, at % inner
    return [
        lax.rem(o + k, OUTER) * inner + lax.rem(i + e, inner)
        for k in range(OUTER)
        for e in range(inner)
    ]


def pick(array, index, axis):
    return lax.dynamic_index_in_dim(array, index, axis, keepdims=False)


def add_low(value, *others):
    total = value.astype(F32)
    for item in others:
        total = total + item.astype(F32)
    return total.astype(BF16)


def position():
    inner = lax.axis_size("shard") // OUTER
    at = lax.axis_index("shard")
    return at // inner, at % inner, lax.axis_index("replica"), inner


def is_square():
    return lax.axis_size("replica") == 2 and lax.axis_size("shard") == 2 * OUTER


def swap_outer(value, flip):
    inner = lax.axis_size("shard") // OUTER
    pairs = [(o * inner + i, (o ^ flip) * inner + i) for o in range(OUTER) for i in range(inner)]
    return lax.ppermute(value, "shard", pairs)


def swap_cross(value):
    return lax.ppermute(value, ("replica", "ctx"), [(a, 3 - a) for a in range(4)])


def sum_apart(chip_sum):
    o, i, y, inner = position()
    grid = chip_sum.reshape(OUTER, inner, *chip_sum.shape[1:])
    got = [shift_inner(pick(grid, lax.rem(i + e, inner), 1), e) for e in range(1, inner)]
    line = add_low(pick(grid, i, 1), *got)
    got = [shift_outer(pick(line, lax.rem(o + d, OUTER), 0), d) for d in range(1, OUTER)]
    total = add_low(pick(line, o, 0), *got)
    got = [shift_replica(total, r) for r in range(1, lax.axis_size("replica"))]
    mine = add_low(total, *got)[None]
    return [mine, swap_cores(mine)]


def small_call(kernel, where, ins, outs, after, name):
    held = pl.BlockSpec(memory_space=pltpu.VMEM)
    return pl.pallas_call(
        functools.partial(kernel, len(ins), len(after)),
        in_specs=[pl.BlockSpec(memory_space=pltpu.SMEM)]
        + [held] * len(ins)
        + [pl.BlockSpec(memory_space=pl.ANY)] * len(after),
        out_specs=[held] * len(outs),
        out_shape=[pltpu.VMEM(shape, BF16) for shape in outs],
        compiler_params=pltpu.CompilerParams(vmem_limit_bytes=SMALL_VMEM),
        cost_estimate=weight_of(1),
        name=name,
    )(where, *[pltpu.with_memory_space_constraint(a, pltpu.VMEM) for a in ins], *after)


def fold_plane_kernel(count, after, where_ref, keep_p, got_p, keep_q, got_q, *rest):
    i, y = where_ref[1], where_ref[2]
    kept_p, send_p, kept_q, send_q = rest[after:]
    for o in range(OUTER):
        for out, at in ((kept_p, y), (send_p, 1 - y)):
            out[o] = add_low(keep_p[o, at], got_p[o, at])
        for out, at in ((kept_q, i), (send_q, 1 - i)):
            out[o] = add_low(keep_q[o, at], got_q[o, at])


def line_order(o):
    near = o + 1 - 2 * lax.rem(o, 2)
    far = lambda at: lax.rem(at + 2, OUTER)
    return (o, far(o)), (near, far(near))


def fold_cross_kernel(count, after, where_ref, keep_p, got_p, keep_q, got_q, *rest):
    for out, order in zip(rest[after:], line_order(where_ref[0])):
        for n, at in enumerate(order):
            out[n, 0] = add_low(keep_p[at], got_p[at])
            out[n, 1] = add_low(keep_q[at], got_q[at])


def fold_turn_kernel(count, after, where_ref, keep, got, *rest):
    for n, out in enumerate(rest[after:]):
        out[...] = add_low(keep[n], got[n])


def fold_line_kernel(count, after, where_ref, *rest):
    rest[count + after][...] = add_low(*(ref[...] for ref in rest[:count]))


def merge_kernel(groups, after, where_ref, *refs):
    outs = refs[4 * sum(groups) + after :]
    for slot, out in enumerate(outs):
        left = chip = 0
        for group in groups:
            for at in range(2):
                parts = []
                for n in range(chip, chip + group):
                    ref = refs[4 * n + slot]
                    parts.append(ref[0, at, 0, 0] if slot % 2 else ref[0, 0, 0, at])
                cut = slice(left, left + parts[0].shape[1])
                out[0, at, :, cut] = parts[0] if group == 1 else add_low(*parts)
            left, chip = cut.stop, chip + group


class Sum:
    def __init__(self, where, *groups):
        self.where, self.rows = where, groups[0][0].shape[1] // 4
        self.columns = sum(group[0].shape[2] for group in groups)
        self.groups = [len(group) for group in groups]
        self.chips = [
            c.reshape(OUTER, 2, 2, 2, self.rows, c.shape[2]) for group in groups for c in group
        ]

    def shape(self, *lead):
        return lead + (self.rows, self.columns)

    def merge(self, after=()):
        def spec(chip, lead, flip):
            def place(o, w):
                at = w[1] if lead == 0 else w[2]
                at = 1 - at if flip else at
                return (o, at, 0, 0, 0, 0) if lead == 0 else (o, 0, 1, at, 0, 0)

            return pl.BlockSpec(((1, 1, 1, 2) if lead == 0 else (1, 2, 1, 1)) + chip.shape[4:], place)

        kinds = ((0, True), (1, True), (0, False), (1, False))
        out_spec = pl.BlockSpec((1, 2, self.rows, self.columns), lambda o, w: (o, 0, 0, 0))
        *sent, keep_p, keep_q = pl.pallas_call(
            functools.partial(merge_kernel, self.groups, len(after)),
            grid_spec=pltpu.PrefetchScalarGridSpec(
                num_scalar_prefetch=1,
                grid=(OUTER,),
                in_specs=[spec(chip, *kind) for chip in self.chips for kind in kinds]
                + [pl.BlockSpec(memory_space=pl.ANY)] * len(after),
                out_specs=[out_spec] * 4,
            ),
            out_shape=[jax.ShapeDtypeStruct(self.shape(OUTER, 2), BF16)] * 4,
            compiler_params=pltpu.CompilerParams(vmem_limit_bytes=SMALL_VMEM),
            cost_estimate=weight_of(4),
            name="merge",
        )(self.where, *[chip for chip in self.chips for _ in range(4)], *after)
        self.kept = [keep_p, shift_inner(sent[0], 1), keep_q, shift_replica(sent[1], 1)]
        return tuple(sent)

    def plane(self, after=()):
        keep_p, send_p, keep_q, send_q = small_call(
            fold_plane_kernel, self.where, self.kept, [self.shape(OUTER)] * 4, after, "fold_plane"
        )
        self.kept = [keep_p, shift_replica(send_p, 1), keep_q, shift_inner(send_q, 1)]
        return (send_p, send_q)

    def cross(self, after=()):
        keep, send = small_call(
            fold_cross_kernel, self.where, self.kept, [self.shape(2, 2)] * 2, after, "fold_cross"
        )
        self.kept = [keep, swap_outer(send, 1)]
        return (send,)

    def turn(self, after=()):
        shapes = [self.kept[0].shape[1:]] * 2
        keep, send = small_call(
            fold_turn_kernel, self.where, self.kept, shapes, after, "fold_turn"
        )
        self.kept = [keep, swap_outer(send, 2)]
        return (send,)

    def line(self, after=()):
        (total,) = small_call(
            fold_line_kernel, self.where, self.kept, [self.kept[0].shape], after, "fold_line"
        )
        self.shares = [total, shift_replica(total, 1), swap_cores(total), swap_cross(total)]
        return (total,)


def update_kernel(groups, after, where_ref, *refs):
    states, shares = refs[:3], refs[3 : 3 + sum(groups)]
    outs, grad_ref = refs[3 + sum(groups) + after : -1], refs[-1]
    rows = shares[0].shape[1]
    across = groups[0] // 2
    for core in range(2):

        @pl.when(pl.program_id(1) == core)
        def _():
            for n in range(across):
                line = where_ref[2] if n == 0 else 1 - where_ref[2]
                line = pl.ds(pl.multiple_of(line * rows, rows), rows) if across > 1 else slice(None)
                if len(groups) == 1:
                    grad_ref[line, :] = shares[across * core + n][0].astype(F32)
                    continue
                left, right = shares[across * core + n], shares[groups[0] + across * core + n]
                width = grad_ref.shape[2]
                pairs = width // PAIR
                for t in range(3):
                    for p in range(pairs):
                        side, at = (left, p) if 2 * p < pairs else (right, p - pairs // 2)
                        part = side[0, :, (3 * at + t) * PAIR : (3 * at + t + 1) * PAIR]
                        grad_ref[t, line, p * PAIR : (p + 1) * PAIR] = part.astype(F32)
                cut = 3 * PAIR * (pairs // 2)
                grad_ref[3, line, :] = left[0, :, cut : cut + width].astype(F32)

    new = adamw(grad_ref[...], states[1][...], states[2][...], states[0][...], RATE_MATRIX)
    for out, value in zip(outs, new + (new[2],)):
        out[...] = value.astype(out.dtype)


def update(where, states, groups, after=()):
    parts, rows = groups[0][0].shape[:2]
    rows = rows * (len(groups[0]) // 2)
    lead = states[0].shape[:-2]
    columns = states[0].shape[-1] // 2
    place = lambda p, v, w: (0,) * len(lead) + (p, w[3] + v - 2 * w[3] * v)
    block = pl.BlockSpec(lead + (rows, columns), place)
    shares = [share for group in groups for share in group]
    share_specs = [pl.BlockSpec((1,) + a.shape[1:], lambda p, v, w: (p, 0, 0)) for a in shares]
    kinds = (F32, F32, F32, BF16)
    return pl.pallas_call(
        functools.partial(update_kernel, [len(group) for group in groups], len(after)),
        grid_spec=pltpu.PrefetchScalarGridSpec(
            num_scalar_prefetch=1,
            grid=(parts, 2),
            in_specs=[block] * 3 + share_specs + [pl.BlockSpec(memory_space=pl.ANY)] * len(after),
            out_specs=[block] * 4,
            scratch_shapes=[pltpu.VMEM(lead + (rows, columns), F32)],
        ),
        out_shape=[jax.ShapeDtypeStruct(states[0].shape, kind) for kind in kinds],
        compiler_params=pltpu.CompilerParams(vmem_limit_bytes=SMALL_VMEM),
        cost_estimate=weight_of(5),
        name="update",
    )(where, *states, *shares, *after)


def input_back_kernel(a_ref, b_ref, left_ref, right_ref, *rest):
    out_ref = rest[-1]
    total = lax.dot_general(a_ref[...], left_ref[...], NT, preferred_element_type=F32)
    total += lax.dot_general(b_ref[...], right_ref[...], NT, preferred_element_type=F32)
    if out_ref.dtype == F32:
        total += rest[0][...].astype(F32) + rest[1][...].astype(F32)
    out_ref[...] = total.astype(out_ref.dtype)


def input_back(grad_a, grad_b, weight, added, after):
    count, cut = grad_a.shape[0] // 2, grad_a.shape[1]
    width = weight.shape[0]
    tile = width // 4
    first = 0 if added else 1
    side = pl.BlockSpec((count, cut), lambda n: (first, 0))
    line = pl.BlockSpec((count, tile), lambda n: (0, n))
    return pl.pallas_call(
        input_back_kernel,
        grid=(width // tile,),
        in_specs=[side, side]
        + [pl.BlockSpec((tile, cut), lambda n, at=at: (n, at)) for at in range(2)]
        + [line] * len(added)
        + [pl.BlockSpec(memory_space=pl.ANY)] * len(after),
        out_specs=line,
        out_shape=jax.ShapeDtypeStruct((count, width), F32 if added else BF16),
        compiler_params=pltpu.CompilerParams(vmem_limit_bytes=SMALL_VMEM),
        cost_estimate=weight_of(5),
        name="input_back",
    )(*[grad_a, grad_b, weight, weight, *added], *after)


def quarter_places(order):
    o, i, y, inner = position()
    kinds = ((i, y), (1 - i, y), (i, 1 - y), (1 - i, 1 - y))
    return [(row * 2 + across, side) for across, side in kinds for row in order]


def relay_kernel(count, after, where_ref, *rest):
    for source, out in zip(rest[:count], rest[count + after :]):
        out[...] = source[...]


def halves_kernel(count, after, where_ref, near_x, near_y, *rest):
    first, second = rest[after:]
    first[...] = near_y[: OUTER // 2]
    second[...] = near_x[OUTER // 2 :]


def pair_kernel(count, after, where_ref, own, other, *rest):
    rest[after][0] = own[...]
    rest[after][1] = other[...]


def bulk_kernel(count, after, where_ref, *rest):
    ins, (bulk, *far) = rest[:count], rest[count + after :]
    at = 0
    for source in ins:
        bulk[at : at + source.shape[0]] = source[...]
        at += source.shape[0]
    for out, source in zip(far, (4, 3)):
        out[...] = ins[source][...]


def relay(where, arrays, after):
    return small_call(relay_kernel, where, arrays, [a.shape for a in arrays], after, "relay")


def project_kernel(after, row_ref, column_ref, mine_ref, theirs_ref, bias_ref, factor_ref, *rest):
    stacks, (out_ref, weight_ref) = rest[: -2 - after], rest[-2:]
    columns = stacks[0].shape[2]
    part = weight_ref.shape[0] * weight_ref.shape[1] // columns
    part = part // sum(stack.shape[0] for stack in stacks)
    at = pl.program_id(0)

    @pl.when(at == 0)
    def _():
        slot = 0
        for stack in stacks:
            for k in range(stack.shape[0]):
                start = pl.multiple_of(row_ref[slot] * part, part)
                left = pl.multiple_of(column_ref[slot] * columns, PAIR)
                weight_ref[pl.ds(start, part), pl.ds(left, columns)] = stack[k, :part, :]
                slot += 1

    def fill(rows):
        acc = jnp.dot(rows, weight_ref[...], preferred_element_type=F32)
        out_ref[...] = ((acc + bias_ref[...]) * factor_ref[...]).astype(BF16)

    @pl.when(at < pl.num_programs(0) // 2)
    def _():
        fill(mine_ref[...])

    @pl.when(at >= pl.num_programs(0) // 2)
    def _():
        fill(theirs_ref[...])


def project(mine, theirs, stacks, places, bias, factor, after):
    count, width = mine.shape
    columns = bias.shape[1]
    tile = 512
    each = count // tile
    whole = lambda shape: pl.BlockSpec(shape, lambda m, *_: (0,) * len(shape))
    tables = [jnp.stack([p[axis] for p in places]).astype(jnp.int32) for axis in range(2)]
    return pl.pallas_call(
        functools.partial(project_kernel, len(after)),
        grid_spec=pltpu.PrefetchScalarGridSpec(
            num_scalar_prefetch=2,
            grid=(2 * each,),
            in_specs=[
                pl.BlockSpec((tile, width), lambda m, *_: (jnp.minimum(m, each - 1), 0)),
                pl.BlockSpec((tile, width), lambda m, *_: (jnp.maximum(m - each, 0), 0)),
                whole((1, columns)),
                whole((1, columns)),
            ]
            + [whole(stack.shape) for stack in stacks]
            + [pl.BlockSpec(memory_space=pl.ANY)] * len(after),
            out_specs=[
                pl.BlockSpec((tile, columns), lambda m, *_: (m, 0)),
                whole((width, columns)),
            ],
        ),
        out_shape=[jax.ShapeDtypeStruct((2 * count, columns), BF16), jax.ShapeDtypeStruct((width, columns), BF16)],
        compiler_params=pltpu.CompilerParams(vmem_limit_bytes=44 * 1024 * 1024),
        cost_estimate=weight_of(11),
        name="project",
    )(*tables, *[mine, theirs, bias, factor, *stacks], *after)


def gelu_and_slope(u):
    d = 1.0 + (0.3275911 * 0.5**0.5) * jnp.abs(u)
    t = pl.reciprocal(d, approx=True).astype(BF16)
    e = jnp.exp2(u * u * (-0.5 * math.log2(math.e))).astype(BF16)
    u = u.astype(BF16)
    a = jnp.abs(u)
    low = lambda value: jnp.asarray(value, BF16)
    series = low(0.5 * 1.061405429) * t - low(0.5 * 1.453152027)
    series = series * t + low(0.5 * 1.421413741)
    series = series * t - low(0.5 * 0.284496736)
    series = series * t + low(0.5 * 0.254829592)
    tail = series * t * e
    active = jnp.maximum(u, low(0.0)) - a * tail
    below = tail - a * (e * low(1.0 / math.sqrt(2.0 * math.pi)))
    return active, jnp.where(u >= low(0.0), low(1.0) - below, below)


def total_rows(value):
    return jnp.sum(value, axis=0, keepdims=True)


def in_parts(count, work):
    def turn(at, carry):
        work(pl.ds(pl.multiple_of(at * 128, 128), 128))
        return carry

    lax.fori_loop(0, count // 128, turn, 0)


def ffn_kernel(
    count_of,
    core_ref,
    row_ref,
    part_ref,
    mine_ref,
    theirs_ref,
    rows_ref,
    cotan_ref,
    vec_ref,
    *more,
):
    stacks, more = more[:count_of], more[count_of:]
    active_ref, slope_ref, inner_out_ref, outer_w_ref, hidden_ref, normed_ref = more[:6]
    scale_ref, result_ref, grad_ref, out_w_ref, sums_ref, resid, acc, pre, inner_w, sems = more[6:]
    w, last = pl.program_id(0), pl.num_programs(0) - 1
    count, width = acc.shape
    chunk = pre.shape[2]
    vec = lambda at: vec_ref[at : at + 1, :]
    half_of = lambda at: out_w_ref[pl.ds(pl.multiple_of(at * (width // 2), width // 2), width // 2), :]
    slots = [(stack, k) for stack in stacks for k in range(stack.shape[0])]
    deep = 4 * width // len(slots)
    thin = width // len(slots)

    def fetch(block):
        for slot, (stack, k) in enumerate(slots):

            @pl.when(part_ref[slot] == block)
            def _():
                start = pl.multiple_of(row_ref[slot] * deep, deep)
                pltpu.make_async_copy(
                    stack.at[k, pl.ds(0, deep), :],
                    inner_w.at[lax.rem(block, 2), pl.ds(start, deep), :],
                    sems.at[lax.rem(block, 2)],
                ).start()

    def fetch_outer(block):
        for slot, (stack, k) in enumerate(slots):

            @pl.when(row_ref[slot] // 2 == block)
            def _():
                start = lax.rem(row_ref[slot], 2) * 4 * deep + part_ref[slot] * deep
                pltpu.make_async_copy(
                    stack.at[k, pl.ds(stack.shape[1] - deep, deep), :],
                    outer_w_ref.at[pl.ds(pl.multiple_of(start, deep), deep), :],
                    sems.at[3],
                ).start()

    def arrived(block):
        target = inner_w.at[lax.rem(block, 2)]
        pltpu.make_async_copy(target, target, sems.at[lax.rem(block, 2)]).wait()

    @pl.when(w == 0)
    def _():
        for slot, (stack, k) in enumerate(slots):
            start = pl.multiple_of(row_ref[slot] * 4 * thin + part_ref[slot] * thin, thin)
            pltpu.make_async_copy(
                stack.at[k, pl.ds(deep, thin), :], out_w_ref.at[pl.ds(start, thin), :], sems.at[2]
            ).start()
        fetch(w)
        pltpu.make_async_copy(out_w_ref, out_w_ref, sems.at[2]).wait()
        acc[...] = jnp.dot(mine_ref[...], half_of(core_ref[0]), preferred_element_type=F32)
        acc[...] += jnp.dot(theirs_ref[...], half_of(1 - core_ref[0]), preferred_element_type=F32)

        def enter(part):
            normed, scale = normalize(acc[part, :] + vec(2) + rows_ref[part, :].astype(F32))
            normed_ref[part, :] = normed.astype(BF16)
            scale_ref[part, :] = scale
            hidden = normed * vec(3) + vec(4)
            resid[part, :] = hidden + vec(5)
            hidden_ref[part, :] = hidden.astype(BF16)

        in_parts(count, enter)

    fetch_outer(w)
    arrived(w)

    @pl.when(w < last)
    def _():
        fetch(w + 1)

    now = lax.rem(w, 2)
    inner_out_ref[...] = inner_w[now]
    bias = vec_ref[pl.ds(8 + w, 1), :]

    def expand(n):
        cut = slice(n * chunk, (n + 1) * chunk)
        weight = inner_w[now, :, cut]
        pre[n % 2] = jnp.dot(hidden_ref[...], weight, preferred_element_type=F32)

    def bend(n):
        cut = slice(n * chunk, (n + 1) * chunk)
        for at in range(0, count, TILE):
            part = slice(at, at + TILE)
            active, slope = gelu_and_slope(pre[n % 2, part, :] + bias[:, cut])
            active_ref[part, cut] = active.astype(BF16)
            slope_ref[part, cut] = slope.astype(BF16)

    chunks = width // chunk
    expand(0)
    for n in range(1, chunks):
        expand(n)
        bend(n - 1)
    bend(chunks - 1)
    pltpu.make_async_copy(outer_w_ref, outer_w_ref, sems.at[3]).wait()

    def contract():
        weight = outer_w_ref[...]
        return jnp.dot(active_ref[...], weight, preferred_element_type=F32)

    @pl.when(w == 0)
    def _():
        acc[...] = contract()

    @pl.when(w > 0)
    def _():
        acc[...] += contract()

    @pl.when(w == last)
    def _():
        sums_ref[...] = jnp.zeros_like(sums_ref)

        def leave(part):
            normed, scale = normalize(resid[part, :] + acc[part, :])
            result_ref[part, :] = (normed * vec(6) + vec(7)).astype(BF16)
            cotan = cotan_ref[part, :].astype(F32)
            grad = norm_back(cotan * vec(6), normed, scale).astype(BF16)
            grad_ref[part, :] = grad
            sums_ref[0:1, :] += total_rows(cotan * normed)
            sums_ref[1:2, :] += total_rows(cotan)
            sums_ref[2:3, :] += total_rows(grad.astype(F32))

        in_parts(count, leave)


def ffn_back_kernel(
    core_ref,
    grad_ref,
    slope_ref,
    normed_ref,
    scale_ref,
    vec_ref,
    out_w_ref,
    inner_w_ref,
    outer_w_ref,
    after_ref,
    pre_grad_ref,
    branch_ref,
    mine_ref,
    theirs_ref,
    sums_ref,
    acc,
    pre,
):
    w = pl.program_id(0)
    count, width = acc.shape
    chunk = pre.shape[2]
    vec = lambda at: vec_ref[at : at + 1, :]

    @pl.when(w == 0)
    def _():
        sums_ref[...] = jnp.zeros_like(sums_ref)

    def pull(n):
        weight = outer_w_ref[n * chunk : (n + 1) * chunk, :]
        pre[n % 2] = lax.dot_general(grad_ref[...], weight, NT, preferred_element_type=F32)

    def bend(n):
        cut = slice(n * chunk, (n + 1) * chunk)
        sums = jnp.zeros((8, chunk), F32)
        for at in range(0, count, TILE):
            part = slice(at, at + TILE)
            back = pre[n % 2, part, :].astype(BF16).astype(F32) * slope_ref[part, cut].astype(F32)
            back = back.astype(BF16)
            pre_grad_ref[part, cut] = back
            sums += jnp.sum(back.astype(F32).reshape(TILE // 8, 8, chunk), axis=0)
        sums_ref[pl.ds(4 + w, 1), cut] += total_rows(sums)

    chunks = width // chunk
    pull(0)
    for n in range(1, chunks):
        pull(n)
        bend(n - 1)
    bend(chunks - 1)

    def contract():
        weight = inner_w_ref[...]
        return lax.dot_general(pre_grad_ref[...], weight, NT, preferred_element_type=F32)

    @pl.when(w == 0)
    def _():
        acc[...] = contract()

    @pl.when(w > 0)
    def _():
        acc[...] += contract()

    @pl.when(w == pl.num_programs(0) - 1)
    def _():
        def leave(part):
            through = acc[part, :].astype(BF16).astype(F32) + grad_ref[part, :].astype(F32)
            normed = normed_ref[part, :].astype(F32)
            branch = norm_back(through * vec(3), normed, scale_ref[part, :]).astype(BF16)
            branch_ref[part, :] = branch
            sums_ref[0:1, :] += total_rows(through * normed)
            sums_ref[1:2, :] += total_rows(through)
            sums_ref[2:3, :] += total_rows(branch.astype(F32))

        in_parts(count, leave)
        part = width // 2
        for out, at in ((mine_ref, core_ref[0]), (theirs_ref, 1 - core_ref[0])):
            weight = out_w_ref[pl.ds(pl.multiple_of(at * part, part), part), :]
            out[...] = lax.dot_general(
                branch_ref[...], weight, NT, preferred_element_type=F32
            ).astype(BF16)


def ffn_call(kernel, scalars, ins, anys, outs, scratch, width, steps, room, name):
    def spec(shape):
        if shape[1] == steps * width:
            return pl.BlockSpec((shape[0], width), lambda w: (0, w))
        if shape[0] == steps * width:
            return pl.BlockSpec((width, width), lambda w: (w, 0))
        return pl.BlockSpec(shape, lambda w: (0, 0), pipeline_mode=pl.Buffered(1))

    return pl.pallas_call(
        kernel,
        grid=(steps,),
        in_specs=[pl.BlockSpec(memory_space=pltpu.SMEM)] * len(scalars)
        + [spec(a.shape) for a in ins]
        + [pl.BlockSpec(memory_space=pl.ANY)] * len(anys),
        out_specs=[spec(shape) for shape, kind in outs],
        out_shape=[jax.ShapeDtypeStruct(shape, kind) for shape, kind in outs],
        scratch_shapes=scratch,
        compiler_params=pltpu.CompilerParams(vmem_limit_bytes=room * 1024 * 1024),
        cost_estimate=weight_of(40),
        name=name,
    )(*scalars, *ins, *anys)


def ffn(core, places, mine, theirs, rows, cotan, vec, stacks):
    count, width = rows.shape
    units = 4 * width
    low = (rows.shape, BF16)
    outs = [((count, units), BF16)] * 2 + [((width, units), BF16), ((units, width), BF16)]
    outs += [low, low, ((count, 1), F32), low, low, ((width, width), BF16), ((8, width), F32)]
    scratch = [
        pltpu.VMEM((count, width), F32),
        pltpu.VMEM((count, width), F32),
        pltpu.VMEM((2, count, 256), F32),
        pltpu.VMEM((2, width, width), BF16),
        pltpu.SemaphoreType.DMA((4,)),
    ]
    tables = [jnp.stack([p[axis] for p in places]).astype(jnp.int32) for axis in range(2)]
    kernel = functools.partial(ffn_kernel, len(stacks))
    ins = [mine, theirs, rows, cotan, vec]
    return ffn_call(kernel, [core, *tables], ins, stacks, outs, scratch, width, 4, 58, "ffn")


def ffn_back(core, grad, slope, normed, scale, vec, out_w, inner_w, outer_w, after):
    count, width = grad.shape
    part = ((count, width // 2), BF16)
    outs = [(slope.shape, BF16), (grad.shape, BF16), part, part, ((8, width), F32)]
    scratch = [pltpu.VMEM((count, width), F32), pltpu.VMEM((2, count, 256), F32)]
    ins = [grad, slope, normed, scale, vec, out_w, inner_w, outer_w]
    return ffn_call(
        ffn_back_kernel, [core], ins, after, outs, scratch, width, 4, 44, "ffn_back"
    )


def product_kernel(count, stacked, after, where_ref, *refs):
    lefts, right_ref, out_ref = refs[:count], refs[count], refs[count + 1 + after]
    if not stacked:
        total, rows = None, lefts[0].shape[0]
        for n, left_ref in enumerate(lefts):
            right = right_ref[n * rows : (n + 1) * rows, :]
            part = lax.dot_general(left_ref[...], right, TN, preferred_element_type=F32)
            total = part if n == 0 else total + part
        out_ref[...] = total.astype(BF16)
        return
    for n, left_ref in enumerate(lefts):

        @pl.when(pl.program_id(0) == n)
        def _():
            out_ref[...] = lax.dot_general(
                left_ref[...], right_ref[...], TN, preferred_element_type=F32
            ).astype(BF16)


def product(where, lefts, right, side, after=(), stacked=False):
    width = right.shape[1] // (1 if side is None else 2)
    tile = 512
    height = sum(left.shape[1] for left in lefts) if stacked else lefts[0].shape[1]
    micros = 2e-9 * height * width * right.shape[0] + 1
    half = lambda a, w: (0, 0 if side is None else (w[3] if side else 1 - w[3]))
    if stacked:
        left_place = lambda a, w: (0, 0)
        place = lambda a, w: (a + w[3] - 2 * a * w[3], 0)
    else:
        left_place = lambda a, w: (0, a)
        place = lambda a, w: (a, 0)
    return pl.pallas_call(
        functools.partial(product_kernel, len(lefts), stacked, len(after)),
        grid_spec=pltpu.PrefetchScalarGridSpec(
            num_scalar_prefetch=1,
            grid=(height // tile,),
            in_specs=[pl.BlockSpec((left.shape[0], tile), left_place) for left in lefts]
            + [pl.BlockSpec((right.shape[0], width), half, pipeline_mode=pl.Buffered(1))]
            + [pl.BlockSpec(memory_space=pl.ANY)] * len(after),
            out_specs=pl.BlockSpec((tile, width), place),
        ),
        out_shape=jax.ShapeDtypeStruct((height, width), BF16),
        compiler_params=pltpu.CompilerParams(vmem_limit_bytes=2 * SMALL_VMEM),
        cost_estimate=weight_of(micros),
        name="product",
    )(where, *[*lefts, right], *after)


def attend_kernel(held, seg_row_ref, seg_col_ref, qkv_ref, *rest):
    rest = rest[held:]
    out_refs, (lse_ref, bias_ref, stat_ref, score_ref, expo_ref) = rest[:2], rest[2:]
    half = qkv_ref.shape[2]
    pair = pl.program_id(1)
    length = bias_ref.shape[0]
    chunk = score_ref.shape[1]

    @pl.when(pair == 0)
    def _():
        bias_ref[...] = jnp.where(seg_col_ref[0] == seg_row_ref[0], 0.0, MASKED)
        stat_ref[...] = jnp.zeros_like(stat_ref)

    block = qkv_ref[:, 0].reshape(length, 3 * PAIR)
    q, k, v = (block[:, i * PAIR : (i + 1) * PAIR] for i in range(3))
    lane = lax.broadcasted_iota(jnp.int32, (length, PAIR), 1)
    low = lane < HD
    zero, one = jnp.zeros_like(q), jnp.ones_like(v)
    q_heads = [jnp.where(low, q, zero), jnp.where(low, zero, q)]
    v_heads = [jnp.where(low, v, one), jnp.where(low, one, v)]
    lane, low = lane[:chunk], low[:chunk]

    def score(step):
        c, h = divmod(step, 2)
        score_ref[step % 2] = lax.dot_general(
            q_heads[h][c * chunk : (c + 1) * chunk], k, NT, preferred_element_type=F32
        )

    def soften(step):
        c, h = divmod(step, 2)
        tops = []
        for at in range(0, chunk, TILE):
            rows = slice(c * chunk + at, c * chunk + at + TILE)
            s = score_ref[step % 2, at : at + TILE, :] + bias_ref[rows, :]
            top = jnp.max(s, axis=1, keepdims=True)
            expo_ref[step % 2, at : at + TILE, :] = jnp.exp(s - top).astype(BF16)
            tops.append(top)
        return jnp.concatenate(tops, 0)

    def mix(step):
        return jnp.dot(expo_ref[step % 2], v_heads[step % 2], preferred_element_type=F32)

    def finish(c, got, tops):
        rows = slice(c * chunk, (c + 1) * chunk)
        total = jnp.where(low, got[1], got[0])
        mixed = jnp.where(low, got[0], got[1]) / pltpu.roll(total, HD, 1)
        log = jnp.log(total)
        stat = stat_ref[rows, :]
        stat = jnp.where(lane == 2 * pair, tops[0] + log[:, HD : HD + 1], stat)
        stat_ref[rows, :] = jnp.where(lane == 2 * pair + 1, tops[1] + log[:, :1], stat)
        part, at = divmod(c * chunk, half)
        out_refs[part][0, at : at + chunk, :] = mixed.astype(BF16)

    steps = 2 * length // chunk
    tops, got = [], []
    score(0)
    for step in range(steps):
        if step + 1 < steps:
            score(step + 1)
        tops.append(soften(step))
        got.append(mix(step))
        if step % 2:
            finish(step // 2, got[-2:], tops[-2:])

    @pl.when(pair == pl.num_programs(1) - 1)
    def _():
        lse_ref[0] = jnp.transpose(stat_ref[...])[: lse_ref.shape[1]]


def attend_back_kernel(first_pair, after, *refs):
    seg_row_ref, seg_col_ref, qkv_ref, out_a, out_b, grad_a, grad_b, lse_ref = refs[:8]
    dqkv_ref, sums_ref, bias_ref, ds_ref, score_ref, slope_ref, prob_ref = refs[8 + after :]
    pair = pl.program_id(1)
    length = bias_ref.shape[0]
    half = qkv_ref.shape[2]
    chunk = score_ref.shape[1]

    @pl.when(pair == 0)
    def _():
        bias_ref[...] = jnp.where(seg_col_ref[0] == seg_row_ref[0], 0.0, MASKED)

    @pl.when((pair == 0) & (pl.program_id(0) == 0))
    def _():
        sums_ref[...] = jnp.zeros_like(sums_ref)

    block = qkv_ref[:, 0].reshape(length, 3 * PAIR)
    q, k, v = (block[:, i * PAIR : (i + 1) * PAIR] for i in range(3))
    out = jnp.concatenate([out_a[0], out_b[0]], 0)
    grad = jnp.concatenate([grad_a[0], grad_b[0]], 0)
    low = lax.broadcasted_iota(jnp.int32, (length, PAIR), 1) < HD
    zero = jnp.zeros_like(q)
    heads = lambda array: [jnp.where(low, array, zero), jnp.where(low, zero, array)]
    q_heads, k_heads, g_heads = heads(q), heads(k), heads(grad)
    product = jnp.transpose(out.astype(F32) * grad.astype(F32))
    chunks = length // chunk
    deltas = [total_rows(product[h * HD : (h + 1) * HD]) for h in range(2)]
    stats = [lse_ref[0, pl.ds(2 * (first_pair + pair) + h, 1), :] for h in range(2)]

    def score(step):
        h, c = divmod(step, chunks)
        rows = slice(c * chunk, (c + 1) * chunk)
        score_ref[step % 2] = lax.dot_general(k[rows], q_heads[h], NT, preferred_element_type=F32)
        slope_ref[step % 2] = lax.dot_general(v[rows], g_heads[h], NT, preferred_element_type=F32)

    def bend(step):
        h, c = divmod(step, chunks)
        for at in range(0, chunk, TILE):
            rows = slice(c * chunk + at, c * chunk + at + TILE)
            part = slice(at, at + TILE)
            p = jnp.exp(score_ref[step % 2, part, :] + bias_ref[rows, :] - stats[h])
            prob_ref[step % 2, part, :] = p.astype(BF16)
            ds_ref[h, rows, :] = (p * (slope_ref[step % 2, part, :] - deltas[h])).astype(BF16)

    steps = 2 * chunks
    dk, dv = [None] * chunks, [None] * chunks
    dq = None
    score(0)
    for step in range(steps):
        h, c = divmod(step, chunks)
        if step + 1 < steps:
            score(step + 1)
        bend(step)
        rows = slice(c * chunk, (c + 1) * chunk)
        v_part = jnp.dot(prob_ref[step % 2], g_heads[h], preferred_element_type=F32)
        k_part = jnp.dot(ds_ref[h, rows, :], q_heads[h], preferred_element_type=F32)
        if h == 0:
            dk[c], dv[c] = k_part, v_part
        else:
            part, at = c * chunk // half, c * chunk % half
            dqkv_ref[part, 0, at : at + chunk, PAIR : 2 * PAIR] = (dk[c] + k_part).astype(BF16)
            dv[c] = (dv[c] + v_part).astype(BF16)
            dqkv_ref[part, 0, at : at + chunk, 2 * PAIR :] = dv[c]
        if c == chunks - 1:
            part = lax.dot_general(ds_ref[h], k_heads[h], TN, preferred_element_type=F32)
            dq = part if h == 0 else dq + part
    dq = (dq * HD**-0.5).astype(BF16)
    dqkv_ref[:, 0, :, :PAIR] = dq.reshape(-1, half, PAIR)
    sums = [total_rows(dq.astype(F32)), sum(total_rows(part.astype(F32)) for part in dv)]
    sums_ref[0:1, pl.ds(pl.multiple_of(pair * PAIR, PAIR), PAIR)] += sums[0]
    sums_ref[1:2, pl.ds(pl.multiple_of(pair * PAIR, PAIR), PAIR)] += sums[1]


def attention_call(
    kernel, seg, arrays, pairs, outs, scratch, name, first=0, after=(), seqs=None, held=()
):
    parts, count, half, columns = arrays[0].shape
    start, seqs = seqs or (0, count)
    micros = 6.5 * seqs if name == "attend" else 3.7 * seqs
    length = parts * half

    def spec(array, first):
        shape = array.shape
        if len(shape) == 4:
            return pl.BlockSpec(
                (parts, 1, half, 3 * PAIR), lambda s, p: (0, start + s, 0, first + p)
            )
        if len(shape) == 3 and shape[1] == half:
            return pl.BlockSpec((1, half, PAIR), lambda s, p: (start + s, 0, first + p))
        if len(shape) == 3:
            return pl.BlockSpec((1,) + shape[1:], lambda s, p: (start + s, 0, 0))
        return pl.BlockSpec(shape, lambda s, p: (0, 0))

    operands = [seg[:, None, :], seg[:, :, None]] + arrays
    return pl.pallas_call(
        kernel,
        grid=(seqs, pairs),
        in_specs=[spec(a, first) for a in operands]
        + [pl.BlockSpec(memory_space=pl.ANY)] * (len(held) + len(after)),
        out_specs=[spec(a, 0) for a in outs],
        out_shape=outs,
        scratch_shapes=scratch(length),
        input_output_aliases={len(operands) + n: n for n in range(len(held))},
        compiler_params=pltpu.CompilerParams(vmem_limit_bytes=SMALL_VMEM),
        cost_estimate=weight_of(micros),
        name=name,
    )(*operands, *held, *after)


def attend(qkv, seg, seqs, held, after):
    parts, count, half, columns = qkv.shape
    pairs = columns // (3 * PAIR)
    outs = [
        jax.ShapeDtypeStruct((count, half, columns // 3), BF16),
        jax.ShapeDtypeStruct((count, half, columns // 3), BF16),
        jax.ShapeDtypeStruct((count, 2 * pairs, parts * half), F32),
    ]
    scratch = lambda length: [
        pltpu.VMEM((length, length), F32),
        pltpu.VMEM((length, PAIR), F32),
        pltpu.VMEM((2, 128, length), F32),
        pltpu.VMEM((2, 128, length), BF16),
    ]
    kernel = functools.partial(attend_kernel, len(held) + len(after))
    return attention_call(
        kernel, seg, [qkv], pairs, outs, scratch, "attend", 0, after, seqs, held
    )


def attend_back(qkv, seg, out, grad, lse, first, pairs, after):
    outs = [
        jax.ShapeDtypeStruct(qkv.shape[:3] + (3 * PAIR * pairs,), BF16),
        jax.ShapeDtypeStruct((8, PAIR * pairs), F32),
    ]
    scratch = lambda length: [
        pltpu.VMEM((length, length), F32),
        pltpu.VMEM((2, length, length), BF16),
        pltpu.VMEM((2, 128, length), F32),
        pltpu.VMEM((2, 128, length), F32),
        pltpu.VMEM((2, 128, length), BF16),
    ]
    kernel = functools.partial(attend_back_kernel, first, len(after))
    arrays = [qkv, *out, *grad, lse]
    return attention_call(kernel, seg, arrays, pairs, outs, scratch, "attend_back", first, after)


def body(
    layer_input,
    segment_ids,
    out_cotangent,
    attn_master,
    inner_master,
    outer_master,
    vector_master,
    attn_moment,
    inner_moment,
    outer_moment,
    vector_moment,
    attn_square,
    inner_square,
    outer_square,
    vector_square,
):
    seqs, half, width = layer_input.shape
    count = seqs * half
    hidden_units = inner_master.shape[1]
    pairs = width // (2 * PAIR)
    part_cols = width // 2
    shards = lax.axis_size("shard")
    owned_rows = attn_master.shape[1]
    core = lax.axis_index("ctx")
    first = core == 0

    def own_half(array, axis):
        size = array.shape[axis] // 2
        return lax.dynamic_slice_in_dim(array, core * size, size, axis)

    def other_half(array, axis):
        size = array.shape[axis] // 2
        return lax.dynamic_slice_in_dim(array, (1 - core) * size, size, axis)

    def in_order(mine, theirs, axis):
        return jnp.concatenate(
            [jnp.where(first, mine, theirs), jnp.where(first, theirs, mine)], axis
        )

    rows = layer_input.reshape(count, width)
    rows_theirs = swap_cores(rows)
    square = is_square()
    o, i, y, inner = position()
    where = jnp.stack([o, i, y, core]).astype(jnp.int32)

    piece = own_half(attn_master[:3], 2).astype(BF16).reshape(3, owned_rows, pairs, PAIR)
    piece = piece.transpose(1, 2, 0, 3).reshape(owned_rows, 3 * part_cols)
    vec_low = vector_master.astype(BF16)
    rider = vec_low[:2].reshape(1, -1)
    if square:
        piece = lax.dynamic_slice_in_dim(piece, y * (piece.shape[1] // 2), piece.shape[1] // 2, 1)
    rider = jnp.pad(rider, ((0, 15), (0, piece.shape[1] - rider.shape[1])))
    piece = jnp.concatenate([piece, rider], 0)

    def every_row(block):
        size = block.shape[0] // (lax.axis_size("replica") * 2)
        part = lax.dynamic_slice_in_dim(block, (2 * y + core) * size, size, 0).astype(BF16)
        return lax.all_gather(part, EVERY, axis=0, tiled=True)

    def placed(found, slots):
        chosen = jnp.stack([place[0] for place in slots[:shards]])
        chosen = (jnp.arange(shards)[:, None] == chosen[None, :]).astype(F32)
        return jnp.einsum("ps,srw->rpw", chosen, found.astype(F32)).reshape(-1, width)

    if square:
        q = 2 * core + y
        vec_rows = jnp.pad(vec_low.reshape(-1), (0, 16 * width - vec_low.size)).reshape(16, width)
        quarter = jnp.concatenate(
            [
                lax.dynamic_slice_in_dim(inner_master, q * width, width, 1).astype(BF16),
                lax.dynamic_slice_in_dim(
                    attn_master[3], q * (owned_rows // 4), owned_rows // 4, 0
                ).astype(BF16),
                vec_rows,
                lax.dynamic_slice_in_dim(
                    outer_master, q * (outer_master.shape[0] // 4), outer_master.shape[0] // 4, 0
                ).astype(BF16),
            ],
            0,
        )
        line = jnp.stack([piece] + [shift_outer(piece, -k) for k in range(1, OUTER)])
        near_x, near_y = shift_inner(line, 1), shift_replica(line, 1)
        (quarter,) = relay(where, [quarter], (line,))
        across = swap_outer(quarter, 2)
        two = (OUTER // 2,)
        far = small_call(
            halves_kernel, where, [near_x, near_y], [two + piece.shape] * 2, (), "halves"
        )
        stacks = [line, near_x, near_y, shift_inner(far[0], 1), shift_replica(far[1], 1)]
        (pair,) = small_call(
            pair_kernel, where, [quarter, across], [two + quarter.shape], tuple(stacks[3:]), "pair"
        )
        places = quarter_places([lax.rem(o + k, OUTER) for k in range(OUTER)])
        other_pair = swap_outer(pair, 1)
        pair_x, pair_y = shift_inner(pair, 1), shift_replica(pair, 1)
        done = (pair,)
    else:
        stacks = [item[None] for item in ring_gather(piece)]
        places = [(owner, 0) for owner in slot_owners()]
        wide = hidden_units // width
        inner_w = every_row(inner_master).reshape(8, -1, wide, width).transpose(0, 2, 1, 3)
        slots = [inner_w.reshape(PARTS, -1, width), every_row(attn_master[3]).reshape(PARTS, -1, width)]
        slots = jnp.pad(jnp.concatenate(slots, 1), ((0, 0), (0, 16), (0, 0)))
        outer_w = every_row(outer_master).reshape(PARTS, -1, width)
        slots = jnp.concatenate([slots, outer_w], 1)
        wide_stacks = [slots[n : n + 2] for n in range(0, PARTS, 2)]
        wide_places = [(jnp.int32(n // 4), jnp.int32(n % 4)) for n in range(PARTS)]
        vec = lax.all_gather(vec_low, "shard", axis=1, tiled=True).astype(F32)
        done = ()
    riders = jnp.concatenate([stack[:, owned_rows] for stack in stacks], 0)[:shards]
    riders = riders[:, : 2 * width // shards].reshape(shards, 2, -1)
    biases = placed(riders, places)

    halves = own_half(biases, 1).reshape(2, pairs, PAIR)
    bias = jnp.stack([halves[0], jnp.zeros_like(halves[0]), halves[1]], 1).reshape(1, -1)
    ones = jnp.ones((pairs, PAIR), F32)
    factor = jnp.stack([ones * HD**-0.5, ones, ones], 1).reshape(1, -1)
    qkv, qkv_w = project(rows, rows_theirs, stacks, places, bias, factor, done)
    qkv = qkv.reshape(2, seqs, half, 3 * part_cols)
    seg = jnp.concatenate([own_half(segment_ids, 1), other_half(segment_ids, 1)], 1)
    if square:
        (other_pair,) = relay(where, [other_pair], (qkv_w,))
        other_x, other_y = shift_inner(other_pair, 1), shift_replica(other_pair, 1)
        early = attend(qkv, seg, (0, seqs // 2), (), (other_pair,))
        near = [pair, other_pair, pair_x, other_x, pair_y, other_y]
        bulk, *relayed = small_call(
            bulk_kernel,
            where,
            near,
            [(12,) + quarter.shape, pair.shape, pair.shape],
            (early[0],),
            "bulk",
        )
        far_pair = [shift_inner(relayed[0], 1), shift_replica(relayed[1], 1)]
        near_rows = bulk[:8, 160:162].reshape(shards, -1)[:, : vec_low.size]
        both = line_order(o)
        places = quarter_places(both[0] + both[1])
        vec = placed(near_rows.reshape((shards,) + vec_low.shape), places)
        wide_places = [(row, 2 * core + side) for row, side in places]
        wide_places += [(row, 2 * (1 - core) + side) for row, side in places]
    else:
        early = attend(qkv, seg, (0, seqs // 2), (), ())
    mixed_mine, mixed_sent, lse = attend(qkv, seg, (seqs // 2, seqs - seqs // 2), early, ())
    if square:
        (far_bulk,) = small_call(
            bulk_kernel, where, far_pair, [(4,) + quarter.shape], (mixed_mine,), "bulk"
        )
        wide_stacks = [bulk, far_bulk, swap_cores(bulk), swap_cores(far_bulk)]
    flat = lambda array: array.reshape(count, part_cols)
    deep = lambda array: array.reshape(seqs, half, part_cols)
    heads_mine, heads_theirs = flat(mixed_mine), swap_cores(flat(mixed_sent))

    cotan = out_cotangent.reshape(count, width)
    core_at = jnp.full((1,), core, jnp.int32)
    forward = ffn(core_at, wide_places, heads_mine, heads_theirs, rows, cotan, vec, wide_stacks)
    active, slope, inner_w, outer_w, hidden_low, normed, scale, result = forward[:8]
    ffn_grad, out_w, sums_two = forward[8:]

    by_shard = lambda array: array.reshape(shards, -1, array.shape[1])

    outer_sent = product(where, [active], ffn_grad, 0)
    outer_kept = product(where, [active], ffn_grad, 1, (outer_sent,))
    outer_chips = [by_shard(outer_kept), by_shard(swap_cores(outer_sent))]
    done = (outer_kept,)
    if square:
        outer = Sum(where, outer_chips)
        done = outer.merge()
    pre_grad, branch_grad, mine, sent, sums_one = ffn_back(
        core_at, ffn_grad, slope, normed, scale, vec, out_w, inner_w, outer_w, done[:1]
    )
    got = swap_cores(sent)
    mixed_grad = [deep(mine), deep(got)]
    done = outer.plane((pre_grad,)) if square else ()
    heads = [heads_mine, heads_theirs]
    inner_kept = product(where, [hidden_low], pre_grad, 1, done)
    done = outer.cross((inner_kept,)) if square else (inner_kept,)
    inner_sent = product(where, [hidden_low], pre_grad, 0, done)
    out_sent = product(where, heads, branch_grad, 0, (inner_sent,), True)
    out_kept = product(where, heads, branch_grad, 1, (out_sent,), True)
    inner_chips = [by_shard(inner_kept), by_shard(swap_cores(inner_sent))]
    out_chips = [by_shard(out_kept), by_shard(swap_cores(out_sent))]

    def back(first, after):
        grad, sums = attend_back(
            qkv, seg, (mixed_mine, mixed_sent), mixed_grad, lse, first, pairs // 2, after
        )
        return grad.reshape(2 * count, -1), sums

    def vector_chip(sums_a, sums_b):
        blank = jnp.zeros((part_cols,), F32)
        ours = jnp.concatenate([sums_a, sums_b], 1)
        attn_biases = jnp.stack([in_order(ours[at], blank, 0) for at in range(2)])
        sums = [attn_biases, sums_one[2:3], sums_one[:2], sums_two[2:3], sums_two[:2]]
        sums = jnp.concatenate(sums + [sums_one[4:8]], 0)
        sums = sums.reshape(-1, shards, width // shards).transpose(1, 0, 2)
        sums = jnp.pad(sums, ((0, 0), (0, owned_rows - sums.shape[1]), (0, 0)))
        return sums.astype(BF16)

    outer_states = (outer_master, outer_moment, outer_square)
    inner_states = (inner_master, inner_moment, inner_square)
    attn_states = (attn_master, attn_moment, attn_square)
    if square:
        inner = Sum(where, inner_chips)
        done = inner.merge((out_kept,))
        done = outer.turn(done)
        grad_a, sums_a = back(0, done)
        done = outer.line((grad_a,))
        ours = by_shard(product(where, [rows, rows_theirs], grad_a, None, done))
        done = inner.plane((ours,))
        sum_a = Sum(where, [ours], out_chips)
        done = sum_a.merge(done)
        grad_b, sums_b = back(pairs // 2, done)
        done = inner.cross((grad_b,))
        done = sum_a.plane(done)
        theirs_part = input_back(grad_a, grad_b, qkv_w, (), done)
        ours = by_shard(product(where, [rows, rows_theirs], grad_b, None, (theirs_part,)))
        sum_b = Sum(where, [ours], [vector_chip(sums_a, sums_b)])
        done = sum_a.cross((ours,))
        done = sum_b.merge(done)
        outer_new = update(where, outer_states, [outer.shares], done)
        input_grad = input_back(
            grad_a, grad_b, qkv_w, (branch_grad, swap_cores(theirs_part)), (outer_new[0],)
        )
        done = sum_b.plane((input_grad,))
        done = inner.turn(done)
        done = sum_a.turn(done)
        done = sum_b.cross(done)
        done = inner.line(done)
        done = sum_b.turn(done)
        inner_new = update(where, inner_states, [inner.shares], done)
        done = sum_a.line((inner_new[0],))
        sum_b.line(done)
        attn_shares = [sum_a.shares, sum_b.shares]
        vector_shares = [
            jnp.concatenate(
                [
                    jnp.where(y == 0, sum_b.shares[at], sum_b.shares[at + 1])[0],
                    jnp.where(y == 0, sum_b.shares[at + 1], sum_b.shares[at])[0],
                ],
                0,
            )
            for at in (0, 2)
        ]
    else:
        grad_a, sums_a = back(0, ())
        grad_b, sums_b = back(pairs // 2, ())
        theirs_part = input_back(grad_a, grad_b, qkv_w, (), ())
        added = (branch_grad, swap_cores(theirs_part))
        input_grad = input_back(grad_a, grad_b, qkv_w, added, ())
        outer_new = update(where, outer_states, [sum_apart(add_low(*outer_chips))])
        inner_new = update(where, inner_states, [sum_apart(add_low(*inner_chips))])
        ours = [by_shard(product(where, [rows, rows_theirs], grad, None)) for grad in (grad_a, grad_b)]
        chip_a = jnp.concatenate([ours[0], add_low(*out_chips)], 2)
        chip_b = jnp.concatenate([ours[1], vector_chip(sums_a, sums_b)], 2)
        attn_shares = [sum_apart(chip_a), sum_apart(chip_b)]
        vector_shares = [share[0] for share in attn_shares[1]]
    attn_new = update(where, attn_states, attn_shares)
    cut = grad_b.shape[1]
    vector_sum = sum(share[: vec_low.shape[0], cut:].astype(F32) for share in vector_shares)
    vector_new = adamw(vector_sum, vector_moment, vector_square, vector_master, RATE_VECTOR)
    vector_new = vector_new + (vector_new[2].astype(BF16),)
    news = (attn_new, inner_new, outer_new, vector_new)
    updates = [[new[at] for new in news] for at in range(4)]
    return (
        result.reshape(seqs, half, width).astype(BF16),
        input_grad.reshape(seqs, half, width),
        *[item for kind in updates for item in kind],
    )


def solution(mesh):
    tokens = P(("replica", "shard"), "ctx", None)
    states = (P(None, "shard", None), P("shard", None), P("shard", None), P(None, "shard"))
    in_specs = (tokens, P(("replica", "shard"), None), tokens) + states * 3
    out_specs = (tokens, tokens) + states * 4
    return jax.shard_map(body, mesh=mesh, in_specs=in_specs, out_specs=out_specs, check_vma=False)
```
